32 devices in a mesh: fsdp: 8 (over z, y), rep: 4 (over x, core).
Axes of the slice: x: 2, y: 2, z: 4, core: 2. Of those that a mesh axis runs over, the one named last changes fastest.
Arguments:
- tokens: bfloat16 [2, 32, 128, 1024], P(None, 'rep', 'fsdp'), may hold values from -6 to 6
- cotangent: bfloat16 [2, 32, 128, 1024], P(None, 'rep', 'fsdp'), may hold values from -6 to 6
- deal: int32 [2, 4, 8], P(None, 'rep'), may hold values from 0 to 7, each once within a row
- lengths: int32 [2, 4, 8], P(None, 'rep', 'fsdp'), may hold values from 16 to 128, as said below
- ln1_gain: float32 [1024], P('fsdp'), may hold values from 0.5 to 1.5
- w_qkv: float32 [1024, 3072], P('fsdp'), may hold values from -0.1875 to 0.1875
- w_out: float32 [1024, 1024], P('fsdp'), may hold values from -2 to 2
- ln2_gain: float32 [1024], P('fsdp'), may hold values from 0.5 to 1.5
- w_in: float32 [1024, 5248], P('fsdp'), may hold values from -0.1875 to 0.1875
- w_down: float32 [2624, 1024], P('fsdp'), may hold values from -0.125 to 0.125
Outputs:
- mixed: bfloat16 [2, 32, 128, 1024], P(None, 'rep', 'fsdp')
- grad_tokens: bfloat16 [2, 32, 128, 1024], P(None, 'rep', 'fsdp')
- grad_ln1: float32 [1024], P('fsdp')
- grad_qkv: float32 [1024, 3072], P('fsdp')
- grad_out: float32 [1024, 1024], P('fsdp')
- grad_ln2: float32 [1024], P('fsdp')
- grad_in: float32 [1024, 5248], P('fsdp')
- grad_down: float32 [2624, 1024], P('fsdp')
The draws below stay inside these ranges and needn't reach their ends.
Inputs may be any that keep to these rules, and one draw needn't show every extreme that they name: For every micro-batch and replica, deal lists each fsdp index exactly once. `lengths`: in every micro-batch and replica one sequence has length exactly 128.
All inputs are finite; a program needn't handle non-finite values.
Results may differ from the reference program's by a relative error of at most 0.017.
The reference program's roundings to bfloat16 on the way count: a program that leaves them out, or rounds other values in their place, can miss the bound.
Values may be sent and summed in bfloat16 or wider, within the bound.
A program may use at most 192 MiB of HBM per device.

```python
import jax
import jax.numpy as jnp
from jax import lax

D = 1024
HEADS = 16
FF = 2624
SLOT = 128
MICRO = 2
SEQS = 32
N_FSDP = 8
N_REP = 4


def draw_lengths(key, part):
    key = jax.random.fold_in(key, 7)
    first_key, second_key = jax.random.split(key)
    ragged = jax.random.randint(first_key, (MICRO, N_REP, N_FSDP), max(1, SLOT // 8), SLOT + 1)
    longest = jax.random.randint(second_key, (MICRO, N_REP, 1), 0, N_FSDP)
    places = jnp.arange(N_FSDP, dtype=jnp.int32)[None, None, :]
    return jnp.where(places == longest, SLOT, ragged).astype(jnp.int32)


def steps_of(own_key, shape, cuts, least, high):
    gain = 1.0
    for dim, shards_of in cuts:
        steps = jax.random.uniform(jax.random.fold_in(jax.random.fold_in(own_key, 6), dim), (shards_of,), jnp.float32, least / len(cuts), high / len(cuts))
        gain = gain * jnp.repeat(jnp.exp(steps), shape[dim] // shards_of).reshape((-1,) + (1,) * (len(shape) - 1 - dim))
    return gain


def centred(stream_key, extent, scale, most, shards=(), held_as=jnp.bfloat16):
    drawn = scale * jax.random.normal(stream_key, extent, jnp.float32)
    if shards:
        drawn = drawn * steps_of(stream_key, extent, shards, -0.22, 0.18)
    return jnp.clip(drawn, -most, most).astype(held_as)


def setup_inputs(seed: int = 0) -> dict:
    streams_of = jax.random.split(jax.random.key(seed), 11)
    tokens = centred(streams_of[0], (MICRO, SEQS, SLOT, D), 1.0, 6.0, ((1, 4), (2, 8)))
    cotangent = centred(streams_of[1], (MICRO, SEQS, SLOT, D), 1.0, 6.0, ((1, 4), (2, 8)))
    deal = jax.vmap(lambda own: jax.random.permutation(own, N_FSDP))(jax.random.split(streams_of[2], MICRO * N_REP)).reshape((MICRO, N_REP, N_FSDP)).astype(jnp.int32)
    lengths = draw_lengths(jax.random.fold_in(streams_of[10], 71), 0)
    ln1_gain = jnp.clip(1.0 + 0.1 * jax.random.normal(streams_of[4], (D,), jnp.float32), 0.5, 1.5)
    w_qkv = centred(streams_of[5], (D, 3 * D), D ** -0.5, 0.1875, ((0, 8),), jnp.float32)
    w_out = centred(streams_of[6], (D, D), (max(1, D // 128)) ** -0.5, 2.0, ((0, 8),), jnp.float32)
    ln2_gain = jnp.clip(1.0 + 0.1 * jax.random.normal(streams_of[7], (D,), jnp.float32), 0.5, 1.5)
    w_in = centred(streams_of[8], (D, 2 * FF), D ** -0.5, 0.1875, ((0, 8),), jnp.float32)
    w_down = centred(streams_of[9], (FF, D), FF ** -0.5, 0.125, ((0, 8),), jnp.float32)
    return {"tokens": tokens, "cotangent": cotangent, "deal": deal, "lengths": lengths, "ln1_gain": ln1_gain, "w_qkv": w_qkv, "w_out": w_out, "ln2_gain": ln2_gain, "w_in": w_in, "w_down": w_down}


rope_base = 160000.0
norm_eps = 1e-05
seq_group = 8

@jax.custom_vjp
def low(v):
    return lax.optimization_barrier(v.astype(jnp.bfloat16)).astype(jnp.float32)

@jax.custom_vjp
def low_back(v):
    return v

def low_keep(v):
    return (low(v), None)

def low_pass(kept, grad):
    return (grad,)

def back_keep(v):
    return (v, None)

def back_low(kept, grad):
    return (low(grad),)
low.defvjp(low_keep, low_pass)
low_back.defvjp(back_keep, back_low)

def layer_norm(values, norm_gain):
    center = values - lax.optimization_barrier(jnp.mean(values, axis=-1, keepdims=True))
    spread = lax.optimization_barrier(jnp.mean(center * center, axis=-1, keepdims=True))
    return center * lax.rsqrt(spread + norm_eps) * norm_gain

def rope_tables(slot_count, head_size):
    half_size = head_size // 2
    frequency = rope_base ** (-(jnp.arange(half_size, dtype=jnp.float32) * 2.0 / head_size))
    angles = jnp.arange(slot_count, dtype=jnp.float32)[:, None] * frequency[None, :]
    return (jnp.cos(angles), jnp.sin(angles))

def rotate(tensor, cosine_table, sine_table):
    half_size = tensor.shape[-1] // 2
    front_half = tensor[..., :half_size]
    back_half = tensor[..., half_size:]
    cos_wide = cosine_table[:, None, :]
    sin_wide = sine_table[:, None, :]
    return jnp.concatenate([front_half * cos_wide - back_half * sin_wide, back_half * cos_wide + front_half * sin_wide], axis=-1)

def gated_gelu(hidden):
    half_size = hidden.shape[-1] // 2
    return jax.nn.gelu(hidden[..., :half_size], approximate=False) * hidden[..., half_size:]

def group_layer(weights, block_tokens, block_lengths):
    gain_one, qkv_weight, out_weight, gain_two, in_weight, down_weight = weights
    groups, slot_count, model_width = block_tokens.shape
    head_count = HEADS
    head_size = model_width // head_count
    highest = lax.Precision.HIGHEST
    live_mask = (jnp.arange(slot_count, dtype=jnp.int32)[None, :] < block_lengths[:, None]).astype(jnp.float32)
    normed = low(layer_norm(block_tokens, gain_one))
    packed = low_back(jnp.einsum('gsd,de->gse', normed, qkv_weight, precision=highest))
    sections = packed.reshape(groups, slot_count, 3, head_count, head_size)
    cosine_table, sine_table = rope_tables(slot_count, head_size)
    queries = low(rotate(sections[:, :, 0], cosine_table, sine_table))
    key_rows = low(rotate(sections[:, :, 1], cosine_table, sine_table))
    value_rows = low(sections[:, :, 2])
    scores = low_back(jnp.einsum('gqhd,gkhd->ghqk', queries, key_rows, precision=highest) * head_size ** (-0.5))
    scores = jnp.where(live_mask[:, None, None, :] > 0, scores, -1e+30)
    row_max = lax.optimization_barrier(jnp.max(scores, axis=-1, keepdims=True))
    exponent = jnp.exp(scores - row_max)
    attn_prob = exponent / lax.optimization_barrier(jnp.sum(exponent, axis=-1, keepdims=True))
    attended = jnp.einsum('ghqk,gkhd->gqhd', low(attn_prob), value_rows, precision=highest)
    attended = low(low_back(attended)).reshape(groups, slot_count, model_width)
    branch_one = low_back(jnp.einsum('gse,ed->gsd', attended, out_weight, precision=highest))
    residual = block_tokens + live_mask[..., None] * branch_one
    ffn_input = low(layer_norm(residual, gain_two))
    ffn_hidden = low_back(jnp.einsum('gsd,df->gsf', ffn_input, in_weight, precision=highest))
    gated_out = low(gated_gelu(ffn_hidden))
    branch_two = low_back(jnp.einsum('gsf,fd->gsd', gated_out, down_weight, precision=highest))
    return residual + live_mask[..., None] * branch_two

def reference(tokens, cotangent, deal, lengths, ln1_gain, w_qkv, w_out, ln2_gain, w_in, w_down):
    micro_count, seq_count, slot_count, model_width = tokens.shape
    seq_lengths = jnp.take_along_axis(lengths, deal, axis=2).reshape(micro_count * seq_count)
    block_count = micro_count * seq_count // seq_group
    shape_blocks = (block_count, seq_group, slot_count, model_width)
    inputs = tokens.astype(jnp.float32).reshape(shape_blocks)
    block_lengths = seq_lengths.reshape(block_count, seq_group)
    layer_fn = jax.checkpoint(group_layer)

    def forward(stacked, *masters):
        rounded = tuple((low(master) for master in masters))
        return lax.map(lambda block_item: layer_fn(rounded, block_item[0], block_item[1]), (stacked, block_lengths))
    outputs, pullback = jax.vjp(forward, inputs, ln1_gain, w_qkv, w_out, ln2_gain, w_in, w_down)
    gradients = pullback(cotangent.astype(jnp.float32).reshape(shape_blocks))
    mixed = outputs.reshape(tokens.shape).astype(jnp.bfloat16)
    grad_tokens = gradients[0].reshape(tokens.shape).astype(jnp.bfloat16)
    return (mixed, grad_tokens, gradients[1], gradients[2], gradients[3], gradients[4], gradients[5], gradients[6])
```

```python
import functools

import jax
import jax.numpy as jnp
from jax import lax
from jax.experimental import pallas as pl
from jax.experimental.pallas import tpu as pltpu
from jax.sharding import PartitionSpec as P

HEADS = 16
ROPE_BASE = 160000.0
NORM_EPS = 1e-05
MESH = pl.DeviceIdType.MESH
MIB = 1 << 20
BF16 = jnp.bfloat16
F32 = jnp.float32


def rope_tables(slot_count, head_size):
    half_size = head_size // 2
    frequency = ROPE_BASE ** (-(jnp.arange(half_size, dtype=F32) * 2.0 / head_size))
    angles = jnp.arange(slot_count, dtype=F32)[:, None] * frequency[None, :]
    return jnp.cos(angles), jnp.sin(angles)


def rotate(values, cosine, sine):
    front, back = jnp.split(values, 2, axis=-1)
    cosine, sine = cosine[:, None, :], sine[:, None, :]
    return jnp.concatenate([front * cosine - back * sine, back * cosine + front * sine], axis=-1)


def normed(values, gain):
    center = values - jnp.mean(values, axis=-1, keepdims=True)
    root = lax.rsqrt(jnp.mean(center * center, axis=-1, keepdims=True) + NORM_EPS)
    vhat = center * root
    return vhat * gain, vhat, root


def norm_back(dy, gain, vhat, root):
    dgain = jnp.sum(dy * vhat, axis=tuple(range(dy.ndim - 1)))
    e = dy * gain
    dz = root * (
        e
        - jnp.mean(e, axis=-1, keepdims=True)
        - vhat * jnp.mean(e * vhat, axis=-1, keepdims=True)
    )
    return dgain, dz


def mm(spec, a, b):
    return jnp.einsum(spec, a, b, preferred_element_type=F32)


def layer(g1, wqkv, wo, g2, win, wdown, tokens, dout, live):
    m, slot, d = tokens.shape
    heads, size = HEADS, d // HEADS
    scale = size ** (-0.5)
    w1, w2 = win
    lv = live[:, :, None]
    x = tokens.astype(F32)
    y, vhat1, root1 = normed(x, g1)
    a = y.astype(BF16)
    qkv = mm("mtd,de->mte", a, wqkv).reshape(m, slot, 3, heads, size)
    cosine, sine = rope_tables(slot, size)
    q = rotate(qkv[:, :, 0], cosine, sine).astype(BF16)
    k = rotate(qkv[:, :, 1], cosine, sine).astype(BF16)
    v = qkv[:, :, 2].astype(BF16)
    s = mm("mqhd,mkhd->mhqk", q, k) * scale
    s = jnp.where(live[:, None, None, :] > 0, s, -1e30)
    p = jax.nn.softmax(s, axis=-1)
    pb = p.astype(BF16)
    o = mm("mhqk,mkhd->mqhd", pb, v).astype(BF16).reshape(m, slot, d)
    h = x + lv * mm("mte,ed->mtd", o, wo)
    y, vhat2, root2 = normed(h, g2)
    hn = y.astype(BF16)
    z1 = mm("mtd,df->mtf", hn, w1)
    z2 = mm("mtd,df->mtf", hn, w2)
    cdf = 0.5 * (1.0 + lax.erf(z1 * (0.5**0.5)))
    pdf = jnp.exp(-0.5 * z1 * z1) * 0.3989422804014327
    act = z1 * cdf
    gg = (act * z2).astype(BF16)
    mixed = (h + lv * mm("mtf,fd->mtd", gg, wdown)).astype(BF16)

    up = dout.astype(F32)
    dy2 = (lv * up).astype(BF16)
    g_down = mm("mtf,mtd->fd", gg, dy2)
    dgg = mm("mtd,fd->mtf", dy2, wdown)
    dw1 = (dgg * z2 * (cdf + z1 * pdf)).astype(BF16)
    dw2 = (dgg * act).astype(BF16)
    g_in = (mm("mtd,mtf->df", hn, dw1), mm("mtd,mtf->df", hn, dw2))
    dhn = mm("mtf,df->mtd", dw1, w1) + mm("mtf,df->mtd", dw2, w2)
    g_g2, dhv = norm_back(dhn, g2, vhat2, root2)
    dh = up + dhv
    dy1 = (lv * dh).astype(BF16)
    g_out = mm("mte,mtd->ed", o, dy1)
    do = mm("mtd,ed->mte", dy1, wo).astype(BF16).reshape(m, slot, heads, size)
    dp = mm("mqhd,mkhd->mhqk", do, v)
    ds = (p * (dp - jnp.sum(dp * p, axis=-1, keepdims=True))).astype(BF16)
    dq = mm("mhqk,mkhd->mqhd", ds, k) * scale
    dk = mm("mhqk,mqhd->mkhd", ds, q) * scale
    dv = mm("mhqk,mqhd->mkhd", pb, do)
    dqkv = jnp.stack([rotate(dq, cosine, -sine), rotate(dk, cosine, -sine), dv], axis=2)
    dqkv = dqkv.reshape(m, slot, 3 * d).astype(BF16)
    g_qkv = mm("mtd,mte->de", a, dqkv)
    da = mm("mte,de->mtd", dqkv, wqkv)
    g_g1, dxv = norm_back(da, g1, vhat1, root1)
    gtok = (dh + dxv).astype(BF16)
    return mixed, gtok, (g_g1, g_qkv, g_out, g_g2, g_in, g_down)


def plain(tokens, cotangent, deal, lengths, ln1_gain, w_qkv, w_out, ln2_gain, w_in, w_down):
    slot = tokens.shape[2] * lax.axis_size("fsdp")
    me = lax.axis_index("fsdp")

    def spread(rows):
        return lax.all_to_all(rows, "fsdp", split_axis=1, concat_axis=2, tiled=True)[:, 0]

    def back(rows):
        return lax.all_to_all(rows[:, None], "fsdp", split_axis=2, concat_axis=1, tiled=True)

    def whole(shard):
        return lax.all_gather(shard.astype(BF16), "fsdp", axis=0, tiled=True)

    table = lax.all_gather(lengths[:, 0], "fsdp", axis=1, tiled=True)
    mine = lax.dynamic_slice_in_dim(deal[:, 0], me, 1, axis=1)
    pick = jnp.arange(table.shape[1], dtype=jnp.int32)[None, :] == mine
    length = jnp.sum(jnp.where(pick, table, 0), axis=1, keepdims=True)
    live = (jnp.arange(slot, dtype=jnp.int32)[None, :] < length).astype(F32)
    win = jnp.split(whole(w_in), 2, axis=1)
    mixed, gtok, grads = layer(
        whole(ln1_gain).astype(F32), whole(w_qkv), whole(w_out), whole(ln2_gain).astype(F32), win, whole(w_down),
        spread(tokens), spread(cotangent), live,
    )
    g_g1, g_qkv, g_out, g_g2, g_in, g_down = grads

    def owned(part):
        part = lax.psum_scatter(part, "fsdp", scatter_dimension=0, tiled=True)
        return lax.psum(part, "rep")

    g_in = jnp.concatenate(g_in, axis=1)
    return (back(mixed), back(gtok)) + tuple(owned(g) for g in (g_g1, g_qkv, g_out, g_g2, g_in, g_down))


class Unit:
    def __init__(self, mat, rows, real, col, width):
        self.mat, self.rows, self.real, self.col, self.width = mat, rows, real, col, width


def split_rows(rows, share):
    a = max(16, round(rows * share / 16) * 16)
    return a, rows - 2 * a


def make_units(d, ffs, n, widths):
    units = []
    pad = -(-ffs // 16) * 16
    totals = {"qkv": 3 * d // 2, "o": d // 2, "i": n * pad, "d": d // 2}
    for mat, parts in widths:
        rows, real = (pad, ffs) if mat == "d" else (d // n, d // n)
        width = totals[mat] // parts
        units += [Unit(mat, rows, real, i * width, width) for i in range(parts)]
    return units


class Place:
    def __init__(self):
        self.f = lax.axis_index("fsdp")
        self.r = lax.axis_index("rep")
        self.z, self.y = lax.div(self.f, 2), lax.rem(self.f, 2)
        self.x, self.c = lax.div(self.r, 2), lax.rem(self.r, 2)
        z = self.z
        self.zs = [z + 1 - 2 * lax.rem(z, 2), lax.rem(z + 2, 4), 3 - z]
        self.yn = self.f + 1 - 2 * self.y
        self.xn = lax.rem(self.r + 2, 4)
        self.cn = self.r + 1 - 2 * self.c

    def others(self):
        return [lax.rem(self.f + k, 8) for k in range(1, 8)]


def at(offset, size, unit=16):
    return pl.ds(pl.multiple_of(offset, unit), size)


def remote(src, dst, send, recv, f, r):
    return pltpu.make_async_remote_copy(
        src_ref=src, dst_ref=dst, send_sem=send, recv_sem=recv,
        device_id={"fsdp": f, "rep": r}, device_id_type=MESH,
    )


def meet(me):
    barrier = pltpu.get_barrier_semaphore()
    friends = [(f, me.r) for f in me.others()] + [(me.f, lax.rem(me.r + k, 4)) for k in (1, 2, 3)]
    for f, r in friends:
        pl.semaphore_signal(barrier, inc=1, device_id={"fsdp": f, "rep": r}, device_id_type=MESH)
    pl.semaphore_wait(barrier, len(friends))


class Gather:
    SHARE = 0.375

    def __init__(self, me, units, shards, whole, recv, send, zsend, local):
        self.me, self.units, self.shards, self.whole = me, units, shards, whole
        self.recv, self.send, self.zsend, self.local = recv, send, zsend, local
        self.pending = []

    def piece(self, u, ref, j, c, part, own=False):
        unit, x = self.units[u], self.me.x
        a, b = split_rows(unit.rows, self.SHARE)
        off = [x * a, x * (unit.rows - a), (1 - x) * (unit.rows - a)][part]
        size = [a + b, a, a][part]
        return ref.at[c, at((0 if own else j * unit.rows) + off, size)]

    def copy(self, u, j, kind, part, f, r, src=None):
        me = self.me
        dst = self.piece(u, self.whole[u], j, me.c, part)
        cp = remote(dst if src is None else src, dst, self.send.at[u, j, kind], self.recv.at[u, j, kind], f, r)
        cp.start()
        self.pending.append(cp)

    def start(self, u):
        me, unit = self.me, self.units[u]
        own = self.piece(u, self.shards[u], me.f, me.c, 0, own=True)
        for k, z in enumerate(me.zs):
            cp = remote(
                own, self.piece(u, self.whole[u], me.f, me.c, 0), self.zsend.at[u, k], self.recv.at[u, me.f, 0],
                2 * z + me.y, me.r,
            )
            cp.start()
            self.pending.append(cp)
            if k == 0:
                self.copy(u, me.f, 0, 0, me.yn, me.r, src=own)
        cp = pltpu.make_async_copy(
            self.shards[u], self.whole[u].at[:, at(me.f * unit.rows, unit.rows)], self.local.at[u]
        )
        cp.start()
        self.pending.append(cp)

    def arrived(self, u, j, kind, part, c):
        ref = self.piece(u, self.whole[u], j, c, part)
        remote(ref, ref, self.send.at[u, j, kind], self.recv.at[u, j, kind], self.me.f, self.me.r).wait_recv()

    def inplane(self, u, k, over_y):
        me = self.me
        z = me.zs[k] if k < 3 else me.z
        j = 2 * z + (1 - me.y if over_y else me.y)
        self.arrived(u, j, 0, 0, me.c)
        if not over_y:
            self.copy(u, j, 0, 0, me.yn, me.r)
        self.copy(u, j, 1, 1, me.f, me.xn)
        self.copy(u, j, 2, 0, me.f, me.cn)

    def over_x(self, u, k):
        me = self.me
        j = lax.rem(me.f + k, 8)
        self.arrived(u, j, 1, 2, me.c)
        self.copy(u, j, 3, 2, me.f, me.cn)

    def complete(self, u):
        me = self.me
        for k in range(1, 8):
            j = lax.rem(me.f + k, 8)
            self.arrived(u, j, 2, 0, 1 - me.c)
            self.arrived(u, j, 3, 2, 1 - me.c)

    ROUTE = ((0, False), (3, True), (1, False), (2, False), (0, True), (1, True), (2, True))

    def finish(self):
        for cp in self.pending:
            cp.wait_send() if cp.is_remote else cp.wait()


def gather_kernel(units, tok, cot, small, *refs):
    n = len(units)
    shards, refs = refs[:n], refs[n:]
    dealt_tok, dealt_cot, smalls = refs[:3]
    whole, refs = refs[3 : 3 + n], refs[3 + n :]
    recv, send, zsend, local, asend, arecv, alocal, ssend, srecv = refs
    me = Place()
    meet(me)
    g = Gather(me, units, shards, whole, recv, send, zsend, local)
    micro, _, rows, _ = tok.shape
    sends, locals_ = [], []
    for k, f in enumerate(me.others()):
        cp = remote(small, smalls.at[me.f], ssend.at[k], srecv.at[k], f, me.r)
        cp.start()
        sends.append(cp)
    cp = pltpu.make_async_copy(small, smalls.at[me.f], alocal.at[4])
    cp.start()
    locals_.append(cp)

    def deal(which, src, dst):
        for m in range(micro):
            cp = pltpu.make_async_copy(src.at[m, me.f], dst.at[m, at(me.f * rows, rows)], alocal.at[which * 2 + m])
            cp.start()
            locals_.append(cp)
            for k, f in enumerate(me.others()):
                cp = remote(
                    src.at[m, f], dst.at[m, at(me.f * rows, rows)], asend.at[which, m, k], arecv.at[which, m, k], f, me.r
                )
                cp.start()
                sends.append(cp)

    deal(0, tok, dealt_tok)
    g.start(0)
    g.start(1)
    for u in range(n):
        for i, (k, over_y) in enumerate(g.ROUTE):
            g.inplane(u, k, over_y)
            if i == 3 and u + 2 < n:
                g.start(u + 2)
        if u == 1:
            deal(1, cot, dealt_cot)
        for k in range(1, 8):
            g.over_x(u, k)
    for u in range(n):
        g.complete(u)
    for cp in sends:
        cp.wait_send()
    for k in range(7):
        src = lax.rem(me.f + 7 - k, 8)
        remote(small, smalls.at[src], ssend.at[k], srecv.at[k], me.f, me.r).wait_recv()
        for which, (s, dst) in enumerate(((tok, dealt_tok), (cot, dealt_cot))):
            for m in range(micro):
                remote(
                    s.at[m, 0], dst.at[m, at(src * rows, rows)], asend.at[which, m, k], arecv.at[which, m, k], me.f, me.r
                ).wait_recv()
    for cp in locals_:
        cp.wait()
    g.finish()


def gather_call(units, tok, cot, small, shards):
    micro, n, rows, d = tok.shape
    u = len(units)
    any_ = pl.BlockSpec(memory_space=pl.ANY)
    return pl.pallas_call(
        functools.partial(gather_kernel, units),
        out_shape=[
            jax.ShapeDtypeStruct((micro, n * rows, d), BF16),
            jax.ShapeDtypeStruct((micro, n * rows, d), BF16),
            jax.ShapeDtypeStruct((n, 8, 128), F32),
        ]
        + [jax.ShapeDtypeStruct((2, n * t.rows, t.width), BF16) for t in units],
        in_specs=[any_] * (3 + u),
        out_specs=[any_] * (3 + u),
        scratch_shapes=[
            pltpu.SemaphoreType.DMA((u, 8, 4)),
            pltpu.SemaphoreType.DMA((u, 8, 4)),
            pltpu.SemaphoreType.DMA((u, 3)),
            pltpu.SemaphoreType.DMA((u,)),
            pltpu.SemaphoreType.DMA((2, micro, 7)),
            pltpu.SemaphoreType.DMA((2, micro, 7)),
            pltpu.SemaphoreType.DMA((5,)),
            pltpu.SemaphoreType.DMA((7,)),
            pltpu.SemaphoreType.DMA((7,)),
        ],
        compiler_params=pltpu.CompilerParams(collective_id=0, has_side_effects=True, vmem_limit_bytes=32 * MIB),
    )(tok, cot, small, *shards)


def add_rows(dst, doff, src, soff, rows):
    def step(i, _):
        d = at(doff + i * 16, 16)
        dst[d, :] = (dst[d, :].astype(F32) + src[at(soff + i * 16, 16), :].astype(F32)).astype(BF16)
        return 0

    lax.fori_loop(0, rows // 16, step, 0)


class Reduce:
    SHARE = 0.25

    def __init__(self, me, units, bufs, outs, sems):
        self.me, self.units, self.bufs, self.outs, self.sems = me, units, bufs, outs, sems
        z, y = me.z, me.y
        zs = list(me.zs) + [z]
        self.order = [2 * k + 1 - y for k in zs] + [2 * k + y for k in zs]
        self.waits = []

    def parts(self, u):
        unit = self.units[u]
        a, b = split_rows(unit.rows, self.SHARE)
        return unit.rows, a, b

    def send(self, src, dst, kind, u, k, f, r, recv_k=None):
        s, r_ = self.sems[kind]
        cp = remote(src, dst, s.at[u, k], r_.at[u, k if recv_k is None else recv_k], f, r)
        cp.start()
        self.waits.append(cp)

    def wait(self, ref, kind, u, k):
        s, r_ = self.sems[kind]
        remote(ref, ref, s.at[u, k], r_.at[u, k], self.me.f, self.me.r).wait_recv()

    def to_sibling(self, u, i, src):
        rows, a, b = self.parts(u)
        me, j = self.me, self.order[i]
        self.send(src, self.bufs["sib"][u].at[at(j * rows, rows)], "core", u, i, me.f, me.cn)

    def chip_sum(self, u, i):
        rows, a, b = self.parts(u)
        me, j = self.me, self.order[i]
        own, sib = self.bufs["own"][u], self.bufs["sib"][u]
        self.wait(sib.at[at(j * rows, rows)], "core", u, i)
        add_rows(own, j * rows, sib, j * rows, rows)
        self.send(
            own.at[at(j * rows + (1 - me.x) * (rows - a), a)], self.bufs["xr"][u].at[i], "x", u, i, me.f, me.xn
        )

    def x_sum(self, u, i):
        rows, a, b = self.parts(u)
        me, j = self.me, self.order[i]
        own, xr = self.bufs["own"][u], self.bufs["xr"][u]
        self.wait(xr.at[i], "x", u, i)
        add_rows(own, j * rows + me.x * (rows - a), xr.at[i], 0, a)
        if i < 4:
            self.send(
                own.at[at(j * rows + me.x * a, a + b)], self.bufs["yr"][u].at[i], "y", u, i, me.yn, me.r
            )

    def y_sum(self, u, i):
        rows, a, b = self.parts(u)
        me, j = self.me, self.order[i]
        own, yr = self.bufs["own"][u], self.bufs["yr"][u]
        self.wait(yr.at[i - 4], "y", u, i - 4)
        add_rows(own, j * rows + me.x * a, yr.at[i - 4], 0, a + b)
        if i < 7:
            self.send(own.at[at(j * rows + me.x * a, a + b)], self.bufs["zr"][u].at[i - 4], "z", u, i - 4, j, me.r)

    def owner_sum(self, u):
        rows, a, b = self.parts(u)
        me = self.me
        own, zr, xs = self.bufs["own"][u], self.bufs["zr"][u], self.bufs["xs"][u]
        for k in range(3):
            self.wait(zr.at[k], "z", u, k)
        base = me.f * rows + me.x * a

        def step(i, _):
            t = at(i * 16, 16)
            total = own[at(base + i * 16, 16), :].astype(F32)
            for k in range(3):
                total = total + zr[k, t, :].astype(F32)
            xs[t, :] = total.astype(BF16)
            return 0

        lax.fori_loop(0, (a + b) // 16, step, 0)
        self.send(xs, self.bufs["xf"][u], "xf", u, 0, me.f, me.xn)

    def final(self, u):
        rows, a, b = self.parts(u)
        me, unit = self.me, self.units[u]
        xs, xf, fin = self.bufs["xs"][u], self.bufs["xf"][u], self.bufs["fin"][u]
        x = me.x
        self.wait(xf, "xf", u, 0)

        def mine(i, _):
            fin[at(x * (rows - a) + i * 16, 16), :] = xs[at(x * b + i * 16, 16), :].astype(F32)
            fin[at((1 - x) * (rows - a) + i * 16, 16), :] = xf[at((1 - x) * b + i * 16, 16), :].astype(F32)
            return 0

        def both(i, _):
            fin[at(a + i * 16, 16), :] = (
                xs[at((1 - x) * a + i * 16, 16), :].astype(F32) + xf[at(x * a + i * 16, 16), :].astype(F32)
            )
            return 0

        lax.fori_loop(0, a // 16, mine, 0)
        lax.fori_loop(0, b // 16, both, 0)
        src, dst = self.out_place(u, me.c)
        self.send(src, dst, "out", u, 0, me.f, me.cn)
        cp = pltpu.make_async_copy(src, dst, self.sems["local"].at[u])
        cp.start()
        self.waits.append(cp)

    def out_place(self, u, c):
        unit = self.units[u]
        half = self.outs[unit.mat].shape[1] // 2
        src = self.bufs["fin"][u].at[pl.ds(0, unit.real)]
        return src, self.outs[unit.mat].at[:, at(c * half + unit.col, unit.width, 128)]

    def drain(self):
        me = self.me
        for u in range(len(self.units)):
            src, dst = self.out_place(u, 1 - me.c)
            s, r_ = self.sems["out"]
            remote(src, dst, s.at[u, 0], r_.at[u, 0], me.f, me.r).wait_recv()
        for cp in self.waits:
            cp.wait_send() if cp.is_remote else cp.wait()


KINDS = ("core", "x", "y", "z", "xf", "out")


def reduce_kernel(units, mixed, gtok, gsmall, *refs):
    n = len(units)
    partial, refs = refs[:n], refs[n:]
    out_mixed, out_gtok, out_small, out_qkv, out_o, out_i, out_d = refs[:7]
    refs = refs[7:]
    bufs = {}
    for name in ("own", "sib", "xr", "yr", "zr", "xs", "xf", "fin"):
        bufs[name], refs = refs[:n], refs[n:]
    slots, reps, svm = refs[:3]
    refs = refs[3:]
    sems = {}
    for kind in KINDS:
        sems[kind], refs = (refs[0], refs[1]), refs[2:]
    sems["local"] = refs[0]
    load, asend, arecv, alocal, ssend, srecv, rsend, rrecv, slocal = refs[1:]
    me = Place()
    meet(me)
    red = Reduce(me, units, bufs, dict(qkv=out_qkv, o=out_o, i=out_i, d=out_d), sems)
    micro, rows = mixed.shape[0], out_mixed.shape[2]
    loads = []
    for u, unit in enumerate(units):
        cp = pltpu.make_async_copy(partial[u].at[me.c], bufs["own"][u], load.at[u])
        cp.start()
        loads.append(cp)
    for u, unit in enumerate(units):
        for i in range(8):
            j = red.order[i]
            red.to_sibling(u, i, partial[u].at[1 - me.c, at(j * unit.rows, unit.rows)])
    sends = []
    for k, f in enumerate(me.others()):
        cp = remote(gsmall.at[f], slots.at[me.f], ssend.at[k], srecv.at[k], f, me.r)
        cp.start()
        sends.append(cp)
    own_small = pltpu.make_async_copy(gsmall.at[me.f], slots.at[me.f], slocal.at[0])
    own_small.start()
    locals_ = []
    for which, (src, dst) in enumerate(((mixed, out_mixed), (gtok, out_gtok))):
        for m in range(micro):
            cp = pltpu.make_async_copy(src.at[m, at(me.f * rows, rows)], dst.at[m, me.f], alocal.at[which * 2 + m])
            cp.start()
            locals_.append(cp)
            for k, f in enumerate(me.others()):
                cp = remote(
                    src.at[m, at(f * rows, rows)], dst.at[m, me.f], asend.at[which, m, k], arecv.at[which, m, k], f, me.r
                )
                cp.start()
                sends.append(cp)

    def small_reduce():
        own_small.wait()
        for k in range(7):
            remote(slots.at[0], slots.at[0], ssend.at[k], srecv.at[k], me.f, me.r).wait_recv()
        total = slots[0]
        for j in range(1, 8):
            total = total + slots[j]
        svm[...] = total
        reps[me.r] = total
        for k in range(3):
            cp = remote(svm, reps.at[me.r], rsend.at[k], rrecv.at[k], me.f, lax.rem(me.r + k + 1, 4))
            cp.start()
            sends.append(cp)

    def small_final():
        for k in range(3):
            remote(svm, reps.at[0], rsend.at[k], rrecv.at[k], me.f, me.r).wait_recv()
        svm2 = reps[0] + reps[1] + reps[2] + reps[3]
        slots[0] = svm2
        cp = pltpu.make_async_copy(slots.at[0], out_small, slocal.at[1])
        cp.start()
        locals_.append(cp)

    def stage(s, u):
        if s == 0:
            loads[u].wait()
            for i in range(8):
                red.chip_sum(u, i)
        elif s == 1:
            for i in range(8):
                red.x_sum(u, i)
                if i >= 4:
                    red.y_sum(u, i)
        elif s == 2:
            red.owner_sum(u)
        else:
            red.final(u)

    for t in range(n + 3):
        for s in range(4):
            u = t - s
            if 0 <= u < n:
                stage(s, u)
        if t == 1:
            small_reduce()
        if t == 3:
            small_final()
    red.drain()
    for cp in sends:
        cp.wait_send()
    for k in range(7):
        for which, dst in enumerate((out_mixed, out_gtok)):
            for m in range(micro):
                remote(dst.at[m, 0], dst.at[m, 0], asend.at[which, m, k], arecv.at[which, m, k], me.f, me.r).wait_recv()
    for cp in locals_:
        cp.wait()


def reduce_call(units, d, ffs, mixed, gtok, gsmall, partial):
    n = 8
    micro, slot, _ = mixed.shape
    rows = slot // n
    u = len(units)
    any_ = pl.BlockSpec(memory_space=pl.ANY)
    ab = [split_rows(t.rows, Reduce.SHARE) for t in units]
    pad = n * (-(-ffs // 16) * 16)
    scratch = (
        [pltpu.VMEM((n * t.rows, t.width), BF16) for t in units]
        + [pltpu.VMEM((n * t.rows, t.width), BF16) for t in units]
        + [pltpu.VMEM((8, a, t.width), BF16) for t, (a, b) in zip(units, ab)]
        + [pltpu.VMEM((4, a + b, t.width), BF16) for t, (a, b) in zip(units, ab)]
        + [pltpu.VMEM((3, a + b, t.width), BF16) for t, (a, b) in zip(units, ab)]
        + [pltpu.VMEM((a + b, t.width), BF16) for t, (a, b) in zip(units, ab)]
        + [pltpu.VMEM((a + b, t.width), BF16) for t, (a, b) in zip(units, ab)]
        + [pltpu.VMEM((t.rows, t.width), F32) for t in units]
        + [pltpu.VMEM((8, 8, 128), F32), pltpu.VMEM((4, 8, 128), F32), pltpu.VMEM((8, 128), F32)]
        + [
            pltpu.SemaphoreType.DMA((u, size))
            for size in (8, 8, 4, 3, 1, 1)
            for _ in range(2)
        ]
        + [
            pltpu.SemaphoreType.DMA((u,)),
            pltpu.SemaphoreType.DMA((u,)),
            pltpu.SemaphoreType.DMA((2, micro, 7)),
            pltpu.SemaphoreType.DMA((2, micro, 7)),
            pltpu.SemaphoreType.DMA((4,)),
            pltpu.SemaphoreType.DMA((7,)),
            pltpu.SemaphoreType.DMA((7,)),
            pltpu.SemaphoreType.DMA((3,)),
            pltpu.SemaphoreType.DMA((3,)),
            pltpu.SemaphoreType.DMA((2,)),
        ]
    )
    return pl.pallas_call(
        functools.partial(reduce_kernel, units),
        out_shape=[
            jax.ShapeDtypeStruct((micro, n, rows, d), BF16),
            jax.ShapeDtypeStruct((micro, n, rows, d), BF16),
            jax.ShapeDtypeStruct((8, 128), F32),
            jax.ShapeDtypeStruct((d // n, 3 * d), F32),
            jax.ShapeDtypeStruct((d // n, d), F32),
            jax.ShapeDtypeStruct((d // n, 2 * pad), F32),
            jax.ShapeDtypeStruct((ffs, d), F32),
        ],
        in_specs=[any_] * (3 + u),
        out_specs=[any_] * 7,
        scratch_shapes=scratch,
        compiler_params=pltpu.CompilerParams(collective_id=1, has_side_effects=True, vmem_limit_bytes=60 * MIB),
    )(mixed, gtok, gsmall, *partial)


def padded(columns, n, pad):
    size = columns.shape[-1] // n
    blocks = columns.reshape(columns.shape[:-1] + (n, size))
    blocks = jnp.pad(blocks, [(0, 0)] * (blocks.ndim - 1) + [(0, pad - size)])
    return blocks.reshape(columns.shape[:-1] + (n * pad,))


def unpadded(columns, n, size):
    blocks = columns.reshape(columns.shape[:-1] + (n, columns.shape[-1] // n))
    return blocks[..., :size].reshape(columns.shape[:-1] + (n * size,))


GATHER_WIDTHS = (("qkv", 2), ("o", 1), ("i", 3), ("d", 1))
REDUCE_WIDTHS = (("d", 1), ("i", 3), ("o", 1), ("qkv", 2))


def routed(tokens, cotangent, deal, lengths, ln1_gain, w_qkv, w_out, ln2_gain, w_in, w_down):
    n = 8
    micro, _, part, d = tokens.shape
    slot = part * n
    ffs = w_down.shape[0]
    pad = -(-ffs // 16) * 16
    units = make_units(d, ffs, n, GATHER_WIDTHS)
    shard = {
        "qkv": jnp.stack(jnp.split(w_qkv.astype(BF16), 2, axis=1)),
        "o": jnp.stack(jnp.split(w_out.astype(BF16), 2, axis=1)),
        "i": padded(jnp.stack(jnp.split(w_in.astype(BF16), 2, axis=1)), n, pad),
        "d": jnp.pad(jnp.stack(jnp.split(w_down.astype(BF16), 2, axis=1)), ((0, 0), (0, pad - ffs), (0, 0))),
    }
    shards = [shard[t.mat][:, :, t.col : t.col + t.width] for t in units]
    gain = [g.astype(BF16).astype(F32)[None] for g in (ln1_gain, ln2_gain)]
    len_row = jnp.pad(lengths[:, 0, 0].astype(F32), (0, 128 - micro))[None]
    small = jnp.concatenate(gain + [len_row, jnp.zeros((5, 128), F32)])
    outs = gather_call(units, tokens, cotangent, small, shards)
    tok, dout, smalls, whole = outs[0], outs[1], outs[2], outs[3:]
    full = {}
    for t, w in zip(units, whole):
        full.setdefault(t.mat, []).append(w)
    full = {k: jnp.concatenate(v, axis=2) for k, v in full.items()}
    flat = lambda w: jnp.concatenate([w[0], w[1]], axis=1)
    g1, g2 = smalls[:, 0].reshape(d), smalls[:, 1].reshape(d)
    me = lax.axis_index("fsdp")
    mine = lax.dynamic_slice_in_dim(deal[:, 0], me, 1, axis=1)
    pick = jnp.arange(n, dtype=jnp.int32)[None, :] == mine
    length = jnp.sum(jnp.where(pick, smalls[:, 2, :micro].T, 0.0), axis=1, keepdims=True)
    live = (jnp.arange(slot, dtype=jnp.int32).astype(F32)[None, :] < length).astype(F32)
    mixed, gtok, grads = layer(
        g1, flat(full["qkv"]), flat(full["o"]), g2, (full["i"][0], full["i"][1]), flat(full["d"]), tok, dout, live
    )
    g_g1, g_qkv, g_out, g_g2, g_in, g_down = grads
    halves = lambda g: jnp.stack(jnp.split(g.astype(BF16), 2, axis=1))
    grad = {"qkv": halves(g_qkv), "o": halves(g_out), "i": jnp.stack([g.astype(BF16) for g in g_in]), "d": halves(g_down)}
    runits = make_units(d, ffs, n, REDUCE_WIDTHS)
    partial = [grad[t.mat][:, :, t.col : t.col + t.width] for t in runits]
    gsmall = jnp.pad(jnp.stack([g_g1.reshape(n, 128), g_g2.reshape(n, 128)], axis=1), ((0, 0), (0, 6), (0, 0)))
    o_mixed, o_gtok, o_small, o_qkv, o_out, o_in, o_down = reduce_call(runits, d, ffs, mixed, gtok, gsmall, partial)
    o_in = jnp.concatenate([unpadded(h, n, ffs) for h in jnp.split(o_in, 2, axis=1)], axis=1)
    return o_mixed, o_gtok, o_small[0], o_qkv, o_out, o_small[1], o_in, o_down


def solution(mesh):
    small = mesh.shape["fsdp"] == 8 and mesh.shape["rep"] == 4
    rows = P(None, "rep", "fsdp", None)
    return jax.shard_map(
        routed if small else plain,
        mesh=mesh,
        in_specs=(
            rows, rows, P(None, "rep", None), P(None, "rep", "fsdp"),
            P("fsdp"), P("fsdp", None), P("fsdp", None), P("fsdp"), P("fsdp", None), P("fsdp", None),
        ),
        out_specs=(rows, rows, P("fsdp"), P("fsdp", None), P("fsdp", None), P("fsdp"), P("fsdp", None), P("fsdp", None)),
        check_vma=False,
    )
```

```python
import functools

import jax
import jax.numpy as jnp
from jax import lax
from jax.experimental import pallas as pl
from jax.experimental.pallas import tpu as pltpu
from jax.sharding import PartitionSpec as P

HEADS = 16
ROPE_BASE = 160000.0
NORM_EPS = 1e-05
MESH = pl.DeviceIdType.MESH
MIB = 1 << 20
BF16 = jnp.bfloat16
F32 = jnp.float32


def rope_tables(slot_count, head_size):
    half_size = head_size // 2
    frequency = ROPE_BASE ** (-(jnp.arange(half_size, dtype=F32) * 2.0 / head_size))
    angles = jnp.arange(slot_count, dtype=F32)[:, None] * frequency[None, :]
    return jnp.cos(angles), jnp.sin(angles)


def rotate(values, cosine, sine):
    front, back = jnp.split(values, 2, axis=-1)
    cosine, sine = cosine[:, None, :], sine[:, None, :]
    return jnp.concatenate([front * cosine - back * sine, back * cosine + front * sine], axis=-1)


def normed(values, gain):
    center = values - jnp.mean(values, axis=-1, keepdims=True)
    root = lax.rsqrt(jnp.mean(center * center, axis=-1, keepdims=True) + NORM_EPS)
    vhat = center * root
    return vhat * gain, vhat, root


def norm_back(dy, gain, vhat, root):
    dgain = jnp.sum(dy * vhat, axis=tuple(range(dy.ndim - 1)))
    e = dy * gain
    dz = root * (
        e
        - jnp.mean(e, axis=-1, keepdims=True)
        - vhat * jnp.mean(e * vhat, axis=-1, keepdims=True)
    )
    return dgain, dz


def mm(spec, a, b):
    return jnp.einsum(spec, a, b, preferred_element_type=F32)


def layer(g1, wqkv, wo, g2, win, wdown, tokens, dout, live):
    m, slot, d = tokens.shape
    heads, size = HEADS, d // HEADS
    scale = size ** (-0.5)
    w1, w2 = win
    lv = live[:, :, None]
    x = tokens.astype(F32)
    y, vhat1, root1 = normed(x, g1)
    a = y.astype(BF16)
    qkv = mm("mtd,de->mte", a, wqkv).reshape(m, slot, 3, heads, size)
    cosine, sine = rope_tables(slot, size)
    q = rotate(qkv[:, :, 0], cosine, sine).astype(BF16)
    k = rotate(qkv[:, :, 1], cosine, sine).astype(BF16)
    v = qkv[:, :, 2].astype(BF16)
    s = mm("mqhd,mkhd->mhqk", q, k) * scale
    s = jnp.where(live[:, None, None, :] > 0, s, -1e30)
    p = jax.nn.softmax(s, axis=-1)
    pb = p.astype(BF16)
    o = mm("mhqk,mkhd->mqhd", pb, v).astype(BF16).reshape(m, slot, d)
    h = x + lv * mm("mte,ed->mtd", o, wo)
    y, vhat2, root2 = normed(h, g2)
    hn = y.astype(BF16)
    z1 = mm("mtd,df->mtf", hn, w1)
    z2 = mm("mtd,df->mtf", hn, w2)
    cdf = 0.5 * (1.0 + lax.erf(z1 * (0.5**0.5)))
    pdf = jnp.exp(-0.5 * z1 * z1) * 0.3989422804014327
    act = z1 * cdf
    gg = (act * z2).astype(BF16)
    mixed = (h + lv * mm("mtf,fd->mtd", gg, wdown)).astype(BF16)

    up = dout.astype(F32)
    dy2 = (lv * up).astype(BF16)
    g_down = mm("mtf,mtd->fd", gg, dy2)
    dgg = mm("mtd,fd->mtf", dy2, wdown)
    dw1 = (dgg * z2 * (cdf + z1 * pdf)).astype(BF16)
    dw2 = (dgg * act).astype(BF16)
    g_in = (mm("mtd,mtf->df", hn, dw1), mm("mtd,mtf->df", hn, dw2))
    dhn = mm("mtf,df->mtd", dw1, w1) + mm("mtf,df->mtd", dw2, w2)
    g_g2, dhv = norm_back(dhn, g2, vhat2, root2)
    dh = up + dhv
    dy1 = (lv * dh).astype(BF16)
    g_out = mm("mte,mtd->ed", o, dy1)
    do = mm("mtd,ed->mte", dy1, wo).astype(BF16).reshape(m, slot, heads, size)
    dp = mm("mqhd,mkhd->mhqk", do, v)
    ds = (p * (dp - jnp.sum(dp * p, axis=-1, keepdims=True))).astype(BF16)
    dq = mm("mhqk,mkhd->mqhd", ds, k) * scale
    dk = mm("mhqk,mqhd->mkhd", ds, q) * scale
    dv = mm("mhqk,mqhd->mkhd", pb, do)
    dqkv = jnp.stack([rotate(dq, cosine, -sine), rotate(dk, cosine, -sine), dv], axis=2)
    dqkv = dqkv.reshape(m, slot, 3 * d).astype(BF16)
    g_qkv = mm("mtd,mte->de", a, dqkv)
    da = mm("mte,de->mtd", dqkv, wqkv)
    g_g1, dxv = norm_back(da, g1, vhat1, root1)
    gtok = (dh + dxv).astype(BF16)
    return mixed, gtok, (g_g1, g_qkv, g_out, g_g2, g_in, g_down)


def plain(tokens, cotangent, deal, lengths, ln1_gain, w_qkv, w_out, ln2_gain, w_in, w_down):
    slot = tokens.shape[2] * lax.axis_size("fsdp")
    me = lax.axis_index("fsdp")

    def spread(rows):
        return lax.all_to_all(rows, "fsdp", split_axis=1, concat_axis=2, tiled=True)[:, 0]

    def back(rows):
        return lax.all_to_all(rows[:, None], "fsdp", split_axis=2, concat_axis=1, tiled=True)

    def whole(shard):
        return lax.all_gather(shard.astype(BF16), "fsdp", axis=0, tiled=True)

    table = lax.all_gather(lengths[:, 0], "fsdp", axis=1, tiled=True)
    mine = lax.dynamic_slice_in_dim(deal[:, 0], me, 1, axis=1)
    pick = jnp.arange(table.shape[1], dtype=jnp.int32)[None, :] == mine
    length = jnp.sum(jnp.where(pick, table, 0), axis=1, keepdims=True)
    live = (jnp.arange(slot, dtype=jnp.int32)[None, :] < length).astype(F32)
    win = jnp.split(whole(w_in), 2, axis=1)
    mixed, gtok, grads = layer(
        whole(ln1_gain).astype(F32), whole(w_qkv), whole(w_out), whole(ln2_gain).astype(F32), win, whole(w_down),
        spread(tokens), spread(cotangent), live,
    )
    g_g1, g_qkv, g_out, g_g2, g_in, g_down = grads

    def owned(part):
        part = lax.psum_scatter(part, "fsdp", scatter_dimension=0, tiled=True)
        return lax.psum(part, "rep")

    g_in = jnp.concatenate(g_in, axis=1)
    return (back(mixed), back(gtok)) + tuple(owned(g) for g in (g_g1, g_qkv, g_out, g_g2, g_in, g_down))


NF, NR, NZ = 8, 4, 4


def at(offset, size, unit=16):
    return pl.ds(pl.multiple_of(offset, unit), size)


def nn(a, b):
    return lax.dot_general(a, b, (((1,), (0,)), ((), ())), preferred_element_type=F32)


def nt(a, b):
    return lax.dot_general(a, b, (((1,), (1,)), ((), ())), preferred_element_type=F32)


def tn(a, b):
    return lax.dot_general(a, b, (((0,), (0,)), ((), ())), preferred_element_type=F32)


def loop(n, body):
    def step(i, carry):
        body(i)
        return carry

    lax.fori_loop(0, n, step, 0)


class Sizes:
    def __init__(self, micro, part, d, ffs):
        self.micro, self.part, self.d, self.ffs = micro, part, d, ffs
        self.slot = part * NF
        self.rows = micro * self.slot
        self.all = NR * self.rows
        self.shard = d // NF
        self.hq = d // NR
        self.ffp = -(-ffs // 16) * 16
        self.tile = 256
        self.ntile = -(-(2 * self.ffp) // self.tile)
        self.fq = self.ntile * self.tile


class Copies:
    def __init__(self, sends, recvs):
        self.sends, self.recvs, self.next = sends, recvs, 0
        self.pending = []

    def take(self, n=1):
        base, self.next = self.next, self.next + n
        return base

    def make(self, src, dst, send, recv, f, r):
        return pltpu.make_async_remote_copy(
            src_ref=src, dst_ref=dst, send_sem=self.sends.at[send], recv_sem=self.recvs.at[recv],
            device_id={"fsdp": f, "rep": r}, device_id_type=MESH,
        )

    def start(self, build, cond=None):
        def go():
            self.make(*build()).start()

        if cond is None:
            go()
        else:
            pl.when(cond)(go)
        self.pending.append((build, cond))

    def arrived(self, ref, recv, f, r):
        self.make(ref, ref, recv, recv, f, r).wait_recv()

    def drain(self, pending=None):
        for build, cond in self.pending if pending is None else pending:

            def go():
                self.make(*build()).wait_send()

            if cond is None:
                go()
            else:
                pl.when(cond)(go)
        if pending is None:
            self.pending = []


def kernel(sz, names, *refs):
    k = dict(zip(names, refs))
    d, rows, slot, micro, part = sz.d, sz.rows, sz.slot, sz.micro, sz.part
    f, r = lax.axis_index("fsdp"), lax.axis_index("rep")
    z, y = lax.div(f, 2), lax.rem(f, 2)
    c = lax.rem(r, 2)
    yn = f + 1 - 2 * y
    cn = r + 1 - 2 * c
    xn = lax.rem(r + 2, 4)
    dn = lax.rem(cn + 2, 4)
    others = [lax.rem(f + i, NF) for i in range(1, NF)]
    cp = Copies(k["sends"], k["recvs"])
    local_pending = []

    def local(src, dst, i):
        copy = pltpu.make_async_copy(src, dst, k["locals"].at[i])
        copy.start()
        return copy

    def block(i):
        return at(i * rows, rows)

    barrier = pltpu.get_barrier_semaphore()
    friends = [(o, r) for o in others] + [(f, o) for o in (cn, xn, dn)]
    for ff, rr in friends:
        pl.semaphore_signal(barrier, inc=1, device_id={"fsdp": ff, "rep": rr}, device_id_type=MESH)

    wq, wo, wi, wd = k["wq"], k["wo"], k["wi"], k["wd"]
    sq, so, si, sd = k["sq"], k["so"], k["si"], k["sd"]
    sh = sz.shard

    class ColumnGather:
        def __init__(self, src, whole, col, width):
            self.src, self.whole, self.cols = src, whole, at(col, width, 128)
            self.recv, self.ysend, self.zsend, self.own = cp.take(NF), cp.take(NF), cp.take(NF), cp.take(3)

        def dst(self, j):
            return self.whole.at[at(j * sh, sh), self.cols]

        def start(self, i):
            src = self.src.at[:, self.cols]
            cp.start(lambda: (src, self.dst(f), self.own, self.recv + f, f + 2, r), z < NZ - 1)
            cp.start(lambda: (src, self.dst(f), self.own + 1, self.recv + f, f - 2, r), z > 0)
            cp.start(lambda: (src, self.dst(f), self.own + 2, self.recv + f, yn, r))
            local_pending.append(local(src, self.dst(f), i))

        def column(self):
            for dist in (1, 2, 3):
                for sign in (-1, 1):
                    j = f + 2 * sign * dist
                    here = (z >= dist) if sign < 0 else (z + dist < NZ)
                    onward = (z < NZ - 1) if sign < 0 else (z > 0)

                    @pl.when(here)
                    def _(j=j):
                        cp.arrived(self.dst(j), self.recv + j, f, r)

                    cp.start(
                        lambda j=j, sign=sign: (self.dst(j), self.dst(j), self.zsend + j, self.recv + j, f - 2 * sign, r),
                        jnp.logical_and(here, onward),
                    )
                    cp.start(lambda j=j: (self.dst(j), self.dst(j), self.ysend + j, self.recv + j, yn, r), here)

        def over_y(self):
            for i in range(NZ):
                j = 2 * i + 1 - y
                cp.arrived(self.dst(j), self.recv + j, f, r)

    class RowGather:
        def __init__(self, src, whole, row, height, pitch):
            self.src, self.whole, self.row, self.height, self.pitch = src, whole, row, height, pitch
            self.recv, self.send, self.own = cp.take(2), cp.take(3), cp.take(3)

        def dst(self, yy):
            return self.whole.at[at(yy * self.pitch + self.row, self.height)]

        def start(self, i):
            src = self.src.at[at(self.row, self.height)]
            mine = z == r
            cp.start(
                lambda: (src, self.dst(y), self.own, self.recv + y, f + 2, r), jnp.logical_and(mine, z < NZ - 1)
            )
            cp.start(lambda: (src, self.dst(y), self.own + 1, self.recv + y, f - 2, r), jnp.logical_and(mine, z > 0))
            cp.start(lambda: (src, self.dst(y), self.own + 2, self.recv + y, yn, r), mine)

            @pl.when(mine)
            def _():
                local(src, self.dst(y), i).wait()

        def column(self):
            @pl.when(z != r)
            def _():
                cp.arrived(self.dst(y), self.recv + y, f, r)

            dst = self.dst(y)
            up = jnp.logical_and(z > r, z < NZ - 1)
            down = jnp.logical_and(z < r, z > 0)
            cp.start(lambda: (dst, dst, self.send, self.recv + y, f + 2, r), up)
            cp.start(lambda: (dst, dst, self.send + 1, self.recv + y, f - 2, r), down)
            cp.start(lambda: (dst, dst, self.send + 2, self.recv + y, yn, r), z != r)

        def over_y(self):
            cp.arrived(self.dst(1 - y), self.recv + 1 - y, f, r)

    t2 = 2 * sz.tile
    g_q = ColumnGather(sq, wq, 0, 3 * sz.hq)
    g_o = [RowGather(so, wo, i * (sh // 2), sh // 2, sh) for i in range(2)]
    g_i = [ColumnGather(si, wi, i * t2, t2) for i in range(sz.ntile)]
    third = sz.ffp // 3
    g_d = [RowGather(sd, wd, i * third, third, sz.ffp) for i in range(3)]

    class Spread:
        def __init__(self, buf):
            self.buf = buf
            self.ids = cp.take(4)
            self.mine = []

        def _start(self, build):
            cp.start(build)
            self.mine.append(cp.pending.pop())

        def start(self):
            own = self.buf.at[block(r)]
            self._start(lambda: (own, own, self.ids + 1, self.ids + 1, f, xn))
            self._start(lambda: (own, own, self.ids, self.ids, f, cn))

        def forward(self):
            got = self.buf.at[block(xn)]
            cp.arrived(got, self.ids + 1, f, r)
            self._start(lambda: (got, got, self.ids + 2, self.ids + 2, f, cn))

        def free(self):
            cp.drain(self.mine)
            self.mine = []

        def done(self):
            cp.arrived(self.buf.at[block(cn)], self.ids, f, r)
            cp.arrived(self.buf.at[block(dn)], self.ids + 2, f, r)

    class Sum:
        def __init__(self, part, sib, xsend, xrecv):
            self.part, self.sib, self.xsend, self.xrecv = part, sib, xsend, xrecv
            self.ids = cp.take(3)
            self.order = (dn, xn, cn, r)
            self.mine = []

        def _start(self, build):
            cp.start(build)
            self.mine.append(cp.pending.pop())

        def ready(self, i):
            if i == 0:
                src = self.part.at[block(dn)]
                self._start(lambda: (src, self.sib.at[0], self.ids, self.ids, f, cn))
            elif i == 1:
                cp.arrived(self.sib.at[0], self.ids, f, r)

                def add(t):
                    s = at(t * 32, 32)
                    self.xsend[s, :] = (self.part[at(xn * rows + t * 32, 32), :] + self.sib[0, s, :]).astype(BF16)

                loop(rows // 32, add)
                self._start(lambda: (self.xsend, self.xrecv, self.ids + 1, self.ids + 1, f, xn))
            elif i == 2:
                src2 = self.part.at[block(cn)]
                self._start(lambda: (src2, self.sib.at[1], self.ids + 2, self.ids + 2, f, cn))

        def done(self):
            cp.arrived(self.sib.at[1], self.ids + 2, f, r)
            cp.arrived(self.xrecv, self.ids + 1, f, r)

        def value(self, t, n):
            s = at(t * n, n)
            return self.part[at(r * rows + t * n, n), :] + self.sib[1, s, :] + self.xrecv[s, :].astype(F32)

        def free(self):
            cp.drain(self.mine)
            self.mine = []

    def add_into(dst, doff, src, n):
        def step(t):
            s = at(doff + t * 16, 16)
            dst[s, :] = (dst[s, :].astype(F32) + src[at(t * 16, 16), :].astype(F32)).astype(BF16)

        loop(n // 16, step)

    class ColumnReduce:
        def __init__(self, grad, yr, zr, fin, out, col, width):
            self.grad, self.yr, self.zr, self.fin, self.out, self.col, self.width = grad, yr, zr, fin, out, col, width
            self.ids, self.zsend, self.zrecv, self.oid = cp.take(NZ), cp.take(NZ), cp.take(NZ + 1), cp.take(4)

        def send(self, j):
            zz = lax.div(j, 2)
            cp.start(lambda: (self.grad.at[at(j * sh, sh)], self.yr.at[zz], self.ids + zz, self.ids + zz, yn, r))

        def add_y(self, j):
            zz = lax.div(j, 2)
            cp.arrived(self.yr.at[zz], self.ids + zz, f, r)
            add_into(self.grad, j * sh, self.yr.at[zz], sh)

        def chain(self, sign, dist):
            j = f + 2 * sign * dist
            here = (z + dist < NZ) if sign > 0 else (z >= dist)
            behind = (z > 0) if sign > 0 else (z < NZ - 1)
            zz = z + sign * dist

            @pl.when(here)
            def _():
                self.add_y(j)

                @pl.when(behind)
                def _():
                    cp.arrived(self.zr.at[zz], self.zrecv + zz, f, r)
                    add_into(self.grad, j * sh, self.zr.at[zz], sh)

            there = NZ if (sign < 0 and dist == 1) else zz
            cp.start(
                lambda: (
                    self.grad.at[at(j * sh, sh)], self.zr.at[there], self.zsend + zz, self.zrecv + there, f + 2 * sign, r
                ),
                here,
            )

        def middle(self):
            for dist in (3, 2, 1):
                for sign in (1, -1):
                    self.chain(sign, dist)

        def final(self, lid):
            self.add_y(f)
            for slot_, cond in ((z, z > 0), (NZ, z < NZ - 1)):

                @pl.when(cond)
                def _(slot_=slot_):
                    cp.arrived(self.zr.at[slot_], self.zrecv + slot_, f, r)
                    add_into(self.grad, f * sh, self.zr.at[slot_], sh)

            src = self.grad.at[at(f * sh, sh)]
            for i, to in enumerate((xn, dn, cn)):
                cp.start(lambda i=i, to=to: (src, self.dst(r), self.oid + i, self.oid + i, f, to))
            local_pending.append(local(src, self.dst(r), lid))

        def dst(self, q):
            return self.out.at[q, :, at(self.col, self.width, 128)]

        def done(self):
            for i, source in enumerate((xn, dn, cn)):
                cp.arrived(self.dst(source), self.oid + i, f, r)

    class RowReduce:
        def __init__(self, grad, yr, zr, out, row, height, pitch):
            self.grad, self.yr, self.zr, self.out = grad, yr, zr, out
            self.row, self.height, self.pitch = row, height, pitch
            self.ids, self.zid, self.oid = cp.take(1), cp.take(4), cp.take(3)

        def rows(self, yy):
            return at(yy * self.pitch + self.row, self.height)

        def send(self):
            src = self.grad.at[self.rows(1 - y)]
            cp.start(lambda: (src, self.yr, self.ids, self.ids, yn, r))

        def middle(self):
            cp.arrived(self.yr, self.ids, f, r)
            mine = y * self.pitch + self.row
            add_into(self.grad, mine, self.yr, self.height)
            src = self.grad.at[self.rows(y)]
            for i, (cond, behind, step) in enumerate(((z < r, z > 0, 2), (z > r, z < NZ - 1, -2))):

                @pl.when(jnp.logical_and(cond, behind))
                def _(i=i):
                    cp.arrived(self.zr.at[i], self.zid + i, f, r)
                    add_into(self.grad, mine, self.zr.at[i], self.height)

                cp.start(
                    lambda i=i, step=step: (src, self.zr.at[i], self.zid + 2 + i, self.zid + i, f + step, r), cond
                )

        def dst(self):
            return self.out.at[at(self.row, self.height)]

        def final(self, lid):
            mine = y * self.pitch + self.row
            owner = z == r
            for i, cond in enumerate((z > 0, z < NZ - 1)):

                @pl.when(jnp.logical_and(owner, cond))
                def _(i=i):
                    cp.arrived(self.zr.at[i], self.zid + i, f, r)
                    add_into(self.grad, mine, self.zr.at[i], self.height)

            src = self.grad.at[self.rows(y)]
            for i, to in enumerate((xn, dn, cn)):
                cp.start(lambda i=i, to=to: (src, self.dst(), self.oid + i, self.oid + i, f, to), owner)

            @pl.when(owner)
            def _():
                local(src, self.dst(), lid).wait()

        def done(self):
            for i, source in enumerate((xn, dn, cn)):

                @pl.when(z == source)
                def _(i=i):
                    cp.arrived(self.dst(), self.oid + i, f, r)

    class Deal:
        def __init__(self, src, dst, lid):
            self.src, self.dst, self.lid, self.ids = src, dst, lid, cp.take(micro * NF)

        def start(self):
            for m in range(micro):
                for i, o in enumerate(others):
                    n = self.ids + m * NF + i
                    cp.start(
                        lambda m=m, o=o, n=n: (
                            self.src.at[m, o], self.dst.at[at(m * slot + f * part, part)], n, n, o, r
                        )
                    )
                local_pending.append(local(self.src.at[m, f], self.dst.at[at(m * slot + f * part, part)], self.lid + m))

        def done(self):
            for m in range(micro):
                for i in range(NF - 1):
                    source = lax.rem(f + NF - 1 - i, NF)
                    cp.arrived(self.dst.at[at(m * slot + source * part, part)], self.ids + m * NF + i, f, r)

    class Back:
        def __init__(self, src, dst, lid):
            self.src, self.dst, self.lid, self.ids = src, dst, lid, cp.take(micro * NF)

        def start(self):
            for m in range(micro):
                for i, o in enumerate(others):
                    n = self.ids + m * NF + i
                    cp.start(
                        lambda m=m, o=o, n=n: (
                            self.src.at[at(m * slot + o * part, part)], self.dst.at[m, f], n, n, o, r
                        )
                    )
                local_pending.append(local(self.src.at[at(m * slot + f * part, part)], self.dst.at[m, f], self.lid + m))

        def done(self):
            for m in range(micro):
                for i in range(NF - 1):
                    source = lax.rem(f + NF - 1 - i, NF)
                    cp.arrived(self.dst.at[m, source], self.ids + m * NF + i, f, r)

    L = iter(range(k["locals"].shape[0]))

    def lid(n=1):
        first = next(L)
        for _ in range(n - 1):
            next(L)
        return first

    smalls, lens = k["smalls"], k["lens"]
    small_ids, len_ids = cp.take(NF), cp.take(3)
    deal_x = Deal(k["tok"], k["xs"], lid(micro))
    deal_c = Deal(k["cot"], k["cs"], lid(micro))
    aall, hall, call = k["aall"], k["hall"], k["call"]
    e_a, e_c, e_h, e_y = Spread(aall), Spread(call), Spread(hall), Spread(hall)
    part_ = k["part"]
    s_1 = Sum(part_, k["sib0"], k["xsend"], k["xrecv0"])
    s_m = Sum(part_, k["sib1"], k["xsend"], k["xrecv1"])
    s_h = Sum(part_, k["sib0"], k["xsend"], k["xrecv0"])
    s_a = Sum(part_, k["sib0"], k["xsend"], k["xrecv0"])

    own_small = local(k["small"], smalls.at[f], lid())
    pl.semaphore_wait(barrier, len(friends))
    for i, o in enumerate(others):
        n = small_ids + i
        cp.start(lambda n=n, o=o: (k["small"], smalls.at[f], n, n, o, r))
    g_q.start(lid())
    deal_x.start()
    lo_ids = [lid() for _ in g_o]
    for g, i in zip(g_o, lo_ids):
        g.start(i)
    g_i[0].start(lid())

    wd[pl.ds(2 * sz.ffp, sz.fq - 2 * sz.ffp), :] = jnp.zeros((sz.fq - 2 * sz.ffp, d), BF16)

    g_q.column()

    own_small.wait()
    for i in range(NF - 1):
        source = lax.rem(f + NF - 1 - i, NF)
        cp.arrived(smalls.at[source], small_ids + i, f, r)
    gains = k["gains"]
    for j in range(NF):
        gains[0:2, j * sh : (j + 1) * sh] = smalls[j, 0:2, :]
    lane = lax.broadcasted_iota(jnp.int32, (1, 128), 1)
    sub = lax.broadcasted_iota(jnp.int32, (NF, 128), 0)
    ownrow = smalls[f]
    len_tab = smalls[:, 2, :]
    table = jnp.zeros((8, 128), F32)
    row8 = lax.broadcasted_iota(jnp.int32, (8, 128), 0)
    for m in range(micro):
        dealt = jnp.sum(jnp.where(lane == f, ownrow[3 + m : 4 + m, :], 0.0), axis=1, keepdims=True)
        hit = jnp.where(sub.astype(F32) == dealt, len_tab, 0.0)
        col = jnp.sum(hit, axis=0, keepdims=True)
        length = jnp.sum(jnp.where(lane == m, col, 0.0), axis=1, keepdims=True)
        table = jnp.where(row8 == m, length, table)
    lens[r] = table
    for i, to in enumerate((xn, dn, cn)):
        cp.start(lambda i=i, to=to: (lens.at[r], lens.at[r], len_ids + i, len_ids + i, f, to))

    def live_rows(m, t, n):
        pos = lax.broadcasted_iota(jnp.int32, (n, 1), 0).astype(F32) + (t * n).astype(F32)
        return pos < lens[r, m : m + 1, 0:1]

    def live_at(t, n):
        per = slot // n
        m = lax.div(t, per)
        pos = lax.broadcasted_iota(jnp.int32, (n, 1), 0) + lax.rem(t, per) * n
        length = lens[r, pl.ds(m, 1), :][:, 0:1]
        return pos.astype(F32) < length

    def normed(v):
        center = v - jnp.mean(v, axis=-1, keepdims=True)
        root = lax.rsqrt(jnp.mean(center * center, axis=-1, keepdims=True) + NORM_EPS)
        return center * root, root

    def norm_back(dy, gain, vhat, root):
        e = dy * gain
        return root * (e - jnp.mean(e, axis=-1, keepdims=True) - vhat * jnp.mean(e * vhat, axis=-1, keepdims=True))

    NL = 32
    xs, cs, hbuf, dhbuf = k["xs"], k["cs"], k["hbuf"], k["dhbuf"]

    deal_x.done()
    for pending in local_pending:
        pending.wait()
    local_pending.clear()

    def norm1(t):
        vhat, _ = normed(xs[at(t * NL, NL), :].astype(F32))
        aall[at(r * rows + t * NL, NL), :] = (vhat * gains[0:1, :]).astype(BF16)

    loop(rows // NL, norm1)
    e_a.start()
    deal_c.start()
    g_i[1].start(lid())
    for g in g_o:
        g.column()
    g_i[0].column()
    g_q.over_y()
    e_a.forward()
    if sz.ntile > 2:
        g_i[2].start(lid())
    for i, to in enumerate((xn, dn, cn)):
        cp.arrived(lens.at[to], len_ids + i, f, r)
    for g in g_o:
        g.over_y()
    e_a.done()
    g_i[1].column()

    qkv, pbuf, obuf = k["qkv"], k["pbuf"], k["obuf"]
    lane128 = lax.broadcasted_iota(jnp.int32, (1, 128), 1)
    front = lax.rem(lane128, 64) < 32
    low = lane128 < 64
    low_b = low.astype(F32).astype(BF16)
    high_b = (1.0 - low.astype(F32)).astype(BF16)
    hq = sz.hq
    npair = hq // 128
    scale = 64 ** (-0.5)

    def swap(v):
        return jnp.where(front, pltpu.roll(v, 96, 1), pltpu.roll(v, 32, 1))

    def both(v):
        return jnp.concatenate([v * low_b, v * high_b], axis=0)

    def joined(v):
        return jnp.where(low, v[:slot], v[slot:])

    def project(b):
        a = aall[block(b), :]
        for which in range(3):
            t = nn(a, wq[:, which * hq : (which + 1) * hq])
            for p in range(npair):
                v = t[:, p * 128 : (p + 1) * 128]
                if which < 2:
                    v = v * k["cos"][...] + swap(v) * k["sin"][...]
                qkv[block(b), which * hq + p * 128 : which * hq + (p + 1) * 128] = v.astype(BF16)

    def triple(s, p):
        return [qkv[at(s * slot, slot), which * hq + p * 128 : which * hq + (p + 1) * 128] for which in range(3)]

    def attend(b):
        def one(m):
            s = b * micro + m
            length = lens[b, pl.ds(m, 1), :]
            for p in range(npair):
                q_, k_, v_ = triple(s, p)
                scores = nt(both(q_), k_) * scale
                scores = jnp.where(lane128.astype(F32) < length, scores, -1e30)
                e = jnp.exp(scores - jnp.max(scores, axis=-1, keepdims=True))
                prob = e / jnp.sum(e, axis=-1, keepdims=True)
                pbuf[s, p] = prob
                out = nn(prob.astype(BF16), v_)
                obuf[at(s * slot, slot), p * 128 : (p + 1) * 128] = joined(out).astype(BF16)

        loop(micro, one)

    def branch_one(b):
        def tile(n):
            cols = at(n * 256, 256, 128)
            part_[block(b), cols] = nn(obuf[block(b), :], wo[:, cols])

        loop(d // 256, tile)

    for i, b in enumerate(s_1.order):
        project(b)
        attend(b)
        branch_one(b)
        s_1.ready(i)
        if i == 0:
            g_i[0].over_y()
            g_i[1].over_y()
        if i == 1 and sz.ntile > 2:
            g_i[2].column()
        if i == 1:
            for g in g_d:
                g.start(lid())

    deal_c.done()
    for pending in local_pending:
        pending.wait()
    local_pending.clear()

    def mask_c(t):
        lv = live_at(t, NL)
        call[at(r * rows + t * NL, NL), :] = jnp.where(lv, cs[at(t * NL, NL), :].astype(F32), 0.0).astype(BF16)

    loop(rows // NL, mask_c)

    s_1.done()

    def norm2(t):
        s = at(t * NL, NL)
        h = xs[s, :].astype(F32) + jnp.where(live_at(t, NL), s_1.value(t, NL), 0.0)
        hbuf[s, :] = h
        vhat, _ = normed(h)
        hall[at(r * rows + t * NL, NL), :] = (vhat * gains[1:2, :]).astype(BF16)

    loop(rows // NL, norm2)
    e_h.start()
    e_c.start()
    for g in g_d:
        g.column()
    for g in g_i[2:]:
        g.over_y()
    s_1.free()
    e_h.forward()
    e_h.done()

    gg, slope = k["gg"], k["slope"]
    tile_ = sz.tile

    def feed(i):
        b = lax.div(i, sz.ntile)
        n = lax.rem(i, sz.ntile)
        rs = at(b * rows, rows)
        w = nn(hall[rs, :], wi[:, at(n * 2 * tile_, 2 * tile_, 128)])
        w1, w2 = w[:, :tile_], w[:, tile_:]
        cdf = 0.5 * (1.0 + lax.erf(w1 * (0.5**0.5)))
        act = w1 * cdf
        pdf = jnp.exp(-0.5 * w1 * w1) * 0.3989422804014327
        cols = at(n * tile_, tile_, 128)
        gg[rs, cols] = (act * w2).astype(BF16)
        part_[rs, cols] = act
        slope[rs, cols] = w2 * (cdf + w1 * pdf)

    loop(NR * sz.ntile, feed)
    e_h.free()
    e_c.forward()
    e_c.done()
    for g in g_d:
        g.over_y()

    gd, gi, go, gq = k["gd"], k["gi"], k["go"], k["gq"]
    r_d = [RowReduce(gd, k["yrd"].at[i], k["zrd"].at[i], k["rd"], i * third, third, sz.ffp) for i in range(3)]
    r_i = [
        ColumnReduce(gi.at[n], k["yri"].at[n], k["zri"].at[n], None, k["ri"], n * t2, t2) for n in range(sz.ntile)
    ]
    r_o = [
        RowReduce(go, k["yro"].at[i], k["zro"].at[i], k["ro"], i * (sh // 2), sh // 2, sh) for i in range(2)
    ]
    r_q = ColumnReduce(gq, k["yrq"], k["zrq"], None, k["rq"], 0, 3 * hq)

    def grad_down(i):
        m = lax.div(i, 2)
        n = lax.rem(i, 2)
        cols = at(n * (d // 2), d // 2, 128)
        gd[at(m * 256, 256), cols] = tn(gg[:, at(m * 256, 256, 128)], call[:, cols]).astype(BF16)

    loop(sz.fq // 256 * 2, grad_down)
    for u in r_d:
        u.send()

    dw = k["dw"]

    def hidden(i):
        b = lax.div(i, sz.ntile)
        n = lax.rem(i, sz.ntile)
        rs = at(b * rows, rows)
        cols = at(n * tile_, tile_, 128)
        dgg = nt(call[rs, :], wd[at(n * tile_, tile_), :])
        dw[rs, at(n * 2 * tile_, tile_, 128)] = (dgg * slope[rs, cols]).astype(BF16)
        dw[rs, at(n * 2 * tile_ + tile_, tile_, 128)] = (dgg * part_[rs, cols]).astype(BF16)

    loop(NR * sz.ntile, hidden)
    for u in r_d:
        u.middle()

    def grad_in(n, j):
        gi[n, at(j * sh, sh), :] = tn(
            hall[:, at(j * sh, sh, 128)], dw[:, at(n * 2 * tile_, 2 * tile_, 128)]
        ).astype(BF16)

    def gin(other):
        for n in range(sz.ntile):

            def one(i, n=n):
                grad_in(n, 2 * i + (1 - y if other else y))

            loop(NZ, one)
            if other:
                for i in range(NZ):
                    r_i[n].send(2 * i + 1 - y)

    gin(True)
    gin(False)

    for i, b in enumerate(s_h.order):

        def tile(n, b=b):
            cols = at(n * 256, 256, 128)
            part_[block(b), cols] = nt(dw[block(b), :], wi[at(n * 256, 256), :])

        loop(d // 256, tile)
        s_h.ready(i)
    for u in r_d:
        u.final(lid())
    r_i[0].middle()
    dg = k["dg"]
    dg[...] = jnp.zeros_like(dg)
    s_h.done()

    def fold(v):
        return jnp.sum(v.reshape(NL // 8, 8, d), axis=0)

    def back2(t):
        s = at(t * NL, NL)
        dy = s_h.value(t, NL)
        vhat, root = normed(hbuf[s, :])
        dg[1] += fold(dy * vhat)
        dh = cs[s, :].astype(F32) + norm_back(dy, gains[1:2, :], vhat, root)
        dhbuf[s, :] = dh
        hall[at(r * rows + t * NL, NL), :] = jnp.where(live_at(t, NL), dh, 0.0).astype(BF16)

    loop(rows // NL, back2)
    e_y.start()
    s_h.free()

    mx = k["mx"]
    for i, b in enumerate(s_m.order):

        def tile(n, b=b):
            cols = at(n * 256, 256, 128)
            part_[block(b), cols] = nn(gg[block(b), :], wd[:, cols])

        loop(d // 256, tile)
        s_m.ready(i)
    r_i[1].middle()
    e_y.forward()
    e_y.done()

    def grad_out(i):
        cols = at(i * 256, 256, 128)
        go[:, cols] = tn(obuf[...], hall[:, cols]).astype(BF16)

    loop(d // 256, grad_out)
    for u in r_o:
        u.send()

    def attend_back(s):
        do_all = nt(hall[at(s * slot, slot), :], wo[...]).astype(BF16)
        for p in range(npair):
            q_, k_, v_ = triple(s, p)
            q2, do2 = both(q_), both(do_all[:, p * 128 : (p + 1) * 128])
            prob = pbuf[s, p]
            dp = nt(do2, v_)
            ds = (prob * (dp - jnp.sum(dp * prob, axis=-1, keepdims=True))).astype(BF16)
            dq = joined(nn(ds, k_)) * scale
            dk = tn(ds, q2) * scale
            dv = tn(prob.astype(BF16), do2)
            cosine, sine = k["cos"][0:slot, :], k["sin"][0:slot, :]
            dq = dq * cosine - swap(dq) * sine
            dk = dk * cosine - swap(dk) * sine
            for which, v in enumerate((dq, dk, dv)):
                dw[at(s * slot, slot), which * hq + p * 128 : which * hq + (p + 1) * 128] = v.astype(BF16)

    loop(NR * micro, attend_back)

    def grad_qkv(j):
        gq[at(j * sh, sh), :] = tn(aall[:, at(j * sh, sh, 128)], dw[:, 0 : 3 * hq]).astype(BF16)

    loop(NZ, lambda i: grad_qkv(2 * i + 1 - y))
    for i in range(NZ):
        r_q.send(2 * i + 1 - y)
    s_m.done()

    def mix(t):
        s = at(t * NL, NL)
        mx[s, :] = (hbuf[s, :] + jnp.where(live_at(t, NL), s_m.value(t, NL), 0.0)).astype(BF16)

    loop(rows // NL, mix)
    back_m = Back(mx, k["o_mixed"], lid(micro))
    back_m.start()
    s_m.free()
    for i, b in enumerate(s_a.order):

        def tile(n, b=b):
            cols = at(n * 256, 256, 128)
            part_[block(b), cols] = nt(dw[block(b), 0 : 3 * hq], wq[at(n * 256, 256), :])

        loop(d // 256, tile)
        s_a.ready(i)
    loop(NZ, lambda i: grad_qkv(2 * i + y))
    for u in r_o:
        u.middle()
    for u in r_i[2:]:
        u.middle()
    r_q.middle()
    s_a.done()
    gt = k["gt"]

    def back1(t):
        s = at(t * NL, NL)
        dy = s_a.value(t, NL)
        vhat, root = normed(xs[s, :].astype(F32))
        dg[0] += fold(dy * vhat)
        gt[s, :] = (dhbuf[s, :] + norm_back(dy, gains[0:1, :], vhat, root)).astype(BF16)

    loop(rows // NL, back1)
    back_t = Back(gt, k["o_gtok"], lid(micro))
    back_t.start()

    gsend, gslots, greps = k["gsend"], k["gslots"], k["greps"]
    for which in range(2):
        total = jnp.sum(dg[which], axis=0, keepdims=True)
        for j in range(NF):
            gsend[j, which : which + 1, :] = total[:, j * sh : (j + 1) * sh]
    gs_ids, gr_ids = cp.take(NF), cp.take(3)
    for i, o in enumerate(others):
        n = gs_ids + i
        cp.start(lambda n=n, o=o: (gsend.at[o], gslots.at[f], n, n, o, r))
    gslots[f] = gsend[f]
    for u in r_i:
        u.final(lid())
    for u in r_o:
        u.final(lid())
    for i in range(NF - 1):
        source = lax.rem(f + NF - 1 - i, NF)
        cp.arrived(gslots.at[source], gs_ids + i, f, r)
    total = gslots[0]
    for j in range(1, NF):
        total = total + gslots[j]
    greps[r] = total
    for i, to in enumerate((xn, dn, cn)):
        cp.start(lambda i=i, to=to: (greps.at[r], greps.at[r], gr_ids + i, gr_ids + i, f, to))
    r_q.final(lid())
    for i, source in enumerate((xn, dn, cn)):
        cp.arrived(greps.at[source], gr_ids + i, f, r)
    gout = k["gout"]
    gout[...] = greps[0] + greps[1] + greps[2] + greps[3]
    local_pending.append(local(gout, k["o_small"], lid()))

    for u in r_d + r_i + r_o + [r_q, back_m, back_t]:
        u.done()
    s_a.free()
    for e in (e_a, e_c, e_y):
        e.free()
    cp.drain()
    for pending in local_pending:
        pending.wait()


def fused(sz, tok, cot, small, cos, sin, sq, so, si, sd):
    d, sh, all_, rows = sz.d, sz.shard, sz.all, sz.rows
    t2 = 2 * sz.tile
    third, half = sz.ffp // 3, sh // 2
    hq3 = 3 * sz.hq
    bf = lambda *s: pltpu.VMEM(s, BF16)
    fl = lambda *s: pltpu.VMEM(s, F32)
    ins = ("tok", "cot", "small", "cos", "sin", "sq", "so", "si", "sd")
    outs = {
        "o_mixed": jax.ShapeDtypeStruct((sz.micro, NF, sz.part, d), BF16),
        "o_gtok": jax.ShapeDtypeStruct((sz.micro, NF, sz.part, d), BF16),
        "o_small": jax.ShapeDtypeStruct((8, 128), F32),
        "rq": jax.ShapeDtypeStruct((NR, sh, hq3), BF16),
        "ro": jax.ShapeDtypeStruct((sh, d), BF16),
        "ri": jax.ShapeDtypeStruct((NR, sh, sz.ntile * t2), BF16),
        "rd": jax.ShapeDtypeStruct((sz.ffp, d), BF16),
    }
    scratch = {
        "wq": bf(d, hq3), "wo": bf(2 * sh, d), "wi": bf(d, sz.ntile * t2), "wd": bf(sz.fq, d),
        "xs": bf(rows, d), "cs": bf(rows, d), "mx": bf(rows, d), "gt": bf(rows, d),
        "aall": bf(all_, d), "hall": bf(all_, d), "call": bf(all_, d),
        "smalls": fl(NF, 8, 128), "lens": fl(NR, 8, 128), "gains": fl(8, d),
        "qkv": bf(all_, hq3), "pbuf": fl(NR * sz.micro, sz.hq // 128, 2 * sz.slot, 128), "obuf": bf(all_, sz.hq),
        "part": fl(all_, d), "sib0": fl(2, rows, d), "sib1": fl(2, rows, d),
        "xsend": bf(rows, d), "xrecv0": bf(rows, d), "xrecv1": bf(rows, d),
        "hbuf": fl(rows, d), "dhbuf": fl(rows, d), "dg": fl(2, 8, d),
        "gg": bf(all_, sz.fq), "slope": fl(all_, sz.fq), "dw": bf(all_, sz.ntile * t2),
        "gd": bf(sz.fq, d), "gi": bf(sz.ntile, d, t2), "go": bf(2 * sh, d), "gq": bf(d, hq3),
        "yrd": bf(3, third, d), "zrd": bf(3, 2, third, d),
        "yri": bf(sz.ntile, NZ, sh, t2), "zri": bf(sz.ntile, NZ + 1, sh, t2),
        "yro": bf(2, half, d), "zro": bf(2, 2, half, d),
        "yrq": bf(NZ, sh, hq3), "zrq": bf(NZ + 1, sh, hq3),
        "gsend": fl(NF, 8, 128), "gslots": fl(NF, 8, 128), "greps": fl(NR, 8, 128), "gout": fl(8, 128),
        "sends": pltpu.SemaphoreType.DMA((384,)), "recvs": pltpu.SemaphoreType.DMA((384,)),
        "locals": pltpu.SemaphoreType.DMA((48,)),
    }
    any_ = pl.BlockSpec(memory_space=pl.ANY)
    vmem = pl.BlockSpec(memory_space=pltpu.VMEM)
    names = ins + tuple(outs) + tuple(scratch)
    return pl.pallas_call(
        functools.partial(kernel, sz, names),
        out_shape=list(outs.values()),
        in_specs=[any_] * 3 + [vmem] * 2 + [any_] * 4,
        out_specs=[any_] * len(outs),
        scratch_shapes=list(scratch.values()),
        compiler_params=pltpu.CompilerParams(collective_id=0, has_side_effects=True, vmem_limit_bytes=64 * MIB),
    )(tok, cot, small, cos, sin, sq, so, si, sd)


def routed(tokens, cotangent, deal, lengths, ln1_gain, w_qkv, w_out, ln2_gain, w_in, w_down):
    micro, _, part, d = tokens.shape
    ffs = w_down.shape[0]
    sz = Sizes(micro, part, d, ffs)
    r = lax.axis_index("rep")
    hq, sh = sz.hq, sz.shard
    quarter = lambda w, start: lax.dynamic_slice_in_dim(w, start, hq, axis=1)
    sq = jnp.concatenate([quarter(w_qkv, i * d + r * hq) for i in range(3)], axis=1).astype(BF16)
    so = w_out.astype(BF16)
    sd = jnp.pad(w_down.astype(BF16), ((0, sz.ffp - ffs), (0, 0)))
    halves = []
    for i in range(2):
        w = lax.dynamic_slice_in_dim(w_in, i * NF * ffs + r * 2 * ffs, 2 * ffs, axis=1).astype(BF16)
        gap = jnp.zeros((sh, sz.ffp - ffs), BF16)
        end = jnp.zeros((sh, sz.fq - 2 * sz.ffp), BF16)
        halves.append(jnp.concatenate([w[:, :ffs], gap, w[:, ffs:], gap, end], axis=1))
    t = sz.tile
    si = jnp.concatenate([h[:, n * t : (n + 1) * t] for n in range(sz.ntile) for h in halves], axis=1)
    gain = [lax.reduce_precision(g, 8, 7)[None] for g in (ln1_gain, ln2_gain)]
    wide = lambda v: jnp.pad(v.astype(F32), ((0, 0), (0, 128 - v.shape[1])))
    small = jnp.concatenate(gain + [wide(lengths[:, 0, 0][None]), wide(deal[:, 0]), jnp.zeros((5 - micro, 128), F32)])
    half = 32
    freq = ROPE_BASE ** (-(jnp.arange(half, dtype=F32) * 2.0 / (2 * half)))
    angles = jnp.arange(sz.slot, dtype=F32)[:, None] * freq[None, :]
    cos = jnp.tile(jnp.cos(angles), (micro, 4))
    sin = jnp.tile(jnp.concatenate([-jnp.sin(angles), jnp.sin(angles)], axis=1), (micro, 2))
    mixed, gtok, osmall, rq, ro, ri, rd = fused(sz, tokens, cotangent, small, cos, sin, sq, so, si, sd)
    grad_qkv = jnp.concatenate(
        [rq[q, :, i * hq : (i + 1) * hq] for i in range(3) for q in range(NR)], axis=1
    ).astype(F32)
    pieces = []
    for i in range(2):
        for q in range(NR):
            w = jnp.concatenate([ri[q, :, (2 * n + i) * t : (2 * n + i + 1) * t] for n in range(sz.ntile)], axis=1)
            pieces += [w[:, :ffs], w[:, sz.ffp : sz.ffp + ffs]]
    grad_in = jnp.concatenate(pieces, axis=1).astype(F32)
    return mixed, gtok, osmall[0], grad_qkv, ro.astype(F32), osmall[1], grad_in, rd[:ffs].astype(F32)


def solution(mesh):
    small = mesh.shape["fsdp"] == NF and mesh.shape["rep"] == NR
    rows = P(None, "rep", "fsdp", None)
    return jax.shard_map(
        routed if small else plain,
        mesh=mesh,
        in_specs=(
            rows, rows, P(None, "rep", None), P(None, "rep", "fsdp"),
            P("fsdp"), P("fsdp", None), P("fsdp", None), P("fsdp"), P("fsdp", None), P("fsdp", None),
        ),
        out_specs=(rows, rows, P("fsdp"), P("fsdp", None), P("fsdp", None), P("fsdp"), P("fsdp", None), P("fsdp", None)),
        check_vma=False,
    )
```

```python
import functools
import types

import jax
import jax.numpy as jnp
import numpy as np
from jax import lax
from jax.experimental import pallas as pl
from jax.experimental.pallas import tpu as pltpu
from jax.sharding import PartitionSpec as P

HEADS = 16
ROPE_BASE = 160000.0
NORM_EPS = 1e-05
MESH = pl.DeviceIdType.MESH
MIB = 1 << 20
BF16 = jnp.bfloat16
F32 = jnp.float32


def rope_tables(slot_count, head_size):
    half_size = head_size // 2
    frequency = ROPE_BASE ** (-(jnp.arange(half_size, dtype=F32) * 2.0 / head_size))
    angles = jnp.arange(slot_count, dtype=F32)[:, None] * frequency[None, :]
    return jnp.cos(angles), jnp.sin(angles)


def rotate(values, cosine, sine):
    front, back = jnp.split(values, 2, axis=-1)
    cosine, sine = cosine[:, None, :], sine[:, None, :]
    return jnp.concatenate([front * cosine - back * sine, back * cosine + front * sine], axis=-1)


def normed(values, gain):
    center = values - jnp.mean(values, axis=-1, keepdims=True)
    root = lax.rsqrt(jnp.mean(center * center, axis=-1, keepdims=True) + NORM_EPS)
    vhat = center * root
    return vhat * gain, vhat, root


def norm_back(dy, gain, vhat, root):
    dgain = jnp.sum(dy * vhat, axis=tuple(range(dy.ndim - 1)))
    e = dy * gain
    dz = root * (
        e
        - jnp.mean(e, axis=-1, keepdims=True)
        - vhat * jnp.mean(e * vhat, axis=-1, keepdims=True)
    )
    return dgain, dz


def mm(spec, a, b):
    return jnp.einsum(spec, a, b, preferred_element_type=F32)


def layer(g1, wqkv, wo, g2, win, wdown, tokens, dout, live):
    m, slot, d = tokens.shape
    heads, size = HEADS, d // HEADS
    scale = size ** (-0.5)
    w1, w2 = win
    lv = live[:, :, None]
    x = tokens.astype(F32)
    y, vhat1, root1 = normed(x, g1)
    a = y.astype(BF16)
    qkv = mm("mtd,de->mte", a, wqkv).reshape(m, slot, 3, heads, size)
    cosine, sine = rope_tables(slot, size)
    q = rotate(qkv[:, :, 0], cosine, sine).astype(BF16)
    k = rotate(qkv[:, :, 1], cosine, sine).astype(BF16)
    v = qkv[:, :, 2].astype(BF16)
    s = mm("mqhd,mkhd->mhqk", q, k) * scale
    s = jnp.where(live[:, None, None, :] > 0, s, -1e30)
    p = jax.nn.softmax(s, axis=-1)
    pb = p.astype(BF16)
    o = mm("mhqk,mkhd->mqhd", pb, v).astype(BF16).reshape(m, slot, d)
    h = x + lv * mm("mte,ed->mtd", o, wo)
    y, vhat2, root2 = normed(h, g2)
    hn = y.astype(BF16)
    z1 = mm("mtd,df->mtf", hn, w1)
    z2 = mm("mtd,df->mtf", hn, w2)
    cdf = 0.5 * (1.0 + lax.erf(z1 * (0.5**0.5)))
    pdf = jnp.exp(-0.5 * z1 * z1) * 0.3989422804014327
    act = z1 * cdf
    gg = (act * z2).astype(BF16)
    mixed = (h + lv * mm("mtf,fd->mtd", gg, wdown)).astype(BF16)

    up = dout.astype(F32)
    dy2 = (lv * up).astype(BF16)
    g_down = mm("mtf,mtd->fd", gg, dy2)
    dgg = mm("mtd,fd->mtf", dy2, wdown)
    dw1 = (dgg * z2 * (cdf + z1 * pdf)).astype(BF16)
    dw2 = (dgg * act).astype(BF16)
    g_in = (mm("mtd,mtf->df", hn, dw1), mm("mtd,mtf->df", hn, dw2))
    dhn = mm("mtf,df->mtd", dw1, w1) + mm("mtf,df->mtd", dw2, w2)
    g_g2, dhv = norm_back(dhn, g2, vhat2, root2)
    dh = up + dhv
    dy1 = (lv * dh).astype(BF16)
    g_out = mm("mte,mtd->ed", o, dy1)
    do = mm("mtd,ed->mte", dy1, wo).astype(BF16).reshape(m, slot, heads, size)
    dp = mm("mqhd,mkhd->mhqk", do, v)
    ds = (p * (dp - jnp.sum(dp * p, axis=-1, keepdims=True))).astype(BF16)
    dq = mm("mhqk,mkhd->mqhd", ds, k) * scale
    dk = mm("mhqk,mqhd->mkhd", ds, q) * scale
    dv = mm("mhqk,mqhd->mkhd", pb, do)
    dqkv = jnp.stack([rotate(dq, cosine, -sine), rotate(dk, cosine, -sine), dv], axis=2)
    dqkv = dqkv.reshape(m, slot, 3 * d).astype(BF16)
    g_qkv = mm("mtd,mte->de", a, dqkv)
    da = mm("mte,de->mtd", dqkv, wqkv)
    g_g1, dxv = norm_back(da, g1, vhat1, root1)
    gtok = (dh + dxv).astype(BF16)
    return mixed, gtok, (g_g1, g_qkv, g_out, g_g2, g_in, g_down)


def plain(tokens, cotangent, deal, lengths, ln1_gain, w_qkv, w_out, ln2_gain, w_in, w_down):
    slot = tokens.shape[2] * lax.axis_size("fsdp")
    me = lax.axis_index("fsdp")

    def spread(rows):
        return lax.all_to_all(rows, "fsdp", split_axis=1, concat_axis=2, tiled=True)[:, 0]

    def back(rows):
        return lax.all_to_all(rows[:, None], "fsdp", split_axis=2, concat_axis=1, tiled=True)

    def whole(shard):
        return lax.all_gather(shard.astype(BF16), "fsdp", axis=0, tiled=True)

    table = lax.all_gather(lengths[:, 0], "fsdp", axis=1, tiled=True)
    mine = lax.dynamic_slice_in_dim(deal[:, 0], me, 1, axis=1)
    pick = jnp.arange(table.shape[1], dtype=jnp.int32)[None, :] == mine
    length = jnp.sum(jnp.where(pick, table, 0), axis=1, keepdims=True)
    live = (jnp.arange(slot, dtype=jnp.int32)[None, :] < length).astype(F32)
    win = jnp.split(whole(w_in), 2, axis=1)
    mixed, gtok, grads = layer(
        whole(ln1_gain).astype(F32), whole(w_qkv), whole(w_out), whole(ln2_gain).astype(F32), win, whole(w_down),
        spread(tokens), spread(cotangent), live,
    )
    g_g1, g_qkv, g_out, g_g2, g_in, g_down = grads

    def owned(part):
        part = lax.psum_scatter(part, "fsdp", scatter_dimension=0, tiled=True)
        return lax.psum(part, "rep")

    g_in = jnp.concatenate(g_in, axis=1)
    return (back(mixed), back(gtok)) + tuple(owned(g) for g in (g_g1, g_qkv, g_out, g_g2, g_in, g_down))


NF, NR, NZ = 8, 4, 4
DN, XN, CN = 0, 1, 2


def at(offset, size, unit=16):
    return pl.ds(pl.multiple_of(offset, unit), size)


def nn(a, b):
    return lax.dot_general(a, b, (((1,), (0,)), ((), ())), preferred_element_type=F32)


def nt(a, b):
    return lax.dot_general(a, b, (((1,), (1,)), ((), ())), preferred_element_type=F32)


def tn(a, b):
    return lax.dot_general(a, b, (((0,), (0,)), ((), ())), preferred_element_type=F32)


def loop(n, body):
    def step(i, carry):
        body(i)
        return carry

    lax.fori_loop(0, n, step, 0)


ORDER = (
    2, 0, 14, 15, 62, 1, 10, 43, 4, 44, 5, 6, 3, 7, 45, 47, 23, 64, 48, 49, 63, 8, 12, 16, 50, 42, 11, 17, 65, 25,
    52, 13, 9, 59, 24, 66, 28, 33, 51, 39, 36, 18, 57, 55, 46, 53, 54, 56, 19, 30, 61, 60, 20, 69, 21, 29, 58, 67,
    31, 71, 22, 26, 34, 72, 68, 76, 70, 40, 75, 32, 73, 74, 27, 80, 79, 37, 81, 41, 77, 78, 82, 38, 35, 86, 83, 93,
    85, 84, 94, 97, 132, 95, 90, 87, 138, 88, 89, 96, 135, 98, 99, 119, 141, 100, 105, 142, 103, 118, 146, 92, 136,
    133, 101, 106, 102, 147, 143, 91, 104, 115, 162, 109, 116, 161, 107, 156, 148, 117, 157, 137, 120, 144, 152,
    121, 108, 110, 111, 166, 139, 167, 112, 114, 122, 123, 171, 149, 163, 113, 176, 124, 126, 168, 151, 172, 173,
    134, 177, 169, 178, 140, 145, 125, 158, 153, 127, 128, 150, 174, 179, 129, 159, 170, 160, 164, 154, 130, 155,
    175, 180, 131, 165, 181,
)


def run_tasks(tasks):
    done = set()
    for i in ORDER or range(len(tasks)):
        deps, fn = tasks[i]
        assert done.issuperset(deps)
        fn()
        done.add(i)
    assert len(done) == len(tasks)


SOURCES = ((1, 0, 3, 2), (2, 2, 1, 1), (3, 3, 0, 0))
SOURCE_BELOW = ((0, 1, 0, 1), (0, 0, 1, 1), (0, 0, 1, 1))
OWNERS = ((3, 3, 0, 0), (2, 2, 1, 1), (1, 0, 3, 2))
OWNER_ABOVE = ((1, 1, 0, 0), (1, 1, 0, 0), (1, 0, 1, 0))
OWNER_SLOT = ((3, 3, 0, 0), (2, 2, 4, 1), (1, 4, 3, 4))


class Sizes:
    def __init__(self, micro, part, d, ffs):
        self.micro, self.part, self.d, self.ffs = micro, part, d, ffs
        self.slot = part * NF
        self.rows = micro * self.slot
        self.all = NR * self.rows
        self.shard = d // NF
        self.hq = d // NR
        self.ffp = -(-ffs // 16) * 16
        self.tile = 256
        self.ntile = -(-(2 * self.ffp) // self.tile)
        self.fq = self.ntile * self.tile


class Copies:
    def __init__(self, sends, recvs):
        self.sends, self.recvs, self.nsend, self.nrecv = sends, recvs, 0, 0
        self.left = []

    def send(self, n=1):
        base, self.nsend = self.nsend, self.nsend + n
        assert self.nsend <= self.sends.shape[0]
        return base

    def recv(self, n=1):
        base, self.nrecv = self.nrecv, self.nrecv + n
        assert self.nrecv <= self.recvs.shape[0]
        return base

    def make(self, src, dst, send, recv, f, r):
        return pltpu.make_async_remote_copy(
            src_ref=src, dst_ref=dst, send_sem=self.sends.at[send], recv_sem=self.recvs.at[recv],
            device_id={"fsdp": f, "rep": r}, device_id_type=MESH,
        )

    def start(self, build, cond=None):
        def go():
            self.make(*build()).start()

        go() if cond is None else pl.when(cond)(go)

    def arrived(self, ref, recv, f, r):
        self.make(ref, ref, 0, recv, f, r).wait_recv()

    def gone(self, ref, send, f, r, cond=None):
        def go():
            self.make(ref, ref, send, 0, f, r).wait_send()

        go() if cond is None else pl.when(cond)(go)

    def at_end(self, ref, send, cond=None):
        self.left.append((ref, send, cond))


def kernel(sz, names, *refs):
    k = types.SimpleNamespace(**dict(zip(names, refs)))
    d, rows, slot, micro, part = sz.d, sz.rows, sz.slot, sz.micro, sz.part
    f, r = lax.axis_index("fsdp"), lax.axis_index("rep")
    z, y = lax.div(f, 2), lax.rem(f, 2)
    c = lax.rem(r, 2)
    yn = f + 1 - 2 * y
    cn = r + 1 - 2 * c
    xn = lax.rem(r + 2, 4)
    dn = lax.rem(cn + 2, 4)
    others = [lax.rem(f + i, NF) for i in range(1, NF)]
    cp = Copies(k.sends, k.recvs)

    def local(src, dst, i):
        copy = pltpu.make_async_copy(src, dst, k.locals.at[i])
        copy.start()
        return copy

    def block(i):
        return at(i * rows, rows)

    barrier = pltpu.get_barrier_semaphore()
    friends = [(o, r) for o in others] + [(f, o) for o in (cn, xn, dn)]
    for ff, rr in friends:
        pl.semaphore_signal(barrier, inc=1, device_id={"fsdp": ff, "rep": rr}, device_id_type=MESH)

    tasks = []

    def task(*deps):
        def register(fn):
            tasks.append((deps, fn))
            return len(tasks) - 1

        return register

    wq, wo, wi, wd = k.wq, k.wo, k.wi, k.wd
    sh = sz.shard
    micros = range(micro)
    ends = []

    eights = (1 + 7 * lax.rem(z, 2)) * (1 + 63 * lax.div(z, 2))

    def by_z(*values):
        code = sum(v << (3 * i) for i, v in enumerate(values))
        return lax.rem(lax.div(jnp.int32(code), eights), 8)

    inner = jnp.logical_and(z > 0, z < NZ - 1)
    order_z = [by_z(*o) for o in OWNERS] + [z]

    class ColumnGather:
        def __init__(self, whole, col, width):
            self.whole, self.cols = whole, at(col, width, 128)
            self.zrecv, self.yrecv, self.zsend, self.ysend = cp.recv(NZ), cp.recv(), cp.send(), cp.send()
            cp.at_end(self.shards(NZ), self.ysend)
            cp.at_end(self.shards(NZ + 1), self.zsend, inner)
            cp.at_end(self.shards(1), self.zsend, jnp.logical_not(inner))

        def shards(self, n):
            return self.whole.at[pl.ds(0, n * sh), self.cols]

        def dst(self, j):
            return self.whole.at[at(j * sh, sh), self.cols]

        def over(self, j):
            dst = self.dst(j)
            cp.start(lambda: (dst, dst, self.ysend, self.yrecv, yn, r))

        def start(self):
            src = self.dst(f)
            cp.start(lambda: (src, src, self.zsend, self.zrecv + z, f + 2, r), z < NZ - 1)
            cp.start(lambda: (src, src, self.zsend, self.zrecv + z, f - 2, r), z > 0)
            self.over(f)

        def along_z(self, i):
            source, up = by_z(*SOURCES[i]), by_z(*SOURCE_BELOW[i])
            j = 2 * source + y
            dst = self.dst(j)
            cp.arrived(dst, self.zrecv + source, f, r)
            cp.start(lambda: (dst, dst, self.zsend, self.zrecv + source, f + 2 * (2 * up - 1), r), inner)
            self.over(j)

        def over_y(self):
            cp.arrived(self.shards(NZ), self.yrecv, f, r)

        def register(self, *deps):
            start = task(*deps)(self.start)
            steps = [task(start)(lambda i=i: self.along_z(i)) for i in range(NZ - 1)]
            self.needs = [start, *steps, task(start)(self.over_y)]

    class LongRowGather:
        def __init__(self, whole, row, height, pitch):
            self.whole, self.row, self.height, self.pitch = whole, row, height, pitch
            self.recv, self.send = cp.recv(2), cp.send(3)
            for n, cond in ((0, z < NZ - 1), (1, z > 0)):
                cp.at_end(self.dst(y), self.send + n, jnp.logical_and((z >= r) if n == 0 else (z <= r), cond))
            cp.at_end(self.dst(y), self.send + 2)

        def dst(self, yy):
            return self.whole.at[at(yy * self.pitch + self.row, self.height)]

        def onward(self):
            dst = self.dst(y)
            up = jnp.logical_and(z >= r, z < NZ - 1)
            down = jnp.logical_and(z <= r, z > 0)
            cp.start(lambda: (dst, dst, self.send, self.recv + y, f + 2, r), up)
            cp.start(lambda: (dst, dst, self.send + 1, self.recv + y, f - 2, r), down)
            cp.start(lambda: (dst, dst, self.send + 2, self.recv + y, yn, r))

        def start(self):
            @pl.when(z == r)
            def _():
                self.onward()

        def pass_on(self):
            @pl.when(z != r)
            def _():
                cp.arrived(self.dst(y), self.recv + y, f, r)
                self.onward()

        def rest(self):
            cp.arrived(self.dst(1 - y), self.recv + 1 - y, f, r)

        def register(self, *deps):
            start = task(*deps)(self.start)
            self.needs = [start, task(start)(self.pass_on), task(start)(self.rest)]

    class RowGather:
        def __init__(self, whole, row, height, pitch):
            self.whole, self.row, self.height, self.pitch = whole, row, height, pitch
            self.recv, self.send = cp.recv(2), cp.send(5)
            for yy, send in ((y, self.send), (1 - y, self.send + 2)):
                cp.at_end(self.dst(yy), send, self.up)
                cp.at_end(self.dst(yy), send + 1, self.down)
            cp.at_end(self.dst(y), self.send + 4, z == r)

        up = jnp.logical_and(z >= r, z < NZ - 1)
        down = jnp.logical_and(z <= r, z > 0)

        def dst(self, yy):
            return self.whole.at[at(yy * self.pitch + self.row, self.height)]

        def onward(self, yy, send):
            dst = self.dst(yy)
            cp.start(lambda: (dst, dst, send, self.recv + yy, f + 2, r), self.up)
            cp.start(lambda: (dst, dst, send + 1, self.recv + yy, f - 2, r), self.down)

        def start(self):
            dst = self.dst(y)
            cp.start(lambda: (dst, dst, self.send + 4, self.recv + y, yn, r), z == r)

        last = jnp.logical_and(z != r, jnp.logical_or(z == 0, z == NZ - 1))

        def pass_on(self, near):
            yy, send = (y, self.send) if near else (1 - y, self.send + 2)
            waits = jnp.logical_not(self.last)

            @pl.when(jnp.logical_and(waits, z != r) if near else waits)
            def _():
                cp.arrived(self.dst(yy), self.recv + yy, f, r)

            self.onward(yy, send)

        def rest(self):
            @pl.when(self.last)
            def _():
                for yy in (y, 1 - y):
                    cp.arrived(self.dst(yy), self.recv + yy, f, r)

        def register(self, *deps):
            start = task(*deps)(self.start)
            self.needs = [task(start)(lambda near=near: self.pass_on(near)) for near in (1, 0)]
            self.needs += [start, task(start)(self.rest)]

    class Spread:
        def __init__(self, buf):
            self.buf = buf
            self.ids, self.out = [cp.recv(3) for _ in micros], cp.send()

        def ref(self, b, m):
            return self.buf.at[at(b * rows + m * slot, slot)]

        def start(self, m):
            own, n = self.ref(r, m), self.ids[m]
            cp.start(lambda: (own, own, self.out, n + 1, f, xn))
            cp.start(lambda: (own, own, self.out, n, f, cn))

        def forward(self, m):
            got, n = self.ref(xn, m), self.ids[m]
            cp.arrived(got, n + 1, f, r)
            cp.start(lambda: (got, got, self.out, n + 2, f, cn))

        def got(self, b):
            for m in micros:
                if b is cn:
                    cp.arrived(self.ref(cn, m), self.ids[m], f, r)
                elif b is dn:
                    cp.arrived(self.ref(dn, m), self.ids[m] + 2, f, r)

        def register(self, deps):
            forward = [task(*deps)(lambda m=m: self.forward(m)) for m in micros]
            got = [task(*deps)(lambda b=b: self.got(b)) for b in (cn, dn)]
            self.need = [[got[1]], forward, [got[0]], list(deps)]
            self.all = [*forward, *got, *deps]

        def free(self):
            cp.gone(self.buf.at[pl.ds(0, 3 * rows)], self.out, f, r)

    class Sum:
        def __init__(self, part, sib, xsend, xrecv):
            self.part, self.sib, self.xsend, self.xrecv = part, sib, xsend, xrecv
            self.ids, self.xids, self.out, self.xout = cp.recv(2), cp.recv(micro), cp.send(), cp.send()

        def ready(self, w):
            if w not in (DN, CN):
                return
            b, i = (dn, 0) if w == DN else (cn, 1)
            src = self.part.at[block(b)]
            cp.start(lambda: (src, self.sib.at[i], self.out, self.ids + i, f, cn))

        def over_x(self):
            cp.arrived(self.sib.at[0], self.ids, f, r)
            for m in micros:

                def add(t, m=m):
                    s = at(m * slot + t * 32, 32)
                    self.xsend[s, :] = (
                        self.part[at(xn * rows + m * slot + t * 32, 32), :] + self.sib[0, s, :]
                    ).astype(BF16)

                loop(slot // 32, add)
                mm = at(m * slot, slot)
                cp.start(lambda m=m, mm=mm: (self.xsend.at[mm], self.xrecv.at[mm], self.xout, self.xids + m, f, xn))

        def done(self, m):
            if m == 0:
                cp.arrived(self.sib.at[1], self.ids + 1, f, r)
            cp.arrived(self.xrecv.at[at(m * slot, slot)], self.xids + m, f, r)

        def value(self, row, n):
            s = at(row, n)
            return self.part[at(r * rows + row, n), :] + self.sib[1, s, :] + self.xrecv[s, :].astype(F32)

        def free(self):
            cp.gone(self.part.at[pl.ds(0, 2 * rows)], self.out, f, r)
            cp.gone(self.xsend, self.xout, f, r)

    def add_into(dst, doff, src, n):
        def step(t):
            s = at(doff + t * 16, 16)
            dst[s, :] = (dst[s, :].astype(F32) + src[at(t * 16, 16), :].astype(F32)).astype(BF16)

        loop(n // 16, step)

    class ColumnReduce:
        def __init__(self, grad, yr, zr, out, col, width):
            self.grad, self.yr, self.zr, self.out = grad, yr, zr, out
            self.col, self.width = col, width
            self.yrecv, self.zrecv, self.orecv = cp.recv(NZ), cp.recv(NZ + 1), cp.recv(2)
            self.ysend, self.zsend, self.osend = cp.send(), cp.send(), cp.send()
            self.lid = lid()
            for n, send in ((NZ, self.ysend), (NZ - 1, self.zsend), (3, self.osend)):
                cp.at_end(grad.at[pl.ds(0, n * sh)], send)

        def send(self, j):
            zz = lax.div(j, 2)
            cp.start(lambda: (self.grad.at[at(j * sh, sh)], self.yr.at[zz], self.ysend, self.yrecv + zz, yn, r))

        def add_y(self, j):
            zz = lax.div(j, 2)
            cp.arrived(self.yr.at[zz], self.yrecv + zz, f, r)
            add_into(self.grad, j * sh, self.yr.at[zz], sh)

        def chain(self, i):
            owner, up, there = by_z(*OWNERS[i]), by_z(*OWNER_ABOVE[i]), by_z(*OWNER_SLOT[i])
            j = 2 * owner + y
            self.add_y(j)

            @pl.when(inner)
            def _():
                cp.arrived(self.zr.at[owner], self.zrecv + owner, f, r)
                add_into(self.grad, j * sh, self.zr.at[owner], sh)

            cp.start(
                lambda: (
                    self.grad.at[at(j * sh, sh)], self.zr.at[there], self.zsend, self.zrecv + there,
                    f + 2 * (2 * up - 1), r,
                )
            )

        def final(self):
            self.add_y(f)
            for slot_, cond in ((z, z > 0), (NZ, z < NZ - 1)):

                @pl.when(cond)
                def _(slot_=slot_):
                    cp.arrived(self.zr.at[slot_], self.zrecv + slot_, f, r)
                    add_into(self.grad, f * sh, self.zr.at[slot_], sh)

            src = self.grad.at[at(f * sh, sh)]
            for i, to in enumerate((xn, cn)):
                cp.start(lambda i=i, to=to: (src, self.dst(r), self.osend, self.orecv + i, f, to))
            ends.append(local(src, self.dst(r), self.lid))

        def dst(self, q):
            return self.out.at[q, :, at(self.col, self.width, 128)]

        def relay(self):
            got = self.dst(xn)
            cp.arrived(got, self.orecv, f, r)
            cp.start(lambda: (got, got, self.osend, self.orecv + 1, f, cn))

        def done(self):
            cp.arrived(self.out.at[pl.ds(0, 2), :, at(self.col, self.width, 128)], self.orecv + 1, f, r)

        def register(self, *deps):
            steps = [task(*deps)(lambda i=i: self.chain(i)) for i in range(NZ - 1)]
            final = task(*deps)(self.final)
            task(final)(self.relay)

    class LongRowReduce:
        def __init__(self, grad, yr, zr, out, row, height, pitch):
            self.grad, self.yr, self.zr, self.out = grad, yr, zr, out
            self.row, self.height, self.pitch = row, height, pitch
            self.yrecv, self.zrecv, self.orecv = cp.recv(), cp.recv(2), cp.recv(2)
            self.ysend, self.zsend, self.osend = cp.send(), cp.send(), cp.send()
            self.lid = lid()
            one = self.grad.at[self.rows(y)]
            cp.at_end(one, self.ysend)
            cp.at_end(one, self.zsend, z != r)
            cp.at_end(self.grad.at[pl.ds(0, 2 * height)], self.osend, z == r)
            cp.at_end(one, self.osend, z == xn)

        def rows(self, yy):
            return at(yy * self.pitch + self.row, self.height)

        def send(self):
            cp.start(lambda: (self.grad.at[self.rows(1 - y)], self.yr, self.ysend, self.yrecv, yn, r))

        def add(self, way):
            cp.arrived(self.zr.at[way], self.zrecv + way, f, r)
            add_into(self.grad, y * self.pitch + self.row, self.zr.at[way], self.height)

        def chain(self):
            cp.arrived(self.yr, self.yrecv, f, r)
            add_into(self.grad, y * self.pitch + self.row, self.yr, self.height)
            src = self.grad.at[self.rows(y)]
            for way, (toward, behind, step) in enumerate(((z < r, z > 0, 2), (z > r, z < NZ - 1, -2))):

                @pl.when(jnp.logical_and(toward, behind))
                def _(way=way):
                    self.add(way)

                cp.start(
                    lambda way=way, step=step: (src, self.zr.at[way], self.zsend, self.zrecv + way, f + step, r), toward
                )

        def dst(self):
            return self.out.at[at(self.row, self.height)]

        def final(self):
            for way, cond in enumerate((z > 0, z < NZ - 1)):

                @pl.when(jnp.logical_and(z == r, cond))
                def _(way=way):
                    self.add(way)

            src = self.grad.at[self.rows(y)]
            for i, to in enumerate((xn, cn)):
                cp.start(lambda i=i, to=to: (src, self.dst(), self.osend, self.orecv + i, f, to), z == r)

            @pl.when(z == r)
            def _():
                local(src, self.dst(), self.lid)

        def relay(self):
            got = self.dst()

            @pl.when(z == xn)
            def _():
                cp.arrived(got, self.orecv, f, r)

            cp.start(lambda: (got, got, self.osend, self.orecv + 1, f, cn), z == xn)

        def done(self):
            @pl.when(jnp.logical_or(z == cn, z == dn))
            def _():
                cp.arrived(self.dst(), self.orecv + 1, f, r)

            @pl.when(z == r)
            def _():
                pltpu.make_async_copy(self.grad.at[self.rows(y)], self.dst(), k.locals.at[self.lid]).wait()

        def register(self, *deps):
            chain = task(*deps)(self.chain)
            task(task(chain)(self.final))(self.relay)

    class RowReduce:
        def __init__(self, grad, yr, zr, out, row, height, pitch):
            self.grad, self.yr, self.zr, self.out = grad, yr, zr, out
            self.row, self.height, self.pitch = row, height, pitch
            self.yrecv, self.zrecv, self.orecv = cp.recv(), cp.recv(4), cp.recv(2)
            self.ysend, self.zsend, self.osend = cp.send(), cp.send(2), cp.send()
            self.lid = lid()
            one = self.grad.at[self.rows(y)]
            cp.at_end(one, self.ysend, z == r)
            for n in range(2):
                cp.at_end(one, self.zsend + n, z != r)
            cp.at_end(self.grad.at[pl.ds(0, 2 * height)], self.osend, z == r)
            cp.at_end(one, self.osend, z == xn)

        def rows(self, yy):
            return at(yy * self.pitch + self.row, self.height)

        def add(self, yy, way):
            cp.arrived(self.zr.at[way, yy], self.zrecv + 2 * way + yy, f, r)
            add_into(self.grad, yy * self.pitch + self.row, self.zr.at[way, yy], self.height)

        def chain(self, far):
            yy = 1 - y if far else y
            src = self.grad.at[self.rows(yy)]
            for way, (toward, behind, step) in enumerate(((z < r, z > 0, 2), (z > r, z < NZ - 1, -2))):

                @pl.when(jnp.logical_and(toward, behind))
                def _(way=way):
                    self.add(yy, way)

                cp.start(
                    lambda way=way, step=step: (
                        src, self.zr.at[way, yy], self.zsend + far, self.zrecv + 2 * way + yy, f + step, r
                    ),
                    toward,
                )

        def gathered(self, yy):
            for way, cond in enumerate((z > 0, z < NZ - 1)):

                @pl.when(jnp.logical_and(z == r, cond))
                def _(way=way):
                    self.add(yy, way)

        def cross(self):
            self.gathered(1 - y)
            cp.start(lambda: (self.grad.at[self.rows(1 - y)], self.yr, self.ysend, self.yrecv, yn, r), z == r)

        def dst(self):
            return self.out.at[at(self.row, self.height)]

        def final(self):
            self.gathered(y)

            @pl.when(z == r)
            def _():
                cp.arrived(self.yr, self.yrecv, f, r)
                add_into(self.grad, y * self.pitch + self.row, self.yr, self.height)

            src = self.grad.at[self.rows(y)]
            for i, to in enumerate((xn, cn)):
                cp.start(lambda i=i, to=to: (src, self.dst(), self.osend, self.orecv + i, f, to), z == r)

            @pl.when(z == r)
            def _():
                local(src, self.dst(), self.lid)

        def relay(self):
            got = self.dst()

            @pl.when(z == xn)
            def _():
                cp.arrived(got, self.orecv, f, r)

            cp.start(lambda: (got, got, self.osend, self.orecv + 1, f, cn), z == xn)

        def done(self):
            @pl.when(jnp.logical_or(z == cn, z == dn))
            def _():
                cp.arrived(self.dst(), self.orecv + 1, f, r)

            @pl.when(z == r)
            def _():
                pltpu.make_async_copy(self.grad.at[self.rows(y)], self.dst(), k.locals.at[self.lid]).wait()

        def register(self, *deps):
            chains = [task(*deps)(lambda far=far: self.chain(far)) for far in (1, 0)]
            cross = task(*chains)(self.cross)
            task(task(cross)(self.final))(self.relay)

    class Deal:
        def __init__(self, src, dst):
            self.src, self.dst, self.recvs, self.sends = src, dst, cp.recv(micro), cp.send(micro)
            self.lid = lid(micro)
            self.local = {}
            for m in micros:
                cp.at_end(self.most(), self.sends + m)

        def most(self):
            return self.dst.at[pl.ds(0, (NF - 1) * part)]

        def start(self, m):
            dst = self.dst.at[at(m * slot + f * part, part)]
            for o in others:
                cp.start(lambda o=o: (self.src.at[m, o], dst, self.sends + m, self.recvs + m, o, r))
            self.local[m] = local(self.src.at[m, f], dst, self.lid + m)

        def done(self, m):
            cp.arrived(self.most(), self.recvs + m, f, r)
            self.local[m].wait()

    class Back:
        def __init__(self, src, dst):
            self.src, self.dst, self.recvs, self.sends = src, dst, cp.recv(micro), cp.send(micro)
            self.lid = lid(micro)
            for m in micros:
                cp.at_end(self.most(), self.sends + m)

        def most(self):
            return self.src.at[pl.ds(0, (NF - 1) * part)]

        def start(self, m):
            for o in others:
                cp.start(
                    lambda o=o: (
                        self.src.at[at(m * slot + o * part, part)], self.dst.at[m, f], self.sends + m, self.recvs + m, o, r
                    )
                )
            ends.append(local(self.src.at[at(m * slot + f * part, part)], self.dst.at[m, f], self.lid + m))

        def done(self):
            for m in micros:
                cp.arrived(self.dst.at[m, pl.ds(0, NF - 1)], self.recvs + m, f, r)

    count = iter(range(k.locals.shape[0]))

    def lid(n=1):
        first = next(count)
        for _ in range(n - 1):
            next(count)
        return first

    t2 = 2 * sz.tile
    hq = sz.hq
    third, half = sz.ffp // 3, sh // 2
    smalls, lens, gains = k.smalls, k.lens, k.gains
    aall, hall, call, yall = k.aall, k.hall, k.call, k.yall
    part_, gg, slope, dw, dqkv = k.part, k.gg, k.slope, k.dw, k.dqkv
    gd, gi, go, gq, dg = k.gd, k.gi, k.go, k.gq, k.dg
    xs, cs, hbuf, dhbuf, mx, gt = k.xs, k.cs, k.hbuf, k.dhbuf, k.mx, k.gt
    qkv, pbuf, obuf = k.qkv, k.pbuf, k.obuf
    g_q = ColumnGather(wq, 0, 3 * hq)
    g_o = [RowGather(wo, i * half, half, sh) for i in range(2)]
    g_i = [ColumnGather(wi, n * t2, t2) for n in range(sz.ntile)]
    g_d = [LongRowGather(wd, i * third, third, sz.ffp) for i in range(3)]
    r_d = [LongRowReduce(gd, k.yrd.at[i], k.zrd.at[i], k.rd, i * third, third, sz.ffp) for i in range(3)]
    r_i = [
        ColumnReduce(gi.at[n], k.yri.at[n], k.zri.at[n], k.ri, n * t2, t2) for n in range(sz.ntile)
    ]
    r_o = [RowReduce(go, k.yro.at[i], k.zro.at[i], k.ro, i * half, half, sh) for i in range(2)]
    r_q = [ColumnReduce(gq.at[n], k.yrq.at[n], k.zrq.at[n], k.rq, n * hq, hq) for n in range(3)]
    small_in, len_in, gs_in, gr_in = (cp.recv() for _ in range(4))
    small_out, len_out, gs_out, gr_out = (cp.send() for _ in range(4))
    cp.at_end(smalls.at[pl.ds(0, NF - 1)], small_out)
    cp.at_end(lens.at[pl.ds(0, NR - 1)], len_out)
    cp.at_end(k.gsend.at[pl.ds(0, NF - 1)], gs_out)
    cp.at_end(k.greps.at[pl.ds(0, NR - 1)], gr_out)
    deal_x, deal_c = Deal(k.tok, xs), Deal(k.cot, cs)
    back_m, back_t = Back(mx, k.o_mixed), Back(gt, k.o_gtok)
    e_a, e_c, e_h, e_y = Spread(aall), Spread(call), Spread(hall), Spread(yall)
    s_1 = Sum(part_, k.sib0, k.xsend, k.xrecv0)
    s_m = Sum(part_, k.sib1, k.xsend, k.xrecv1)
    s_h = Sum(part_, k.sib0, k.xsend, k.xrecv0)
    s_a = Sum(part_, k.sib0, k.xsend, k.xrecv0)
    blocks = [dn, xn, cn, r]

    lane = lax.broadcasted_iota(jnp.int32, (1, 128), 1)
    front = lax.rem(lane, 64) < 32
    low = lane < 64
    low_b = low.astype(F32).astype(BF16)
    high_b = (1.0 - low.astype(F32)).astype(BF16)
    npair = hq // 128
    scale = 64 ** (-0.5)
    tile_ = sz.tile
    NL = 32

    def live(m, t, n):
        pos = lax.broadcasted_iota(jnp.int32, (n, 1), 0) + t * n
        return pos.astype(F32) < lens[r, m : m + 1, 0:1]

    def normed(v):
        center = v - jnp.mean(v, axis=-1, keepdims=True)
        root = lax.rsqrt(jnp.mean(center * center, axis=-1, keepdims=True) + NORM_EPS)
        return center * root, root

    def norm_back(dy, gain, vhat, root):
        e = dy * gain
        return root * (e - jnp.mean(e, axis=-1, keepdims=True) - vhat * jnp.mean(e * vhat, axis=-1, keepdims=True))

    def swap(v):
        return jnp.where(front, pltpu.roll(v, 96, 1), pltpu.roll(v, 32, 1))

    def both(v):
        return jnp.concatenate([v * low_b, v * high_b], axis=0)

    def joined(v):
        return jnp.where(low, v[:slot], v[slot:])

    def fold(v):
        return jnp.sum(v.reshape(NL // 8, 8, d), axis=0)

    def triple(s, p):
        return [qkv[at(s * slot, slot), i * hq + p * 128 : i * hq + (p + 1) * 128] for i in range(3)]

    own_small = local(k.small, smalls.at[f], lid())
    qf, of = k.hbuf.at[pl.ds(0, sh)], k.hbuf.at[pl.ds(sh, sh)]
    q_in = [local(k.fq.at[:, at(i * d + r * hq, hq, 128)], qf.at[:, pl.ds(i * hq, hq)], lid()) for i in range(3)]
    o_lid, i_in, d_lid = lid(), [], lid(2)
    mine = z == r
    df = [k.sib1.at[0], k.sib1.at[1, pl.ds(0, sz.ffs - rows)]]
    d_parts = [(k.fd.at[pl.ds(0, rows)], df[0]), (k.fd.at[pl.ds(rows, sz.ffs - rows)], df[1])]

    @pl.when(mine)
    def _():
        local(k.fo, of, o_lid)

    shifts = []
    for i in range(2):
        first = i * NF * sz.ffs + r * 2 * sz.ffs
        base = lax.div(first, 128) * 128
        shifts.append(first - base)
        i_in.append(local(k.fi.at[:, at(base, sz.fq, 128)], k.dhbuf.at[pl.ds(i * sh, sh), pl.ds(0, sz.fq)], lid()))

    @pl.when(mine)
    def _():
        for n, (src, dst) in enumerate(d_parts):
            local(src, dst, d_lid + n)

    @task()
    def met():
        pl.semaphore_wait(barrier, len(friends))
        for o in others:
            cp.start(lambda o=o: (k.small, smalls.at[f], small_out, small_in, o, r))

    @task()
    def prepare_q():
        for copy in q_in:
            copy.wait()

        def cast_q(t):
            wq[at(f * sh + t * 32, 32), :] = qf[at(t * 32, 32), pl.ds(0, 3 * hq)].astype(BF16)

        loop(sh // 32, cast_q)

    @task()
    def prepare_o():
        @pl.when(mine)
        def _():
            pltpu.make_async_copy(k.fo, of, k.locals.at[o_lid]).wait()

            def cast_o(t):
                wo[at(y * sh + t * 32, 32), :] = of[at(t * 32, 32), :].astype(BF16)

            loop(sh // 32, cast_o)

    @task()
    def prepare_i():
        for i in range(2):
            i_in[i].wait()
        lane_f = lax.broadcasted_iota(jnp.int32, (1, sz.fq), 1)
        first = lane_f < sz.ffs
        second = jnp.logical_and(lane_f >= sz.ffp, lane_f < sz.ffp + sz.ffs)

        def cast_i(t):
            for i in range(2):
                v = k.dhbuf[at(i * sh + t * 32, 32), pl.ds(0, sz.fq)]
                v = pltpu.roll(v, lax.rem(sz.fq - shifts[i], sz.fq), 1)
                v = jnp.where(first, v, jnp.where(second, pltpu.roll(v, sz.ffp - sz.ffs, 1), 0.0)).astype(BF16)
                for n in range(sz.ntile):
                    wi[at(f * sh + t * 32, 32), n * t2 + i * tile_ : n * t2 + (i + 1) * tile_] = v[
                        :, n * tile_ : (n + 1) * tile_
                    ]

        loop(sh // 32, cast_i)

    @task()
    def prepare_d():
        @pl.when(mine)
        def _():
            for n, (src, dst) in enumerate(d_parts):
                pltpu.make_async_copy(src, dst, k.locals.at[d_lid + n]).wait()
            for n, ref in enumerate(df):

                def cast_d(t, n=n, ref=ref):
                    wd[at(y * sz.ffp + n * rows + t * 16, 16), :] = ref[at(t * 16, 16), :].astype(BF16)

                loop(ref.shape[0] // 16, cast_d)
            left = sz.ffs % 16
            if left:
                v = df[1][ref.shape[0] - left :, :]
                v = jnp.concatenate([v, jnp.zeros((sz.ffp - sz.ffs, d), F32)], axis=0)
                wd[at(y * sz.ffp + sz.ffp - 16, 16), :] = v.astype(BF16)

    g_q.register(met, prepare_q)
    for u in g_o:
        u.register(met, prepare_o)
    for u in g_i:
        u.register(met, prepare_i)
    for u in g_d:
        u.register(met, prepare_d)
    q_needs, o_needs, i_needs, d_needs = [[n for u in g for n in u.needs] for g in ([g_q], g_o, g_i, g_d)]

    @task()
    def zero():
        wd[pl.ds(2 * sz.ffp, sz.fq - 2 * sz.ffp), :] = jnp.zeros((sz.fq - 2 * sz.ffp, d), BF16)
        dg[...] = jnp.zeros_like(dg)

    deals = [task(met)(lambda m=m: deal_x.start(m)) for m in micros]

    @task(met)
    def small():
        own_small.wait()
        cp.arrived(smalls.at[pl.ds(0, NF - 1)], small_in, f, r)
        for j in range(NF):
            gains[0:2, j * sh : (j + 1) * sh] = smalls[j, 0:2, :]
        sub = lax.broadcasted_iota(jnp.int32, (NF, 128), 0)
        row8 = lax.broadcasted_iota(jnp.int32, (8, 128), 0)
        ownrow = smalls[f]
        len_tab = smalls[:, 2, :]
        table = jnp.zeros((8, 128), F32)
        for m in micros:
            dealt = jnp.sum(jnp.where(lane == f, ownrow[3 + m : 4 + m, :], 0.0), axis=1, keepdims=True)
            col = jnp.sum(jnp.where(sub.astype(F32) == dealt, len_tab, 0.0), axis=0, keepdims=True)
            length = jnp.sum(jnp.where(lane == m, col, 0.0), axis=1, keepdims=True)
            table = jnp.where(row8 == m, length, table)
        lens[r] = table
        for to in (xn, dn, cn):
            cp.start(lambda to=to: (lens.at[r], lens.at[r], len_out, len_in, f, to))

    @task(small)
    def lengths():
        cp.arrived(lens.at[pl.ds(0, NR - 1)], len_in, f, r)

    norm1s = []
    for m in micros:

        @task(small, deals[m])
        def step(m=m):
            deal_x.done(m)

            def norm1(t):
                vhat, _ = normed(xs[at(m * slot + t * NL, NL), :].astype(F32))
                aall[at(r * rows + m * slot + t * NL, NL), :] = (vhat * gains[0:1, :]).astype(BF16)

            loop(slot // NL, norm1)
            e_a.start(m)

        norm1s.append(step)
    e_a.register(norm1s)

    def project(b):
        a = aall[block(b), :]
        for i in range(3):
            t = nn(a, wq[:, i * hq : (i + 1) * hq])
            for p in range(npair):
                v = t[:, p * 128 : (p + 1) * 128]
                for m in micros:
                    u = v[m * slot : (m + 1) * slot]
                    if i < 2:
                        u = u * k.cos[...] + swap(u) * k.sin[...]
                    qkv[at(b * rows + m * slot, slot), i * hq + p * 128 : i * hq + (p + 1) * 128] = u.astype(BF16)

    def attend(b):
        def attend_one(m):
            s = b * micro + m
            length = lens[b, pl.ds(m, 1), :]
            for p in range(npair):
                q_, k_, v_ = triple(s, p)
                scores = nt(both(q_), k_) * scale
                scores = jnp.where(lane.astype(F32) < length, scores, -1e30)
                e = jnp.exp(scores - jnp.max(scores, axis=-1, keepdims=True))
                prob = e / jnp.sum(e, axis=-1, keepdims=True)
                pbuf[s, p] = prob
                out = nn(prob.astype(BF16), v_)
                obuf[at(s * slot, slot), p * 128 : (p + 1) * 128] = joined(out).astype(BF16)

        loop(micro, attend_one)

    def branch_one(b):
        def branch_tile(n):
            cols = at(n * 256, 256, 128)
            part_[block(b), cols] = nn(obuf[block(b), :], wo[:, cols])

        loop(d // 256, branch_tile)

    firsts = []
    for w in range(NR):

        @task(*e_a.need[w], *q_needs)
        def projected(w=w):
            project(blocks[w])

        @task(projected, lengths, *o_needs)
        def attended(w=w):
            attend(blocks[w])
            branch_one(blocks[w])
            s_1.ready(w)

        firsts.append(attended)
    crossed = task(firsts[DN], firsts[XN])(s_1.over_x)

    masks = []
    for m in micros:
        dealt = task(met)(lambda m=m: deal_c.start(m))

        @task(dealt, small)
        def step(m=m):
            deal_c.done(m)

            def mask_c(t):
                s = at(m * slot + t * NL, NL)
                masked = jnp.where(live(m, t, NL), cs[s, :].astype(F32), 0.0)
                call[at(r * rows + m * slot + t * NL, NL), :] = masked.astype(BF16)

            loop(slot // NL, mask_c)

        masks.append(step)

    @task(*masks)
    def spread_c():
        for m in micros:
            e_c.start(m)

    e_c.register([spread_c])

    norm2s = []
    for m in micros:

        @task(crossed, *firsts, *norm2s)
        def step(m=m):
            s_1.done(m)

            def norm2(t):
                row = m * slot + t * NL
                s = at(row, NL)
                h = xs[s, :].astype(F32) + jnp.where(live(m, t, NL), s_1.value(row, NL), 0.0)
                hbuf[s, :] = h
                vhat, _ = normed(h)
                hall[at(r * rows + row, NL), :] = (vhat * gains[1:2, :]).astype(BF16)

            loop(slot // NL, norm2)
            e_h.start(m)

        norm2s.append(step)
    freed = task(*norm2s)(s_1.free)
    e_h.register(norm2s)

    feeds = []
    for w in range(NR):

        @task(freed, *e_h.need[w], *i_needs)
        def step(w=w):
            rs = block(blocks[w])

            def feed(n):
                v = nn(hall[rs, :], wi[:, at(n * t2, t2, 128)])
                w1, w2 = v[:, :tile_], v[:, tile_:]
                cdf = 0.5 * (1.0 + lax.erf(w1 * (0.5**0.5)))
                act = w1 * cdf
                pdf = jnp.exp(-0.5 * w1 * w1) * 0.3989422804014327
                cols = at(n * tile_, tile_, 128)
                gg[rs, cols] = (act * w2).astype(BF16)
                part_[rs, cols] = act
                slope[rs, cols] = w2 * (cdf + w1 * pdf)

            loop(sz.ntile, feed)

        feeds.append(step)

    @task(*feeds, *e_c.all)
    def gdown():
        def grad_down(i):
            m, n = lax.div(i, 2), lax.rem(i, 2)
            cols = at(n * (d // 2), d // 2, 128)
            gd[at(m * 256, 256), cols] = tn(gg[:, at(m * 256, 256, 128)], call[:, cols]).astype(BF16)

        loop(sz.fq // 256 * 2, grad_down)
        for u in r_d:
            u.send()

    hids = []
    for w in range(NR):

        @task(feeds[w], zero, *e_c.need[w], *d_needs)
        def step(w=w):
            rs = block(blocks[w])

            def hidden(n):
                cols = at(n * tile_, tile_, 128)
                dgg = nt(call[rs, :], wd[at(n * tile_, tile_), :])
                dw[rs, at(n * t2, tile_, 128)] = (dgg * slope[rs, cols]).astype(BF16)
                dw[rs, at(n * t2 + tile_, tile_, 128)] = (dgg * part_[rs, cols]).astype(BF16)

            loop(sz.ntile, hidden)

        hids.append(step)

    gins = []
    for n in range(sz.ntile):
        for which in range(2):

            @task(*hids, *e_h.all)
            def step(n=n, which=which):
                def grad_in(i):
                    j = 2 * i + (y if which else 1 - y)
                    gi[n, at(j * sh, sh), :] = tn(
                        hall[:, at(j * sh, sh, 128)], dw[:, at(n * t2, t2, 128)]
                    ).astype(BF16)

                loop(NZ, grad_in)
                if not which:
                    for owner in order_z:
                        r_i[n].send(2 * owner + 1 - y)

            gins.append(step)

    dhns = []
    for w in range(NR):

        @task(hids[w])
        def step(w=w):
            b = blocks[w]

            def dhn_tile(n):
                part_[block(b), at(n * 256, 256, 128)] = nt(dw[block(b), :], wi[at(n * 256, 256), :])

            loop(d // 256, dhn_tile)
            s_h.ready(w)

        dhns.append(step)
    crossed = task(dhns[DN], dhns[XN])(s_h.over_x)
    back2s = []
    for m in micros:

        @task(crossed, zero, *dhns, *back2s)
        def step(m=m):
            s_h.done(m)

            def back2(t):
                row = m * slot + t * NL
                s = at(row, NL)
                dy = s_h.value(row, NL)
                vhat, root = normed(hbuf[s, :])
                dg[1] += fold(dy * vhat)
                dh = cs[s, :].astype(F32) + norm_back(dy, gains[1:2, :], vhat, root)
                dhbuf[s, :] = dh
                yall[at(r * rows + row, NL), :] = jnp.where(live(m, t, NL), dh, 0.0).astype(BF16)

            loop(slot // NL, back2)
            e_y.start(m)

        back2s.append(step)
    freed = task(*back2s)(s_h.free)
    e_y.register(back2s)

    mixes = []
    for w in range(NR):

        @task(freed, zero, feeds[w], *d_needs)
        def step(w=w):
            b = blocks[w]

            def mix_tile(n):
                cols = at(n * 256, 256, 128)
                part_[block(b), cols] = nn(gg[block(b), :], wd[:, cols])

            loop(d // 256, mix_tile)
            s_m.ready(w)

        mixes.append(step)
    crossed = task(mixes[DN], mixes[XN])(s_m.over_x)
    mixeds = []
    for m in micros:

        @task(crossed, *mixes, *mixeds)
        def step(m=m):
            s_m.done(m)

            def mix(t):
                row = m * slot + t * NL
                s = at(row, NL)
                mx[s, :] = (hbuf[s, :] + jnp.where(live(m, t, NL), s_m.value(row, NL), 0.0)).astype(BF16)

            loop(slot // NL, mix)

        mixeds.append(step)
        task(step)(lambda m=m: back_m.start(m))
    freed = task(*mixeds)(s_m.free)

    @task(*firsts, *e_y.all)
    def gout():
        def grad_out(i):
            cols = at(i * 256, 256, 128)
            go[:, cols] = tn(obuf[...], yall[:, cols]).astype(BF16)

        loop(d // 256, grad_out)

    abacks = []
    for w in range(NR):

        @task(firsts[w], *e_y.need[w])
        def step(w=w):
            def attend_back(m):
                s = blocks[w] * micro + m
                do_all = nt(yall[at(s * slot, slot), :], wo[...]).astype(BF16)
                for p in range(npair):
                    q_, k_, v_ = triple(s, p)
                    q2, do2 = both(q_), both(do_all[:, p * 128 : (p + 1) * 128])
                    prob = pbuf[s, p]
                    dp = nt(do2, v_)
                    ds = (prob * (dp - jnp.sum(dp * prob, axis=-1, keepdims=True))).astype(BF16)
                    dq = joined(nn(ds, k_)) * scale
                    dk = tn(ds, q2) * scale
                    dv = tn(prob.astype(BF16), do2)
                    cosine, sine = k.cos[...], k.sin[...]
                    dq = dq * cosine - swap(dq) * sine
                    dk = dk * cosine - swap(dk) * sine
                    for i, v in enumerate((dq, dk, dv)):
                        dqkv[at(s * slot, slot), i * hq + p * 128 : i * hq + (p + 1) * 128] = v.astype(BF16)

            loop(micro, attend_back)

        abacks.append(step)

    gqkvs = []
    for which in range(2):

        @task(*abacks, *e_a.all)
        def step(which=which):
            def grad_qkv(i):
                j = 2 * i + (y if which else 1 - y)
                g = tn(aall[:, at(j * sh, sh, 128)], dqkv[...]).astype(BF16)
                for n in range(3):
                    gq[n, at(j * sh, sh), :] = g[:, n * hq : (n + 1) * hq]

            loop(NZ, grad_qkv)
            if not which:
                for n in range(3):
                    for owner in order_z:
                        r_q[n].send(2 * owner + 1 - y)

        gqkvs.append(step)

    das = []
    for w in range(NR):

        @task(abacks[w], freed)
        def step(w=w):
            b = blocks[w]

            def da_tile(n):
                part_[block(b), at(n * 256, 256, 128)] = nt(dqkv[block(b), :], wq[at(n * 256, 256), :])

            loop(d // 256, da_tile)
            s_a.ready(w)

        das.append(step)
    crossed = task(das[DN], das[XN])(s_a.over_x)
    back1s = []
    for m in micros:

        @task(crossed, *das, *back1s)
        def step(m=m):
            s_a.done(m)

            def back1(t):
                row = m * slot + t * NL
                s = at(row, NL)
                dy = s_a.value(row, NL)
                vhat, root = normed(xs[s, :].astype(F32))
                dg[0] += fold(dy * vhat)
                gt[s, :] = (dhbuf[s, :] + norm_back(dy, gains[0:1, :], vhat, root)).astype(BF16)

            loop(slot // NL, back1)
            back_t.start(m)

        back1s.append(step)

    gsend, gslots, greps, gout_ = k.gsend, k.gslots, k.greps, k.gout

    @task(*back1s, *back2s)
    def gain_parts():
        for which in range(2):
            total = jnp.sum(dg[which], axis=0, keepdims=True)
            for j in range(NF):
                gsend[j, which : which + 1, :] = total[:, j * sh : (j + 1) * sh]
        for o in others:
            cp.start(lambda o=o: (gsend.at[o], gslots.at[f], gs_out, gs_in, o, r))
        gslots[f] = gsend[f]

    @task(gain_parts)
    def gain_sums():
        cp.arrived(gslots.at[pl.ds(0, NF - 1)], gs_in, f, r)
        total = gslots[0]
        for j in range(1, NF):
            total = total + gslots[j]
        greps[r] = total
        for to in (xn, dn, cn):
            cp.start(lambda to=to: (greps.at[r], greps.at[r], gr_out, gr_in, f, to))

    glid = lid()

    @task(gain_sums)
    def gain_totals():
        cp.arrived(greps.at[pl.ds(0, NR - 1)], gr_in, f, r)
        gout_[...] = greps[0] + greps[1] + greps[2] + greps[3]
        ends.append(local(gout_, k.o_small, glid))

    for u in r_d:
        u.register(gdown)
    for n, u in enumerate(r_i):
        u.register(*gins[2 * n : 2 * n + 2])
    for u in r_o:
        u.register(gout)
    for u in r_q:
        u.register(*gqkvs)

    @task(*range(len(tasks)))
    def end():
        for u in r_d + r_i + r_o + r_q + [back_m, back_t]:
            u.done()
        s_a.free()
        for e in (e_a, e_c, e_h, e_y):
            e.free()
        for ref, send, cond in cp.left:
            cp.gone(ref, send, f, r, cond)
        for copy in ends:
            copy.wait()

    run_tasks(tasks)


def fused(sz, tok, cot, small, cos, sin, fq, fo, fi, fd):
    d, sh, all_, rows = sz.d, sz.shard, sz.all, sz.rows
    t2 = 2 * sz.tile
    third, half = sz.ffp // 3, sh // 2
    hq3 = 3 * sz.hq
    bf = lambda *s: pltpu.VMEM(s, BF16)
    fl = lambda *s: pltpu.VMEM(s, F32)
    ins = dict(tok=tok, cot=cot, small=small, cos=cos, sin=sin, fq=fq, fo=fo, fi=fi, fd=fd)
    outs = dict(
        o_mixed=jax.ShapeDtypeStruct((sz.micro, NF, sz.part, d), BF16),
        o_gtok=jax.ShapeDtypeStruct((sz.micro, NF, sz.part, d), BF16),
        o_small=jax.ShapeDtypeStruct((8, 128), F32),
        rq=jax.ShapeDtypeStruct((NR, sh, hq3), BF16),
        ro=jax.ShapeDtypeStruct((sh, d), BF16),
        ri=jax.ShapeDtypeStruct((NR, sh, sz.ntile * t2), BF16),
        rd=jax.ShapeDtypeStruct((sz.ffp, d), BF16),
    )
    scratch = dict(
        wq=bf(d, hq3), wo=bf(2 * sh, d), wi=bf(d, sz.ntile * t2), wd=bf(sz.fq, d),
        xs=bf(rows, d), cs=bf(rows, d), mx=bf(rows, d), gt=bf(rows, d),
        aall=bf(all_, d), hall=bf(all_, d), call=bf(all_, d), yall=bf(all_, d),
        smalls=fl(NF, 8, 128), lens=fl(NR, 8, 128), gains=fl(8, d),
        qkv=bf(all_, hq3), pbuf=fl(NR * sz.micro, sz.hq // 128, 2 * sz.slot, 128), obuf=bf(all_, sz.hq),
        part=fl(all_, d), sib0=fl(2, rows, d), sib1=fl(2, rows, d),
        xsend=bf(rows, d), xrecv0=bf(rows, d), xrecv1=bf(rows, d),
        hbuf=fl(rows, d), dhbuf=fl(rows, d), dg=fl(2, 8, d),
        gg=bf(all_, sz.fq), slope=fl(all_, sz.fq), dw=bf(all_, sz.ntile * t2), dqkv=bf(all_, hq3),
        gd=bf(sz.fq, d), gi=bf(sz.ntile, d, t2), go=bf(2 * sh, d), gq=bf(3, d, sz.hq),
        yrd=bf(3, third, d), zrd=bf(3, 2, third, d),
        yri=bf(sz.ntile, NZ, sh, t2), zri=bf(sz.ntile, NZ + 1, sh, t2),
        yro=bf(2, half, d), zro=bf(2, 2, 2, half, d),
        yrq=bf(3, NZ, sh, sz.hq), zrq=bf(3, NZ + 1, sh, sz.hq),
        gsend=fl(NF, 8, 128), gslots=fl(NF, 8, 128), greps=fl(NR, 8, 128), gout=fl(8, 128),
        sends=pltpu.SemaphoreType.DMA((96,)), recvs=pltpu.SemaphoreType.DMA((184,)),
        locals=pltpu.SemaphoreType.DMA((32,)),
    )
    any_ = pl.BlockSpec(memory_space=pl.ANY)
    vmem = pl.BlockSpec(memory_space=pltpu.VMEM)
    names = (*ins, *outs, *scratch)
    return pl.pallas_call(
        functools.partial(kernel, sz, names),
        out_shape=list(outs.values()),
        in_specs=[any_] * 3 + [vmem] * 2 + [any_] * 4,
        out_specs=[any_] * len(outs),
        scratch_shapes=list(scratch.values()),
        compiler_params=pltpu.CompilerParams(collective_id=0, has_side_effects=True, vmem_limit_bytes=64 * MIB),
    )(*ins.values())


def finish_kernel(sz, rq, ro, ri, rd, gq, go, gi, gd):
    hq, t, ffs, ffp = sz.hq, sz.tile, sz.ffs, sz.ffp
    for i in range(3):
        for q in range(NR):
            gq[:, i * sz.d + q * hq : i * sz.d + (q + 1) * hq] = rq[q, :, i * hq : (i + 1) * hq].astype(F32)
    go[...] = ro[...].astype(F32)
    gd[...] = rd[...].astype(F32)
    pieces = []
    for i in range(2):
        for q in range(NR):
            v = [ri[q, :, (2 * n + i) * t : (2 * n + i + 1) * t].astype(F32) for n in range(sz.ntile)]
            v = jnp.concatenate(v, axis=1)
            pieces += [v[:, :ffs], v[:, ffp : ffp + ffs]]
    gi[...] = jnp.concatenate(pieces, axis=1)


def finish(sz, rq, ro, ri, rd):
    d, sh = sz.d, sz.shard
    steps, n = sh // 16, sz.ffp // 16
    down = -(-n // steps) * 16
    last = -(-sz.ffp // down) - 1
    row = lambda w: pl.BlockSpec((16, w), lambda i: (i, 0))
    low = pl.BlockSpec((down, d), lambda i: (jnp.minimum(i, last), 0))
    quarters = lambda w: pl.BlockSpec((NR, 16, w), lambda i: (0, i, 0))
    return pl.pallas_call(
        functools.partial(finish_kernel, sz),
        grid=(steps,),
        out_shape=[
            jax.ShapeDtypeStruct((sh, 3 * d), F32),
            jax.ShapeDtypeStruct((sh, d), F32),
            jax.ShapeDtypeStruct((sh, 2 * NF * sz.ffs), F32),
            jax.ShapeDtypeStruct((sz.ffs, d), F32),
        ],
        in_specs=[quarters(rq.shape[2]), row(d), quarters(ri.shape[2]), low],
        out_specs=[row(3 * d), row(d), row(2 * NF * sz.ffs), low],
        compiler_params=pltpu.CompilerParams(vmem_limit_bytes=60 * MIB),
    )(rq, ro, ri, rd)


def routed(tokens, cotangent, deal, lengths, ln1_gain, w_qkv, w_out, ln2_gain, w_in, w_down):
    micro, _, part, d = tokens.shape
    ffs = w_down.shape[0]
    sz = Sizes(micro, part, d, ffs)
    gain = [lax.reduce_precision(g, 8, 7)[None] for g in (ln1_gain, ln2_gain)]
    wide = lambda v: jnp.pad(v.astype(F32), ((0, 0), (0, 128 - v.shape[1])))
    small = jnp.concatenate(gain + [wide(lengths[:, 0, 0][None]), wide(deal[:, 0]), jnp.zeros((5 - micro, 128), F32)])
    half = d // HEADS // 2
    freq = np.float32(ROPE_BASE) ** (-(np.arange(half, dtype=np.float32) * np.float32(2.0 / (2 * half))))
    angles = np.arange(sz.slot, dtype=np.float32)[:, None] * freq[None, :]
    cos = jnp.asarray(np.tile(np.cos(angles), (1, 4)))
    sin = jnp.asarray(np.tile(np.concatenate([-np.sin(angles), np.sin(angles)], axis=1), (1, 2)))
    mixed, gtok, osmall, rq, ro, ri, rd = fused(sz, tokens, cotangent, small, cos, sin, w_qkv, w_out, w_in, w_down)
    g_qkv, g_out, g_in, g_down = finish(sz, rq, ro, ri, rd)
    return mixed, gtok, osmall[0], g_qkv, g_out, osmall[1], g_in, g_down


def solution(mesh):
    small = mesh.shape["fsdp"] == NF and mesh.shape["rep"] == NR
    rows = P(None, "rep", "fsdp", None)
    return jax.shard_map(
        routed if small else plain,
        mesh=mesh,
        in_specs=(
            rows, rows, P(None, "rep", None), P(None, "rep", "fsdp"),
            P("fsdp"), P("fsdp", None), P("fsdp", None), P("fsdp"), P("fsdp", None), P("fsdp", None),
        ),
        out_specs=(rows, rows, P("fsdp"), P("fsdp", None), P("fsdp", None), P("fsdp"), P("fsdp", None), P("fsdp", None)),
        check_vma=False,
    )
```

```python
import functools
import types

import jax
import jax.numpy as jnp
import numpy as np
from jax import lax
from jax.experimental import pallas as pl
from jax.experimental.pallas import tpu as pltpu
from jax.sharding import PartitionSpec as P

HEADS = 16
ROPE_BASE = 160000.0
NORM_EPS = 1e-05
MESH = pl.DeviceIdType.MESH
MIB = 1 << 20
BF16 = jnp.bfloat16
F32 = jnp.float32


def rope_tables(slot_count, head_size):
    half_size = head_size // 2
    frequency = ROPE_BASE ** (-(jnp.arange(half_size, dtype=F32) * 2.0 / head_size))
    angles = jnp.arange(slot_count, dtype=F32)[:, None] * frequency[None, :]
    return jnp.cos(angles), jnp.sin(angles)


def rotate(values, cosine, sine):
    front, back = jnp.split(values, 2, axis=-1)
    cosine, sine = cosine[:, None, :], sine[:, None, :]
    return jnp.concatenate([front * cosine - back * sine, back * cosine + front * sine], axis=-1)


def normed(values, gain):
    center = values - jnp.mean(values, axis=-1, keepdims=True)
    root = lax.rsqrt(jnp.mean(center * center, axis=-1, keepdims=True) + NORM_EPS)
    vhat = center * root
    return vhat * gain, vhat, root


def norm_back(dy, gain, vhat, root):
    dgain = jnp.sum(dy * vhat, axis=tuple(range(dy.ndim - 1)))
    e = dy * gain
    dz = root * (
        e
        - jnp.mean(e, axis=-1, keepdims=True)
        - vhat * jnp.mean(e * vhat, axis=-1, keepdims=True)
    )
    return dgain, dz


def mm(spec, a, b):
    return jnp.einsum(spec, a, b, preferred_element_type=F32)


def layer(g1, wqkv, wo, g2, win, wdown, tokens, dout, live):
    m, slot, d = tokens.shape
    heads, size = HEADS, d // HEADS
    scale = size ** (-0.5)
    w1, w2 = win
    lv = live[:, :, None]
    x = tokens.astype(F32)
    y, vhat1, root1 = normed(x, g1)
    a = y.astype(BF16)
    qkv = mm("mtd,de->mte", a, wqkv).reshape(m, slot, 3, heads, size)
    cosine, sine = rope_tables(slot, size)
    q = rotate(qkv[:, :, 0], cosine, sine).astype(BF16)
    k = rotate(qkv[:, :, 1], cosine, sine).astype(BF16)
    v = qkv[:, :, 2].astype(BF16)
    s = mm("mqhd,mkhd->mhqk", q, k) * scale
    s = jnp.where(live[:, None, None, :] > 0, s, -1e30)
    p = jax.nn.softmax(s, axis=-1)
    pb = p.astype(BF16)
    o = mm("mhqk,mkhd->mqhd", pb, v).astype(BF16).reshape(m, slot, d)
    h = x + lv * mm("mte,ed->mtd", o, wo)
    y, vhat2, root2 = normed(h, g2)
    hn = y.astype(BF16)
    z1 = mm("mtd,df->mtf", hn, w1)
    z2 = mm("mtd,df->mtf", hn, w2)
    cdf = 0.5 * (1.0 + lax.erf(z1 * (0.5**0.5)))
    pdf = jnp.exp(-0.5 * z1 * z1) * 0.3989422804014327
    act = z1 * cdf
    gg = (act * z2).astype(BF16)
    mixed = (h + lv * mm("mtf,fd->mtd", gg, wdown)).astype(BF16)

    up = dout.astype(F32)
    dy2 = (lv * up).astype(BF16)
    g_down = mm("mtf,mtd->fd", gg, dy2)
    dgg = mm("mtd,fd->mtf", dy2, wdown)
    dw1 = (dgg * z2 * (cdf + z1 * pdf)).astype(BF16)
    dw2 = (dgg * act).astype(BF16)
    g_in = (mm("mtd,mtf->df", hn, dw1), mm("mtd,mtf->df", hn, dw2))
    dhn = mm("mtf,df->mtd", dw1, w1) + mm("mtf,df->mtd", dw2, w2)
    g_g2, dhv = norm_back(dhn, g2, vhat2, root2)
    dh = up + dhv
    dy1 = (lv * dh).astype(BF16)
    g_out = mm("mte,mtd->ed", o, dy1)
    do = mm("mtd,ed->mte", dy1, wo).astype(BF16).reshape(m, slot, heads, size)
    dp = mm("mqhd,mkhd->mhqk", do, v)
    ds = (p * (dp - jnp.sum(dp * p, axis=-1, keepdims=True))).astype(BF16)
    dq = mm("mhqk,mkhd->mqhd", ds, k) * scale
    dk = mm("mhqk,mqhd->mkhd", ds, q) * scale
    dv = mm("mhqk,mqhd->mkhd", pb, do)
    dqkv = jnp.stack([rotate(dq, cosine, -sine), rotate(dk, cosine, -sine), dv], axis=2)
    dqkv = dqkv.reshape(m, slot, 3 * d).astype(BF16)
    g_qkv = mm("mtd,mte->de", a, dqkv)
    da = mm("mte,de->mtd", dqkv, wqkv)
    g_g1, dxv = norm_back(da, g1, vhat1, root1)
    gtok = (dh + dxv).astype(BF16)
    return mixed, gtok, (g_g1, g_qkv, g_out, g_g2, g_in, g_down)


def plain(tokens, cotangent, deal, lengths, ln1_gain, w_qkv, w_out, ln2_gain, w_in, w_down):
    slot = tokens.shape[2] * lax.axis_size("fsdp")
    me = lax.axis_index("fsdp")

    def spread(rows):
        return lax.all_to_all(rows, "fsdp", split_axis=1, concat_axis=2, tiled=True)[:, 0]

    def back(rows):
        return lax.all_to_all(rows[:, None], "fsdp", split_axis=2, concat_axis=1, tiled=True)

    def whole(shard):
        return lax.all_gather(shard.astype(BF16), "fsdp", axis=0, tiled=True)

    table = lax.all_gather(lengths[:, 0], "fsdp", axis=1, tiled=True)
    mine = lax.dynamic_slice_in_dim(deal[:, 0], me, 1, axis=1)
    pick = jnp.arange(table.shape[1], dtype=jnp.int32)[None, :] == mine
    length = jnp.sum(jnp.where(pick, table, 0), axis=1, keepdims=True)
    live = (jnp.arange(slot, dtype=jnp.int32)[None, :] < length).astype(F32)
    win = jnp.split(whole(w_in), 2, axis=1)
    mixed, gtok, grads = layer(
        whole(ln1_gain).astype(F32), whole(w_qkv), whole(w_out), whole(ln2_gain).astype(F32), win, whole(w_down),
        spread(tokens), spread(cotangent), live,
    )
    g_g1, g_qkv, g_out, g_g2, g_in, g_down = grads

    def owned(part):
        part = lax.psum_scatter(part, "fsdp", scatter_dimension=0, tiled=True)
        return lax.psum(part, "rep")

    g_in = jnp.concatenate(g_in, axis=1)
    return (back(mixed), back(gtok)) + tuple(owned(g) for g in (g_g1, g_qkv, g_out, g_g2, g_in, g_down))


NF, NR, NZ = 8, 4, 4
DN, XN, CN = 0, 1, 2


def at(offset, size, unit=16):
    return pl.ds(pl.multiple_of(offset, unit), size)


def nn(a, b):
    return lax.dot_general(a, b, (((1,), (0,)), ((), ())), preferred_element_type=F32)


def nt(a, b):
    return lax.dot_general(a, b, (((1,), (1,)), ((), ())), preferred_element_type=F32)


def tn(a, b):
    return lax.dot_general(a, b, (((0,), (0,)), ((), ())), preferred_element_type=F32)


def once(i, body):
    body(i)


def loop(n, body):
    def step(i, carry):
        body(i)
        return carry

    lax.fori_loop(0, n, step, 0)


ORDER = (
    2, 0, 24, 25, 72, 1, 20, 53, 4, 54, 5, 10, 15, 6, 11, 16, 3, 7, 12, 17, 55, 57, 33, 74, 58, 59, 73, 8, 13, 18,
    22, 26, 60, 52, 21, 27, 75, 35, 62, 23, 9, 14, 19, 69, 34, 76, 38, 43, 61, 49, 46, 28, 67, 65, 56, 63, 64, 66,
    29, 40, 71, 70, 30, 79, 31, 39, 68, 77, 41, 81, 32, 36, 44, 82, 78, 86, 80, 50, 85, 42, 83, 84, 37, 90, 89, 47,
    91, 51, 87, 88, 92, 48, 45, 96, 93, 103, 95, 94, 104, 107, 141, 105, 100, 97, 147, 98, 99, 106, 144, 108, 109,
    128, 150, 110, 115, 151, 113, 127, 155, 102, 145, 142, 111, 116, 112, 156, 152, 101, 114, 124, 171, 119, 125,
    170, 117, 165, 157, 126, 166, 146, 129, 153, 161, 130, 118, 120, 121, 175, 148, 176, 122, 131, 132, 180, 158,
    172, 123, 185, 133, 135, 177, 160, 181, 182, 143, 186, 178, 187, 149, 154, 134, 167, 162, 136, 137, 159, 183,
    188, 138, 168, 179, 169, 173, 163, 139, 164, 184, 189, 140, 174, 190,
)


def run_tasks(tasks):
    done = set()
    for i in ORDER or range(len(tasks)):
        deps, fn = tasks[i]
        assert done.issuperset(deps)
        fn()
        done.add(i)
    assert len(done) == len(tasks)


SOURCES = ((1, 0, 3, 2), (2, 2, 1, 1), (3, 3, 0, 0))
SOURCE_BELOW = ((0, 1, 0, 1), (0, 0, 1, 1), (0, 0, 1, 1))
OWNERS = ((3, 3, 0, 0), (2, 2, 1, 1), (1, 0, 3, 2))
OWNER_ABOVE = ((1, 1, 0, 0), (1, 1, 0, 0), (1, 0, 1, 0))
OWNER_SLOT = ((3, 3, 0, 0), (2, 2, 4, 1), (1, 4, 3, 4))


class Sizes:
    def __init__(self, micro, part, d, ffs):
        self.micro, self.part, self.d, self.ffs = micro, part, d, ffs
        self.slot = part * NF
        self.rows = micro * self.slot
        self.all = NR * self.rows
        self.shard = d // NF
        self.hq = d // NR
        self.ffp = -(-ffs // 16) * 16
        self.tile = 256
        self.ntile = -(-(2 * self.ffp) // self.tile)
        self.fq = self.ntile * self.tile
        last = 2 * self.ffp - (self.ntile - 1) * self.tile
        self.shift = -(-last // 64) * 64 if last <= self.tile - 64 else self.tile
        self.units = [(n * 2 * self.tile, 2 * self.tile) for n in range(self.ntile - 1)]
        self.units.append(((self.ntile - 1) * 2 * self.tile, 2 * self.shift))
        self.iw = sum(w for _, w in self.units)


def side_by_side(sz, n, one, two):
    if sz.units[n][1] == 2 * sz.tile:
        return jnp.concatenate([one, two], axis=1)
    room = jnp.zeros((one.shape[0], sz.units[n][1] - sz.tile), F32)
    return jnp.concatenate([one, room], axis=1) + pltpu.roll(jnp.concatenate([two, room], axis=1), sz.shift, 1)


def apart(sz, n, v):
    if sz.units[n][1] == 2 * sz.tile:
        return v[:, : sz.tile], v[:, sz.tile :]
    return v[:, : sz.tile], pltpu.roll(v, v.shape[1] - sz.shift, 1)[:, : sz.tile]


class Copies:
    def __init__(self, sends, recvs):
        self.sends, self.recvs, self.nsend, self.nrecv = sends, recvs, 0, 0
        self.left = []

    def send(self, n=1):
        base, self.nsend = self.nsend, self.nsend + n
        assert self.nsend <= self.sends.shape[0]
        return base

    def recv(self, n=1):
        base, self.nrecv = self.nrecv, self.nrecv + n
        assert self.nrecv <= self.recvs.shape[0]
        return base

    def make(self, src, dst, send, recv, f, r):
        return pltpu.make_async_remote_copy(
            src_ref=src, dst_ref=dst, send_sem=self.sends.at[send], recv_sem=self.recvs.at[recv],
            device_id={"fsdp": f, "rep": r}, device_id_type=MESH,
        )

    def start(self, build, cond=None):
        def go():
            self.make(*build()).start()

        go() if cond is None else pl.when(cond)(go)

    def arrived(self, ref, recv, f, r):
        self.make(ref, ref, 0, recv, f, r).wait_recv()

    def gone(self, ref, send, f, r, cond=None):
        def go():
            self.make(ref, ref, send, 0, f, r).wait_send()

        go() if cond is None else pl.when(cond)(go)

    def at_end(self, ref, send, cond=None):
        self.left.append((ref, send, cond))


def kernel(sz, names, *refs):
    k = types.SimpleNamespace(**dict(zip(names, refs)))
    d, rows, slot, micro, part = sz.d, sz.rows, sz.slot, sz.micro, sz.part
    f, r = lax.axis_index("fsdp"), lax.axis_index("rep")
    z, y = lax.div(f, 2), lax.rem(f, 2)
    c = lax.rem(r, 2)
    yn = f + 1 - 2 * y
    cn = r + 1 - 2 * c
    xn = lax.rem(r + 2, 4)
    dn = lax.rem(cn + 2, 4)
    others = [lax.rem(f + i, NF) for i in range(1, NF)]
    cp = Copies(k.sends, k.recvs)

    def local(src, dst, i):
        copy = pltpu.make_async_copy(src, dst, k.locals.at[i])
        copy.start()
        return copy

    def block(i):
        return at(i * rows, rows)

    barrier = pltpu.get_barrier_semaphore()
    friends = [(o, r) for o in others] + [(f, o) for o in (cn, xn, dn)]
    for ff, rr in friends:
        pl.semaphore_signal(barrier, inc=1, device_id={"fsdp": ff, "rep": rr}, device_id_type=MESH)

    tasks = []

    def task(*deps):
        def register(fn):
            tasks.append((deps, fn))
            return len(tasks) - 1

        return register

    wq, wo, wi, wd = k.wq, k.wo, k.wi, k.wd
    sh = sz.shard
    micros = range(micro)
    ends = []

    eights = (1 + 7 * lax.rem(z, 2)) * (1 + 63 * lax.div(z, 2))

    def by_z(*values):
        code = sum(v << (3 * i) for i, v in enumerate(values))
        return lax.rem(lax.div(jnp.int32(code), eights), 8)

    inner = jnp.logical_and(z > 0, z < NZ - 1)
    order_z = [by_z(*o) for o in OWNERS] + [z]

    class ColumnGather:
        def __init__(self, whole, col, width):
            self.whole, self.cols = whole, at(col, width, 128)
            self.zrecv, self.yrecv, self.zsend, self.ysend = cp.recv(NZ), cp.recv(), cp.send(), cp.send()
            cp.at_end(self.shards(NZ), self.ysend)
            cp.at_end(self.shards(NZ + 1), self.zsend, inner)
            cp.at_end(self.shards(1), self.zsend, jnp.logical_not(inner))

        def shards(self, n):
            return self.whole.at[pl.ds(0, n * sh), self.cols]

        def dst(self, j):
            return self.whole.at[at(j * sh, sh), self.cols]

        def over(self, j):
            dst = self.dst(j)
            cp.start(lambda: (dst, dst, self.ysend, self.yrecv, yn, r))

        def start(self):
            src = self.dst(f)
            cp.start(lambda: (src, src, self.zsend, self.zrecv + z, f + 2, r), z < NZ - 1)
            cp.start(lambda: (src, src, self.zsend, self.zrecv + z, f - 2, r), z > 0)
            self.over(f)

        def along_z(self, i):
            source, up = by_z(*SOURCES[i]), by_z(*SOURCE_BELOW[i])
            j = 2 * source + y
            dst = self.dst(j)
            cp.arrived(dst, self.zrecv + source, f, r)
            cp.start(lambda: (dst, dst, self.zsend, self.zrecv + source, f + 2 * (2 * up - 1), r), inner)
            self.over(j)

        def over_y(self):
            cp.arrived(self.shards(NZ), self.yrecv, f, r)

        def register(self, *deps):
            start = task(*deps)(self.start)
            steps = [task(start)(lambda i=i: self.along_z(i)) for i in range(NZ - 1)]
            self.needs = [start, *steps, task(start)(self.over_y)]

    class LongRowGather:
        def __init__(self, whole, row, height, pitch):
            self.whole, self.row, self.height, self.pitch = whole, row, height, pitch
            self.recv, self.send = cp.recv(2), cp.send(3)
            for n, cond in ((0, z < NZ - 1), (1, z > 0)):
                cp.at_end(self.dst(y), self.send + n, jnp.logical_and((z >= r) if n == 0 else (z <= r), cond))
            cp.at_end(self.dst(y), self.send + 2)

        def dst(self, yy):
            return self.whole.at[at(yy * self.pitch + self.row, self.height)]

        def onward(self):
            dst = self.dst(y)
            up = jnp.logical_and(z >= r, z < NZ - 1)
            down = jnp.logical_and(z <= r, z > 0)
            cp.start(lambda: (dst, dst, self.send, self.recv + y, f + 2, r), up)
            cp.start(lambda: (dst, dst, self.send + 1, self.recv + y, f - 2, r), down)
            cp.start(lambda: (dst, dst, self.send + 2, self.recv + y, yn, r))

        def start(self):
            @pl.when(z == r)
            def _():
                self.onward()

        def pass_on(self):
            @pl.when(z != r)
            def _():
                cp.arrived(self.dst(y), self.recv + y, f, r)
                self.onward()

        def rest(self):
            cp.arrived(self.dst(1 - y), self.recv + 1 - y, f, r)

        def register(self, *deps):
            start = task(*deps)(self.start)
            self.needs = [start, task(start)(self.pass_on), task(start)(self.rest)]

    class RowGather:
        def __init__(self, whole, row, height, pitch):
            self.whole, self.row, self.height, self.pitch = whole, row, height, pitch
            self.recv, self.send = cp.recv(2), cp.send(5)
            for yy, send in ((y, self.send), (1 - y, self.send + 2)):
                cp.at_end(self.dst(yy), send, self.up)
                cp.at_end(self.dst(yy), send + 1, self.down)
            cp.at_end(self.dst(y), self.send + 4, z == r)

        up = jnp.logical_and(z >= r, z < NZ - 1)
        down = jnp.logical_and(z <= r, z > 0)

        def dst(self, yy):
            return self.whole.at[at(yy * self.pitch + self.row, self.height)]

        def onward(self, yy, send):
            dst = self.dst(yy)
            cp.start(lambda: (dst, dst, send, self.recv + yy, f + 2, r), self.up)
            cp.start(lambda: (dst, dst, send + 1, self.recv + yy, f - 2, r), self.down)

        def start(self):
            dst = self.dst(y)
            cp.start(lambda: (dst, dst, self.send + 4, self.recv + y, yn, r), z == r)

        last = jnp.logical_and(z != r, jnp.logical_or(z == 0, z == NZ - 1))

        def pass_on(self, near):
            yy, send = (y, self.send) if near else (1 - y, self.send + 2)
            waits = jnp.logical_not(self.last)

            @pl.when(jnp.logical_and(waits, z != r) if near else waits)
            def _():
                cp.arrived(self.dst(yy), self.recv + yy, f, r)

            self.onward(yy, send)

        def rest(self):
            @pl.when(self.last)
            def _():
                for yy in (y, 1 - y):
                    cp.arrived(self.dst(yy), self.recv + yy, f, r)

        def register(self, *deps):
            start = task(*deps)(self.start)
            self.needs = [task(start)(lambda near=near: self.pass_on(near)) for near in (1, 0)]
            self.needs += [start, task(start)(self.rest)]

    class Spread:
        def __init__(self, buf):
            self.buf = buf
            self.ids, self.out = [cp.recv(3) for _ in micros], cp.send()

        def ref(self, b, m):
            return self.buf.at[at(b * rows + m * slot, slot)]

        def start(self, m):
            own, n = self.ref(r, m), self.ids[m]
            cp.start(lambda: (own, own, self.out, n + 1, f, xn))
            cp.start(lambda: (own, own, self.out, n, f, cn))

        def forward(self, m):
            got, n = self.ref(xn, m), self.ids[m]
            cp.arrived(got, n + 1, f, r)
            cp.start(lambda: (got, got, self.out, n + 2, f, cn))

        def got(self, b):
            for m in micros:
                if b is cn:
                    cp.arrived(self.ref(cn, m), self.ids[m], f, r)
                elif b is dn:
                    cp.arrived(self.ref(dn, m), self.ids[m] + 2, f, r)

        def register(self, deps):
            forward = [task(*deps)(lambda m=m: self.forward(m)) for m in micros]
            got = [task(*deps)(lambda b=b: self.got(b)) for b in (cn, dn)]
            self.need = [[got[1]], forward, [got[0]], list(deps)]
            self.all = [*forward, *got, *deps]

        def free(self):
            cp.gone(self.buf.at[pl.ds(0, 3 * rows)], self.out, f, r)

    class Sum:
        def __init__(self, part, sib, xsend, xrecv):
            self.part, self.sib, self.xsend, self.xrecv = part, sib, xsend, xrecv
            self.ids, self.xids, self.out, self.xout = cp.recv(2), cp.recv(micro), cp.send(), cp.send()

        def ready(self, w):
            if w not in (DN, CN):
                return
            b, i = (dn, 0) if w == DN else (cn, 1)
            src = self.part.at[block(b)]
            cp.start(lambda: (src, self.sib.at[i], self.out, self.ids + i, f, cn))

        def over_x(self):
            cp.arrived(self.sib.at[0], self.ids, f, r)
            for m in micros:

                def add(t, m=m):
                    s = at(m * slot + t * 32, 32)
                    self.xsend[s, :] = (
                        self.part[at(xn * rows + m * slot + t * 32, 32), :] + self.sib[0, s, :]
                    ).astype(BF16)

                loop(slot // 32, add)
                mm = at(m * slot, slot)
                cp.start(lambda m=m, mm=mm: (self.xsend.at[mm], self.xrecv.at[mm], self.xout, self.xids + m, f, xn))

        def done(self, m):
            if m == 0:
                cp.arrived(self.sib.at[1], self.ids + 1, f, r)
            cp.arrived(self.xrecv.at[at(m * slot, slot)], self.xids + m, f, r)

        def value(self, row, n):
            s = at(row, n)
            return self.part[at(r * rows + row, n), :] + self.sib[1, s, :] + self.xrecv[s, :].astype(F32)

        def free(self):
            cp.gone(self.part.at[pl.ds(0, 2 * rows)], self.out, f, r)
            cp.gone(self.xsend, self.xout, f, r)

    def add_into(dst, doff, src, n):
        def step(t):
            s = at(doff + t * 16, 16)
            dst[s, :] = (dst[s, :].astype(F32) + src[at(t * 16, 16), :].astype(F32)).astype(BF16)

        loop(n // 16, step)

    class ColumnReduce:
        def __init__(self, grad, yr, zr, out, col, width):
            self.grad, self.yr, self.zr, self.out = grad, yr, zr, out
            self.col, self.width = col, width
            self.yrecv, self.zrecv, self.orecv = cp.recv(NZ), cp.recv(NZ + 1), cp.recv(2)
            self.ysend, self.zsend, self.osend = cp.send(), cp.send(), cp.send()
            self.lid = lid()
            for n, send in ((NZ, self.ysend), (NZ - 1, self.zsend), (3, self.osend)):
                cp.at_end(grad.at[pl.ds(0, n * sh)], send)

        def send(self, j):
            zz = lax.div(j, 2)
            cp.start(lambda: (self.grad.at[at(j * sh, sh)], self.yr.at[zz], self.ysend, self.yrecv + zz, yn, r))

        def add_y(self, j):
            zz = lax.div(j, 2)
            cp.arrived(self.yr.at[zz], self.yrecv + zz, f, r)
            add_into(self.grad, j * sh, self.yr.at[zz], sh)

        def chain(self, i):
            owner, up, there = by_z(*OWNERS[i]), by_z(*OWNER_ABOVE[i]), by_z(*OWNER_SLOT[i])
            j = 2 * owner + y
            self.add_y(j)

            @pl.when(inner)
            def _():
                cp.arrived(self.zr.at[owner], self.zrecv + owner, f, r)
                add_into(self.grad, j * sh, self.zr.at[owner], sh)

            cp.start(
                lambda: (
                    self.grad.at[at(j * sh, sh)], self.zr.at[there], self.zsend, self.zrecv + there,
                    f + 2 * (2 * up - 1), r,
                )
            )

        def final(self):
            self.add_y(f)
            for slot_, cond in ((z, z > 0), (NZ, z < NZ - 1)):

                @pl.when(cond)
                def _(slot_=slot_):
                    cp.arrived(self.zr.at[slot_], self.zrecv + slot_, f, r)
                    add_into(self.grad, f * sh, self.zr.at[slot_], sh)

            src = self.grad.at[at(f * sh, sh)]
            for i, to in enumerate((xn, cn)):
                cp.start(lambda i=i, to=to: (src, self.dst(r), self.osend, self.orecv + i, f, to))
            ends.append(local(src, self.dst(r), self.lid))

        def dst(self, q):
            return self.out.at[q, :, at(self.col, self.width, 128)]

        def relay(self):
            got = self.dst(xn)
            cp.arrived(got, self.orecv, f, r)
            cp.start(lambda: (got, got, self.osend, self.orecv + 1, f, cn))

        def done(self):
            cp.arrived(self.out.at[pl.ds(0, 2), :, at(self.col, self.width, 128)], self.orecv + 1, f, r)

        def register(self, *deps):
            steps = [task(*deps)(lambda i=i: self.chain(i)) for i in range(NZ - 1)]
            final = task(*deps)(self.final)
            task(final)(self.relay)

    class LongRowReduce:
        def __init__(self, grad, yr, zr, out, row, height, pitch):
            self.grad, self.yr, self.zr, self.out = grad, yr, zr, out
            self.row, self.height, self.pitch = row, height, pitch
            self.yrecv, self.zrecv, self.orecv = cp.recv(), cp.recv(2), cp.recv(2)
            self.ysend, self.zsend, self.osend = cp.send(), cp.send(), cp.send()
            self.lid = lid()
            one = self.grad.at[self.rows(y)]
            cp.at_end(one, self.ysend)
            cp.at_end(one, self.zsend, z != r)
            cp.at_end(self.grad.at[pl.ds(0, 2 * height)], self.osend, z == r)
            cp.at_end(one, self.osend, z == xn)

        def rows(self, yy):
            return at(yy * self.pitch + self.row, self.height)

        def send(self):
            cp.start(lambda: (self.grad.at[self.rows(1 - y)], self.yr, self.ysend, self.yrecv, yn, r))

        def add(self, way):
            cp.arrived(self.zr.at[way], self.zrecv + way, f, r)
            add_into(self.grad, y * self.pitch + self.row, self.zr.at[way], self.height)

        def chain(self):
            cp.arrived(self.yr, self.yrecv, f, r)
            add_into(self.grad, y * self.pitch + self.row, self.yr, self.height)
            src = self.grad.at[self.rows(y)]
            for way, (toward, behind, step) in enumerate(((z < r, z > 0, 2), (z > r, z < NZ - 1, -2))):

                @pl.when(jnp.logical_and(toward, behind))
                def _(way=way):
                    self.add(way)

                cp.start(
                    lambda way=way, step=step: (src, self.zr.at[way], self.zsend, self.zrecv + way, f + step, r), toward
                )

        def dst(self):
            return self.out.at[at(self.row, self.height)]

        def final(self):
            for way, cond in enumerate((z > 0, z < NZ - 1)):

                @pl.when(jnp.logical_and(z == r, cond))
                def _(way=way):
                    self.add(way)

            src = self.grad.at[self.rows(y)]
            for i, to in enumerate((xn, cn)):
                cp.start(lambda i=i, to=to: (src, self.dst(), self.osend, self.orecv + i, f, to), z == r)

            @pl.when(z == r)
            def _():
                local(src, self.dst(), self.lid)

        def relay(self):
            got = self.dst()

            @pl.when(z == xn)
            def _():
                cp.arrived(got, self.orecv, f, r)

            cp.start(lambda: (got, got, self.osend, self.orecv + 1, f, cn), z == xn)

        def done(self):
            @pl.when(jnp.logical_or(z == cn, z == dn))
            def _():
                cp.arrived(self.dst(), self.orecv + 1, f, r)

            @pl.when(z == r)
            def _():
                pltpu.make_async_copy(self.grad.at[self.rows(y)], self.dst(), k.locals.at[self.lid]).wait()

        def register(self, *deps):
            chain = task(*deps)(self.chain)
            task(task(chain)(self.final))(self.relay)

    class RowReduce:
        def __init__(self, grad, yr, zr, out, row, height, pitch):
            self.grad, self.yr, self.zr, self.out = grad, yr, zr, out
            self.row, self.height, self.pitch = row, height, pitch
            self.yrecv, self.zrecv, self.orecv = cp.recv(), cp.recv(4), cp.recv(2)
            self.ysend, self.zsend, self.osend = cp.send(), cp.send(2), cp.send()
            self.lid = lid()
            one = self.grad.at[self.rows(y)]
            cp.at_end(one, self.ysend, z == r)
            for n in range(2):
                cp.at_end(one, self.zsend + n, z != r)
            cp.at_end(self.grad.at[pl.ds(0, 2 * height)], self.osend, z == r)
            cp.at_end(one, self.osend, z == xn)

        def rows(self, yy):
            return at(yy * self.pitch + self.row, self.height)

        def add(self, yy, way):
            cp.arrived(self.zr.at[way, yy], self.zrecv + 2 * way + yy, f, r)
            add_into(self.grad, yy * self.pitch + self.row, self.zr.at[way, yy], self.height)

        def chain(self, far):
            yy = 1 - y if far else y
            src = self.grad.at[self.rows(yy)]
            for way, (toward, behind, step) in enumerate(((z < r, z > 0, 2), (z > r, z < NZ - 1, -2))):

                @pl.when(jnp.logical_and(toward, behind))
                def _(way=way):
                    self.add(yy, way)

                cp.start(
                    lambda way=way, step=step: (
                        src, self.zr.at[way, yy], self.zsend + far, self.zrecv + 2 * way + yy, f + step, r
                    ),
                    toward,
                )

        def gathered(self, yy):
            for way, cond in enumerate((z > 0, z < NZ - 1)):

                @pl.when(jnp.logical_and(z == r, cond))
                def _(way=way):
                    self.add(yy, way)

        def cross(self):
            self.gathered(1 - y)
            cp.start(lambda: (self.grad.at[self.rows(1 - y)], self.yr, self.ysend, self.yrecv, yn, r), z == r)

        def dst(self):
            return self.out.at[at(self.row, self.height)]

        def final(self):
            self.gathered(y)

            @pl.when(z == r)
            def _():
                cp.arrived(self.yr, self.yrecv, f, r)
                add_into(self.grad, y * self.pitch + self.row, self.yr, self.height)

            src = self.grad.at[self.rows(y)]
            for i, to in enumerate((xn, cn)):
                cp.start(lambda i=i, to=to: (src, self.dst(), self.osend, self.orecv + i, f, to), z == r)

            @pl.when(z == r)
            def _():
                local(src, self.dst(), self.lid)

        def relay(self):
            got = self.dst()

            @pl.when(z == xn)
            def _():
                cp.arrived(got, self.orecv, f, r)

            cp.start(lambda: (got, got, self.osend, self.orecv + 1, f, cn), z == xn)

        def done(self):
            @pl.when(jnp.logical_or(z == cn, z == dn))
            def _():
                cp.arrived(self.dst(), self.orecv + 1, f, r)

            @pl.when(z == r)
            def _():
                pltpu.make_async_copy(self.grad.at[self.rows(y)], self.dst(), k.locals.at[self.lid]).wait()

        def register(self, *deps):
            chains = [task(*deps)(lambda far=far: self.chain(far)) for far in (1, 0)]
            cross = task(*chains)(self.cross)
            task(task(cross)(self.final))(self.relay)

    class Deal:
        def __init__(self, src, dst):
            self.src, self.dst, self.recvs, self.sends = src, dst, cp.recv(micro), cp.send(micro)
            self.lid = lid(micro)
            self.local = {}
            for m in micros:
                cp.at_end(self.most(), self.sends + m)

        def most(self):
            return self.dst.at[pl.ds(0, (NF - 1) * part)]

        def start(self, m):
            dst = self.dst.at[at(m * slot + f * part, part)]
            for o in others:
                cp.start(lambda o=o: (self.src.at[m, o], dst, self.sends + m, self.recvs + m, o, r))
            self.local[m] = local(self.src.at[m, f], dst, self.lid + m)

        def done(self, m):
            cp.arrived(self.most(), self.recvs + m, f, r)
            self.local[m].wait()

    class Back:
        def __init__(self, src, dst):
            self.src, self.dst, self.recvs, self.sends = src, dst, cp.recv(micro), cp.send(micro)
            self.lid = lid(micro)
            for m in micros:
                cp.at_end(self.most(), self.sends + m)

        def most(self):
            return self.src.at[pl.ds(0, (NF - 1) * part)]

        def start(self, m):
            for o in others:
                cp.start(
                    lambda o=o: (
                        self.src.at[at(m * slot + o * part, part)], self.dst.at[m, f], self.sends + m, self.recvs + m, o, r
                    )
                )
            ends.append(local(self.src.at[at(m * slot + f * part, part)], self.dst.at[m, f], self.lid + m))

        def done(self):
            for m in micros:
                cp.arrived(self.dst.at[m, pl.ds(0, NF - 1)], self.recvs + m, f, r)

    count = iter(range(k.locals.shape[0]))

    def lid(n=1):
        first = next(count)
        for _ in range(n - 1):
            next(count)
        return first

    t2 = 2 * sz.tile
    hq = sz.hq
    third, half = sz.ffp // 3, sh // 2
    smalls, lens, gains = k.smalls, k.lens, k.gains
    aall, hall, call, yall = k.aall, k.hall, k.call, k.yall
    part_, gg, slope, dw, dqkv = k.part, k.gg, k.slope, k.dw, k.dqkv
    gd, gi, go, gq, dg = k.gd, k.gi, k.go, k.gq, k.dg
    xs, cs, hbuf, dhbuf, mx, gt = k.xs, k.cs, k.hbuf, k.dhbuf, k.mx, k.gt
    qkv, pbuf, obuf = k.qkv, k.pbuf, k.obuf
    g_q = [ColumnGather(wq, i * hq, hq) for i in range(3)]
    g_o = [RowGather(wo, i * half, half, sh) for i in range(2)]
    g_i = [ColumnGather(wi, col, w) for col, w in sz.units]
    g_d = [LongRowGather(wd, i * third, third, sz.ffp) for i in range(3)]
    r_d = [LongRowReduce(gd, k.yrd.at[i], k.zrd.at[i], k.rd, i * third, third, sz.ffp) for i in range(3)]
    r_i = [
        ColumnReduce(
            gi.at[:, pl.ds(col, w)], k.yri.at[n, :, :, pl.ds(0, w)], k.zri.at[n, :, :, pl.ds(0, w)], k.ri, col, w
        )
        for n, (col, w) in enumerate(sz.units)
    ]
    r_o = [RowReduce(go, k.yro.at[i], k.zro.at[i], k.ro, i * half, half, sh) for i in range(2)]
    r_q = [ColumnReduce(gq.at[n], k.yrq.at[n], k.zrq.at[n], k.rq, n * hq, hq) for n in range(3)]
    small_in, len_in, gs_in, gr_in = (cp.recv() for _ in range(4))
    small_out, len_out, gs_out, gr_out = (cp.send() for _ in range(4))
    cp.at_end(smalls.at[pl.ds(0, NF - 1)], small_out)
    cp.at_end(lens.at[pl.ds(0, NR - 1)], len_out)
    cp.at_end(k.gsend.at[pl.ds(0, NF - 1)], gs_out)
    cp.at_end(k.greps.at[pl.ds(0, NR - 1)], gr_out)
    deal_x, deal_c = Deal(k.tok, xs), Deal(k.cot, cs)
    back_m, back_t = Back(mx, k.o_mixed), Back(gt, k.o_gtok)
    e_a, e_c, e_h, e_y = Spread(aall), Spread(call), Spread(hall), Spread(yall)
    s_1 = Sum(part_, k.sib0, k.xsend, k.xrecv0)
    s_m = Sum(k.part2, k.sib1, k.xsend2, k.xrecv1)
    s_h = Sum(part_, k.sib0, k.xsend, k.xrecv0)
    s_a = Sum(part_, k.sib0, k.xsend, k.xrecv0)
    blocks = [dn, xn, cn, r]

    lane = lax.broadcasted_iota(jnp.int32, (1, 128), 1)
    front = lax.rem(lane, 64) < 32
    low = lane < 64
    low_b = low.astype(F32).astype(BF16)
    high_b = (1.0 - low.astype(F32)).astype(BF16)
    npair = hq // 128
    scale = 64 ** (-0.5)
    tile_ = sz.tile
    NL = 32

    def live(m, t, n):
        pos = lax.broadcasted_iota(jnp.int32, (n, 1), 0) + t * n
        return pos.astype(F32) < lens[r, m : m + 1, 0:1]

    def normed(v):
        center = v - jnp.mean(v, axis=-1, keepdims=True)
        root = lax.rsqrt(jnp.mean(center * center, axis=-1, keepdims=True) + NORM_EPS)
        return center * root, root

    def norm_back(dy, gain, vhat, root):
        e = dy * gain
        return root * (e - jnp.mean(e, axis=-1, keepdims=True) - vhat * jnp.mean(e * vhat, axis=-1, keepdims=True))

    def swap(v):
        return jnp.where(front, pltpu.roll(v, 96, 1), pltpu.roll(v, 32, 1))

    def both(v):
        return jnp.concatenate([v * low_b, v * high_b], axis=0)

    def joined(v):
        return jnp.where(low, v[:slot], v[slot:])

    def fold(v):
        return jnp.sum(v.reshape(NL // 8, 8, d), axis=0)

    def triple(s, p):
        return [qkv[at(s * slot, slot), i * hq + p * 128 : i * hq + (p + 1) * 128] for i in range(3)]

    mini = k.mini
    mini[...] = jnp.zeros_like(mini)
    mini[0:1, :] = k.g1[...].astype(BF16).astype(F32)
    mini[1:2, :] = k.g2[...].astype(BF16).astype(F32)
    for m in micros:
        mini[2:3, :] += jnp.where(lane == m, k.len[0:1, m : m + 1].astype(F32), 0.0)
    smalls[f] = mini[...]
    qf, of = k.hbuf.at[pl.ds(0, sh)], k.hbuf.at[pl.ds(sh, sh)]
    q_in = [local(k.fq.at[:, at(i * d + r * hq, hq, 128)], qf.at[:, pl.ds(i * hq, hq)], lid()) for i in range(3)]
    o_lid, i_in, d_lid = lid(), [], lid()
    mine = z == r
    df = k.part2.at[pl.ds(0, sz.ffs)]

    @pl.when(mine)
    def _():
        local(k.fo, of, o_lid)

    shifts = []
    for i in range(2):
        first = i * NF * sz.ffs + r * 2 * sz.ffs
        base = lax.div(first, 128) * 128
        shifts.append(first - base)
        i_in.append(local(k.fi.at[:, at(base, sz.fq, 128)], k.dhbuf.at[pl.ds(i * sh, sh), pl.ds(0, sz.fq)], lid()))

    @pl.when(mine)
    def _():
        local(k.fd, df, d_lid)

    @task()
    def met():
        pl.semaphore_wait(barrier, len(friends))
        for o in others:
            cp.start(lambda o=o: (mini, smalls.at[f], small_out, small_in, o, r))

    @task()
    def prepare_q():
        for copy in q_in:
            copy.wait()

        def cast_q(t):
            wq[at(f * sh + t * 32, 32), :] = qf[at(t * 32, 32), pl.ds(0, 3 * hq)].astype(BF16)

        loop(sh // 32, cast_q)

    @task()
    def prepare_o():
        @pl.when(mine)
        def _():
            pltpu.make_async_copy(k.fo, of, k.locals.at[o_lid]).wait()

            def cast_o(t):
                wo[at(y * sh + t * 32, 32), :] = of[at(t * 32, 32), :].astype(BF16)

            loop(sh // 32, cast_o)

    @task()
    def prepare_i():
        for i in range(2):
            i_in[i].wait()
        lane_f = lax.broadcasted_iota(jnp.int32, (1, sz.fq), 1)
        first = lane_f < sz.ffs
        second = jnp.logical_and(lane_f >= sz.ffp, lane_f < sz.ffp + sz.ffs)

        def cast_i(t):
            halves = []
            for i in range(2):
                v = k.dhbuf[at(i * sh + t * 32, 32), pl.ds(0, sz.fq)]
                v = pltpu.roll(v, lax.rem(sz.fq - shifts[i], sz.fq), 1)
                halves.append(jnp.where(first, v, jnp.where(second, pltpu.roll(v, sz.ffp - sz.ffs, 1), 0.0)))
            for n, (col, w) in enumerate(sz.units):
                one, two = [v[:, n * tile_ : (n + 1) * tile_] for v in halves]
                wi[at(f * sh + t * 32, 32), pl.ds(col, w)] = side_by_side(sz, n, one, two).astype(BF16)

        loop(sh // 32, cast_i)

    @task()
    def prepare_d():
        @pl.when(mine)
        def _():
            pltpu.make_async_copy(k.fd, df, k.locals.at[d_lid]).wait()

            def cast_d(t):
                wd[at(y * sz.ffp + t * 16, 16), :] = df[at(t * 16, 16), :].astype(BF16)

            loop(sz.ffs // 16, cast_d)
            left = sz.ffs % 16
            if left:
                v = df[pl.ds(sz.ffs - left, left), :]
                v = jnp.concatenate([v, jnp.zeros((sz.ffp - sz.ffs, d), F32)], axis=0)
                wd[at(y * sz.ffp + sz.ffp - 16, 16), :] = v.astype(BF16)

    for u in g_q:
        u.register(met, prepare_q)
    for u in g_o:
        u.register(met, prepare_o)
    for u in g_i:
        u.register(met, prepare_i)
    for u in g_d:
        u.register(met, prepare_d)
    q_needs, o_needs, i_needs, d_needs = [[n for u in g for n in u.needs] for g in (g_q, g_o, g_i, g_d)]

    @task()
    def zero():
        wd[pl.ds(2 * sz.ffp, sz.fq - 2 * sz.ffp), :] = jnp.zeros((sz.fq - 2 * sz.ffp, d), BF16)
        dg[...] = jnp.zeros_like(dg)

    deals = [task(met)(lambda m=m: deal_x.start(m)) for m in micros]

    @task(met)
    def small():
        cp.arrived(smalls.at[pl.ds(0, NF - 1)], small_in, f, r)
        for j in range(NF):
            gains[0:2, j * sh : (j + 1) * sh] = smalls[j, 0:2, :]
        sub = lax.broadcasted_iota(jnp.int32, (NF, 128), 0)
        row8 = lax.broadcasted_iota(jnp.int32, (8, 128), 0)
        lane8 = lax.broadcasted_iota(jnp.int32, (1, NF), 1)
        len_tab = smalls[:, 2, :]
        table = jnp.zeros((8, 128), F32)
        for m in micros:
            dealt = jnp.where(lane8 == f, k.deal[m : m + 1, :].astype(F32), 0.0)
            dealt = jnp.sum(dealt, axis=1, keepdims=True)
            col = jnp.sum(jnp.where(sub.astype(F32) == dealt, len_tab, 0.0), axis=0, keepdims=True)
            length = jnp.sum(jnp.where(lane == m, col, 0.0), axis=1, keepdims=True)
            table = jnp.where(row8 == m, length, table)
        lens[r] = table
        for to in (xn, dn, cn):
            cp.start(lambda to=to: (lens.at[r], lens.at[r], len_out, len_in, f, to))

    @task(small)
    def lengths():
        cp.arrived(lens.at[pl.ds(0, NR - 1)], len_in, f, r)

    norm1s = []
    for m in micros:

        @task(small, deals[m])
        def step(m=m):
            deal_x.done(m)

            def norm1(t):
                vhat, _ = normed(xs[at(m * slot + t * NL, NL), :].astype(F32))
                aall[at(r * rows + m * slot + t * NL, NL), :] = (vhat * gains[0:1, :]).astype(BF16)

            loop(slot // NL, norm1)
            e_a.start(m)

        norm1s.append(step)
    e_a.register(norm1s)

    def project(b):
        a = aall[block(b), :]
        for i in range(3):
            t = nn(a, wq[:, i * hq : (i + 1) * hq])
            for p in range(npair):
                v = t[:, p * 128 : (p + 1) * 128]
                for m in micros:
                    u = v[m * slot : (m + 1) * slot]
                    if i < 2:
                        u = u * k.cos[...] + swap(u) * k.sin[...]
                    qkv[at(b * rows + m * slot, slot), i * hq + p * 128 : i * hq + (p + 1) * 128] = u.astype(BF16)

    def attend(b):
        def attend_one(m):
            s = b * micro + m
            length = lens[b, pl.ds(m, 1), :]
            for p in range(npair):
                q_, k_, v_ = triple(s, p)
                scores = nt(both(q_), k_) * scale
                scores = jnp.where(lane.astype(F32) < length, scores, -1e30)
                e = jnp.exp(scores - jnp.max(scores, axis=-1, keepdims=True))
                prob = e / jnp.sum(e, axis=-1, keepdims=True)
                pbuf[s, p] = prob
                out = nn(prob.astype(BF16), v_)
                obuf[at(s * slot, slot), p * 128 : (p + 1) * 128] = joined(out).astype(BF16)

        loop(micro, attend_one)

    def branch_one(b):
        def branch_tile(n):
            cols = at(n * 256, 256, 128)
            part_[block(b), cols] = nn(obuf[block(b), :], wo[:, cols])

        loop(d // 256, branch_tile)

    firsts = []
    for w in range(NR):

        @task(*e_a.need[w], *q_needs)
        def projected(w=w):
            project(blocks[w])

        @task(projected, lengths, *o_needs)
        def attended(w=w):
            attend(blocks[w])
            branch_one(blocks[w])
            s_1.ready(w)

        firsts.append(attended)
    crossed = task(firsts[DN], firsts[XN])(s_1.over_x)

    masks = []
    for m in micros:
        dealt = task(met)(lambda m=m: deal_c.start(m))

        @task(dealt, small)
        def step(m=m):
            deal_c.done(m)

            def mask_c(t):
                s = at(m * slot + t * NL, NL)
                masked = jnp.where(live(m, t, NL), cs[s, :].astype(F32), 0.0)
                call[at(r * rows + m * slot + t * NL, NL), :] = masked.astype(BF16)

            loop(slot // NL, mask_c)

        masks.append(step)

    @task(*masks)
    def spread_c():
        for m in micros:
            e_c.start(m)

    e_c.register([spread_c])

    norm2s = []
    for m in micros:

        @task(crossed, *firsts, *norm2s)
        def step(m=m):
            s_1.done(m)

            def norm2(t):
                row = m * slot + t * NL
                s = at(row, NL)
                h = xs[s, :].astype(F32) + jnp.where(live(m, t, NL), s_1.value(row, NL), 0.0)
                hbuf[s, :] = h
                vhat, _ = normed(h)
                hall[at(r * rows + row, NL), :] = (vhat * gains[1:2, :]).astype(BF16)

            loop(slot // NL, norm2)
            e_h.start(m)

        norm2s.append(step)
    freed = task(*norm2s)(s_1.free)
    e_h.register(norm2s)

    feeds = []
    for w in range(NR):

        @task(freed, *e_h.need[w], *i_needs)
        def step(w=w):
            rs = block(blocks[w])

            def feed(n):
                col, w = sz.units[n]
                w1, w2 = apart(sz, n, nn(hall[rs, :], wi[:, pl.ds(col, w)]))
                cdf = 0.5 * (1.0 + lax.erf(w1 * (0.5**0.5)))
                act = w1 * cdf
                pdf = jnp.exp(-0.5 * w1 * w1) * 0.3989422804014327
                cols = pl.ds(n * tile_, tile_)
                gg[rs, cols] = (act * w2).astype(BF16)
                part_[rs, cols] = act
                slope[rs, cols] = w2 * (cdf + w1 * pdf)

            for n in range(sz.ntile):
                once(n, feed)

        feeds.append(step)

    @task(*feeds, *e_c.all)
    def gdown():
        def grad_down(i):
            m, n = lax.div(i, 2), lax.rem(i, 2)
            cols = at(n * (d // 2), d // 2, 128)
            gd[at(m * 256, 256), cols] = tn(gg[:, at(m * 256, 256, 128)], call[:, cols]).astype(BF16)

        loop(sz.fq // 256 * 2, grad_down)
        for u in r_d:
            u.send()

    hids = []
    for w in range(NR):

        @task(feeds[w], zero, *e_c.need[w], *d_needs)
        def step(w=w):
            rs = block(blocks[w])

            def hidden(n):
                cols = pl.ds(n * tile_, tile_)
                dgg = nt(call[rs, :], wd[pl.ds(n * tile_, tile_), :])
                v = side_by_side(sz, n, dgg * slope[rs, cols], dgg * part_[rs, cols])
                dw[rs, pl.ds(*sz.units[n])] = v.astype(BF16)

            for n in range(sz.ntile):
                once(n, hidden)

        hids.append(step)

    gins = []
    for n in range(sz.ntile):
        for which in range(2):

            @task(*hids, *e_h.all)
            def step(n=n, which=which):
                def grad_in(i):
                    j = 2 * i + (y if which else 1 - y)
                    cols = pl.ds(*sz.units[n])
                    gi[at(j * sh, sh), cols] = tn(hall[:, at(j * sh, sh, 128)], dw[:, cols]).astype(BF16)

                loop(NZ, grad_in)
                if not which:
                    for owner in order_z:
                        r_i[n].send(2 * owner + 1 - y)

            gins.append(step)

    dhns = []
    for w in range(NR):

        @task(hids[w])
        def step(w=w):
            b = blocks[w]

            def dhn_tile(n):
                part_[block(b), at(n * 256, 256, 128)] = nt(dw[block(b), :], wi[at(n * 256, 256), :])

            loop(d // 256, dhn_tile)
            s_h.ready(w)

        dhns.append(step)
    crossed = task(dhns[DN], dhns[XN])(s_h.over_x)
    back2s = []
    for m in micros:

        @task(crossed, zero, *dhns, *back2s)
        def step(m=m):
            s_h.done(m)

            def back2(t):
                row = m * slot + t * NL
                s = at(row, NL)
                dy = s_h.value(row, NL)
                vhat, root = normed(hbuf[s, :])
                dg[1] += fold(dy * vhat)
                dh = cs[s, :].astype(F32) + norm_back(dy, gains[1:2, :], vhat, root)
                dhbuf[s, :] = dh
                yall[at(r * rows + row, NL), :] = jnp.where(live(m, t, NL), dh, 0.0).astype(BF16)

            loop(slot // NL, back2)
            e_y.start(m)

        back2s.append(step)
    freed = task(*back2s)(s_h.free)
    e_y.register(back2s)

    mixes = []
    for w in range(NR):

        @task(zero, feeds[w], *d_needs)
        def step(w=w):
            b = blocks[w]

            def mix_tile(n):
                cols = at(n * 256, 256, 128)
                k.part2[block(b), cols] = nn(gg[block(b), :], wd[:, cols])

            loop(d // 256, mix_tile)
            s_m.ready(w)

        mixes.append(step)
    crossed = task(mixes[DN], mixes[XN])(s_m.over_x)
    mixeds = []
    for m in micros:

        @task(crossed, *mixes, *mixeds)
        def step(m=m):
            s_m.done(m)

            def mix(t):
                row = m * slot + t * NL
                s = at(row, NL)
                mx[s, :] = (hbuf[s, :] + jnp.where(live(m, t, NL), s_m.value(row, NL), 0.0)).astype(BF16)

            loop(slot // NL, mix)

        mixeds.append(step)
        task(step)(lambda m=m: back_m.start(m))

    @task(*firsts, *e_y.all)
    def gout():
        def grad_out(i):
            cols = at(i * 256, 256, 128)
            go[:, cols] = tn(obuf[...], yall[:, cols]).astype(BF16)

        loop(d // 256, grad_out)

    abacks = []
    for w in range(NR):

        @task(firsts[w], *e_y.need[w])
        def step(w=w):
            def attend_back(m):
                s = blocks[w] * micro + m
                do_all = nt(yall[at(s * slot, slot), :], wo[...]).astype(BF16)
                for p in range(npair):
                    q_, k_, v_ = triple(s, p)
                    q2, do2 = both(q_), both(do_all[:, p * 128 : (p + 1) * 128])
                    prob = pbuf[s, p]
                    dp = nt(do2, v_)
                    ds = (prob * (dp - jnp.sum(dp * prob, axis=-1, keepdims=True))).astype(BF16)
                    dq = joined(nn(ds, k_)) * scale
                    dk = tn(ds, q2) * scale
                    dv = tn(prob.astype(BF16), do2)
                    cosine, sine = k.cos[...], k.sin[...]
                    dq = dq * cosine - swap(dq) * sine
                    dk = dk * cosine - swap(dk) * sine
                    for i, v in enumerate((dq, dk, dv)):
                        dqkv[at(s * slot, slot), i * hq + p * 128 : i * hq + (p + 1) * 128] = v.astype(BF16)

            loop(micro, attend_back)

        abacks.append(step)

    gqkvs = []
    for which in range(2):

        @task(*abacks, *e_a.all)
        def step(which=which):
            def grad_qkv(i):
                j = 2 * i + (y if which else 1 - y)
                g = tn(aall[:, at(j * sh, sh, 128)], dqkv[...]).astype(BF16)
                for n in range(3):
                    gq[n, at(j * sh, sh), :] = g[:, n * hq : (n + 1) * hq]

            loop(NZ, grad_qkv)
            if not which:
                for n in range(3):
                    for owner in order_z:
                        r_q[n].send(2 * owner + 1 - y)

        gqkvs.append(step)

    das = []
    for w in range(NR):

        @task(abacks[w], freed)
        def step(w=w):
            b = blocks[w]

            def da_tile(n):
                part_[block(b), at(n * 256, 256, 128)] = nt(dqkv[block(b), :], wq[at(n * 256, 256), :])

            loop(d // 256, da_tile)
            s_a.ready(w)

        das.append(step)
    crossed = task(das[DN], das[XN])(s_a.over_x)
    back1s = []
    for m in micros:

        @task(crossed, *das, *back1s)
        def step(m=m):
            s_a.done(m)

            def back1(t):
                row = m * slot + t * NL
                s = at(row, NL)
                dy = s_a.value(row, NL)
                vhat, root = normed(xs[s, :].astype(F32))
                dg[0] += fold(dy * vhat)
                gt[s, :] = (dhbuf[s, :] + norm_back(dy, gains[0:1, :], vhat, root)).astype(BF16)

            loop(slot // NL, back1)
            back_t.start(m)

        back1s.append(step)

    gsend, gslots, greps, gout_ = k.gsend, k.gslots, k.greps, k.gout

    @task(*back1s, *back2s)
    def gain_parts():
        for which in range(2):
            total = jnp.sum(dg[which], axis=0, keepdims=True)
            for j in range(NF):
                gsend[j, which : which + 1, :] = total[:, j * sh : (j + 1) * sh]
        for o in others:
            cp.start(lambda o=o: (gsend.at[o], gslots.at[f], gs_out, gs_in, o, r))
        gslots[f] = gsend[f]

    @task(gain_parts)
    def gain_sums():
        cp.arrived(gslots.at[pl.ds(0, NF - 1)], gs_in, f, r)
        total = gslots[0]
        for j in range(1, NF):
            total = total + gslots[j]
        greps[r] = total
        for to in (xn, dn, cn):
            cp.start(lambda to=to: (greps.at[r], greps.at[r], gr_out, gr_in, f, to))

    glid = lid()

    @task(gain_sums)
    def gain_totals():
        cp.arrived(greps.at[pl.ds(0, NR - 1)], gr_in, f, r)
        gout_[...] = greps[0] + greps[1] + greps[2] + greps[3]
        ends.append(local(gout_, k.o_small, glid))

    for u in r_d:
        u.register(gdown)
    for n, u in enumerate(r_i):
        u.register(*gins[2 * n : 2 * n + 2])
    for u in r_o:
        u.register(gout)
    for u in r_q:
        u.register(*gqkvs)

    @task(*range(len(tasks)))
    def end():
        for u in r_d + r_i + r_o + r_q + [back_m, back_t]:
            u.done()
        s_a.free()
        s_m.free()
        for e in (e_a, e_c, e_h, e_y):
            e.free()
        for ref, send, cond in cp.left:
            cp.gone(ref, send, f, r, cond)
        for copy in ends:
            copy.wait()

    run_tasks(tasks)


def fused(sz, tok, cot, g1, g2, length, deal, cos, sin, fq, fo, fi, fd):
    d, sh, all_, rows = sz.d, sz.shard, sz.all, sz.rows
    t2 = 2 * sz.tile
    third, half = sz.ffp // 3, sh // 2
    hq3 = 3 * sz.hq
    bf = lambda *s: pltpu.VMEM(s, BF16)
    fl = lambda *s: pltpu.VMEM(s, F32)
    ins = dict(tok=tok, cot=cot, g1=g1, g2=g2, len=length, deal=deal, cos=cos, sin=sin, fq=fq, fo=fo, fi=fi, fd=fd)
    outs = dict(
        o_mixed=jax.ShapeDtypeStruct((sz.micro, NF, sz.part, d), BF16),
        o_gtok=jax.ShapeDtypeStruct((sz.micro, NF, sz.part, d), BF16),
        o_small=jax.ShapeDtypeStruct((8, 128), F32),
        rq=jax.ShapeDtypeStruct((NR, sh, hq3), BF16),
        ro=jax.ShapeDtypeStruct((sh, d), BF16),
        ri=jax.ShapeDtypeStruct((NR, sh, sz.iw), BF16),
        rd=jax.ShapeDtypeStruct((sz.ffp, d), BF16),
    )
    scratch = dict(
        wq=bf(d, hq3), wo=bf(2 * sh, d), wi=bf(d, sz.iw), wd=bf(sz.fq, d),
        xs=bf(rows, d), cs=bf(rows, d), mx=bf(rows, d), gt=bf(rows, d),
        aall=bf(all_, d), hall=bf(all_, d), call=bf(all_, d), yall=bf(all_, d),
        smalls=fl(NF, 8, 128), mini=fl(8, 128), lens=fl(NR, 8, 128), gains=fl(8, d),
        qkv=bf(all_, hq3), pbuf=fl(NR * sz.micro, sz.hq // 128, 2 * sz.slot, 128), obuf=bf(all_, sz.hq),
        part=fl(all_, d), part2=fl(all_, d), sib0=fl(2, rows, d), sib1=fl(2, rows, d),
        xsend=bf(rows, d), xsend2=bf(rows, d), xrecv0=bf(rows, d), xrecv1=bf(rows, d),
        hbuf=fl(rows, d), dhbuf=fl(rows, d), dg=fl(2, 8, d),
        gg=bf(all_, sz.fq), slope=fl(all_, sz.fq), dw=bf(all_, sz.iw), dqkv=bf(all_, hq3),
        gd=bf(sz.fq, d), gi=bf(d, sz.iw), go=bf(2 * sh, d), gq=bf(3, d, sz.hq),
        yrd=bf(3, third, d), zrd=bf(3, 2, third, d),
        yri=bf(sz.ntile, NZ, sh, t2), zri=bf(sz.ntile, NZ + 1, sh, t2),
        yro=bf(2, half, d), zro=bf(2, 2, 2, half, d),
        yrq=bf(3, NZ, sh, sz.hq), zrq=bf(3, NZ + 1, sh, sz.hq),
        gsend=fl(NF, 8, 128), gslots=fl(NF, 8, 128), greps=fl(NR, 8, 128), gout=fl(8, 128),
        sends=pltpu.SemaphoreType.DMA((90,)), recvs=pltpu.SemaphoreType.DMA((187,)),
        locals=pltpu.SemaphoreType.DMA((32,)),
    )
    any_ = pl.BlockSpec(memory_space=pl.ANY)
    vmem = pl.BlockSpec(memory_space=pltpu.VMEM)
    names = (*ins, *outs, *scratch)
    return pl.pallas_call(
        functools.partial(kernel, sz, names),
        out_shape=list(outs.values()),
        in_specs=[any_] * 2 + [vmem] * 6 + [any_] * 4,
        out_specs=[any_] * len(outs),
        scratch_shapes=list(scratch.values()),
        compiler_params=pltpu.CompilerParams(collective_id=0, has_side_effects=True, vmem_limit_bytes=64 * MIB),
    )(*ins.values())


def finish_kernel(sz, small, mixed, gtok, rq, ro, ri, rd, out_m, out_t, g1, gq, go, g2, gi, gd):
    hq, ffs, ffp = sz.hq, sz.ffs, sz.ffp
    for i in range(3):
        for q in range(NR):
            gq[:, i * sz.d + q * hq : i * sz.d + (q + 1) * hq] = rq[q, :, i * hq : (i + 1) * hq].astype(F32)
    g1[...], g2[...] = small[0:1, :], small[1:2, :]
    out_m[...], out_t[...] = mixed[...], gtok[...]
    go[...] = ro[...].astype(F32)
    gd[...] = rd[...].astype(F32)
    pieces = [[], []]
    for q in range(NR):
        tiles = [apart(sz, n, ri[q, :, col : col + w].astype(F32)) for n, (col, w) in enumerate(sz.units)]
        for i in range(2):
            v = jnp.concatenate([two[i] for two in tiles], axis=1)
            pieces[i] += [v[:, :ffs], v[:, ffp : ffp + ffs]]
    gi[...] = jnp.concatenate(pieces[0] + pieces[1], axis=1)


def finish(sz, small, mixed, gtok, rq, ro, ri, rd):
    d, sh = sz.d, sz.shard
    steps, n = sh // 16, sz.ffp // 16
    down = -(-n // steps) * 16
    last = -(-sz.ffp // down) - 1
    row = lambda w: pl.BlockSpec((16, w), lambda i: (i, 0))
    low = pl.BlockSpec((down, d), lambda i: (jnp.minimum(i, last), 0))
    rows = sz.micro * NF * sz.part // steps
    each = pl.BlockSpec((rows, d), lambda i: (i, 0))
    one = lambda n: pl.BlockSpec((n, sh), lambda i: (0, 0))
    quarters = lambda w: pl.BlockSpec((NR, 16, w), lambda i: (0, i, 0))
    return pl.pallas_call(
        functools.partial(finish_kernel, sz),
        grid=(steps,),
        out_shape=[
            jax.ShapeDtypeStruct((rows * steps, d), BF16),
            jax.ShapeDtypeStruct((rows * steps, d), BF16),
            jax.ShapeDtypeStruct((1, sh), F32),
            jax.ShapeDtypeStruct((sh, 3 * d), F32),
            jax.ShapeDtypeStruct((sh, d), F32),
            jax.ShapeDtypeStruct((1, sh), F32),
            jax.ShapeDtypeStruct((sh, 2 * NF * sz.ffs), F32),
            jax.ShapeDtypeStruct((sz.ffs, d), F32),
        ],
        in_specs=[one(8), each, each, quarters(rq.shape[2]), row(d), quarters(ri.shape[2]), low],
        out_specs=[each, each, one(1), row(3 * d), row(d), one(1), row(2 * NF * sz.ffs), low],
        compiler_params=pltpu.CompilerParams(vmem_limit_bytes=60 * MIB),
    )(small, mixed.reshape(-1, d), gtok.reshape(-1, d), rq, ro, ri, rd)


def routed(tokens, cotangent, deal, lengths, ln1_gain, w_qkv, w_out, ln2_gain, w_in, w_down):
    micro, _, part, d = tokens.shape
    ffs = w_down.shape[0]
    sz = Sizes(micro, part, d, ffs)
    half = d // HEADS // 2
    freq = np.float32(ROPE_BASE) ** (-(np.arange(half, dtype=np.float32) * np.float32(2.0 / (2 * half))))
    angles = np.arange(sz.slot, dtype=np.float32)[:, None] * freq[None, :]
    cos = jnp.asarray(np.tile(np.cos(angles), (1, 4)))
    sin = jnp.asarray(np.tile(np.concatenate([-np.sin(angles), np.sin(angles)], axis=1), (1, 2)))
    mixed, gtok, osmall, rq, ro, ri, rd = fused(
        sz, tokens, cotangent, ln1_gain[None], ln2_gain[None], lengths.reshape(1, micro), deal[:, 0],
        cos, sin, w_qkv, w_out, w_in, w_down,
    )
    mixed, gtok, g_1, g_qkv, g_out, g_2, g_in, g_down = finish(sz, osmall, mixed, gtok, rq, ro, ri, rd)
    return mixed.reshape(tokens.shape), gtok.reshape(tokens.shape), g_1[0], g_qkv, g_out, g_2[0], g_in, g_down


def solution(mesh):
    small = mesh.shape["fsdp"] == NF and mesh.shape["rep"] == NR
    rows = P(None, "rep", "fsdp", None)
    return jax.shard_map(
        routed if small else plain,
        mesh=mesh,
        in_specs=(
            rows, rows, P(None, "rep", None), P(None, "rep", "fsdp"),
            P("fsdp"), P("fsdp", None), P("fsdp", None), P("fsdp"), P("fsdp", None), P("fsdp", None),
        ),
        out_specs=(rows, rows, P("fsdp"), P("fsdp", None), P("fsdp", None), P("fsdp"), P("fsdp", None), P("fsdp", None)),
        check_vma=False,
    )
```

```python
import functools
import types

import jax
import jax.numpy as jnp
import numpy as np
from jax import lax
from jax.experimental import pallas as pl
from jax.experimental.pallas import tpu as pltpu
from jax.sharding import PartitionSpec as P

HEADS = 16
ROPE_BASE = 160000.0
NORM_EPS = 1e-05
MESH = pl.DeviceIdType.MESH
MIB = 1 << 20
BF16 = jnp.bfloat16
F32 = jnp.float32


def rope_tables(slot_count, head_size):
    half_size = head_size // 2
    frequency = ROPE_BASE ** (-(jnp.arange(half_size, dtype=F32) * 2.0 / head_size))
    angles = jnp.arange(slot_count, dtype=F32)[:, None] * frequency[None, :]
    return jnp.cos(angles), jnp.sin(angles)


def rotate(values, cosine, sine):
    front, back = jnp.split(values, 2, axis=-1)
    cosine, sine = cosine[:, None, :], sine[:, None, :]
    return jnp.concatenate([front * cosine - back * sine, back * cosine + front * sine], axis=-1)


def normed(values, gain):
    center = values - jnp.mean(values, axis=-1, keepdims=True)
    root = lax.rsqrt(jnp.mean(center * center, axis=-1, keepdims=True) + NORM_EPS)
    vhat = center * root
    return vhat * gain, vhat, root


def norm_back(dy, gain, vhat, root):
    dgain = jnp.sum(dy * vhat, axis=tuple(range(dy.ndim - 1)))
    e = dy * gain
    dz = root * (
        e
        - jnp.mean(e, axis=-1, keepdims=True)
        - vhat * jnp.mean(e * vhat, axis=-1, keepdims=True)
    )
    return dgain, dz


def mm(spec, a, b):
    return jnp.einsum(spec, a, b, preferred_element_type=F32)


def layer(g1, wqkv, wo, g2, win, wdown, tokens, dout, live):
    m, slot, d = tokens.shape
    heads, size = HEADS, d // HEADS
    scale = size ** (-0.5)
    w1, w2 = win
    lv = live[:, :, None]
    x = tokens.astype(F32)
    y, vhat1, root1 = normed(x, g1)
    a = y.astype(BF16)
    qkv = mm("mtd,de->mte", a, wqkv).reshape(m, slot, 3, heads, size)
    cosine, sine = rope_tables(slot, size)
    q = rotate(qkv[:, :, 0], cosine, sine).astype(BF16)
    k = rotate(qkv[:, :, 1], cosine, sine).astype(BF16)
    v = qkv[:, :, 2].astype(BF16)
    s = mm("mqhd,mkhd->mhqk", q, k) * scale
    s = jnp.where(live[:, None, None, :] > 0, s, -1e30)
    p = jax.nn.softmax(s, axis=-1)
    pb = p.astype(BF16)
    o = mm("mhqk,mkhd->mqhd", pb, v).astype(BF16).reshape(m, slot, d)
    h = x + lv * mm("mte,ed->mtd", o, wo)
    y, vhat2, root2 = normed(h, g2)
    hn = y.astype(BF16)
    z1 = mm("mtd,df->mtf", hn, w1)
    z2 = mm("mtd,df->mtf", hn, w2)
    cdf = 0.5 * (1.0 + lax.erf(z1 * (0.5**0.5)))
    pdf = jnp.exp(-0.5 * z1 * z1) * 0.3989422804014327
    act = z1 * cdf
    gg = (act * z2).astype(BF16)
    mixed = (h + lv * mm("mtf,fd->mtd", gg, wdown)).astype(BF16)

    up = dout.astype(F32)
    dy2 = (lv * up).astype(BF16)
    g_down = mm("mtf,mtd->fd", gg, dy2)
    dgg = mm("mtd,fd->mtf", dy2, wdown)
    dw1 = (dgg * z2 * (cdf + z1 * pdf)).astype(BF16)
    dw2 = (dgg * act).astype(BF16)
    g_in = (mm("mtd,mtf->df", hn, dw1), mm("mtd,mtf->df", hn, dw2))
    dhn = mm("mtf,df->mtd", dw1, w1) + mm("mtf,df->mtd", dw2, w2)
    g_g2, dhv = norm_back(dhn, g2, vhat2, root2)
    dh = up + dhv
    dy1 = (lv * dh).astype(BF16)
    g_out = mm("mte,mtd->ed", o, dy1)
    do = mm("mtd,ed->mte", dy1, wo).astype(BF16).reshape(m, slot, heads, size)
    dp = mm("mqhd,mkhd->mhqk", do, v)
    ds = (p * (dp - jnp.sum(dp * p, axis=-1, keepdims=True))).astype(BF16)
    dq = mm("mhqk,mkhd->mqhd", ds, k) * scale
    dk = mm("mhqk,mqhd->mkhd", ds, q) * scale
    dv = mm("mhqk,mqhd->mkhd", pb, do)
    dqkv = jnp.stack([rotate(dq, cosine, -sine), rotate(dk, cosine, -sine), dv], axis=2)
    dqkv = dqkv.reshape(m, slot, 3 * d).astype(BF16)
    g_qkv = mm("mtd,mte->de", a, dqkv)
    da = mm("mte,de->mtd", dqkv, wqkv)
    g_g1, dxv = norm_back(da, g1, vhat1, root1)
    gtok = (dh + dxv).astype(BF16)
    return mixed, gtok, (g_g1, g_qkv, g_out, g_g2, g_in, g_down)


def plain(tokens, cotangent, deal, lengths, ln1_gain, w_qkv, w_out, ln2_gain, w_in, w_down):
    slot = tokens.shape[2] * lax.axis_size("fsdp")
    me = lax.axis_index("fsdp")

    def spread(rows):
        return lax.all_to_all(rows, "fsdp", split_axis=1, concat_axis=2, tiled=True)[:, 0]

    def back(rows):
        return lax.all_to_all(rows[:, None], "fsdp", split_axis=2, concat_axis=1, tiled=True)

    def whole(shard):
        return lax.all_gather(shard.astype(BF16), "fsdp", axis=0, tiled=True)

    table = lax.all_gather(lengths[:, 0], "fsdp", axis=1, tiled=True)
    mine = lax.dynamic_slice_in_dim(deal[:, 0], me, 1, axis=1)
    pick = jnp.arange(table.shape[1], dtype=jnp.int32)[None, :] == mine
    length = jnp.sum(jnp.where(pick, table, 0), axis=1, keepdims=True)
    live = (jnp.arange(slot, dtype=jnp.int32)[None, :] < length).astype(F32)
    win = jnp.split(whole(w_in), 2, axis=1)
    mixed, gtok, grads = layer(
        whole(ln1_gain).astype(F32), whole(w_qkv), whole(w_out), whole(ln2_gain).astype(F32), win, whole(w_down),
        spread(tokens), spread(cotangent), live,
    )
    g_g1, g_qkv, g_out, g_g2, g_in, g_down = grads

    def owned(part):
        part = lax.psum_scatter(part, "fsdp", scatter_dimension=0, tiled=True)
        return lax.psum(part, "rep")

    g_in = jnp.concatenate(g_in, axis=1)
    return (back(mixed), back(gtok)) + tuple(owned(g) for g in (g_g1, g_qkv, g_out, g_g2, g_in, g_down))


NF, NR, NZ = 8, 4, 4
DN, XN, CN = 0, 1, 2


def at(offset, size, unit=16):
    return pl.ds(pl.multiple_of(offset, unit), size)


def nn(a, b):
    return lax.dot_general(a, b, (((1,), (0,)), ((), ())), preferred_element_type=F32)


def nt(a, b):
    return lax.dot_general(a, b, (((1,), (1,)), ((), ())), preferred_element_type=F32)


def tn(a, b):
    return lax.dot_general(a, b, (((0,), (0,)), ((), ())), preferred_element_type=F32)


def once(i, body):
    body(i)


def loop(n, body):
    def step(i, carry):
        body(i)
        return carry

    lax.fori_loop(0, n, step, 0)


ORDER = (
    3, 1, 2, 0, 24, 4, 15, 10, 5, 16, 54, 28, 17, 20, 53, 72, 12, 55, 11, 58, 18, 7, 6, 57, 56, 60, 74, 30, 13, 8,
    25, 21, 22, 73, 19, 59, 26, 75, 76, 33, 14, 27, 23, 52, 9, 62, 29, 38, 63, 64, 39, 61, 65, 35, 34, 66, 31, 71,
    46, 67, 40, 68, 49, 69, 36, 77, 70, 41, 78, 43, 47, 81, 82, 83, 50, 37, 86, 79, 42, 80, 32, 91, 90, 84, 44, 48,
    85, 87, 88, 89, 92, 51, 45, 93, 103, 94, 104, 141, 107, 96, 95, 105, 97, 144, 106, 116, 115, 108, 147, 99, 98,
    150, 100, 109, 128, 152, 111, 151, 112, 155, 101, 113, 142, 102, 114, 124, 171, 119, 165, 148, 126, 127, 145,
    166, 125, 160, 129, 156, 161, 130, 117, 153, 170, 175, 110, 162, 118, 134, 131, 133, 176, 120, 167, 180, 122,
    123, 149, 172, 132, 185, 181, 135, 157, 154, 186, 136, 177, 187, 143, 158, 168, 173, 182, 137, 138, 121, 146,
    174, 169, 163, 159, 178, 188, 183, 164, 139, 179, 189, 184, 140, 190,
)


def run_tasks(tasks):
    done = set()
    for i in ORDER or range(len(tasks)):
        deps, fn = tasks[i]
        assert done.issuperset(deps)
        fn()
        done.add(i)
    assert len(done) == len(tasks)


SOURCES = ((1, 0, 3, 2), (2, 2, 1, 1), (3, 3, 0, 0))
SOURCE_BELOW = ((0, 1, 0, 1), (0, 0, 1, 1), (0, 0, 1, 1))
OWNERS = ((3, 3, 0, 0), (2, 2, 1, 1), (1, 0, 3, 2))
OWNER_ABOVE = ((1, 1, 0, 0), (1, 1, 0, 0), (1, 0, 1, 0))
OWNER_SLOT = ((3, 3, 0, 0), (2, 2, 4, 1), (1, 4, 3, 4))


class Sizes:
    def __init__(self, micro, part, d, ffs):
        self.micro, self.part, self.d, self.ffs = micro, part, d, ffs
        self.slot = part * NF
        self.rows = micro * self.slot
        self.all = NR * self.rows
        self.shard = d // NF
        self.hq = d // NR
        self.ffp = -(-ffs // 16) * 16
        self.tile = 256
        self.ntile = -(-(2 * self.ffp) // self.tile)
        self.fq = self.ntile * self.tile
        last = 2 * self.ffp - (self.ntile - 1) * self.tile
        self.shift = -(-last // 64) * 64 if last <= self.tile - 64 else self.tile
        self.units = [(n * 2 * self.tile, 2 * self.tile) for n in range(self.ntile - 1)]
        self.units.append(((self.ntile - 1) * 2 * self.tile, 2 * self.shift))
        self.iw = sum(w for _, w in self.units)


def side_by_side(sz, n, one, two):
    if sz.units[n][1] == 2 * sz.tile:
        return jnp.concatenate([one, two], axis=1)
    room = jnp.zeros((one.shape[0], sz.units[n][1] - sz.tile), F32)
    return jnp.concatenate([one, room], axis=1) + pltpu.roll(jnp.concatenate([two, room], axis=1), sz.shift, 1)


def apart(sz, n, v):
    if sz.units[n][1] == 2 * sz.tile:
        return v[:, : sz.tile], v[:, sz.tile :]
    return v[:, : sz.tile], pltpu.roll(v, v.shape[1] - sz.shift, 1)[:, : sz.tile]


class Copies:
    def __init__(self, sends, recvs):
        self.sends, self.recvs, self.nsend, self.nrecv = sends, recvs, 0, 0
        self.left = []

    def send(self, n=1):
        base, self.nsend = self.nsend, self.nsend + n
        assert self.nsend <= self.sends.shape[0]
        return base

    def recv(self, n=1):
        base, self.nrecv = self.nrecv, self.nrecv + n
        assert self.nrecv <= self.recvs.shape[0]
        return base

    def make(self, src, dst, send, recv, f, r):
        return pltpu.make_async_remote_copy(
            src_ref=src, dst_ref=dst, send_sem=self.sends.at[send], recv_sem=self.recvs.at[recv],
            device_id={"fsdp": f, "rep": r}, device_id_type=MESH,
        )

    def start(self, build, cond=None):
        def go():
            self.make(*build()).start()

        go() if cond is None else pl.when(cond)(go)

    def arrived(self, ref, recv, f, r):
        self.make(ref, ref, 0, recv, f, r).wait_recv()

    def gone(self, ref, send, f, r, cond=None):
        def go():
            self.make(ref, ref, send, 0, f, r).wait_send()

        go() if cond is None else pl.when(cond)(go)

    def at_end(self, ref, send, cond=None):
        self.left.append((ref, send, cond))


def kernel(sz, names, *refs):
    k = types.SimpleNamespace(**dict(zip(names, refs)))
    d, rows, slot, micro, part = sz.d, sz.rows, sz.slot, sz.micro, sz.part
    f, r = lax.axis_index("fsdp"), lax.axis_index("rep")
    z, y = lax.div(f, 2), lax.rem(f, 2)
    c = lax.rem(r, 2)
    yn = f + 1 - 2 * y
    cn = r + 1 - 2 * c
    xn = lax.rem(r + 2, 4)
    dn = lax.rem(cn + 2, 4)
    others = [lax.rem(f + i, NF) for i in range(1, NF)]
    cp = Copies(k.sends, k.recvs)

    def local(src, dst, i):
        copy = pltpu.make_async_copy(src, dst, k.locals.at[i])
        copy.start()
        return copy

    def block(i):
        return at(i * rows, rows)

    barrier = pltpu.get_barrier_semaphore()
    friends = [(o, r) for o in others] + [(f, o) for o in (cn, xn, dn)]
    for ff, rr in friends:
        pl.semaphore_signal(barrier, inc=1, device_id={"fsdp": ff, "rep": rr}, device_id_type=MESH)

    tasks = []

    def task(*deps):
        def register(fn):
            tasks.append((deps, fn))
            return len(tasks) - 1

        return register

    wq, wo, wi, wd = k.wq, k.wo, k.wi, k.wd
    sh = sz.shard
    micros = range(micro)
    ends = []

    eights = (1 + 7 * lax.rem(z, 2)) * (1 + 63 * lax.div(z, 2))

    def by_z(*values):
        code = sum(v << (3 * i) for i, v in enumerate(values))
        return lax.rem(lax.div(jnp.int32(code), eights), 8)

    inner = jnp.logical_and(z > 0, z < NZ - 1)
    order_z = [by_z(*o) for o in OWNERS] + [z]

    class ColumnGather:
        def __init__(self, whole, col, width):
            self.whole, self.cols = whole, at(col, width, 128)
            self.zrecv, self.yrecv, self.zsend, self.ysend = cp.recv(NZ), cp.recv(), cp.send(), cp.send()
            cp.at_end(self.shards(NZ), self.ysend)
            cp.at_end(self.shards(NZ + 1), self.zsend, inner)
            cp.at_end(self.shards(1), self.zsend, jnp.logical_not(inner))

        def shards(self, n):
            return self.whole.at[pl.ds(0, n * sh), self.cols]

        def dst(self, j):
            return self.whole.at[at(j * sh, sh), self.cols]

        def over(self, j):
            dst = self.dst(j)
            cp.start(lambda: (dst, dst, self.ysend, self.yrecv, yn, r))

        def start(self):
            src = self.dst(f)
            cp.start(lambda: (src, src, self.zsend, self.zrecv + z, f + 2, r), z < NZ - 1)
            cp.start(lambda: (src, src, self.zsend, self.zrecv + z, f - 2, r), z > 0)
            self.over(f)

        def along_z(self, i):
            source, up = by_z(*SOURCES[i]), by_z(*SOURCE_BELOW[i])
            j = 2 * source + y
            dst = self.dst(j)
            cp.arrived(dst, self.zrecv + source, f, r)
            cp.start(lambda: (dst, dst, self.zsend, self.zrecv + source, f + 2 * (2 * up - 1), r), inner)
            self.over(j)

        def over_y(self):
            cp.arrived(self.shards(NZ), self.yrecv, f, r)

        def register(self, *deps):
            start = task(*deps)(self.start)
            steps = [task(start)(lambda i=i: self.along_z(i)) for i in range(NZ - 1)]
            self.needs = [start, *steps, task(start)(self.over_y)]

    class LongRowGather:
        def __init__(self, whole, row, height, pitch):
            self.whole, self.row, self.height, self.pitch = whole, row, height, pitch
            self.recv, self.send = cp.recv(2), cp.send(3)
            for n, cond in ((0, z < NZ - 1), (1, z > 0)):
                cp.at_end(self.dst(y), self.send + n, jnp.logical_and((z >= r) if n == 0 else (z <= r), cond))
            cp.at_end(self.dst(y), self.send + 2)

        def dst(self, yy):
            return self.whole.at[at(yy * self.pitch + self.row, self.height)]

        def onward(self):
            dst = self.dst(y)
            up = jnp.logical_and(z >= r, z < NZ - 1)
            down = jnp.logical_and(z <= r, z > 0)
            cp.start(lambda: (dst, dst, self.send, self.recv + y, f + 2, r), up)
            cp.start(lambda: (dst, dst, self.send + 1, self.recv + y, f - 2, r), down)
            cp.start(lambda: (dst, dst, self.send + 2, self.recv + y, yn, r))

        def start(self):
            @pl.when(z == r)
            def _():
                self.onward()

        def pass_on(self):
            @pl.when(z != r)
            def _():
                cp.arrived(self.dst(y), self.recv + y, f, r)
                self.onward()

        def rest(self):
            cp.arrived(self.dst(1 - y), self.recv + 1 - y, f, r)

        def register(self, *deps):
            start = task(*deps)(self.start)
            self.needs = [start, task(start)(self.pass_on), task(start)(self.rest)]

    class RowGather:
        def __init__(self, whole, row, height, pitch):
            self.whole, self.row, self.height, self.pitch = whole, row, height, pitch
            self.recv, self.send = cp.recv(2), cp.send(5)
            for yy, send in ((y, self.send), (1 - y, self.send + 2)):
                cp.at_end(self.dst(yy), send, self.up)
                cp.at_end(self.dst(yy), send + 1, self.down)
            cp.at_end(self.dst(y), self.send + 4, z == r)

        up = jnp.logical_and(z >= r, z < NZ - 1)
        down = jnp.logical_and(z <= r, z > 0)

        def dst(self, yy):
            return self.whole.at[at(yy * self.pitch + self.row, self.height)]

        def onward(self, yy, send):
            dst = self.dst(yy)
            cp.start(lambda: (dst, dst, send, self.recv + yy, f + 2, r), self.up)
            cp.start(lambda: (dst, dst, send + 1, self.recv + yy, f - 2, r), self.down)

        def start(self):
            dst = self.dst(y)
            cp.start(lambda: (dst, dst, self.send + 4, self.recv + y, yn, r), z == r)

        last = jnp.logical_and(z != r, jnp.logical_or(z == 0, z == NZ - 1))

        def pass_on(self, near):
            yy, send = (y, self.send) if near else (1 - y, self.send + 2)
            waits = jnp.logical_not(self.last)

            @pl.when(jnp.logical_and(waits, z != r) if near else waits)
            def _():
                cp.arrived(self.dst(yy), self.recv + yy, f, r)

            self.onward(yy, send)

        def rest(self):
            @pl.when(self.last)
            def _():
                for yy in (y, 1 - y):
                    cp.arrived(self.dst(yy), self.recv + yy, f, r)

        def register(self, *deps):
            start = task(*deps)(self.start)
            self.needs = [task(start)(lambda near=near: self.pass_on(near)) for near in (1, 0)]
            self.needs += [start, task(start)(self.rest)]

    class Spread:
        def __init__(self, buf):
            self.buf = buf
            self.ids, self.out = [cp.recv(3) for _ in micros], cp.send()

        def ref(self, b, m):
            return self.buf.at[at(b * rows + m * slot, slot)]

        def start(self, m):
            own, n = self.ref(r, m), self.ids[m]
            cp.start(lambda: (own, own, self.out, n + 1, f, xn))
            cp.start(lambda: (own, own, self.out, n, f, cn))

        def forward(self, m):
            got, n = self.ref(xn, m), self.ids[m]
            cp.arrived(got, n + 1, f, r)
            cp.start(lambda: (got, got, self.out, n + 2, f, cn))

        def got(self, b):
            for m in micros:
                if b is cn:
                    cp.arrived(self.ref(cn, m), self.ids[m], f, r)
                elif b is dn:
                    cp.arrived(self.ref(dn, m), self.ids[m] + 2, f, r)

        def register(self, deps):
            forward = [task(*deps)(lambda m=m: self.forward(m)) for m in micros]
            got = [task(*deps)(lambda b=b: self.got(b)) for b in (cn, dn)]
            self.need = [[got[1]], forward, [got[0]], list(deps)]
            self.all = [*forward, *got, *deps]

        def free(self):
            cp.gone(self.buf.at[pl.ds(0, 3 * rows)], self.out, f, r)

    class Sum:
        def __init__(self, part, sib, xsend, xrecv):
            self.part, self.sib, self.xsend, self.xrecv = part, sib, xsend, xrecv
            self.ids, self.xids, self.out, self.xout = cp.recv(2), cp.recv(micro), cp.send(), cp.send()

        def ready(self, w):
            if w not in (DN, CN):
                return
            b, i = (dn, 0) if w == DN else (cn, 1)
            src = self.part.at[block(b)]
            cp.start(lambda: (src, self.sib.at[i], self.out, self.ids + i, f, cn))

        def over_x(self):
            cp.arrived(self.sib.at[0], self.ids, f, r)
            for m in micros:

                def add(t, m=m):
                    s = at(m * slot + t * 32, 32)
                    self.xsend[s, :] = (
                        self.part[at(xn * rows + m * slot + t * 32, 32), :] + self.sib[0, s, :]
                    ).astype(BF16)

                loop(slot // 32, add)
                mm = at(m * slot, slot)
                cp.start(lambda m=m, mm=mm: (self.xsend.at[mm], self.xrecv.at[mm], self.xout, self.xids + m, f, xn))

        def done(self, m):
            if m == 0:
                cp.arrived(self.sib.at[1], self.ids + 1, f, r)
            cp.arrived(self.xrecv.at[at(m * slot, slot)], self.xids + m, f, r)

        def value(self, row, n):
            s = at(row, n)
            return self.part[at(r * rows + row, n), :] + self.sib[1, s, :] + self.xrecv[s, :].astype(F32)

        def free(self):
            cp.gone(self.part.at[pl.ds(0, 2 * rows)], self.out, f, r)
            cp.gone(self.xsend, self.xout, f, r)

    def add_into(dst, doff, src, n):
        def step(t):
            s = at(doff + t * 16, 16)
            dst[s, :] = (dst[s, :].astype(F32) + src[at(t * 16, 16), :].astype(F32)).astype(BF16)

        loop(n // 16, step)

    class ColumnReduce:
        def __init__(self, grad, yr, zr, out, col, width):
            self.grad, self.yr, self.zr, self.out = grad, yr, zr, out
            self.col, self.width = col, width
            self.yrecv, self.zrecv, self.orecv = cp.recv(NZ), cp.recv(NZ + 1), cp.recv(2)
            self.ysend, self.zsend, self.osend = cp.send(), cp.send(), cp.send()
            self.lid = lid()
            for n, send in ((NZ, self.ysend), (NZ - 1, self.zsend), (3, self.osend)):
                cp.at_end(grad.at[pl.ds(0, n * sh)], send)

        def send(self, j):
            zz = lax.div(j, 2)
            cp.start(lambda: (self.grad.at[at(j * sh, sh)], self.yr.at[zz], self.ysend, self.yrecv + zz, yn, r))

        def add_y(self, j):
            zz = lax.div(j, 2)
            cp.arrived(self.yr.at[zz], self.yrecv + zz, f, r)
            add_into(self.grad, j * sh, self.yr.at[zz], sh)

        def chain(self, i):
            owner, up, there = by_z(*OWNERS[i]), by_z(*OWNER_ABOVE[i]), by_z(*OWNER_SLOT[i])
            j = 2 * owner + y
            self.add_y(j)

            @pl.when(inner)
            def _():
                cp.arrived(self.zr.at[owner], self.zrecv + owner, f, r)
                add_into(self.grad, j * sh, self.zr.at[owner], sh)

            cp.start(
                lambda: (
                    self.grad.at[at(j * sh, sh)], self.zr.at[there], self.zsend, self.zrecv + there,
                    f + 2 * (2 * up - 1), r,
                )
            )

        def final(self):
            self.add_y(f)
            for slot_, cond in ((z, z > 0), (NZ, z < NZ - 1)):

                @pl.when(cond)
                def _(slot_=slot_):
                    cp.arrived(self.zr.at[slot_], self.zrecv + slot_, f, r)
                    add_into(self.grad, f * sh, self.zr.at[slot_], sh)

            src = self.grad.at[at(f * sh, sh)]
            for i, to in enumerate((xn, cn)):
                cp.start(lambda i=i, to=to: (src, self.dst(r), self.osend, self.orecv + i, f, to))
            ends.append(local(src, self.dst(r), self.lid))

        def dst(self, q):
            return self.out.at[q, :, at(self.col, self.width, 128)]

        def relay(self):
            got = self.dst(xn)
            cp.arrived(got, self.orecv, f, r)
            cp.start(lambda: (got, got, self.osend, self.orecv + 1, f, cn))

        def done(self):
            cp.arrived(self.out.at[pl.ds(0, 2), :, at(self.col, self.width, 128)], self.orecv + 1, f, r)

        def register(self, *deps):
            steps = [task(*deps)(lambda i=i: self.chain(i)) for i in range(NZ - 1)]
            final = task(*deps)(self.final)
            task(final)(self.relay)

    class LongRowReduce:
        def __init__(self, grad, yr, zr, out, row, height, pitch):
            self.grad, self.yr, self.zr, self.out = grad, yr, zr, out
            self.row, self.height, self.pitch = row, height, pitch
            self.yrecv, self.zrecv, self.orecv = cp.recv(), cp.recv(2), cp.recv(2)
            self.ysend, self.zsend, self.osend = cp.send(), cp.send(), cp.send()
            self.lid = lid()
            one = self.grad.at[self.rows(y)]
            cp.at_end(one, self.ysend)
            cp.at_end(one, self.zsend, z != r)
            cp.at_end(self.grad.at[pl.ds(0, 2 * height)], self.osend, z == r)
            cp.at_end(one, self.osend, z == xn)

        def rows(self, yy):
            return at(yy * self.pitch + self.row, self.height)

        def send(self):
            cp.start(lambda: (self.grad.at[self.rows(1 - y)], self.yr, self.ysend, self.yrecv, yn, r))

        def add(self, way):
            cp.arrived(self.zr.at[way], self.zrecv + way, f, r)
            add_into(self.grad, y * self.pitch + self.row, self.zr.at[way], self.height)

        def chain(self):
            cp.arrived(self.yr, self.yrecv, f, r)
            add_into(self.grad, y * self.pitch + self.row, self.yr, self.height)
            src = self.grad.at[self.rows(y)]
            for way, (toward, behind, step) in enumerate(((z < r, z > 0, 2), (z > r, z < NZ - 1, -2))):

                @pl.when(jnp.logical_and(toward, behind))
                def _(way=way):
                    self.add(way)

                cp.start(
                    lambda way=way, step=step: (src, self.zr.at[way], self.zsend, self.zrecv + way, f + step, r), toward
                )

        def dst(self):
            return self.out.at[at(self.row, self.height)]

        def final(self):
            for way, cond in enumerate((z > 0, z < NZ - 1)):

                @pl.when(jnp.logical_and(z == r, cond))
                def _(way=way):
                    self.add(way)

            src = self.grad.at[self.rows(y)]
            for i, to in enumerate((xn, cn)):
                cp.start(lambda i=i, to=to: (src, self.dst(), self.osend, self.orecv + i, f, to), z == r)

            @pl.when(z == r)
            def _():
                local(src, self.dst(), self.lid)

        def relay(self):
            got = self.dst()

            @pl.when(z == xn)
            def _():
                cp.arrived(got, self.orecv, f, r)

            cp.start(lambda: (got, got, self.osend, self.orecv + 1, f, cn), z == xn)

        def done(self):
            @pl.when(jnp.logical_or(z == cn, z == dn))
            def _():
                cp.arrived(self.dst(), self.orecv + 1, f, r)

            @pl.when(z == r)
            def _():
                pltpu.make_async_copy(self.grad.at[self.rows(y)], self.dst(), k.locals.at[self.lid]).wait()

        def register(self, *deps):
            chain = task(*deps)(self.chain)
            task(task(chain)(self.final))(self.relay)

    class RowReduce:
        def __init__(self, grad, yr, zr, out, row, height, pitch):
            self.grad, self.yr, self.zr, self.out = grad, yr, zr, out
            self.row, self.height, self.pitch = row, height, pitch
            self.yrecv, self.zrecv, self.orecv = cp.recv(), cp.recv(4), cp.recv(2)
            self.ysend, self.zsend, self.osend = cp.send(), cp.send(2), cp.send()
            self.lid = lid()
            one = self.grad.at[self.rows(y)]
            cp.at_end(one, self.ysend, z == r)
            for n in range(2):
                cp.at_end(one, self.zsend + n, z != r)
            cp.at_end(self.grad.at[pl.ds(0, 2 * height)], self.osend, z == r)
            cp.at_end(one, self.osend, z == xn)

        def rows(self, yy):
            return at(yy * self.pitch + self.row, self.height)

        def add(self, yy, way):
            cp.arrived(self.zr.at[way, yy], self.zrecv + 2 * way + yy, f, r)
            add_into(self.grad, yy * self.pitch + self.row, self.zr.at[way, yy], self.height)

        def chain(self, far):
            yy = 1 - y if far else y
            src = self.grad.at[self.rows(yy)]
            for way, (toward, behind, step) in enumerate(((z < r, z > 0, 2), (z > r, z < NZ - 1, -2))):

                @pl.when(jnp.logical_and(toward, behind))
                def _(way=way):
                    self.add(yy, way)

                cp.start(
                    lambda way=way, step=step: (
                        src, self.zr.at[way, yy], self.zsend + far, self.zrecv + 2 * way + yy, f + step, r
                    ),
                    toward,
                )

        def gathered(self, yy):
            for way, cond in enumerate((z > 0, z < NZ - 1)):

                @pl.when(jnp.logical_and(z == r, cond))
                def _(way=way):
                    self.add(yy, way)

        def cross(self):
            self.gathered(1 - y)
            cp.start(lambda: (self.grad.at[self.rows(1 - y)], self.yr, self.ysend, self.yrecv, yn, r), z == r)

        def dst(self):
            return self.out.at[at(self.row, self.height)]

        def final(self):
            self.gathered(y)

            @pl.when(z == r)
            def _():
                cp.arrived(self.yr, self.yrecv, f, r)
                add_into(self.grad, y * self.pitch + self.row, self.yr, self.height)

            src = self.grad.at[self.rows(y)]
            for i, to in enumerate((xn, cn)):
                cp.start(lambda i=i, to=to: (src, self.dst(), self.osend, self.orecv + i, f, to), z == r)

            @pl.when(z == r)
            def _():
                local(src, self.dst(), self.lid)

        def relay(self):
            got = self.dst()

            @pl.when(z == xn)
            def _():
                cp.arrived(got, self.orecv, f, r)

            cp.start(lambda: (got, got, self.osend, self.orecv + 1, f, cn), z == xn)

        def done(self):
            @pl.when(jnp.logical_or(z == cn, z == dn))
            def _():
                cp.arrived(self.dst(), self.orecv + 1, f, r)

            @pl.when(z == r)
            def _():
                pltpu.make_async_copy(self.grad.at[self.rows(y)], self.dst(), k.locals.at[self.lid]).wait()

        def register(self, *deps):
            chains = [task(*deps)(lambda far=far: self.chain(far)) for far in (1, 0)]
            cross = task(*chains)(self.cross)
            task(task(cross)(self.final))(self.relay)

    class Deal:
        def __init__(self, src, dst):
            self.src, self.dst, self.recvs, self.sends = src, dst, cp.recv(micro), cp.send(micro)
            self.lid = lid(micro)
            self.local = {}
            for m in micros:
                cp.at_end(self.most(), self.sends + m)

        def most(self):
            return self.dst.at[pl.ds(0, (NF - 1) * part)]

        def start(self, m):
            dst = self.dst.at[at(m * slot + f * part, part)]
            for o in others:
                cp.start(lambda o=o: (self.src.at[m, o], dst, self.sends + m, self.recvs + m, o, r))
            self.local[m] = local(self.src.at[m, f], dst, self.lid + m)

        def done(self, m):
            cp.arrived(self.most(), self.recvs + m, f, r)
            self.local[m].wait()

    class Back:
        def __init__(self, src, dst):
            self.src, self.dst, self.recvs, self.sends = src, dst, cp.recv(micro), cp.send(micro)
            self.lid = lid(micro)
            for m in micros:
                cp.at_end(self.most(), self.sends + m)

        def most(self):
            return self.src.at[pl.ds(0, (NF - 1) * part)]

        def start(self, m):
            for o in others:
                cp.start(
                    lambda o=o: (
                        self.src.at[at(m * slot + o * part, part)], self.dst.at[m, f], self.sends + m, self.recvs + m, o, r
                    )
                )
            ends.append(local(self.src.at[at(m * slot + f * part, part)], self.dst.at[m, f], self.lid + m))

        def done(self):
            for m in micros:
                cp.arrived(self.dst.at[m, pl.ds(0, NF - 1)], self.recvs + m, f, r)

    count = iter(range(k.locals.shape[0]))

    def lid(n=1):
        first = next(count)
        for _ in range(n - 1):
            next(count)
        return first

    t2 = 2 * sz.tile
    hq = sz.hq
    third, half = sz.ffp // 3, sh // 2
    smalls, lens, gains = k.smalls, k.lens, k.gains
    aall, hall, call, yall = k.aall, k.hall, k.call, k.yall
    part_, gg, slope, dw, dqkv = k.part, k.gg, k.slope, k.dw, k.dqkv
    gd, gi, go, gq, dg = k.gd, k.gi, k.go, k.gq, k.dg
    xs, cs, hbuf, dhbuf, mx, gt = k.xs, k.cs, k.hbuf, k.dhbuf, k.mx, k.gt
    qkv, pbuf, obuf = k.qkv, k.pbuf, k.obuf
    g_q = [ColumnGather(wq, i * hq, hq) for i in range(3)]
    g_o = [RowGather(wo, i * half, half, sh) for i in range(2)]
    g_i = [ColumnGather(wi, col, w) for col, w in sz.units]
    g_d = [LongRowGather(wd, i * third, third, sz.ffp) for i in range(3)]
    r_d = [LongRowReduce(gd, k.yrd.at[i], k.zrd.at[i], k.rd, i * third, third, sz.ffp) for i in range(3)]
    r_i = [
        ColumnReduce(
            gi.at[:, pl.ds(col, w)], k.yri.at[n, :, :, pl.ds(0, w)], k.zri.at[n, :, :, pl.ds(0, w)], k.ri, col, w
        )
        for n, (col, w) in enumerate(sz.units)
    ]
    r_o = [RowReduce(go, k.yro.at[i], k.zro.at[i], k.ro, i * half, half, sh) for i in range(2)]
    r_q = [ColumnReduce(gq.at[n], k.yrq.at[n], k.zrq.at[n], k.rq, n * hq, hq) for n in range(3)]
    small_in, len_in, gs_in, gr_in = (cp.recv() for _ in range(4))
    small_out, len_out, gs_out, gr_out = (cp.send() for _ in range(4))
    cp.at_end(smalls.at[pl.ds(0, NF - 1)], small_out)
    cp.at_end(lens.at[pl.ds(0, NR - 1)], len_out)
    cp.at_end(k.gsend.at[pl.ds(0, NF - 1)], gs_out)
    cp.at_end(k.greps.at[pl.ds(0, NR - 1)], gr_out)
    deal_x, deal_c = Deal(k.tok, xs), Deal(k.cot, cs)
    back_m, back_t = Back(mx, k.o_mixed), Back(gt, k.o_gtok)
    e_a, e_c, e_h, e_y = Spread(aall), Spread(call), Spread(hall), Spread(yall)
    s_1 = Sum(part_, k.sib0, k.xsend, k.xrecv0)
    s_m = Sum(k.part2, k.sib1, k.xsend2, k.xrecv1)
    s_h = Sum(part_, k.sib0, k.xsend, k.xrecv0)
    s_a = Sum(part_, k.sib0, k.xsend, k.xrecv0)
    blocks = [dn, xn, cn, r]

    lane = lax.broadcasted_iota(jnp.int32, (1, 128), 1)
    front = lax.rem(lane, 64) < 32
    low = lane < 64
    low_b = low.astype(F32).astype(BF16)
    high_b = (1.0 - low.astype(F32)).astype(BF16)
    npair = hq // 128
    scale = 64 ** (-0.5)
    tile_ = sz.tile
    NL = 32

    def live(m, t, n):
        pos = lax.broadcasted_iota(jnp.int32, (n, 1), 0) + t * n
        return pos.astype(F32) < lens[r, m : m + 1, 0:1]

    def normed(v):
        center = v - jnp.mean(v, axis=-1, keepdims=True)
        root = lax.rsqrt(jnp.mean(center * center, axis=-1, keepdims=True) + NORM_EPS)
        return center * root, root

    def norm_back(dy, gain, vhat, root):
        e = dy * gain
        return root * (e - jnp.mean(e, axis=-1, keepdims=True) - vhat * jnp.mean(e * vhat, axis=-1, keepdims=True))

    def swap(v):
        return jnp.where(front, pltpu.roll(v, 96, 1), pltpu.roll(v, 32, 1))

    def both(v):
        return jnp.concatenate([v * low_b, v * high_b], axis=0)

    def joined(v):
        return jnp.where(low, v[:slot], v[slot:])

    def fold(v):
        return jnp.sum(v.reshape(NL // 8, 8, d), axis=0)

    def triple(s, p):
        return [qkv[at(s * slot, slot), i * hq + p * 128 : i * hq + (p + 1) * 128] for i in range(3)]

    mini = k.mini
    mini[...] = jnp.zeros_like(mini)
    mini[0:1, :] = k.g1[...].astype(BF16).astype(F32)
    mini[1:2, :] = k.g2[...].astype(BF16).astype(F32)
    for m in micros:
        mini[2:3, :] += jnp.where(lane == m, k.len[0:1, m : m + 1].astype(F32), 0.0)
    smalls[f] = mini[...]
    qf, of = k.hbuf.at[pl.ds(0, sh)], k.hbuf.at[pl.ds(sh, sh)]
    q_in = [local(k.fq.at[:, at(i * d + r * hq, hq, 128)], qf.at[:, pl.ds(i * hq, hq)], lid()) for i in range(3)]
    o_lid, i_in, d_lid = lid(), [], lid()
    mine = z == r
    df = k.part2.at[pl.ds(0, sz.ffs)]

    @pl.when(mine)
    def _():
        local(k.fo, of, o_lid)

    shifts = []
    for i in range(2):
        first = i * NF * sz.ffs + r * 2 * sz.ffs
        base = lax.div(first, 128) * 128
        shifts.append(first - base)
        i_in.append(local(k.fi.at[:, at(base, sz.fq, 128)], k.dhbuf.at[pl.ds(i * sh, sh), pl.ds(0, sz.fq)], lid()))

    @pl.when(mine)
    def _():
        local(k.fd, df, d_lid)

    @task()
    def met():
        pl.semaphore_wait(barrier, len(friends))
        for o in others:
            cp.start(lambda o=o: (mini, smalls.at[f], small_out, small_in, o, r))

    @task()
    def prepare_q():
        for copy in q_in:
            copy.wait()

        def cast_q(t):
            wq[at(f * sh + t * 32, 32), :] = qf[at(t * 32, 32), pl.ds(0, 3 * hq)].astype(BF16)

        loop(sh // 32, cast_q)

    @task()
    def prepare_o():
        @pl.when(mine)
        def _():
            pltpu.make_async_copy(k.fo, of, k.locals.at[o_lid]).wait()

            def cast_o(t):
                wo[at(y * sh + t * 32, 32), :] = of[at(t * 32, 32), :].astype(BF16)

            loop(sh // 32, cast_o)

    @task()
    def prepare_i():
        for i in range(2):
            i_in[i].wait()
        lane_f = lax.broadcasted_iota(jnp.int32, (1, sz.fq), 1)
        first = lane_f < sz.ffs
        second = jnp.logical_and(lane_f >= sz.ffp, lane_f < sz.ffp + sz.ffs)

        def cast_i(t):
            halves = []
            for i in range(2):
                v = k.dhbuf[at(i * sh + t * 32, 32), pl.ds(0, sz.fq)]
                v = pltpu.roll(v, lax.rem(sz.fq - shifts[i], sz.fq), 1)
                halves.append(jnp.where(first, v, jnp.where(second, pltpu.roll(v, sz.ffp - sz.ffs, 1), 0.0)))
            for n, (col, w) in enumerate(sz.units):
                one, two = [v[:, n * tile_ : (n + 1) * tile_] for v in halves]
                wi[at(f * sh + t * 32, 32), pl.ds(col, w)] = side_by_side(sz, n, one, two).astype(BF16)

        loop(sh // 32, cast_i)

    @task()
    def prepare_d():
        @pl.when(mine)
        def _():
            pltpu.make_async_copy(k.fd, df, k.locals.at[d_lid]).wait()

            def cast_d(t):
                wd[at(y * sz.ffp + t * 16, 16), :] = df[at(t * 16, 16), :].astype(BF16)

            loop(sz.ffs // 16, cast_d)
            left = sz.ffs % 16
            if left:
                v = df[pl.ds(sz.ffs - left, left), :]
                v = jnp.concatenate([v, jnp.zeros((sz.ffp - sz.ffs, d), F32)], axis=0)
                wd[at(y * sz.ffp + sz.ffp - 16, 16), :] = v.astype(BF16)

    for u in g_q:
        u.register(met, prepare_q)
    for u in g_o:
        u.register(met, prepare_o)
    for u in g_i:
        u.register(met, prepare_i)
    for u in g_d:
        u.register(met, prepare_d)
    q_needs, o_needs, i_needs, d_needs = [[n for u in g for n in u.needs] for g in (g_q, g_o, g_i, g_d)]

    @task()
    def zero():
        wd[pl.ds(2 * sz.ffp, sz.fq - 2 * sz.ffp), :] = jnp.zeros((sz.fq - 2 * sz.ffp, d), BF16)
        dg[...] = jnp.zeros_like(dg)

    deals = [task(met)(lambda m=m: deal_x.start(m)) for m in micros]

    @task(met)
    def small():
        cp.arrived(smalls.at[pl.ds(0, NF - 1)], small_in, f, r)
        for j in range(NF):
            gains[0:2, j * sh : (j + 1) * sh] = smalls[j, 0:2, :]
        sub = lax.broadcasted_iota(jnp.int32, (NF, 128), 0)
        row8 = lax.broadcasted_iota(jnp.int32, (8, 128), 0)
        lane8 = lax.broadcasted_iota(jnp.int32, (1, NF), 1)
        len_tab = smalls[:, 2, :]
        table = jnp.zeros((8, 128), F32)
        for m in micros:
            dealt = jnp.where(lane8 == f, k.deal[m : m + 1, :].astype(F32), 0.0)
            dealt = jnp.sum(dealt, axis=1, keepdims=True)
            col = jnp.sum(jnp.where(sub.astype(F32) == dealt, len_tab, 0.0), axis=0, keepdims=True)
            length = jnp.sum(jnp.where(lane == m, col, 0.0), axis=1, keepdims=True)
            table = jnp.where(row8 == m, length, table)
        lens[r] = table
        for to in (xn, dn, cn):
            cp.start(lambda to=to: (lens.at[r], lens.at[r], len_out, len_in, f, to))

    @task(small)
    def lengths():
        cp.arrived(lens.at[pl.ds(0, NR - 1)], len_in, f, r)

    norm1s = []
    for m in micros:

        @task(small, deals[m])
        def step(m=m):
            deal_x.done(m)

            def norm1(t):
                vhat, _ = normed(xs[at(m * slot + t * NL, NL), :].astype(F32))
                aall[at(r * rows + m * slot + t * NL, NL), :] = (vhat * gains[0:1, :]).astype(BF16)

            loop(slot // NL, norm1)
            e_a.start(m)

        norm1s.append(step)
    e_a.register(norm1s)

    def project(b):
        a = aall[block(b), :]
        for i in range(3):
            t = nn(a, wq[:, i * hq : (i + 1) * hq])
            for p in range(npair):
                v = t[:, p * 128 : (p + 1) * 128]
                for m in micros:
                    u = v[m * slot : (m + 1) * slot]
                    if i < 2:
                        u = u * k.cos[...] + swap(u) * k.sin[...]
                    qkv[at(b * rows + m * slot, slot), i * hq + p * 128 : i * hq + (p + 1) * 128] = u.astype(BF16)

    def attend(b):
        def attend_one(m):
            s = b * micro + m
            length = lens[b, pl.ds(m, 1), :]
            for p in range(npair):
                q_, k_, v_ = triple(s, p)
                scores = nt(both(q_), k_) * scale
                scores = jnp.where(lane.astype(F32) < length, scores, -1e30)
                e = jnp.exp(scores - jnp.max(scores, axis=-1, keepdims=True))
                prob = e / jnp.sum(e, axis=-1, keepdims=True)
                pbuf[s, p] = prob
                out = nn(prob.astype(BF16), v_)
                obuf[at(s * slot, slot), p * 128 : (p + 1) * 128] = joined(out).astype(BF16)

        loop(micro, attend_one)

    def branch_one(b):
        def branch_tile(n):
            cols = at(n * 256, 256, 128)
            part_[block(b), cols] = nn(obuf[block(b), :], wo[:, cols])

        loop(d // 256, branch_tile)

    firsts = []
    for w in range(NR):

        @task(*e_a.need[w], *q_needs)
        def projected(w=w):
            project(blocks[w])

        @task(projected, lengths, *o_needs)
        def attended(w=w):
            attend(blocks[w])
            branch_one(blocks[w])
            s_1.ready(w)

        firsts.append(attended)
    crossed = task(firsts[DN], firsts[XN])(s_1.over_x)

    masks = []
    for m in micros:
        dealt = task(met)(lambda m=m: deal_c.start(m))

        @task(dealt, small)
        def step(m=m):
            deal_c.done(m)

            def mask_c(t):
                s = at(m * slot + t * NL, NL)
                masked = jnp.where(live(m, t, NL), cs[s, :].astype(F32), 0.0)
                call[at(r * rows + m * slot + t * NL, NL), :] = masked.astype(BF16)

            loop(slot // NL, mask_c)

        masks.append(step)

    @task(*masks)
    def spread_c():
        for m in micros:
            e_c.start(m)

    e_c.register([spread_c])

    norm2s = []
    for m in micros:

        @task(crossed, *firsts, *norm2s)
        def step(m=m):
            s_1.done(m)

            def norm2(t):
                row = m * slot + t * NL
                s = at(row, NL)
                h = xs[s, :].astype(F32) + jnp.where(live(m, t, NL), s_1.value(row, NL), 0.0)
                hbuf[s, :] = h
                vhat, _ = normed(h)
                hall[at(r * rows + row, NL), :] = (vhat * gains[1:2, :]).astype(BF16)

            loop(slot // NL, norm2)
            e_h.start(m)

        norm2s.append(step)
    freed = task(*norm2s)(s_1.free)
    e_h.register(norm2s)

    feeds = []
    for w in range(NR):

        @task(freed, *e_h.need[w], *i_needs)
        def step(w=w):
            rs = block(blocks[w])

            def feed(n):
                col, w = sz.units[n]
                w1, w2 = apart(sz, n, nn(hall[rs, :], wi[:, pl.ds(col, w)]))
                cdf = 0.5 * (1.0 + lax.erf(w1 * (0.5**0.5)))
                act = w1 * cdf
                pdf = jnp.exp(-0.5 * w1 * w1) * 0.3989422804014327
                cols = pl.ds(n * tile_, tile_)
                gg[rs, cols] = (act * w2).astype(BF16)
                part_[rs, cols] = act
                slope[rs, cols] = w2 * (cdf + w1 * pdf)

            for n in range(sz.ntile):
                once(n, feed)

        feeds.append(step)

    @task(*feeds, *e_c.all)
    def gdown():
        def grad_down(i):
            m, n = lax.div(i, 2), lax.rem(i, 2)
            cols = at(n * (d // 2), d // 2, 128)
            gd[at(m * 256, 256), cols] = tn(gg[:, at(m * 256, 256, 128)], call[:, cols]).astype(BF16)

        loop(sz.fq // 256 * 2, grad_down)
        for u in r_d:
            u.send()

    hids = []
    for w in range(NR):

        @task(feeds[w], zero, *e_c.need[w], *d_needs)
        def step(w=w):
            rs = block(blocks[w])

            def hidden(n):
                cols = pl.ds(n * tile_, tile_)
                dgg = nt(call[rs, :], wd[pl.ds(n * tile_, tile_), :])
                v = side_by_side(sz, n, dgg * slope[rs, cols], dgg * part_[rs, cols])
                dw[rs, pl.ds(*sz.units[n])] = v.astype(BF16)

            for n in range(sz.ntile):
                once(n, hidden)

        hids.append(step)

    gins = []
    for n in range(sz.ntile):
        for which in range(2):

            @task(*hids, *e_h.all)
            def step(n=n, which=which):
                def grad_in(i):
                    j = 2 * i + (y if which else 1 - y)
                    cols = pl.ds(*sz.units[n])
                    gi[at(j * sh, sh), cols] = tn(hall[:, at(j * sh, sh, 128)], dw[:, cols]).astype(BF16)

                loop(NZ, grad_in)
                if not which:
                    for owner in order_z:
                        r_i[n].send(2 * owner + 1 - y)

            gins.append(step)

    dhns = []
    for w in range(NR):

        @task(hids[w])
        def step(w=w):
            b = blocks[w]

            def dhn_tile(n):
                part_[block(b), at(n * 256, 256, 128)] = nt(dw[block(b), :], wi[at(n * 256, 256), :])

            loop(d // 256, dhn_tile)
            s_h.ready(w)

        dhns.append(step)
    crossed = task(dhns[DN], dhns[XN])(s_h.over_x)
    back2s = []
    for m in micros:

        @task(crossed, zero, *dhns, *back2s)
        def step(m=m):
            s_h.done(m)

            def back2(t):
                row = m * slot + t * NL
                s = at(row, NL)
                dy = s_h.value(row, NL)
                vhat, root = normed(hbuf[s, :])
                dg[1] += fold(dy * vhat)
                dh = cs[s, :].astype(F32) + norm_back(dy, gains[1:2, :], vhat, root)
                dhbuf[s, :] = dh
                yall[at(r * rows + row, NL), :] = jnp.where(live(m, t, NL), dh, 0.0).astype(BF16)

            loop(slot // NL, back2)
            e_y.start(m)

        back2s.append(step)
    freed = task(*back2s)(s_h.free)
    e_y.register(back2s)

    mixes = []
    for w in range(NR):

        @task(zero, feeds[w], *d_needs)
        def step(w=w):
            b = blocks[w]

            def mix_tile(n):
                cols = at(n * 256, 256, 128)
                k.part2[block(b), cols] = nn(gg[block(b), :], wd[:, cols])

            loop(d // 256, mix_tile)
            s_m.ready(w)

        mixes.append(step)
    crossed = task(mixes[DN], mixes[XN])(s_m.over_x)
    mixeds = []
    for m in micros:

        @task(crossed, *mixes, *mixeds)
        def step(m=m):
            s_m.done(m)

            def mix(t):
                row = m * slot + t * NL
                s = at(row, NL)
                mx[s, :] = (hbuf[s, :] + jnp.where(live(m, t, NL), s_m.value(row, NL), 0.0)).astype(BF16)

            loop(slot // NL, mix)

        mixeds.append(step)
        task(step)(lambda m=m: back_m.start(m))

    @task(*firsts, *e_y.all)
    def gout():
        def grad_out(i):
            cols = at(i * 256, 256, 128)
            go[:, cols] = tn(obuf[...], yall[:, cols]).astype(BF16)

        loop(d // 256, grad_out)

    abacks = []
    for w in range(NR):

        @task(firsts[w], *e_y.need[w])
        def step(w=w):
            def attend_back(m):
                s = blocks[w] * micro + m
                do_all = nt(yall[at(s * slot, slot), :], wo[...]).astype(BF16)
                for p in range(npair):
                    q_, k_, v_ = triple(s, p)
                    q2, do2 = both(q_), both(do_all[:, p * 128 : (p + 1) * 128])
                    prob = pbuf[s, p]
                    dp = nt(do2, v_)
                    ds = (prob * (dp - jnp.sum(dp * prob, axis=-1, keepdims=True))).astype(BF16)
                    dq = joined(nn(ds, k_)) * scale
                    dk = tn(ds, q2) * scale
                    dv = tn(prob.astype(BF16), do2)
                    cosine, sine = k.cos[...], k.sin[...]
                    dq = dq * cosine - swap(dq) * sine
                    dk = dk * cosine - swap(dk) * sine
                    for i, v in enumerate((dq, dk, dv)):
                        dqkv[at(s * slot, slot), i * hq + p * 128 : i * hq + (p + 1) * 128] = v.astype(BF16)

            loop(micro, attend_back)

        abacks.append(step)

    gqkvs = []
    for which in range(2):

        @task(*abacks, *e_a.all)
        def step(which=which):
            def grad_qkv(i):
                j = 2 * i + (y if which else 1 - y)
                g = tn(aall[:, at(j * sh, sh, 128)], dqkv[...]).astype(BF16)
                for n in range(3):
                    gq[n, at(j * sh, sh), :] = g[:, n * hq : (n + 1) * hq]

            loop(NZ, grad_qkv)
            if not which:
                for n in range(3):
                    for owner in order_z:
                        r_q[n].send(2 * owner + 1 - y)

        gqkvs.append(step)

    das = []
    for w in range(NR):

        @task(abacks[w], freed)
        def step(w=w):
            b = blocks[w]

            def da_tile(n):
                part_[block(b), at(n * 256, 256, 128)] = nt(dqkv[block(b), :], wq[at(n * 256, 256), :])

            loop(d // 256, da_tile)
            s_a.ready(w)

        das.append(step)
    crossed = task(das[DN], das[XN])(s_a.over_x)
    back1s = []
    for m in micros:

        @task(crossed, *das, *back1s)
        def step(m=m):
            s_a.done(m)

            def back1(t):
                row = m * slot + t * NL
                s = at(row, NL)
                dy = s_a.value(row, NL)
                vhat, root = normed(xs[s, :].astype(F32))
                dg[0] += fold(dy * vhat)
                gt[s, :] = (dhbuf[s, :] + norm_back(dy, gains[0:1, :], vhat, root)).astype(BF16)

            loop(slot // NL, back1)
            back_t.start(m)

        back1s.append(step)

    gsend, gslots, greps, gout_ = k.gsend, k.gslots, k.greps, k.gout

    @task(*back1s, *back2s)
    def gain_parts():
        for which in range(2):
            total = jnp.sum(dg[which], axis=0, keepdims=True)
            for j in range(NF):
                gsend[j, which : which + 1, :] = total[:, j * sh : (j + 1) * sh]
        for o in others:
            cp.start(lambda o=o: (gsend.at[o], gslots.at[f], gs_out, gs_in, o, r))
        gslots[f] = gsend[f]

    @task(gain_parts)
    def gain_sums():
        cp.arrived(gslots.at[pl.ds(0, NF - 1)], gs_in, f, r)
        total = gslots[0]
        for j in range(1, NF):
            total = total + gslots[j]
        greps[r] = total
        for to in (xn, dn, cn):
            cp.start(lambda to=to: (greps.at[r], greps.at[r], gr_out, gr_in, f, to))

    glid = lid()

    @task(gain_sums)
    def gain_totals():
        cp.arrived(greps.at[pl.ds(0, NR - 1)], gr_in, f, r)
        gout_[...] = greps[0] + greps[1] + greps[2] + greps[3]
        ends.append(local(gout_, k.o_small, glid))

    for u in r_d:
        u.register(gdown)
    for n, u in enumerate(r_i):
        u.register(*gins[2 * n : 2 * n + 2])
    for u in r_o:
        u.register(gout)
    for u in r_q:
        u.register(*gqkvs)

    @task(*range(len(tasks)))
    def end():
        for u in r_d + r_i + r_o + r_q + [back_m, back_t]:
            u.done()
        s_a.free()
        s_m.free()
        for e in (e_a, e_c, e_h, e_y):
            e.free()
        for ref, send, cond in cp.left:
            cp.gone(ref, send, f, r, cond)
        for copy in ends:
            copy.wait()

    run_tasks(tasks)


def fused(sz, tok, cot, g1, g2, length, deal, cos, sin, fq, fo, fi, fd):
    d, sh, all_, rows = sz.d, sz.shard, sz.all, sz.rows
    t2 = 2 * sz.tile
    third, half = sz.ffp // 3, sh // 2
    hq3 = 3 * sz.hq
    bf = lambda *s: pltpu.VMEM(s, BF16)
    fl = lambda *s: pltpu.VMEM(s, F32)
    ins = dict(tok=tok, cot=cot, g1=g1, g2=g2, len=length, deal=deal, cos=cos, sin=sin, fq=fq, fo=fo, fi=fi, fd=fd)
    outs = dict(
        o_mixed=jax.ShapeDtypeStruct((sz.micro, NF, sz.part, d), BF16),
        o_gtok=jax.ShapeDtypeStruct((sz.micro, NF, sz.part, d), BF16),
        o_small=jax.ShapeDtypeStruct((8, 128), F32),
        rq=jax.ShapeDtypeStruct((NR, sh, hq3), BF16),
        ro=jax.ShapeDtypeStruct((sh, d), BF16),
        ri=jax.ShapeDtypeStruct((NR, sh, sz.iw), BF16),
        rd=jax.ShapeDtypeStruct((sz.ffp, d), BF16),
    )
    scratch = dict(
        wq=bf(d, hq3), wo=bf(2 * sh, d), wi=bf(d, sz.iw), wd=bf(sz.fq, d),
        xs=bf(rows, d), cs=bf(rows, d), mx=bf(rows, d), gt=bf(rows, d),
        aall=bf(all_, d), hall=bf(all_, d), call=bf(all_, d), yall=bf(all_, d),
        smalls=fl(NF, 8, 128), mini=fl(8, 128), lens=fl(NR, 8, 128), gains=fl(8, d),
        qkv=bf(all_, hq3), pbuf=fl(NR * sz.micro, sz.hq // 128, 2 * sz.slot, 128), obuf=bf(all_, sz.hq),
        part=fl(all_, d), part2=fl(all_, d), sib0=fl(2, rows, d), sib1=fl(2, rows, d),
        xsend=bf(rows, d), xsend2=bf(rows, d), xrecv0=bf(rows, d), xrecv1=bf(rows, d),
        hbuf=fl(rows, d), dhbuf=fl(rows, d), dg=fl(2, 8, d),
        gg=bf(all_, sz.fq), slope=fl(all_, sz.fq), dw=bf(all_, sz.iw), dqkv=bf(all_, hq3),
        gd=bf(sz.fq, d), gi=bf(d, sz.iw), go=bf(2 * sh, d), gq=bf(3, d, sz.hq),
        yrd=bf(3, third, d), zrd=bf(3, 2, third, d),
        yri=bf(sz.ntile, NZ, sh, t2), zri=bf(sz.ntile, NZ + 1, sh, t2),
        yro=bf(2, half, d), zro=bf(2, 2, 2, half, d),
        yrq=bf(3, NZ, sh, sz.hq), zrq=bf(3, NZ + 1, sh, sz.hq),
        gsend=fl(NF, 8, 128), gslots=fl(NF, 8, 128), greps=fl(NR, 8, 128), gout=fl(8, 128),
        sends=pltpu.SemaphoreType.DMA((90,)), recvs=pltpu.SemaphoreType.DMA((187,)),
        locals=pltpu.SemaphoreType.DMA((32,)),
    )
    any_ = pl.BlockSpec(memory_space=pl.ANY)
    vmem = pl.BlockSpec(memory_space=pltpu.VMEM)
    names = (*ins, *outs, *scratch)
    return pl.pallas_call(
        functools.partial(kernel, sz, names),
        out_shape=list(outs.values()),
        in_specs=[any_] * 2 + [vmem] * 6 + [any_] * 4,
        out_specs=[any_] * len(outs),
        scratch_shapes=list(scratch.values()),
        compiler_params=pltpu.CompilerParams(collective_id=0, has_side_effects=True, vmem_limit_bytes=64 * MIB),
    )(*ins.values())


def finish_kernel(sz, small, mixed, gtok, rq, ro, ri, rd, out_m, out_t, g1, gq, go, g2, gi, gd):
    hq, ffs, ffp = sz.hq, sz.ffs, sz.ffp
    for i in range(3):
        for q in range(NR):
            gq[:, i * sz.d + q * hq : i * sz.d + (q + 1) * hq] = rq[q, :, i * hq : (i + 1) * hq].astype(F32)
    g1[...], g2[...] = small[0:1, :], small[1:2, :]
    out_m[...], out_t[...] = mixed[...], gtok[...]
    go[...] = ro[...].astype(F32)
    gd[...] = rd[...].astype(F32)
    pieces = [[], []]
    for q in range(NR):
        tiles = [apart(sz, n, ri[q, :, col : col + w].astype(F32)) for n, (col, w) in enumerate(sz.units)]
        for i in range(2):
            v = jnp.concatenate([two[i] for two in tiles], axis=1)
            pieces[i] += [v[:, :ffs], v[:, ffp : ffp + ffs]]
    gi[...] = jnp.concatenate(pieces[0] + pieces[1], axis=1)


def finish(sz, small, mixed, gtok, rq, ro, ri, rd):
    d, sh = sz.d, sz.shard
    grain = 32
    steps, n = sh // grain, sz.ffp // 16
    down = -(-n // steps) * 16
    last = -(-sz.ffp // down) - 1
    row = lambda w: pl.BlockSpec((grain, w), lambda i: (i, 0))
    low = pl.BlockSpec((down, d), lambda i: (jnp.minimum(i, last), 0))
    rows = sz.micro * NF * sz.part // steps
    each = pl.BlockSpec((rows, d), lambda i: (i, 0))
    one = lambda n: pl.BlockSpec((n, sh), lambda i: (0, 0))
    quarters = lambda w: pl.BlockSpec((NR, grain, w), lambda i: (0, i, 0))
    return pl.pallas_call(
        functools.partial(finish_kernel, sz),
        grid=(steps,),
        out_shape=[
            jax.ShapeDtypeStruct((rows * steps, d), BF16),
            jax.ShapeDtypeStruct((rows * steps, d), BF16),
            jax.ShapeDtypeStruct((1, sh), F32),
            jax.ShapeDtypeStruct((sh, 3 * d), F32),
            jax.ShapeDtypeStruct((sh, d), F32),
            jax.ShapeDtypeStruct((1, sh), F32),
            jax.ShapeDtypeStruct((sh, 2 * NF * sz.ffs), F32),
            jax.ShapeDtypeStruct((sz.ffs, d), F32),
        ],
        in_specs=[one(8), each, each, quarters(rq.shape[2]), row(d), quarters(ri.shape[2]), low],
        out_specs=[each, each, one(1), row(3 * d), row(d), one(1), row(2 * NF * sz.ffs), low],
        compiler_params=pltpu.CompilerParams(vmem_limit_bytes=60 * MIB),
    )(small, mixed.reshape(-1, d), gtok.reshape(-1, d), rq, ro, ri, rd)


def routed(tokens, cotangent, deal, lengths, ln1_gain, w_qkv, w_out, ln2_gain, w_in, w_down):
    micro, _, part, d = tokens.shape
    ffs = w_down.shape[0]
    sz = Sizes(micro, part, d, ffs)
    half = d // HEADS // 2
    freq = np.float32(ROPE_BASE) ** (-(np.arange(half, dtype=np.float32) * np.float32(2.0 / (2 * half))))
    angles = np.arange(sz.slot, dtype=np.float32)[:, None] * freq[None, :]
    cos = jnp.asarray(np.tile(np.cos(angles), (1, 4)))
    sin = jnp.asarray(np.tile(np.concatenate([-np.sin(angles), np.sin(angles)], axis=1), (1, 2)))
    mixed, gtok, osmall, rq, ro, ri, rd = fused(
        sz, tokens, cotangent, ln1_gain[None], ln2_gain[None], lengths.reshape(1, micro), deal[:, 0],
        cos, sin, w_qkv, w_out, w_in, w_down,
    )
    mixed, gtok, g_1, g_qkv, g_out, g_2, g_in, g_down = finish(sz, osmall, mixed, gtok, rq, ro, ri, rd)
    return mixed.reshape(tokens.shape), gtok.reshape(tokens.shape), g_1[0], g_qkv, g_out, g_2[0], g_in, g_down


def solution(mesh):
    small = mesh.shape["fsdp"] == NF and mesh.shape["rep"] == NR
    rows = P(None, "rep", "fsdp", None)
    return jax.shard_map(
        routed if small else plain,
        mesh=mesh,
        in_specs=(
            rows, rows, P(None, "rep", None), P(None, "rep", "fsdp"),
            P("fsdp"), P("fsdp", None), P("fsdp", None), P("fsdp"), P("fsdp", None), P("fsdp", None),
        ),
        out_specs=(rows, rows, P("fsdp"), P("fsdp", None), P("fsdp", None), P("fsdp"), P("fsdp", None), P("fsdp", None)),
        check_vma=False,
    )
```

```python
import functools
import types

import jax
import jax.numpy as jnp
import numpy as np
from jax import lax
from jax.experimental import pallas as pl
from jax.experimental.pallas import tpu as pltpu
from jax.sharding import PartitionSpec as P

HEADS = 16
ROPE_BASE = 160000.0
NORM_EPS = 1e-05
MESH = pl.DeviceIdType.MESH
MIB = 1 << 20
BF16 = jnp.bfloat16
F32 = jnp.float32


def rope_tables(slot_count, head_size):
    half_size = head_size // 2
    frequency = ROPE_BASE ** (-(jnp.arange(half_size, dtype=F32) * 2.0 / head_size))
    angles = jnp.arange(slot_count, dtype=F32)[:, None] * frequency[None, :]
    return jnp.cos(angles), jnp.sin(angles)


def rotate(values, cosine, sine):
    front, back = jnp.split(values, 2, axis=-1)
    cosine, sine = cosine[:, None, :], sine[:, None, :]
    return jnp.concatenate([front * cosine - back * sine, back * cosine + front * sine], axis=-1)


def normed(values, gain):
    center = values - jnp.mean(values, axis=-1, keepdims=True)
    root = lax.rsqrt(jnp.mean(center * center, axis=-1, keepdims=True) + NORM_EPS)
    vhat = center * root
    return vhat * gain, vhat, root


def norm_back(dy, gain, vhat, root):
    dgain = jnp.sum(dy * vhat, axis=tuple(range(dy.ndim - 1)))
    e = dy * gain
    dz = root * (
        e
        - jnp.mean(e, axis=-1, keepdims=True)
        - vhat * jnp.mean(e * vhat, axis=-1, keepdims=True)
    )
    return dgain, dz


def mm(spec, a, b):
    return jnp.einsum(spec, a, b, preferred_element_type=F32)


def layer(g1, wqkv, wo, g2, win, wdown, tokens, dout, live):
    m, slot, d = tokens.shape
    heads, size = HEADS, d // HEADS
    scale = size ** (-0.5)
    w1, w2 = win
    lv = live[:, :, None]
    x = tokens.astype(F32)
    y, vhat1, root1 = normed(x, g1)
    a = y.astype(BF16)
    qkv = mm("mtd,de->mte", a, wqkv).reshape(m, slot, 3, heads, size)
    cosine, sine = rope_tables(slot, size)
    q = rotate(qkv[:, :, 0], cosine, sine).astype(BF16)
    k = rotate(qkv[:, :, 1], cosine, sine).astype(BF16)
    v = qkv[:, :, 2].astype(BF16)
    s = mm("mqhd,mkhd->mhqk", q, k) * scale
    s = jnp.where(live[:, None, None, :] > 0, s, -1e30)
    p = jax.nn.softmax(s, axis=-1)
    pb = p.astype(BF16)
    o = mm("mhqk,mkhd->mqhd", pb, v).astype(BF16).reshape(m, slot, d)
    h = x + lv * mm("mte,ed->mtd", o, wo)
    y, vhat2, root2 = normed(h, g2)
    hn = y.astype(BF16)
    z1 = mm("mtd,df->mtf", hn, w1)
    z2 = mm("mtd,df->mtf", hn, w2)
    cdf = 0.5 * (1.0 + lax.erf(z1 * (0.5**0.5)))
    pdf = jnp.exp(-0.5 * z1 * z1) * 0.3989422804014327
    act = z1 * cdf
    gg = (act * z2).astype(BF16)
    mixed = (h + lv * mm("mtf,fd->mtd", gg, wdown)).astype(BF16)

    up = dout.astype(F32)
    dy2 = (lv * up).astype(BF16)
    g_down = mm("mtf,mtd->fd", gg, dy2)
    dgg = mm("mtd,fd->mtf", dy2, wdown)
    dw1 = (dgg * z2 * (cdf + z1 * pdf)).astype(BF16)
    dw2 = (dgg * act).astype(BF16)
    g_in = (mm("mtd,mtf->df", hn, dw1), mm("mtd,mtf->df", hn, dw2))
    dhn = mm("mtf,df->mtd", dw1, w1) + mm("mtf,df->mtd", dw2, w2)
    g_g2, dhv = norm_back(dhn, g2, vhat2, root2)
    dh = up + dhv
    dy1 = (lv * dh).astype(BF16)
    g_out = mm("mte,mtd->ed", o, dy1)
    do = mm("mtd,ed->mte", dy1, wo).astype(BF16).reshape(m, slot, heads, size)
    dp = mm("mqhd,mkhd->mhqk", do, v)
    ds = (p * (dp - jnp.sum(dp * p, axis=-1, keepdims=True))).astype(BF16)
    dq = mm("mhqk,mkhd->mqhd", ds, k) * scale
    dk = mm("mhqk,mqhd->mkhd", ds, q) * scale
    dv = mm("mhqk,mqhd->mkhd", pb, do)
    dqkv = jnp.stack([rotate(dq, cosine, -sine), rotate(dk, cosine, -sine), dv], axis=2)
    dqkv = dqkv.reshape(m, slot, 3 * d).astype(BF16)
    g_qkv = mm("mtd,mte->de", a, dqkv)
    da = mm("mte,de->mtd", dqkv, wqkv)
    g_g1, dxv = norm_back(da, g1, vhat1, root1)
    gtok = (dh + dxv).astype(BF16)
    return mixed, gtok, (g_g1, g_qkv, g_out, g_g2, g_in, g_down)


def plain(tokens, cotangent, deal, lengths, ln1_gain, w_qkv, w_out, ln2_gain, w_in, w_down):
    slot = tokens.shape[2] * lax.axis_size("fsdp")
    me = lax.axis_index("fsdp")

    def spread(rows):
        return lax.all_to_all(rows, "fsdp", split_axis=1, concat_axis=2, tiled=True)[:, 0]

    def back(rows):
        return lax.all_to_all(rows[:, None], "fsdp", split_axis=2, concat_axis=1, tiled=True)

    def whole(shard):
        return lax.all_gather(shard.astype(BF16), "fsdp", axis=0, tiled=True)

    table = lax.all_gather(lengths[:, 0], "fsdp", axis=1, tiled=True)
    mine = lax.dynamic_slice_in_dim(deal[:, 0], me, 1, axis=1)
    pick = jnp.arange(table.shape[1], dtype=jnp.int32)[None, :] == mine
    length = jnp.sum(jnp.where(pick, table, 0), axis=1, keepdims=True)
    live = (jnp.arange(slot, dtype=jnp.int32)[None, :] < length).astype(F32)
    win = jnp.split(whole(w_in), 2, axis=1)
    mixed, gtok, grads = layer(
        whole(ln1_gain).astype(F32), whole(w_qkv), whole(w_out), whole(ln2_gain).astype(F32), win, whole(w_down),
        spread(tokens), spread(cotangent), live,
    )
    g_g1, g_qkv, g_out, g_g2, g_in, g_down = grads

    def owned(part):
        part = lax.psum_scatter(part, "fsdp", scatter_dimension=0, tiled=True)
        return lax.psum(part, "rep")

    g_in = jnp.concatenate(g_in, axis=1)
    return (back(mixed), back(gtok)) + tuple(owned(g) for g in (g_g1, g_qkv, g_out, g_g2, g_in, g_down))


NF, NR, NZ = 8, 4, 4
DN, XN, CN = 0, 1, 2


def at(offset, size, unit=16):
    return pl.ds(pl.multiple_of(offset, unit), size)


def nn(a, b):
    return lax.dot_general(a, b, (((1,), (0,)), ((), ())), preferred_element_type=F32)


def nt(a, b):
    return lax.dot_general(a, b, (((1,), (1,)), ((), ())), preferred_element_type=F32)


def tn(a, b):
    return lax.dot_general(a, b, (((0,), (0,)), ((), ())), preferred_element_type=F32)


def once(i, body):
    body(i)


def loop(n, body):
    def step(i, carry):
        body(i)
        return carry

    lax.fori_loop(0, n, step, 0)


ORDER = (
    1, 0, 15, 2, 24, 3, 10, 5, 52, 16, 54, 20, 28, 17, 53, 72, 55, 56, 12, 58, 11, 18, 6, 7, 57, 60, 74, 30, 13, 8,
    25, 59, 26, 22, 21, 27, 73, 75, 76, 4, 33, 19, 23, 29, 38, 62, 14, 9, 63, 64, 34, 79, 39, 69, 65, 35, 66, 31,
    71, 46, 49, 61, 67, 68, 40, 36, 70, 78, 77, 41, 81, 47, 82, 43, 32, 83, 50, 42, 37, 91, 86, 90, 84, 80, 44, 85,
    87, 88, 48, 89, 92, 51, 45, 93, 103, 94, 104, 141, 96, 107, 95, 105, 144, 106, 97, 115, 147, 108, 98, 150, 109,
    99, 151, 128, 111, 100, 152, 110, 113, 116, 112, 155, 101, 102, 114, 124, 165, 171, 125, 127, 145, 166, 126,
    160, 119, 129, 161, 133, 170, 167, 142, 156, 146, 117, 162, 134, 131, 153, 148, 130, 175, 118, 176, 120, 122,
    123, 180, 132, 135, 185, 181, 157, 186, 177, 136, 158, 143, 182, 172, 178, 187, 137, 138, 163, 183, 188, 173,
    168, 184, 179, 164, 154, 121, 139, 169, 189, 149, 140, 159, 174, 190,
)


def run_tasks(tasks):
    done = set()
    for i in ORDER or range(len(tasks)):
        deps, fn = tasks[i]
        assert done.issuperset(deps)
        fn()
        done.add(i)
    assert len(done) == len(tasks)


SOURCES = ((1, 0, 3, 2), (2, 2, 1, 1), (3, 3, 0, 0))
SOURCE_BELOW = ((0, 1, 0, 1), (0, 0, 1, 1), (0, 0, 1, 1))
OWNERS = ((3, 3, 0, 0), (2, 2, 1, 1), (1, 0, 3, 2))
OWNER_ABOVE = ((1, 1, 0, 0), (1, 1, 0, 0), (1, 0, 1, 0))
OWNER_SLOT = ((3, 3, 0, 0), (2, 2, 4, 1), (1, 4, 3, 4))


class Sizes:
    def __init__(self, micro, part, d, ffs):
        self.micro, self.part, self.d, self.ffs = micro, part, d, ffs
        self.slot = part * NF
        self.rows = micro * self.slot
        self.all = NR * self.rows
        self.shard = d // NF
        self.hq = d // NR
        self.ffp = -(-ffs // 16) * 16
        self.tile = 256
        self.ntile = -(-(2 * self.ffp) // self.tile)
        self.fq = self.ntile * self.tile
        last = 2 * self.ffp - (self.ntile - 1) * self.tile
        self.shift = -(-last // 64) * 64 if last <= self.tile - 64 else self.tile
        self.units = [(n * 2 * self.tile, 2 * self.tile) for n in range(self.ntile - 1)]
        self.units.append(((self.ntile - 1) * 2 * self.tile, 2 * self.shift))
        self.iw = sum(w for _, w in self.units)


def side_by_side(sz, n, one, two):
    if sz.units[n][1] == 2 * sz.tile:
        return jnp.concatenate([one, two], axis=1)
    room = jnp.zeros((one.shape[0], sz.units[n][1] - sz.tile), F32)
    return jnp.concatenate([one, room], axis=1) + pltpu.roll(jnp.concatenate([two, room], axis=1), sz.shift, 1)


def apart(sz, n, v):
    if sz.units[n][1] == 2 * sz.tile:
        return v[:, : sz.tile], v[:, sz.tile :]
    return v[:, : sz.tile], pltpu.roll(v, v.shape[1] - sz.shift, 1)[:, : sz.tile]


class Copies:
    def __init__(self, sends, recvs):
        self.sends, self.recvs, self.nsend, self.nrecv = sends, recvs, 0, 0
        self.left = []

    def send(self, n=1):
        base, self.nsend = self.nsend, self.nsend + n
        assert self.nsend <= self.sends.shape[0]
        return base

    def recv(self, n=1):
        base, self.nrecv = self.nrecv, self.nrecv + n
        assert self.nrecv <= self.recvs.shape[0]
        return base

    def make(self, src, dst, send, recv, f, r):
        return pltpu.make_async_remote_copy(
            src_ref=src, dst_ref=dst, send_sem=self.sends.at[send], recv_sem=self.recvs.at[recv],
            device_id={"fsdp": f, "rep": r}, device_id_type=MESH,
        )

    def start(self, build, cond=None):
        def go():
            self.make(*build()).start()

        go() if cond is None else pl.when(cond)(go)

    def arrived(self, ref, recv, f, r):
        self.make(ref, ref, 0, recv, f, r).wait_recv()

    def gone(self, ref, send, f, r, cond=None):
        def go():
            self.make(ref, ref, send, 0, f, r).wait_send()

        go() if cond is None else pl.when(cond)(go)

    def at_end(self, ref, send, cond=None):
        self.left.append((ref, send, cond))


def kernel(sz, names, *refs):
    k = types.SimpleNamespace(**dict(zip(names, refs)))
    d, rows, slot, micro, part = sz.d, sz.rows, sz.slot, sz.micro, sz.part
    f, r = lax.axis_index("fsdp"), lax.axis_index("rep")
    z, y = lax.div(f, 2), lax.rem(f, 2)
    c = lax.rem(r, 2)
    yn = f + 1 - 2 * y
    cn = r + 1 - 2 * c
    xn = lax.rem(r + 2, 4)
    dn = lax.rem(cn + 2, 4)
    others = [lax.rem(f + i, NF) for i in range(1, NF)]
    cp = Copies(k.sends, k.recvs)

    def local(src, dst, i):
        copy = pltpu.make_async_copy(src, dst, k.locals.at[i])
        copy.start()
        return copy

    def block(i):
        return at(i * rows, rows)

    barrier = pltpu.get_barrier_semaphore()
    friends = [(o, r) for o in others] + [(f, o) for o in (cn, xn, dn)]
    for ff, rr in friends:
        pl.semaphore_signal(barrier, inc=1, device_id={"fsdp": ff, "rep": rr}, device_id_type=MESH)

    tasks = []

    def task(*deps):
        def register(fn):
            tasks.append((deps, fn))
            return len(tasks) - 1

        return register

    wq, wo, wi, wd = k.wq, k.wo, k.wi, k.wd
    sh = sz.shard
    micros = range(micro)
    ends = []

    eights = (1 + 7 * lax.rem(z, 2)) * (1 + 63 * lax.div(z, 2))

    def by_z(*values):
        code = sum(v << (3 * i) for i, v in enumerate(values))
        return lax.rem(lax.div(jnp.int32(code), eights), 8)

    inner = jnp.logical_and(z > 0, z < NZ - 1)
    order_z = [by_z(*o) for o in OWNERS] + [z]

    class ColumnGather:
        def __init__(self, whole, col, width):
            self.whole, self.cols = whole, at(col, width, 128)
            self.zrecv, self.yrecv, self.zsend, self.ysend = cp.recv(NZ), cp.recv(), cp.send(), cp.send()
            cp.at_end(self.shards(NZ), self.ysend)
            cp.at_end(self.shards(NZ + 1), self.zsend, inner)
            cp.at_end(self.shards(1), self.zsend, jnp.logical_not(inner))

        def shards(self, n):
            return self.whole.at[pl.ds(0, n * sh), self.cols]

        def dst(self, j):
            return self.whole.at[at(j * sh, sh), self.cols]

        def over(self, j):
            dst = self.dst(j)
            cp.start(lambda: (dst, dst, self.ysend, self.yrecv, yn, r))

        def start(self):
            src = self.dst(f)
            cp.start(lambda: (src, src, self.zsend, self.zrecv + z, f + 2, r), z < NZ - 1)
            cp.start(lambda: (src, src, self.zsend, self.zrecv + z, f - 2, r), z > 0)
            self.over(f)

        def along_z(self, i):
            source, up = by_z(*SOURCES[i]), by_z(*SOURCE_BELOW[i])
            j = 2 * source + y
            dst = self.dst(j)
            cp.arrived(dst, self.zrecv + source, f, r)
            cp.start(lambda: (dst, dst, self.zsend, self.zrecv + source, f + 2 * (2 * up - 1), r), inner)
            self.over(j)

        def over_y(self):
            cp.arrived(self.shards(NZ), self.yrecv, f, r)

        def register(self, *deps):
            start = task(*deps)(self.start)
            steps = [task(start)(lambda i=i: self.along_z(i)) for i in range(NZ - 1)]
            self.needs = [start, *steps, task(start)(self.over_y)]

    class LongRowGather:
        def __init__(self, whole, row, height, pitch):
            self.whole, self.row, self.height, self.pitch = whole, row, height, pitch
            self.recv, self.send = cp.recv(2), cp.send(3)
            for n, cond in ((0, z < NZ - 1), (1, z > 0)):
                cp.at_end(self.dst(y), self.send + n, jnp.logical_and((z >= r) if n == 0 else (z <= r), cond))
            cp.at_end(self.dst(y), self.send + 2)

        def dst(self, yy):
            return self.whole.at[at(yy * self.pitch + self.row, self.height)]

        def onward(self):
            dst = self.dst(y)
            up = jnp.logical_and(z >= r, z < NZ - 1)
            down = jnp.logical_and(z <= r, z > 0)
            cp.start(lambda: (dst, dst, self.send, self.recv + y, f + 2, r), up)
            cp.start(lambda: (dst, dst, self.send + 1, self.recv + y, f - 2, r), down)
            cp.start(lambda: (dst, dst, self.send + 2, self.recv + y, yn, r))

        def start(self):
            @pl.when(z == r)
            def _():
                self.onward()

        def pass_on(self):
            @pl.when(z != r)
            def _():
                cp.arrived(self.dst(y), self.recv + y, f, r)
                self.onward()

        def rest(self):
            cp.arrived(self.dst(1 - y), self.recv + 1 - y, f, r)

        def register(self, *deps):
            start = task(*deps)(self.start)
            self.needs = [start, task(start)(self.pass_on), task(start)(self.rest)]

    class RowGather:
        def __init__(self, whole, row, height, pitch):
            self.whole, self.row, self.height, self.pitch = whole, row, height, pitch
            self.recv, self.send = cp.recv(2), cp.send(5)
            for yy, send in ((y, self.send), (1 - y, self.send + 2)):
                cp.at_end(self.dst(yy), send, self.up)
                cp.at_end(self.dst(yy), send + 1, self.down)
            cp.at_end(self.dst(y), self.send + 4, z == r)

        up = jnp.logical_and(z >= r, z < NZ - 1)
        down = jnp.logical_and(z <= r, z > 0)

        def dst(self, yy):
            return self.whole.at[at(yy * self.pitch + self.row, self.height)]

        def onward(self, yy, send):
            dst = self.dst(yy)
            cp.start(lambda: (dst, dst, send, self.recv + yy, f + 2, r), self.up)
            cp.start(lambda: (dst, dst, send + 1, self.recv + yy, f - 2, r), self.down)

        def start(self):
            dst = self.dst(y)
            cp.start(lambda: (dst, dst, self.send + 4, self.recv + y, yn, r), z == r)

        last = jnp.logical_and(z != r, jnp.logical_or(z == 0, z == NZ - 1))

        def pass_on(self, near):
            yy, send = (y, self.send) if near else (1 - y, self.send + 2)
            waits = jnp.logical_not(self.last)

            @pl.when(jnp.logical_and(waits, z != r) if near else waits)
            def _():
                cp.arrived(self.dst(yy), self.recv + yy, f, r)

            self.onward(yy, send)

        def rest(self):
            @pl.when(self.last)
            def _():
                for yy in (y, 1 - y):
                    cp.arrived(self.dst(yy), self.recv + yy, f, r)

        def register(self, *deps):
            start = task(*deps)(self.start)
            self.needs = [task(start)(lambda near=near: self.pass_on(near)) for near in (1, 0)]
            self.needs += [start, task(start)(self.rest)]

    class Spread:
        def __init__(self, buf):
            self.buf = buf
            self.ids, self.out = [cp.recv(3) for _ in micros], cp.send()

        def ref(self, b, m):
            return self.buf.at[at(b * rows + m * slot, slot)]

        def start(self, m):
            own, n = self.ref(r, m), self.ids[m]
            cp.start(lambda: (own, own, self.out, n + 1, f, xn))
            cp.start(lambda: (own, own, self.out, n, f, cn))

        def forward(self, m):
            got, n = self.ref(xn, m), self.ids[m]
            cp.arrived(got, n + 1, f, r)
            cp.start(lambda: (got, got, self.out, n + 2, f, cn))

        def got(self, b):
            for m in micros:
                if b is cn:
                    cp.arrived(self.ref(cn, m), self.ids[m], f, r)
                elif b is dn:
                    cp.arrived(self.ref(dn, m), self.ids[m] + 2, f, r)

        def register(self, deps):
            forward = [task(*deps)(lambda m=m: self.forward(m)) for m in micros]
            got = [task(*deps)(lambda b=b: self.got(b)) for b in (cn, dn)]
            self.need = [[got[1]], forward, [got[0]], list(deps)]
            self.all = [*forward, *got, *deps]

        def free(self):
            cp.gone(self.buf.at[pl.ds(0, 3 * rows)], self.out, f, r)

    class Sum:
        def __init__(self, part, sib, xsend, xrecv):
            self.part, self.sib, self.xsend, self.xrecv = part, sib, xsend, xrecv
            self.ids, self.xids, self.out, self.xout = cp.recv(2), cp.recv(micro), cp.send(), cp.send()

        def ready(self, w):
            if w not in (DN, CN):
                return
            b, i = (dn, 0) if w == DN else (cn, 1)
            src = self.part.at[block(b)]
            cp.start(lambda: (src, self.sib.at[i], self.out, self.ids + i, f, cn))

        def over_x(self):
            cp.arrived(self.sib.at[0], self.ids, f, r)
            for m in micros:

                def add(t, m=m):
                    s = at(m * slot + t * 32, 32)
                    self.xsend[s, :] = (
                        self.part[at(xn * rows + m * slot + t * 32, 32), :] + self.sib[0, s, :]
                    ).astype(BF16)

                loop(slot // 32, add)
                mm = at(m * slot, slot)
                cp.start(lambda m=m, mm=mm: (self.xsend.at[mm], self.xrecv.at[mm], self.xout, self.xids + m, f, xn))

        def done(self, m):
            if m == 0:
                cp.arrived(self.sib.at[1], self.ids + 1, f, r)
            cp.arrived(self.xrecv.at[at(m * slot, slot)], self.xids + m, f, r)

        def value(self, row, n):
            s = at(row, n)
            return self.part[at(r * rows + row, n), :] + self.sib[1, s, :] + self.xrecv[s, :].astype(F32)

        def free(self):
            cp.gone(self.part.at[pl.ds(0, 2 * rows)], self.out, f, r)
            cp.gone(self.xsend, self.xout, f, r)

    def add_into(dst, doff, src, n):
        def step(t):
            s = at(doff + t * 16, 16)
            dst[s, :] = (dst[s, :].astype(F32) + src[at(t * 16, 16), :].astype(F32)).astype(BF16)

        loop(n // 16, step)

    class ColumnReduce:
        def __init__(self, grad, yr, zr, out, col, width):
            self.grad, self.yr, self.zr, self.out = grad, yr, zr, out
            self.col, self.width = col, width
            self.yrecv, self.zrecv, self.orecv = cp.recv(NZ), cp.recv(NZ + 1), cp.recv(2)
            self.ysend, self.zsend, self.osend = cp.send(), cp.send(), cp.send()
            self.lid = lid()
            for n, send in ((NZ, self.ysend), (NZ - 1, self.zsend), (3, self.osend)):
                cp.at_end(grad.at[pl.ds(0, n * sh)], send)

        def send(self, j):
            zz = lax.div(j, 2)
            cp.start(lambda: (self.grad.at[at(j * sh, sh)], self.yr.at[zz], self.ysend, self.yrecv + zz, yn, r))

        def add_y(self, j):
            zz = lax.div(j, 2)
            cp.arrived(self.yr.at[zz], self.yrecv + zz, f, r)
            add_into(self.grad, j * sh, self.yr.at[zz], sh)

        def chain(self, i):
            owner, up, there = by_z(*OWNERS[i]), by_z(*OWNER_ABOVE[i]), by_z(*OWNER_SLOT[i])
            j = 2 * owner + y
            self.add_y(j)

            @pl.when(inner)
            def _():
                cp.arrived(self.zr.at[owner], self.zrecv + owner, f, r)
                add_into(self.grad, j * sh, self.zr.at[owner], sh)

            cp.start(
                lambda: (
                    self.grad.at[at(j * sh, sh)], self.zr.at[there], self.zsend, self.zrecv + there,
                    f + 2 * (2 * up - 1), r,
                )
            )

        def final(self):
            self.add_y(f)
            for slot_, cond in ((z, z > 0), (NZ, z < NZ - 1)):

                @pl.when(cond)
                def _(slot_=slot_):
                    cp.arrived(self.zr.at[slot_], self.zrecv + slot_, f, r)
                    add_into(self.grad, f * sh, self.zr.at[slot_], sh)

            src = self.grad.at[at(f * sh, sh)]
            for i, to in enumerate((xn, cn)):
                cp.start(lambda i=i, to=to: (src, self.dst(r), self.osend, self.orecv + i, f, to))
            ends.append(local(src, self.dst(r), self.lid))

        def dst(self, q):
            return self.out.at[q, :, at(self.col, self.width, 128)]

        def relay(self):
            got = self.dst(xn)
            cp.arrived(got, self.orecv, f, r)
            cp.start(lambda: (got, got, self.osend, self.orecv + 1, f, cn))

        def done(self):
            cp.arrived(self.out.at[pl.ds(0, 2), :, at(self.col, self.width, 128)], self.orecv + 1, f, r)

        def register(self, *deps):
            steps = [task(*deps)(lambda i=i: self.chain(i)) for i in range(NZ - 1)]
            final = task(*deps)(self.final)
            task(final)(self.relay)

    class LongRowReduce:
        def __init__(self, grad, yr, zr, out, row, height, pitch):
            self.grad, self.yr, self.zr, self.out = grad, yr, zr, out
            self.row, self.height, self.pitch = row, height, pitch
            self.yrecv, self.zrecv, self.orecv = cp.recv(), cp.recv(2), cp.recv(2)
            self.ysend, self.zsend, self.osend = cp.send(), cp.send(), cp.send()
            self.lid = lid()
            one = self.grad.at[self.rows(y)]
            cp.at_end(one, self.ysend)
            cp.at_end(one, self.zsend, z != r)
            cp.at_end(self.grad.at[pl.ds(0, 2 * height)], self.osend, z == r)
            cp.at_end(one, self.osend, z == xn)

        def rows(self, yy):
            return at(yy * self.pitch + self.row, self.height)

        def send(self):
            cp.start(lambda: (self.grad.at[self.rows(1 - y)], self.yr, self.ysend, self.yrecv, yn, r))

        def add(self, way):
            cp.arrived(self.zr.at[way], self.zrecv + way, f, r)
            add_into(self.grad, y * self.pitch + self.row, self.zr.at[way], self.height)

        def chain(self):
            cp.arrived(self.yr, self.yrecv, f, r)
            add_into(self.grad, y * self.pitch + self.row, self.yr, self.height)
            src = self.grad.at[self.rows(y)]
            for way, (toward, behind, step) in enumerate(((z < r, z > 0, 2), (z > r, z < NZ - 1, -2))):

                @pl.when(jnp.logical_and(toward, behind))
                def _(way=way):
                    self.add(way)

                cp.start(
                    lambda way=way, step=step: (src, self.zr.at[way], self.zsend, self.zrecv + way, f + step, r), toward
                )

        def dst(self):
            return self.out.at[at(self.row, self.height)]

        def final(self):
            for way, cond in enumerate((z > 0, z < NZ - 1)):

                @pl.when(jnp.logical_and(z == r, cond))
                def _(way=way):
                    self.add(way)

            src = self.grad.at[self.rows(y)]
            for i, to in enumerate((xn, cn)):
                cp.start(lambda i=i, to=to: (src, self.dst(), self.osend, self.orecv + i, f, to), z == r)

            @pl.when(z == r)
            def _():
                local(src, self.dst(), self.lid)

        def relay(self):
            got = self.dst()

            @pl.when(z == xn)
            def _():
                cp.arrived(got, self.orecv, f, r)

            cp.start(lambda: (got, got, self.osend, self.orecv + 1, f, cn), z == xn)

        def done(self):
            @pl.when(jnp.logical_or(z == cn, z == dn))
            def _():
                cp.arrived(self.dst(), self.orecv + 1, f, r)

            @pl.when(z == r)
            def _():
                pltpu.make_async_copy(self.grad.at[self.rows(y)], self.dst(), k.locals.at[self.lid]).wait()

        def register(self, *deps):
            chain = task(*deps)(self.chain)
            task(task(chain)(self.final))(self.relay)

    class RowReduce:
        def __init__(self, grad, yr, zr, out, row, height, pitch):
            self.grad, self.yr, self.zr, self.out = grad, yr, zr, out
            self.row, self.height, self.pitch = row, height, pitch
            self.yrecv, self.zrecv, self.orecv = cp.recv(), cp.recv(4), cp.recv(2)
            self.ysend, self.zsend, self.osend = cp.send(), cp.send(2), cp.send()
            self.lid = lid()
            one = self.grad.at[self.rows(y)]
            cp.at_end(one, self.ysend, z == r)
            for n in range(2):
                cp.at_end(one, self.zsend + n, z != r)
            cp.at_end(self.grad.at[pl.ds(0, 2 * height)], self.osend, z == r)
            cp.at_end(one, self.osend, z == xn)

        def rows(self, yy):
            return at(yy * self.pitch + self.row, self.height)

        def add(self, yy, way):
            cp.arrived(self.zr.at[way, yy], self.zrecv + 2 * way + yy, f, r)
            add_into(self.grad, yy * self.pitch + self.row, self.zr.at[way, yy], self.height)

        def chain(self, far):
            yy = 1 - y if far else y
            src = self.grad.at[self.rows(yy)]
            for way, (toward, behind, step) in enumerate(((z < r, z > 0, 2), (z > r, z < NZ - 1, -2))):

                @pl.when(jnp.logical_and(toward, behind))
                def _(way=way):
                    self.add(yy, way)

                cp.start(
                    lambda way=way, step=step: (
                        src, self.zr.at[way, yy], self.zsend + far, self.zrecv + 2 * way + yy, f + step, r
                    ),
                    toward,
                )

        def gathered(self, yy):
            for way, cond in enumerate((z > 0, z < NZ - 1)):

                @pl.when(jnp.logical_and(z == r, cond))
                def _(way=way):
                    self.add(yy, way)

        def cross(self):
            self.gathered(1 - y)
            cp.start(lambda: (self.grad.at[self.rows(1 - y)], self.yr, self.ysend, self.yrecv, yn, r), z == r)

        def dst(self):
            return self.out.at[at(self.row, self.height)]

        def final(self):
            self.gathered(y)

            @pl.when(z == r)
            def _():
                cp.arrived(self.yr, self.yrecv, f, r)
                add_into(self.grad, y * self.pitch + self.row, self.yr, self.height)

            src = self.grad.at[self.rows(y)]
            for i, to in enumerate((xn, cn)):
                cp.start(lambda i=i, to=to: (src, self.dst(), self.osend, self.orecv + i, f, to), z == r)

            @pl.when(z == r)
            def _():
                local(src, self.dst(), self.lid)

        def relay(self):
            got = self.dst()

            @pl.when(z == xn)
            def _():
                cp.arrived(got, self.orecv, f, r)

            cp.start(lambda: (got, got, self.osend, self.orecv + 1, f, cn), z == xn)

        def done(self):
            @pl.when(jnp.logical_or(z == cn, z == dn))
            def _():
                cp.arrived(self.dst(), self.orecv + 1, f, r)

            @pl.when(z == r)
            def _():
                pltpu.make_async_copy(self.grad.at[self.rows(y)], self.dst(), k.locals.at[self.lid]).wait()

        def register(self, *deps):
            chains = [task(*deps)(lambda far=far: self.chain(far)) for far in (1, 0)]
            cross = task(*chains)(self.cross)
            task(task(cross)(self.final))(self.relay)

    class Deal:
        def __init__(self, src, dst):
            self.src, self.dst, self.recvs, self.sends = src, dst, cp.recv(micro), cp.send(micro)
            self.lid = lid(micro)
            self.local = {}
            for m in micros:
                cp.at_end(self.most(), self.sends + m)

        def most(self):
            return self.dst.at[pl.ds(0, (NF - 1) * part)]

        def start(self, m):
            dst = self.dst.at[at(m * slot + f * part, part)]
            for o in others:
                cp.start(lambda o=o: (self.src.at[m, o], dst, self.sends + m, self.recvs + m, o, r))
            self.local[m] = local(self.src.at[m, f], dst, self.lid + m)

        def done(self, m):
            cp.arrived(self.most(), self.recvs + m, f, r)
            self.local[m].wait()

    class Back:
        def __init__(self, src, dst):
            self.src, self.dst, self.recvs, self.sends = src, dst, cp.recv(micro), cp.send(micro)
            self.lid = lid(micro)
            for m in micros:
                cp.at_end(self.most(), self.sends + m)

        def most(self):
            return self.src.at[pl.ds(0, (NF - 1) * part)]

        def start(self, m):
            for o in others:
                cp.start(
                    lambda o=o: (
                        self.src.at[at(m * slot + o * part, part)], self.dst.at[m, f], self.sends + m, self.recvs + m, o, r
                    )
                )
            ends.append(local(self.src.at[at(m * slot + f * part, part)], self.dst.at[m, f], self.lid + m))

        def done(self):
            for m in micros:
                cp.arrived(self.dst.at[m, pl.ds(0, NF - 1)], self.recvs + m, f, r)

    count = iter(range(k.locals.shape[0]))

    def lid(n=1):
        first = next(count)
        for _ in range(n - 1):
            next(count)
        return first

    t2 = 2 * sz.tile
    hq = sz.hq
    third, half = sz.ffp // 3, sh // 2
    smalls, lens, gains = k.smalls, k.lens, k.gains
    aall, hall, call, yall = k.aall, k.hall, k.call, k.yall
    part_, gg, slope, dw, dqkv = k.part, k.gg, k.slope, k.dw, k.dqkv
    gd, gi, go, gq, dg = k.gd, k.gi, k.go, k.gq, k.dg
    xs, cs, hbuf, dhbuf, mx, gt = k.xs, k.cs, k.hbuf, k.dhbuf, k.mx, k.gt
    qkv, pbuf, obuf = k.qkv, k.pbuf, k.obuf
    g_q = [ColumnGather(wq, i * hq, hq) for i in range(3)]
    g_o = [RowGather(wo, i * half, half, sh) for i in range(2)]
    g_i = [ColumnGather(wi, col, w) for col, w in sz.units]
    g_d = [LongRowGather(wd, i * third, third, sz.ffp) for i in range(3)]
    r_d = [LongRowReduce(gd, k.yrd.at[i], k.zrd.at[i], k.rd, i * third, third, sz.ffp) for i in range(3)]
    r_i = [
        ColumnReduce(
            gi.at[:, pl.ds(col, w)], k.yri.at[n, :, :, pl.ds(0, w)], k.zri.at[n, :, :, pl.ds(0, w)], k.ri, col, w
        )
        for n, (col, w) in enumerate(sz.units)
    ]
    r_o = [RowReduce(go, k.yro.at[i], k.zro.at[i], k.ro, i * half, half, sh) for i in range(2)]
    r_q = [ColumnReduce(gq.at[n], k.yrq.at[n], k.zrq.at[n], k.rq, n * hq, hq) for n in range(3)]
    small_in, len_in, gs_in, gr_in = (cp.recv() for _ in range(4))
    small_out, len_out, gs_out, gr_out = (cp.send() for _ in range(4))
    cp.at_end(smalls.at[pl.ds(0, NF - 1)], small_out)
    cp.at_end(lens.at[pl.ds(0, NR - 1)], len_out)
    cp.at_end(k.gsend.at[pl.ds(0, NF - 1)], gs_out)
    cp.at_end(k.greps.at[pl.ds(0, NR - 1)], gr_out)
    deal_x, deal_c = Deal(k.tok, xs), Deal(k.cot, cs)
    back_m, back_t = Back(mx, k.o_mixed), Back(gt, k.o_gtok)
    e_a, e_c, e_h, e_y = Spread(aall), Spread(call), Spread(hall), Spread(yall)
    s_1 = Sum(part_, k.sib0, k.xsend, k.xrecv0)
    s_m = Sum(k.part2, k.sib1, k.xsend2, k.xrecv1)
    s_h = Sum(part_, k.sib0, k.xsend, k.xrecv0)
    s_a = Sum(part_, k.sib0, k.xsend, k.xrecv0)
    blocks = [dn, xn, cn, r]

    lane = lax.broadcasted_iota(jnp.int32, (1, 128), 1)
    front = lax.rem(lane, 64) < 32
    low = lane < 64
    low_b = low.astype(F32).astype(BF16)
    high_b = (1.0 - low.astype(F32)).astype(BF16)
    npair = hq // 128
    scale = 64 ** (-0.5)
    tile_ = sz.tile
    NL = 32

    def live(m, t, n):
        pos = lax.broadcasted_iota(jnp.int32, (n, 1), 0) + t * n
        return pos.astype(F32) < lens[r, m : m + 1, 0:1]

    def normed(v):
        center = v - jnp.mean(v, axis=-1, keepdims=True)
        root = lax.rsqrt(jnp.mean(center * center, axis=-1, keepdims=True) + NORM_EPS)
        return center * root, root

    def norm_back(dy, gain, vhat, root):
        e = dy * gain
        return root * (e - jnp.mean(e, axis=-1, keepdims=True) - vhat * jnp.mean(e * vhat, axis=-1, keepdims=True))

    def swap(v):
        return jnp.where(front, pltpu.roll(v, 96, 1), pltpu.roll(v, 32, 1))

    def both(v):
        return jnp.concatenate([v * low_b, v * high_b], axis=0)

    def joined(v):
        return jnp.where(low, v[:slot], v[slot:])

    def fold(v):
        return jnp.sum(v.reshape(NL // 8, 8, d), axis=0)

    def triple(s, p):
        return [qkv[at(s * slot, slot), i * hq + p * 128 : i * hq + (p + 1) * 128] for i in range(3)]

    mini = k.mini
    mini[...] = jnp.zeros_like(mini)
    mini[0:1, :] = k.g1[...].astype(BF16).astype(F32)
    mini[1:2, :] = k.g2[...].astype(BF16).astype(F32)
    for m in micros:
        mini[2:3, :] += jnp.where(lane == m, k.len[0:1, m : m + 1].astype(F32), 0.0)
    smalls[f] = mini[...]
    qf, of = k.hbuf.at[pl.ds(0, sh)], k.hbuf.at[pl.ds(sh, sh)]
    q_in = [local(k.fq.at[:, at(i * d + r * hq, hq, 128)], qf.at[:, pl.ds(i * hq, hq)], lid()) for i in range(3)]
    o_lid, i_in, d_lid = lid(), [], lid()
    mine = z == r
    df = k.part2.at[pl.ds(0, sz.ffs)]

    @pl.when(mine)
    def _():
        local(k.fo, of, o_lid)

    shifts = []
    for i in range(2):
        first = i * NF * sz.ffs + r * 2 * sz.ffs
        base = lax.div(first, 128) * 128
        shifts.append(first - base)
        i_in.append(local(k.fi.at[:, at(base, sz.fq, 128)], k.dhbuf.at[pl.ds(i * sh, sh), pl.ds(0, sz.fq)], lid()))

    @pl.when(mine)
    def _():
        local(k.fd, df, d_lid)

    @task()
    def met():
        pl.semaphore_wait(barrier, len(friends))
        for o in others:
            cp.start(lambda o=o: (mini, smalls.at[f], small_out, small_in, o, r))

    @task()
    def prepare_q():
        for copy in q_in:
            copy.wait()

        def cast_q(t):
            wq[at(f * sh + t * 32, 32), :] = qf[at(t * 32, 32), pl.ds(0, 3 * hq)].astype(BF16)

        loop(sh // 32, cast_q)

    @task()
    def prepare_o():
        @pl.when(mine)
        def _():
            pltpu.make_async_copy(k.fo, of, k.locals.at[o_lid]).wait()

            def cast_o(t):
                wo[at(y * sh + t * 32, 32), :] = of[at(t * 32, 32), :].astype(BF16)

            loop(sh // 32, cast_o)

    @task()
    def prepare_i():
        for i in range(2):
            i_in[i].wait()
        lane_f = lax.broadcasted_iota(jnp.int32, (1, sz.fq), 1)
        first = lane_f < sz.ffs
        second = jnp.logical_and(lane_f >= sz.ffp, lane_f < sz.ffp + sz.ffs)

        def cast_i(t):
            halves = []
            for i in range(2):
                v = k.dhbuf[at(i * sh + t * 32, 32), pl.ds(0, sz.fq)]
                v = pltpu.roll(v, lax.rem(sz.fq - shifts[i], sz.fq), 1)
                halves.append(jnp.where(first, v, jnp.where(second, pltpu.roll(v, sz.ffp - sz.ffs, 1), 0.0)))
            for n, (col, w) in enumerate(sz.units):
                one, two = [v[:, n * tile_ : (n + 1) * tile_] for v in halves]
                wi[at(f * sh + t * 32, 32), pl.ds(col, w)] = side_by_side(sz, n, one, two).astype(BF16)

        loop(sh // 32, cast_i)

    @task()
    def prepare_d():
        @pl.when(mine)
        def _():
            pltpu.make_async_copy(k.fd, df, k.locals.at[d_lid]).wait()

            def cast_d(t):
                wd[at(y * sz.ffp + t * 16, 16), :] = df[at(t * 16, 16), :].astype(BF16)

            loop(sz.ffs // 16, cast_d)
            left = sz.ffs % 16
            if left:
                v = df[pl.ds(sz.ffs - left, left), :]
                v = jnp.concatenate([v, jnp.zeros((sz.ffp - sz.ffs, d), F32)], axis=0)
                wd[at(y * sz.ffp + sz.ffp - 16, 16), :] = v.astype(BF16)

    for u in g_q:
        u.register(met, prepare_q)
    for u in g_o:
        u.register(met, prepare_o)
    for u in g_i:
        u.register(met, prepare_i)
    for u in g_d:
        u.register(met, prepare_d)
    q_needs, o_needs, i_needs, d_needs = [[n for u in g for n in u.needs] for g in (g_q, g_o, g_i, g_d)]

    @task()
    def zero():
        wd[pl.ds(2 * sz.ffp, sz.fq - 2 * sz.ffp), :] = jnp.zeros((sz.fq - 2 * sz.ffp, d), BF16)
        dg[...] = jnp.zeros_like(dg)

    deals = [task(met)(lambda m=m: deal_x.start(m)) for m in micros]

    @task(met)
    def small():
        cp.arrived(smalls.at[pl.ds(0, NF - 1)], small_in, f, r)
        for j in range(NF):
            gains[0:2, j * sh : (j + 1) * sh] = smalls[j, 0:2, :]
        sub = lax.broadcasted_iota(jnp.int32, (NF, 128), 0)
        row8 = lax.broadcasted_iota(jnp.int32, (8, 128), 0)
        lane8 = lax.broadcasted_iota(jnp.int32, (1, NF), 1)
        len_tab = smalls[:, 2, :]
        table = jnp.zeros((8, 128), F32)
        for m in micros:
            dealt = jnp.where(lane8 == f, k.deal[m : m + 1, :].astype(F32), 0.0)
            dealt = jnp.sum(dealt, axis=1, keepdims=True)
            col = jnp.sum(jnp.where(sub.astype(F32) == dealt, len_tab, 0.0), axis=0, keepdims=True)
            length = jnp.sum(jnp.where(lane == m, col, 0.0), axis=1, keepdims=True)
            table = jnp.where(row8 == m, length, table)
        lens[r] = table
        for to in (xn, dn, cn):
            cp.start(lambda to=to: (lens.at[r], lens.at[r], len_out, len_in, f, to))

    @task(small)
    def lengths():
        cp.arrived(lens.at[pl.ds(0, NR - 1)], len_in, f, r)

    norm1s = []
    for m in micros:

        @task(small, deals[m])
        def step(m=m):
            deal_x.done(m)

            def norm1(t):
                vhat, _ = normed(xs[at(m * slot + t * NL, NL), :].astype(F32))
                aall[at(r * rows + m * slot + t * NL, NL), :] = (vhat * gains[0:1, :]).astype(BF16)

            loop(slot // NL, norm1)
            e_a.start(m)

        norm1s.append(step)
    e_a.register(norm1s)

    def project(b):
        a = aall[block(b), :]
        for i in range(3):
            t = nn(a, wq[:, i * hq : (i + 1) * hq])
            for p in range(npair):
                v = t[:, p * 128 : (p + 1) * 128]
                for m in micros:
                    u = v[m * slot : (m + 1) * slot]
                    if i < 2:
                        u = u * k.cos[...] + swap(u) * k.sin[...]
                    qkv[at(b * rows + m * slot, slot), i * hq + p * 128 : i * hq + (p + 1) * 128] = u.astype(BF16)

    def attend(b):
        def attend_one(m):
            s = b * micro + m
            length = lens[b, pl.ds(m, 1), :]
            for p in range(npair):
                q_, k_, v_ = triple(s, p)
                scores = nt(both(q_), k_) * scale
                scores = jnp.where(lane.astype(F32) < length, scores, -1e30)
                e = jnp.exp(scores - jnp.max(scores, axis=-1, keepdims=True))
                prob = e / jnp.sum(e, axis=-1, keepdims=True)
                pbuf[s, p] = prob
                out = nn(prob.astype(BF16), v_)
                obuf[at(s * slot, slot), p * 128 : (p + 1) * 128] = joined(out).astype(BF16)

        loop(micro, attend_one)

    def branch_one(b):
        def branch_tile(n):
            cols = at(n * 256, 256, 128)
            part_[block(b), cols] = nn(obuf[block(b), :], wo[:, cols])

        loop(d // 256, branch_tile)

    firsts = []
    for w in range(NR):

        @task(*e_a.need[w], *q_needs)
        def projected(w=w):
            project(blocks[w])

        @task(projected, lengths, *o_needs)
        def attended(w=w):
            attend(blocks[w])
            branch_one(blocks[w])
            s_1.ready(w)

        firsts.append(attended)
    crossed = task(firsts[DN], firsts[XN])(s_1.over_x)

    masks = []
    for m in micros:
        dealt = task(met)(lambda m=m: deal_c.start(m))

        @task(dealt, small)
        def step(m=m):
            deal_c.done(m)

            def mask_c(t):
                s = at(m * slot + t * NL, NL)
                masked = jnp.where(live(m, t, NL), cs[s, :].astype(F32), 0.0)
                call[at(r * rows + m * slot + t * NL, NL), :] = masked.astype(BF16)

            loop(slot // NL, mask_c)

        masks.append(step)

    @task(*masks)
    def spread_c():
        for m in micros:
            e_c.start(m)

    e_c.register([spread_c])

    norm2s = []
    for m in micros:

        @task(crossed, *firsts, *norm2s)
        def step(m=m):
            s_1.done(m)

            def norm2(t):
                row = m * slot + t * NL
                s = at(row, NL)
                h = xs[s, :].astype(F32) + jnp.where(live(m, t, NL), s_1.value(row, NL), 0.0)
                hbuf[s, :] = h
                vhat, _ = normed(h)
                hall[at(r * rows + row, NL), :] = (vhat * gains[1:2, :]).astype(BF16)

            loop(slot // NL, norm2)
            e_h.start(m)

        norm2s.append(step)
    freed = task(*norm2s)(s_1.free)
    e_h.register(norm2s)

    feeds = []
    for w in range(NR):

        @task(freed, *e_h.need[w], *i_needs)
        def step(w=w):
            rs = block(blocks[w])

            def feed(n):
                col, w = sz.units[n]
                w1, w2 = apart(sz, n, nn(hall[rs, :], wi[:, pl.ds(col, w)]))
                cdf = 0.5 * (1.0 + lax.erf(w1 * (0.5**0.5)))
                act = w1 * cdf
                pdf = jnp.exp(-0.5 * w1 * w1) * 0.3989422804014327
                cols = pl.ds(n * tile_, tile_)
                gg[rs, cols] = (act * w2).astype(BF16)
                part_[rs, cols] = act
                slope[rs, cols] = w2 * (cdf + w1 * pdf)

            for n in range(sz.ntile):
                once(n, feed)

        feeds.append(step)

    @task(*feeds, *e_c.all)
    def gdown():
        def grad_down(i):
            m, n = lax.div(i, 2), lax.rem(i, 2)
            cols = at(n * (d // 2), d // 2, 128)
            gd[at(m * 256, 256), cols] = tn(gg[:, at(m * 256, 256, 128)], call[:, cols]).astype(BF16)

        loop(sz.fq // 256 * 2, grad_down)
        for u in r_d:
            u.send()

    hids = []
    for w in range(NR):

        @task(feeds[w], zero, *e_c.need[w], *d_needs)
        def step(w=w):
            rs = block(blocks[w])

            def hidden(n):
                cols = pl.ds(n * tile_, tile_)
                dgg = nt(call[rs, :], wd[pl.ds(n * tile_, tile_), :])
                v = side_by_side(sz, n, dgg * slope[rs, cols], dgg * part_[rs, cols])
                dw[rs, pl.ds(*sz.units[n])] = v.astype(BF16)

            for n in range(sz.ntile):
                once(n, hidden)

        hids.append(step)

    gins = []
    for n in range(sz.ntile):
        for which in range(2):

            @task(*hids, *e_h.all)
            def step(n=n, which=which):
                def grad_in(i):
                    j = 2 * i + (y if which else 1 - y)
                    cols = pl.ds(*sz.units[n])
                    gi[at(j * sh, sh), cols] = tn(hall[:, at(j * sh, sh, 128)], dw[:, cols]).astype(BF16)

                loop(NZ, grad_in)
                if not which:
                    for owner in order_z:
                        r_i[n].send(2 * owner + 1 - y)

            gins.append(step)

    dhns = []
    for w in range(NR):

        @task(hids[w])
        def step(w=w):
            b = blocks[w]

            def dhn_tile(n):
                part_[block(b), at(n * 256, 256, 128)] = nt(dw[block(b), :], wi[at(n * 256, 256), :])

            loop(d // 256, dhn_tile)
            s_h.ready(w)

        dhns.append(step)
    crossed = task(dhns[DN], dhns[XN])(s_h.over_x)
    back2s = []
    for m in micros:

        @task(crossed, zero, *dhns, *back2s)
        def step(m=m):
            s_h.done(m)

            def back2(t):
                row = m * slot + t * NL
                s = at(row, NL)
                dy = s_h.value(row, NL)
                vhat, root = normed(hbuf[s, :])
                dg[1] += fold(dy * vhat)
                dh = cs[s, :].astype(F32) + norm_back(dy, gains[1:2, :], vhat, root)
                dhbuf[s, :] = dh
                yall[at(r * rows + row, NL), :] = jnp.where(live(m, t, NL), dh, 0.0).astype(BF16)

            loop(slot // NL, back2)
            e_y.start(m)

        back2s.append(step)
    freed = task(*back2s)(s_h.free)
    e_y.register(back2s)

    mixes = []
    for w in range(NR):

        @task(zero, feeds[w], *d_needs)
        def step(w=w):
            b = blocks[w]

            def mix_tile(n):
                cols = at(n * 256, 256, 128)
                k.part2[block(b), cols] = nn(gg[block(b), :], wd[:, cols])

            loop(d // 256, mix_tile)
            s_m.ready(w)

        mixes.append(step)
    crossed = task(mixes[DN], mixes[XN])(s_m.over_x)
    mixeds = []
    for m in micros:

        @task(crossed, *mixes, *mixeds)
        def step(m=m):
            s_m.done(m)

            def mix(t):
                row = m * slot + t * NL
                s = at(row, NL)
                mx[s, :] = (hbuf[s, :] + jnp.where(live(m, t, NL), s_m.value(row, NL), 0.0)).astype(BF16)

            loop(slot // NL, mix)

        mixeds.append(step)
        task(step)(lambda m=m: back_m.start(m))

    @task(*firsts, *e_y.all)
    def gout():
        def grad_out(i):
            cols = at(i * 256, 256, 128)
            go[:, cols] = tn(obuf[...], yall[:, cols]).astype(BF16)

        loop(d // 256, grad_out)

    abacks = []
    for w in range(NR):

        @task(firsts[w], *e_y.need[w])
        def step(w=w):
            def attend_back(m):
                s = blocks[w] * micro + m
                do_all = nt(yall[at(s * slot, slot), :], wo[...]).astype(BF16)
                for p in range(npair):
                    q_, k_, v_ = triple(s, p)
                    q2, do2 = both(q_), both(do_all[:, p * 128 : (p + 1) * 128])
                    prob = pbuf[s, p]
                    dp = nt(do2, v_)
                    ds = (prob * (dp - jnp.sum(dp * prob, axis=-1, keepdims=True))).astype(BF16)
                    dq = joined(nn(ds, k_)) * scale
                    dk = tn(ds, q2) * scale
                    dv = tn(prob.astype(BF16), do2)
                    cosine, sine = k.cos[...], k.sin[...]
                    dq = dq * cosine - swap(dq) * sine
                    dk = dk * cosine - swap(dk) * sine
                    for i, v in enumerate((dq, dk, dv)):
                        dqkv[at(s * slot, slot), i * hq + p * 128 : i * hq + (p + 1) * 128] = v.astype(BF16)

            loop(micro, attend_back)

        abacks.append(step)

    gqkvs = []
    for which in range(2):

        @task(*abacks, *e_a.all)
        def step(which=which):
            def grad_qkv(i):
                j = 2 * i + (y if which else 1 - y)
                g = tn(aall[:, at(j * sh, sh, 128)], dqkv[...]).astype(BF16)
                for n in range(3):
                    gq[n, at(j * sh, sh), :] = g[:, n * hq : (n + 1) * hq]

            loop(NZ, grad_qkv)
            if not which:
                for n in range(3):
                    for owner in order_z:
                        r_q[n].send(2 * owner + 1 - y)

        gqkvs.append(step)

    das = []
    for w in range(NR):

        @task(abacks[w], freed)
        def step(w=w):
            b = blocks[w]

            def da_tile(n):
                part_[block(b), at(n * 256, 256, 128)] = nt(dqkv[block(b), :], wq[at(n * 256, 256), :])

            loop(d // 256, da_tile)
            s_a.ready(w)

        das.append(step)
    crossed = task(das[DN], das[XN])(s_a.over_x)
    back1s = []
    for m in micros:

        @task(crossed, *das, *back1s)
        def step(m=m):
            s_a.done(m)

            def back1(t):
                row = m * slot + t * NL
                s = at(row, NL)
                dy = s_a.value(row, NL)
                vhat, root = normed(xs[s, :].astype(F32))
                dg[0] += fold(dy * vhat)
                gt[s, :] = (dhbuf[s, :] + norm_back(dy, gains[0:1, :], vhat, root)).astype(BF16)

            loop(slot // NL, back1)
            back_t.start(m)

        back1s.append(step)

    gsend, gslots, greps, gout_ = k.gsend, k.gslots, k.greps, k.gout

    @task(*back1s, *back2s)
    def gain_parts():
        for which in range(2):
            total = jnp.sum(dg[which], axis=0, keepdims=True)
            for j in range(NF):
                gsend[j, which : which + 1, :] = total[:, j * sh : (j + 1) * sh]
        for o in others:
            cp.start(lambda o=o: (gsend.at[o], gslots.at[f], gs_out, gs_in, o, r))
        gslots[f] = gsend[f]

    @task(gain_parts)
    def gain_sums():
        cp.arrived(gslots.at[pl.ds(0, NF - 1)], gs_in, f, r)
        total = gslots[0]
        for j in range(1, NF):
            total = total + gslots[j]
        greps[r] = total
        for to in (xn, dn, cn):
            cp.start(lambda to=to: (greps.at[r], greps.at[r], gr_out, gr_in, f, to))

    glid = lid()

    @task(gain_sums)
    def gain_totals():
        cp.arrived(greps.at[pl.ds(0, NR - 1)], gr_in, f, r)
        gout_[...] = greps[0] + greps[1] + greps[2] + greps[3]
        ends.append(local(gout_, k.o_small, glid))

    for u in r_d:
        u.register(gdown)
    for n, u in enumerate(r_i):
        u.register(*gins[2 * n : 2 * n + 2])
    for u in r_o:
        u.register(gout)
    for u in r_q:
        u.register(*gqkvs)

    @task(*range(len(tasks)))
    def end():
        for u in r_d + r_i + r_o + r_q + [back_m, back_t]:
            u.done()
        s_a.free()
        s_m.free()
        for e in (e_a, e_c, e_h, e_y):
            e.free()
        for ref, send, cond in cp.left:
            cp.gone(ref, send, f, r, cond)
        for copy in ends:
            copy.wait()

    run_tasks(tasks)


def fused(sz, tok, cot, g1, g2, length, deal, cos, sin, fq, fo, fi, fd):
    d, sh, all_, rows = sz.d, sz.shard, sz.all, sz.rows
    t2 = 2 * sz.tile
    third, half = sz.ffp // 3, sh // 2
    hq3 = 3 * sz.hq
    bf = lambda *s: pltpu.VMEM(s, BF16)
    fl = lambda *s: pltpu.VMEM(s, F32)
    ins = dict(tok=tok, cot=cot, g1=g1, g2=g2, len=length, deal=deal, cos=cos, sin=sin, fq=fq, fo=fo, fi=fi, fd=fd)
    outs = dict(
        o_mixed=jax.ShapeDtypeStruct((sz.micro, NF, sz.part, d), BF16),
        o_gtok=jax.ShapeDtypeStruct((sz.micro, NF, sz.part, d), BF16),
        o_small=jax.ShapeDtypeStruct((8, 128), F32),
        rq=jax.ShapeDtypeStruct((NR, sh, hq3), BF16),
        ro=jax.ShapeDtypeStruct((sh, d), BF16),
        ri=jax.ShapeDtypeStruct((NR, sh, sz.iw), BF16),
        rd=jax.ShapeDtypeStruct((sz.ffp, d), BF16),
    )
    scratch = dict(
        wq=bf(d, hq3), wo=bf(2 * sh, d), wi=bf(d, sz.iw), wd=bf(sz.fq, d),
        xs=bf(rows, d), cs=bf(rows, d), mx=bf(rows, d), gt=bf(rows, d),
        aall=bf(all_, d), hall=bf(all_, d), call=bf(all_, d), yall=bf(all_, d),
        smalls=fl(NF, 8, 128), mini=fl(8, 128), lens=fl(NR, 8, 128), gains=fl(8, d),
        qkv=bf(all_, hq3), pbuf=fl(NR * sz.micro, sz.hq // 128, 2 * sz.slot, 128), obuf=bf(all_, sz.hq),
        part=fl(all_, d), part2=fl(all_, d), sib0=fl(2, rows, d), sib1=fl(2, rows, d),
        xsend=bf(rows, d), xsend2=bf(rows, d), xrecv0=bf(rows, d), xrecv1=bf(rows, d),
        hbuf=fl(rows, d), dhbuf=fl(rows, d), dg=fl(2, 8, d),
        gg=bf(all_, sz.fq), slope=fl(all_, sz.fq), dw=bf(all_, sz.iw), dqkv=bf(all_, hq3),
        gd=bf(sz.fq, d), gi=bf(d, sz.iw), go=bf(2 * sh, d), gq=bf(3, d, sz.hq),
        yrd=bf(3, third, d), zrd=bf(3, 2, third, d),
        yri=bf(sz.ntile, NZ, sh, t2), zri=bf(sz.ntile, NZ + 1, sh, t2),
        yro=bf(2, half, d), zro=bf(2, 2, 2, half, d),
        yrq=bf(3, NZ, sh, sz.hq), zrq=bf(3, NZ + 1, sh, sz.hq),
        gsend=fl(NF, 8, 128), gslots=fl(NF, 8, 128), greps=fl(NR, 8, 128), gout=fl(8, 128),
        sends=pltpu.SemaphoreType.DMA((90,)), recvs=pltpu.SemaphoreType.DMA((187,)),
        locals=pltpu.SemaphoreType.DMA((32,)),
    )
    any_ = pl.BlockSpec(memory_space=pl.ANY)
    vmem = pl.BlockSpec(memory_space=pltpu.VMEM)
    names = (*ins, *outs, *scratch)
    return pl.pallas_call(
        functools.partial(kernel, sz, names),
        out_shape=list(outs.values()),
        in_specs=[any_] * 2 + [vmem] * 6 + [any_] * 4,
        out_specs=[any_] * len(outs),
        scratch_shapes=list(scratch.values()),
        compiler_params=pltpu.CompilerParams(collective_id=0, has_side_effects=True, vmem_limit_bytes=64 * MIB),
    )(*ins.values())


def finish_kernel(sz, small, mixed, gtok, rq, ro, ri, rd, out_m, out_t, g1, gq, go, g2, gi, gd):
    hq, ffs, ffp = sz.hq, sz.ffs, sz.ffp
    for i in range(3):
        for q in range(NR):
            gq[:, i * sz.d + q * hq : i * sz.d + (q + 1) * hq] = rq[q, :, i * hq : (i + 1) * hq].astype(F32)
    g1[...], g2[...] = small[0:1, :], small[1:2, :]
    out_m[...], out_t[...] = mixed[...], gtok[...]
    go[...] = ro[...].astype(F32)
    gd[...] = rd[...].astype(F32)
    pieces = [[], []]
    for q in range(NR):
        tiles = [apart(sz, n, ri[q, :, col : col + w].astype(F32)) for n, (col, w) in enumerate(sz.units)]
        for i in range(2):
            v = jnp.concatenate([two[i] for two in tiles], axis=1)
            pieces[i] += [v[:, :ffs], v[:, ffp : ffp + ffs]]
    gi[...] = jnp.concatenate(pieces[0] + pieces[1], axis=1)


def finish(sz, small, mixed, gtok, rq, ro, ri, rd):
    d, sh = sz.d, sz.shard
    grain = 32
    steps, n = sh // grain, sz.ffp // 16
    down = -(-n // steps) * 16
    last = -(-sz.ffp // down) - 1
    row = lambda w: pl.BlockSpec((grain, w), lambda i: (i, 0))
    low = pl.BlockSpec((down, d), lambda i: (jnp.minimum(i, last), 0))
    rows = sz.micro * NF * sz.part // steps
    each = pl.BlockSpec((rows, d), lambda i: (i, 0))
    one = lambda n: pl.BlockSpec((n, sh), lambda i: (0, 0))
    quarters = lambda w: pl.BlockSpec((NR, grain, w), lambda i: (0, i, 0))
    return pl.pallas_call(
        functools.partial(finish_kernel, sz),
        grid=(steps,),
        out_shape=[
            jax.ShapeDtypeStruct((rows * steps, d), BF16),
            jax.ShapeDtypeStruct((rows * steps, d), BF16),
            jax.ShapeDtypeStruct((1, sh), F32),
            jax.ShapeDtypeStruct((sh, 3 * d), F32),
            jax.ShapeDtypeStruct((sh, d), F32),
            jax.ShapeDtypeStruct((1, sh), F32),
            jax.ShapeDtypeStruct((sh, 2 * NF * sz.ffs), F32),
            jax.ShapeDtypeStruct((sz.ffs, d), F32),
        ],
        in_specs=[one(8), each, each, quarters(rq.shape[2]), row(d), quarters(ri.shape[2]), low],
        out_specs=[each, each, one(1), row(3 * d), row(d), one(1), row(2 * NF * sz.ffs), low],
        compiler_params=pltpu.CompilerParams(vmem_limit_bytes=60 * MIB),
    )(small, mixed.reshape(-1, d), gtok.reshape(-1, d), rq, ro, ri, rd)


def routed(tokens, cotangent, deal, lengths, ln1_gain, w_qkv, w_out, ln2_gain, w_in, w_down):
    micro, _, part, d = tokens.shape
    ffs = w_down.shape[0]
    sz = Sizes(micro, part, d, ffs)
    half = d // HEADS // 2
    freq = np.float32(ROPE_BASE) ** (-(np.arange(half, dtype=np.float32) * np.float32(2.0 / (2 * half))))
    angles = np.arange(sz.slot, dtype=np.float32)[:, None] * freq[None, :]
    cos = jnp.asarray(np.tile(np.cos(angles), (1, 4)))
    sin = jnp.asarray(np.tile(np.concatenate([-np.sin(angles), np.sin(angles)], axis=1), (1, 2)))
    mixed, gtok, osmall, rq, ro, ri, rd = fused(
        sz, tokens, cotangent, ln1_gain[None], ln2_gain[None], lengths.reshape(1, micro), deal[:, 0],
        cos, sin, w_qkv, w_out, w_in, w_down,
    )
    mixed, gtok, g_1, g_qkv, g_out, g_2, g_in, g_down = finish(sz, osmall, mixed, gtok, rq, ro, ri, rd)
    return mixed.reshape(tokens.shape), gtok.reshape(tokens.shape), g_1[0], g_qkv, g_out, g_2[0], g_in, g_down


def solution(mesh):
    small = mesh.shape["fsdp"] == NF and mesh.shape["rep"] == NR
    rows = P(None, "rep", "fsdp", None)
    return jax.shard_map(
        routed if small else plain,
        mesh=mesh,
        in_specs=(
            rows, rows, P(None, "rep", None), P(None, "rep", "fsdp"),
            P("fsdp"), P("fsdp", None), P("fsdp", None), P("fsdp"), P("fsdp", None), P("fsdp", None),
        ),
        out_specs=(rows, rows, P("fsdp"), P("fsdp", None), P("fsdp", None), P("fsdp"), P("fsdp", None), P("fsdp", None)),
        check_vma=False,
    )
```

```python
import functools
import types

import jax
import jax.numpy as jnp
import numpy as np
from jax import lax
from jax.experimental import pallas as pl
from jax.experimental.pallas import tpu as pltpu
from jax.sharding import PartitionSpec as P

HEADS = 16
ROPE_BASE = 160000.0
NORM_EPS = 1e-05
MESH = pl.DeviceIdType.MESH
MIB = 1 << 20
BF16 = jnp.bfloat16
F32 = jnp.float32


def rope_tables(slot_count, head_size):
    half_size = head_size // 2
    frequency = ROPE_BASE ** (-(jnp.arange(half_size, dtype=F32) * 2.0 / head_size))
    angles = jnp.arange(slot_count, dtype=F32)[:, None] * frequency[None, :]
    return jnp.cos(angles), jnp.sin(angles)


def rotate(values, cosine, sine):
    front, back = jnp.split(values, 2, axis=-1)
    cosine, sine = cosine[:, None, :], sine[:, None, :]
    return jnp.concatenate([front * cosine - back * sine, back * cosine + front * sine], axis=-1)


def normed(values, gain):
    center = values - jnp.mean(values, axis=-1, keepdims=True)
    root = lax.rsqrt(jnp.mean(center * center, axis=-1, keepdims=True) + NORM_EPS)
    vhat = center * root
    return vhat * gain, vhat, root


def norm_back(dy, gain, vhat, root):
    dgain = jnp.sum(dy * vhat, axis=tuple(range(dy.ndim - 1)))
    e = dy * gain
    dz = root * (
        e
        - jnp.mean(e, axis=-1, keepdims=True)
        - vhat * jnp.mean(e * vhat, axis=-1, keepdims=True)
    )
    return dgain, dz


def mm(spec, a, b):
    return jnp.einsum(spec, a, b, preferred_element_type=F32)


def layer(g1, wqkv, wo, g2, win, wdown, tokens, dout, live):
    m, slot, d = tokens.shape
    heads, size = HEADS, d // HEADS
    scale = size ** (-0.5)
    w1, w2 = win
    lv = live[:, :, None]
    x = tokens.astype(F32)
    y, vhat1, root1 = normed(x, g1)
    a = y.astype(BF16)
    qkv = mm("mtd,de->mte", a, wqkv).reshape(m, slot, 3, heads, size)
    cosine, sine = rope_tables(slot, size)
    q = rotate(qkv[:, :, 0], cosine, sine).astype(BF16)
    k = rotate(qkv[:, :, 1], cosine, sine).astype(BF16)
    v = qkv[:, :, 2].astype(BF16)
    s = mm("mqhd,mkhd->mhqk", q, k) * scale
    s = jnp.where(live[:, None, None, :] > 0, s, -1e30)
    p = jax.nn.softmax(s, axis=-1)
    pb = p.astype(BF16)
    o = mm("mhqk,mkhd->mqhd", pb, v).astype(BF16).reshape(m, slot, d)
    h = x + lv * mm("mte,ed->mtd", o, wo)
    y, vhat2, root2 = normed(h, g2)
    hn = y.astype(BF16)
    z1 = mm("mtd,df->mtf", hn, w1)
    z2 = mm("mtd,df->mtf", hn, w2)
    cdf = 0.5 * (1.0 + lax.erf(z1 * (0.5**0.5)))
    pdf = jnp.exp(-0.5 * z1 * z1) * 0.3989422804014327
    act = z1 * cdf
    gg = (act * z2).astype(BF16)
    mixed = (h + lv * mm("mtf,fd->mtd", gg, wdown)).astype(BF16)

    up = dout.astype(F32)
    dy2 = (lv * up).astype(BF16)
    g_down = mm("mtf,mtd->fd", gg, dy2)
    dgg = mm("mtd,fd->mtf", dy2, wdown)
    dw1 = (dgg * z2 * (cdf + z1 * pdf)).astype(BF16)
    dw2 = (dgg * act).astype(BF16)
    g_in = (mm("mtd,mtf->df", hn, dw1), mm("mtd,mtf->df", hn, dw2))
    dhn = mm("mtf,df->mtd", dw1, w1) + mm("mtf,df->mtd", dw2, w2)
    g_g2, dhv = norm_back(dhn, g2, vhat2, root2)
    dh = up + dhv
    dy1 = (lv * dh).astype(BF16)
    g_out = mm("mte,mtd->ed", o, dy1)
    do = mm("mtd,ed->mte", dy1, wo).astype(BF16).reshape(m, slot, heads, size)
    dp = mm("mqhd,mkhd->mhqk", do, v)
    ds = (p * (dp - jnp.sum(dp * p, axis=-1, keepdims=True))).astype(BF16)
    dq = mm("mhqk,mkhd->mqhd", ds, k) * scale
    dk = mm("mhqk,mqhd->mkhd", ds, q) * scale
    dv = mm("mhqk,mqhd->mkhd", pb, do)
    dqkv = jnp.stack([rotate(dq, cosine, -sine), rotate(dk, cosine, -sine), dv], axis=2)
    dqkv = dqkv.reshape(m, slot, 3 * d).astype(BF16)
    g_qkv = mm("mtd,mte->de", a, dqkv)
    da = mm("mte,de->mtd", dqkv, wqkv)
    g_g1, dxv = norm_back(da, g1, vhat1, root1)
    gtok = (dh + dxv).astype(BF16)
    return mixed, gtok, (g_g1, g_qkv, g_out, g_g2, g_in, g_down)


def plain(tokens, cotangent, deal, lengths, ln1_gain, w_qkv, w_out, ln2_gain, w_in, w_down):
    slot = tokens.shape[2] * lax.axis_size("fsdp")
    me = lax.axis_index("fsdp")

    def spread(rows):
        return lax.all_to_all(rows, "fsdp", split_axis=1, concat_axis=2, tiled=True)[:, 0]

    def back(rows):
        return lax.all_to_all(rows[:, None], "fsdp", split_axis=2, concat_axis=1, tiled=True)

    def whole(shard):
        return lax.all_gather(shard.astype(BF16), "fsdp", axis=0, tiled=True)

    table = lax.all_gather(lengths[:, 0], "fsdp", axis=1, tiled=True)
    mine = lax.dynamic_slice_in_dim(deal[:, 0], me, 1, axis=1)
    pick = jnp.arange(table.shape[1], dtype=jnp.int32)[None, :] == mine
    length = jnp.sum(jnp.where(pick, table, 0), axis=1, keepdims=True)
    live = (jnp.arange(slot, dtype=jnp.int32)[None, :] < length).astype(F32)
    win = jnp.split(whole(w_in), 2, axis=1)
    mixed, gtok, grads = layer(
        whole(ln1_gain).astype(F32), whole(w_qkv), whole(w_out), whole(ln2_gain).astype(F32), win, whole(w_down),
        spread(tokens), spread(cotangent), live,
    )
    g_g1, g_qkv, g_out, g_g2, g_in, g_down = grads

    def owned(part):
        part = lax.psum_scatter(part, "fsdp", scatter_dimension=0, tiled=True)
        return lax.psum(part, "rep")

    g_in = jnp.concatenate(g_in, axis=1)
    return (back(mixed), back(gtok)) + tuple(owned(g) for g in (g_g1, g_qkv, g_out, g_g2, g_in, g_down))


NF, NR, NZ = 8, 4, 4
DN, XN, CN = 0, 1, 2


def at(offset, size, unit=16):
    return pl.ds(pl.multiple_of(offset, unit), size)


def nn(a, b):
    return lax.dot_general(a, b, (((1,), (0,)), ((), ())), preferred_element_type=F32)


def nt(a, b):
    return lax.dot_general(a, b, (((1,), (1,)), ((), ())), preferred_element_type=F32)


def tn(a, b):
    return lax.dot_general(a, b, (((0,), (0,)), ((), ())), preferred_element_type=F32)


def once(i, body):
    body(i)


def loop(n, body):
    def step(i, carry):
        body(i)
        return carry

    lax.fori_loop(0, n, step, 0)


ORDER = (
    1, 0, 15, 2, 24, 3, 10, 5, 52, 16, 54, 20, 28, 17, 53, 72, 55, 56, 12, 58, 11, 18, 6, 7, 57, 60, 74, 30, 13, 8,
    25, 59, 26, 22, 21, 27, 73, 75, 76, 4, 33, 19, 23, 29, 38, 62, 14, 9, 63, 64, 34, 79, 39, 69, 65, 35, 66, 31,
    71, 46, 49, 61, 67, 68, 40, 36, 70, 78, 77, 41, 81, 47, 82, 43, 32, 83, 50, 42, 37, 91, 86, 90, 84, 80, 44, 85,
    87, 88, 48, 89, 92, 51, 45, 93, 103, 94, 104, 141, 96, 107, 95, 105, 144, 106, 97, 115, 147, 108, 98, 150, 109,
    99, 151, 128, 111, 100, 152, 110, 113, 116, 112, 155, 101, 102, 114, 124, 165, 171, 125, 127, 145, 166, 126,
    160, 119, 129, 161, 133, 170, 167, 142, 156, 146, 117, 162, 134, 131, 153, 148, 130, 175, 118, 176, 120, 122,
    123, 180, 132, 135, 185, 181, 157, 186, 177, 136, 158, 143, 182, 172, 178, 187, 137, 138, 163, 183, 188, 173,
    168, 184, 179, 164, 154, 121, 139, 169, 189, 149, 140, 159, 174, 190,
)


def run_tasks(tasks):
    done = set()
    for i in ORDER or range(len(tasks)):
        deps, fn = tasks[i]
        assert done.issuperset(deps)
        fn()
        done.add(i)
    assert len(done) == len(tasks)


SOURCES = ((1, 0, 3, 2), (2, 2, 1, 1), (3, 3, 0, 0))
SOURCE_BELOW = ((0, 1, 0, 1), (0, 0, 1, 1), (0, 0, 1, 1))
OWNERS = ((3, 3, 0, 0), (2, 2, 1, 1), (1, 0, 3, 2))
OWNER_ABOVE = ((1, 1, 0, 0), (1, 1, 0, 0), (1, 0, 1, 0))
OWNER_SLOT = ((3, 3, 0, 0), (2, 2, 4, 1), (1, 4, 3, 4))


class Sizes:
    def __init__(self, micro, part, d, ffs):
        self.micro, self.part, self.d, self.ffs = micro, part, d, ffs
        self.slot = part * NF
        self.rows = micro * self.slot
        self.all = NR * self.rows
        self.shard = d // NF
        self.hq = d // NR
        self.ffp = -(-ffs // 16) * 16
        self.tile = 256
        self.ntile = -(-(2 * self.ffp) // self.tile)
        self.fq = self.ntile * self.tile
        last = 2 * self.ffp - (self.ntile - 1) * self.tile
        self.shift = -(-last // 64) * 64 if last <= self.tile - 64 else self.tile
        self.units = [(n * 2 * self.tile, 2 * self.tile) for n in range(self.ntile - 1)]
        self.units.append(((self.ntile - 1) * 2 * self.tile, 2 * self.shift))
        self.iw = sum(w for _, w in self.units)


def side_by_side(sz, n, one, two):
    if sz.units[n][1] == 2 * sz.tile:
        return jnp.concatenate([one, two], axis=1)
    room = jnp.zeros((one.shape[0], sz.units[n][1] - sz.tile), F32)
    return jnp.concatenate([one, room], axis=1) + pltpu.roll(jnp.concatenate([two, room], axis=1), sz.shift, 1)


def apart(sz, n, v):
    if sz.units[n][1] == 2 * sz.tile:
        return v[:, : sz.tile], v[:, sz.tile :]
    return v[:, : sz.tile], pltpu.roll(v, v.shape[1] - sz.shift, 1)[:, : sz.tile]


class Copies:
    def __init__(self, sends, recvs):
        self.sends, self.recvs, self.nsend, self.nrecv = sends, recvs, 0, 0
        self.left = []

    def send(self, n=1):
        base, self.nsend = self.nsend, self.nsend + n
        assert self.nsend <= self.sends.shape[0]
        return base

    def recv(self, n=1):
        base, self.nrecv = self.nrecv, self.nrecv + n
        assert self.nrecv <= self.recvs.shape[0]
        return base

    def make(self, src, dst, send, recv, f, r):
        return pltpu.make_async_remote_copy(
            src_ref=src, dst_ref=dst, send_sem=self.sends.at[send], recv_sem=self.recvs.at[recv],
            device_id={"fsdp": f, "rep": r}, device_id_type=MESH,
        )

    def start(self, build, cond=None):
        def go():
            self.make(*build()).start()

        go() if cond is None else pl.when(cond)(go)

    def arrived(self, ref, recv, f, r):
        self.make(ref, ref, 0, recv, f, r).wait_recv()

    def gone(self, ref, send, f, r, cond=None):
        def go():
            self.make(ref, ref, send, 0, f, r).wait_send()

        go() if cond is None else pl.when(cond)(go)

    def at_end(self, ref, send, cond=None):
        self.left.append((ref, send, cond))


def kernel(sz, names, *refs):
    k = types.SimpleNamespace(**dict(zip(names, refs)))
    d, rows, slot, micro, part = sz.d, sz.rows, sz.slot, sz.micro, sz.part
    f, r = lax.axis_index("fsdp"), lax.axis_index("rep")
    z, y = lax.div(f, 2), lax.rem(f, 2)
    c = lax.rem(r, 2)
    yn = f + 1 - 2 * y
    cn = r + 1 - 2 * c
    xn = lax.rem(r + 2, 4)
    dn = lax.rem(cn + 2, 4)
    others = [lax.rem(f + i, NF) for i in range(1, NF)]
    cp = Copies(k.sends, k.recvs)

    def local(src, dst, i):
        copy = pltpu.make_async_copy(src, dst, k.locals.at[i])
        copy.start()
        return copy

    def block(i):
        return at(i * rows, rows)

    barrier = pltpu.get_barrier_semaphore()
    friends = [(o, r) for o in others] + [(f, o) for o in (cn, xn, dn)]
    for ff, rr in friends:
        pl.semaphore_signal(barrier, inc=1, device_id={"fsdp": ff, "rep": rr}, device_id_type=MESH)

    tasks = []

    def task(*deps):
        def register(fn):
            tasks.append((deps, fn))
            return len(tasks) - 1

        return register

    wq, wo, wi, wd = k.wq, k.wo, k.wi, k.wd
    sh = sz.shard
    micros = range(micro)
    ends = []

    eights = (1 + 7 * lax.rem(z, 2)) * (1 + 63 * lax.div(z, 2))

    def by_z(*values):
        code = sum(v << (3 * i) for i, v in enumerate(values))
        return lax.rem(lax.div(jnp.int32(code), eights), 8)

    inner = jnp.logical_and(z > 0, z < NZ - 1)
    order_z = [by_z(*o) for o in OWNERS] + [z]

    class ColumnGather:
        def __init__(self, whole, col, width):
            self.whole, self.cols = whole, at(col, width, 128)
            self.zrecv, self.yrecv, self.zsend, self.ysend = cp.recv(NZ), cp.recv(), cp.send(), cp.send()
            cp.at_end(self.shards(NZ), self.ysend)
            cp.at_end(self.shards(NZ + 1), self.zsend, inner)
            cp.at_end(self.shards(1), self.zsend, jnp.logical_not(inner))

        def shards(self, n):
            return self.whole.at[pl.ds(0, n * sh), self.cols]

        def dst(self, j):
            return self.whole.at[at(j * sh, sh), self.cols]

        def over(self, j):
            dst = self.dst(j)
            cp.start(lambda: (dst, dst, self.ysend, self.yrecv, yn, r))

        def start(self):
            src = self.dst(f)
            cp.start(lambda: (src, src, self.zsend, self.zrecv + z, f + 2, r), z < NZ - 1)
            cp.start(lambda: (src, src, self.zsend, self.zrecv + z, f - 2, r), z > 0)
            self.over(f)

        def along_z(self, i):
            source, up = by_z(*SOURCES[i]), by_z(*SOURCE_BELOW[i])
            j = 2 * source + y
            dst = self.dst(j)
            cp.arrived(dst, self.zrecv + source, f, r)
            cp.start(lambda: (dst, dst, self.zsend, self.zrecv + source, f + 2 * (2 * up - 1), r), inner)
            self.over(j)

        def over_y(self):
            cp.arrived(self.shards(NZ), self.yrecv, f, r)

        def register(self, *deps):
            start = task(*deps)(self.start)
            steps = [task(start)(lambda i=i: self.along_z(i)) for i in range(NZ - 1)]
            self.needs = [start, *steps, task(start)(self.over_y)]

    class LongRowGather:
        def __init__(self, whole, row, height, pitch):
            self.whole, self.row, self.height, self.pitch = whole, row, height, pitch
            self.recv, self.send = cp.recv(2), cp.send(3)
            for n, cond in ((0, z < NZ - 1), (1, z > 0)):
                cp.at_end(self.dst(y), self.send + n, jnp.logical_and((z >= r) if n == 0 else (z <= r), cond))
            cp.at_end(self.dst(y), self.send + 2)

        def dst(self, yy):
            return self.whole.at[at(yy * self.pitch + self.row, self.height)]

        def onward(self):
            dst = self.dst(y)
            up = jnp.logical_and(z >= r, z < NZ - 1)
            down = jnp.logical_and(z <= r, z > 0)
            cp.start(lambda: (dst, dst, self.send, self.recv + y, f + 2, r), up)
            cp.start(lambda: (dst, dst, self.send + 1, self.recv + y, f - 2, r), down)
            cp.start(lambda: (dst, dst, self.send + 2, self.recv + y, yn, r))

        def start(self):
            @pl.when(z == r)
            def _():
                self.onward()

        def pass_on(self):
            @pl.when(z != r)
            def _():
                cp.arrived(self.dst(y), self.recv + y, f, r)
                self.onward()

        def rest(self):
            cp.arrived(self.dst(1 - y), self.recv + 1 - y, f, r)

        def register(self, *deps):
            start = task(*deps)(self.start)
            self.needs = [start, task(start)(self.pass_on), task(start)(self.rest)]

    class RowGather:
        def __init__(self, whole, row, height, pitch):
            self.whole, self.row, self.height, self.pitch = whole, row, height, pitch
            self.recv, self.send = cp.recv(2), cp.send(5)
            for yy, send in ((y, self.send), (1 - y, self.send + 2)):
                cp.at_end(self.dst(yy), send, self.up)
                cp.at_end(self.dst(yy), send + 1, self.down)
            cp.at_end(self.dst(y), self.send + 4, z == r)

        up = jnp.logical_and(z >= r, z < NZ - 1)
        down = jnp.logical_and(z <= r, z > 0)

        def dst(self, yy):
            return self.whole.at[at(yy * self.pitch + self.row, self.height)]

        def onward(self, yy, send):
            dst = self.dst(yy)
            cp.start(lambda: (dst, dst, send, self.recv + yy, f + 2, r), self.up)
            cp.start(lambda: (dst, dst, send + 1, self.recv + yy, f - 2, r), self.down)

        def start(self):
            dst = self.dst(y)
            cp.start(lambda: (dst, dst, self.send + 4, self.recv + y, yn, r), z == r)

        last = jnp.logical_and(z != r, jnp.logical_or(z == 0, z == NZ - 1))

        def pass_on(self, near):
            yy, send = (y, self.send) if near else (1 - y, self.send + 2)
            waits = jnp.logical_not(self.last)

            @pl.when(jnp.logical_and(waits, z != r) if near else waits)
            def _():
                cp.arrived(self.dst(yy), self.recv + yy, f, r)

            self.onward(yy, send)

        def rest(self):
            @pl.when(self.last)
            def _():
                for yy in (y, 1 - y):
                    cp.arrived(self.dst(yy), self.recv + yy, f, r)

        def register(self, *deps):
            start = task(*deps)(self.start)
            self.needs = [task(start)(lambda near=near: self.pass_on(near)) for near in (1, 0)]
            self.needs += [start, task(start)(self.rest)]

    class Spread:
        def __init__(self, buf):
            self.buf = buf
            self.ids, self.out = [cp.recv(3) for _ in micros], cp.send()

        def ref(self, b, m):
            return self.buf.at[at(b * rows + m * slot, slot)]

        def start(self, m):
            own, n = self.ref(r, m), self.ids[m]
            cp.start(lambda: (own, own, self.out, n + 1, f, xn))
            cp.start(lambda: (own, own, self.out, n, f, cn))

        def forward(self, m):
            got, n = self.ref(xn, m), self.ids[m]
            cp.arrived(got, n + 1, f, r)
            cp.start(lambda: (got, got, self.out, n + 2, f, cn))

        def got(self, b):
            for m in micros:
                if b is cn:
                    cp.arrived(self.ref(cn, m), self.ids[m], f, r)
                elif b is dn:
                    cp.arrived(self.ref(dn, m), self.ids[m] + 2, f, r)

        def register(self, deps):
            forward = [task(*deps)(lambda m=m: self.forward(m)) for m in micros]
            got = [task(*deps)(lambda b=b: self.got(b)) for b in (cn, dn)]
            self.need = [[got[1]], forward, [got[0]], list(deps)]
            self.all = [*forward, *got, *deps]

        def free(self):
            cp.gone(self.buf.at[pl.ds(0, 3 * rows)], self.out, f, r)

    class Sum:
        def __init__(self, part, sib, xsend, xrecv):
            self.part, self.sib, self.xsend, self.xrecv = part, sib, xsend, xrecv
            self.ids, self.xids, self.out, self.xout = cp.recv(2), cp.recv(micro), cp.send(), cp.send()

        def ready(self, w):
            if w not in (DN, CN):
                return
            b, i = (dn, 0) if w == DN else (cn, 1)
            src = self.part.at[block(b)]
            cp.start(lambda: (src, self.sib.at[i], self.out, self.ids + i, f, cn))

        def over_x(self):
            cp.arrived(self.sib.at[0], self.ids, f, r)
            for m in micros:

                def add(t, m=m):
                    s = at(m * slot + t * 32, 32)
                    self.xsend[s, :] = (
                        self.part[at(xn * rows + m * slot + t * 32, 32), :] + self.sib[0, s, :]
                    ).astype(BF16)

                loop(slot // 32, add)
                mm = at(m * slot, slot)
                cp.start(lambda m=m, mm=mm: (self.xsend.at[mm], self.xrecv.at[mm], self.xout, self.xids + m, f, xn))

        def done(self, m):
            if m == 0:
                cp.arrived(self.sib.at[1], self.ids + 1, f, r)
            cp.arrived(self.xrecv.at[at(m * slot, slot)], self.xids + m, f, r)

        def value(self, row, n):
            s = at(row, n)
            return self.part[at(r * rows + row, n), :] + self.sib[1, s, :] + self.xrecv[s, :].astype(F32)

        def free(self):
            cp.gone(self.part.at[pl.ds(0, 2 * rows)], self.out, f, r)
            cp.gone(self.xsend, self.xout, f, r)

    def add_into(dst, doff, src, n):
        def step(t):
            s = at(doff + t * 16, 16)
            dst[s, :] = (dst[s, :].astype(F32) + src[at(t * 16, 16), :].astype(F32)).astype(BF16)

        loop(n // 16, step)

    class ColumnReduce:
        def __init__(self, grad, yr, zr, out, col, width):
            self.grad, self.yr, self.zr, self.out = grad, yr, zr, out
            self.col, self.width = col, width
            self.yrecv, self.zrecv, self.orecv = cp.recv(NZ), cp.recv(NZ + 1), cp.recv(2)
            self.ysend, self.zsend, self.osend = cp.send(), cp.send(), cp.send()
            self.lid = lid()
            for n, send in ((NZ, self.ysend), (NZ - 1, self.zsend), (3, self.osend)):
                cp.at_end(grad.at[pl.ds(0, n * sh)], send)

        def send(self, j):
            zz = lax.div(j, 2)
            cp.start(lambda: (self.grad.at[at(j * sh, sh)], self.yr.at[zz], self.ysend, self.yrecv + zz, yn, r))

        def add_y(self, j):
            zz = lax.div(j, 2)
            cp.arrived(self.yr.at[zz], self.yrecv + zz, f, r)
            add_into(self.grad, j * sh, self.yr.at[zz], sh)

        def chain(self, i):
            owner, up, there = by_z(*OWNERS[i]), by_z(*OWNER_ABOVE[i]), by_z(*OWNER_SLOT[i])
            j = 2 * owner + y
            self.add_y(j)

            @pl.when(inner)
            def _():
                cp.arrived(self.zr.at[owner], self.zrecv + owner, f, r)
                add_into(self.grad, j * sh, self.zr.at[owner], sh)

            cp.start(
                lambda: (
                    self.grad.at[at(j * sh, sh)], self.zr.at[there], self.zsend, self.zrecv + there,
                    f + 2 * (2 * up - 1), r,
                )
            )

        def final(self):
            self.add_y(f)
            for slot_, cond in ((z, z > 0), (NZ, z < NZ - 1)):

                @pl.when(cond)
                def _(slot_=slot_):
                    cp.arrived(self.zr.at[slot_], self.zrecv + slot_, f, r)
                    add_into(self.grad, f * sh, self.zr.at[slot_], sh)

            src = self.grad.at[at(f * sh, sh)]
            for i, to in enumerate((xn, cn)):
                cp.start(lambda i=i, to=to: (src, self.dst(r), self.osend, self.orecv + i, f, to))
            ends.append(local(src, self.dst(r), self.lid))

        def dst(self, q):
            return self.out.at[q, :, at(self.col, self.width, 128)]

        def relay(self):
            got = self.dst(xn)
            cp.arrived(got, self.orecv, f, r)
            cp.start(lambda: (got, got, self.osend, self.orecv + 1, f, cn))

        def done(self):
            cp.arrived(self.out.at[pl.ds(0, 2), :, at(self.col, self.width, 128)], self.orecv + 1, f, r)

        def register(self, *deps):
            steps = [task(*deps)(lambda i=i: self.chain(i)) for i in range(NZ - 1)]
            final = task(*deps)(self.final)
            task(final)(self.relay)

    class LongRowReduce:
        def __init__(self, grad, yr, zr, out, row, height, pitch):
            self.grad, self.yr, self.zr, self.out = grad, yr, zr, out
            self.row, self.height, self.pitch = row, height, pitch
            self.yrecv, self.zrecv, self.orecv = cp.recv(), cp.recv(2), cp.recv(2)
            self.ysend, self.zsend, self.osend = cp.send(), cp.send(), cp.send()
            self.lid = lid()
            one = self.grad.at[self.rows(y)]
            cp.at_end(one, self.ysend)
            cp.at_end(one, self.zsend, z != r)
            cp.at_end(self.grad.at[pl.ds(0, 2 * height)], self.osend, z == r)
            cp.at_end(one, self.osend, z == xn)

        def rows(self, yy):
            return at(yy * self.pitch + self.row, self.height)

        def send(self):
            cp.start(lambda: (self.grad.at[self.rows(1 - y)], self.yr, self.ysend, self.yrecv, yn, r))

        def add(self, way):
            cp.arrived(self.zr.at[way], self.zrecv + way, f, r)
            add_into(self.grad, y * self.pitch + self.row, self.zr.at[way], self.height)

        def chain(self):
            cp.arrived(self.yr, self.yrecv, f, r)
            add_into(self.grad, y * self.pitch + self.row, self.yr, self.height)
            src = self.grad.at[self.rows(y)]
            for way, (toward, behind, step) in enumerate(((z < r, z > 0, 2), (z > r, z < NZ - 1, -2))):

                @pl.when(jnp.logical_and(toward, behind))
                def _(way=way):
                    self.add(way)

                cp.start(
                    lambda way=way, step=step: (src, self.zr.at[way], self.zsend, self.zrecv + way, f + step, r), toward
                )

        def dst(self):
            return self.out.at[at(self.row, self.height)]

        def final(self):
            for way, cond in enumerate((z > 0, z < NZ - 1)):

                @pl.when(jnp.logical_and(z == r, cond))
                def _(way=way):
                    self.add(way)

            src = self.grad.at[self.rows(y)]
            for i, to in enumerate((xn, cn)):
                cp.start(lambda i=i, to=to: (src, self.dst(), self.osend, self.orecv + i, f, to), z == r)

            @pl.when(z == r)
            def _():
                local(src, self.dst(), self.lid)

        def relay(self):
            got = self.dst()

            @pl.when(z == xn)
            def _():
                cp.arrived(got, self.orecv, f, r)

            cp.start(lambda: (got, got, self.osend, self.orecv + 1, f, cn), z == xn)

        def done(self):
            @pl.when(jnp.logical_or(z == cn, z == dn))
            def _():
                cp.arrived(self.dst(), self.orecv + 1, f, r)

            @pl.when(z == r)
            def _():
                pltpu.make_async_copy(self.grad.at[self.rows(y)], self.dst(), k.locals.at[self.lid]).wait()

        def register(self, *deps):
            chain = task(*deps)(self.chain)
            task(task(chain)(self.final))(self.relay)

    class RowReduce:
        def __init__(self, grad, yr, zr, out, row, height, pitch):
            self.grad, self.yr, self.zr, self.out = grad, yr, zr, out
            self.row, self.height, self.pitch = row, height, pitch
            self.yrecv, self.zrecv, self.orecv = cp.recv(), cp.recv(4), cp.recv(2)
            self.ysend, self.zsend, self.osend = cp.send(), cp.send(2), cp.send()
            self.lid = lid()
            one = self.grad.at[self.rows(y)]
            cp.at_end(one, self.ysend, z == r)
            for n in range(2):
                cp.at_end(one, self.zsend + n, z != r)
            cp.at_end(self.grad.at[pl.ds(0, 2 * height)], self.osend, z == r)
            cp.at_end(one, self.osend, z == xn)

        def rows(self, yy):
            return at(yy * self.pitch + self.row, self.height)

        def add(self, yy, way):
            cp.arrived(self.zr.at[way, yy], self.zrecv + 2 * way + yy, f, r)
            add_into(self.grad, yy * self.pitch + self.row, self.zr.at[way, yy], self.height)

        def chain(self, far):
            yy = 1 - y if far else y
            src = self.grad.at[self.rows(yy)]
            for way, (toward, behind, step) in enumerate(((z < r, z > 0, 2), (z > r, z < NZ - 1, -2))):

                @pl.when(jnp.logical_and(toward, behind))
                def _(way=way):
                    self.add(yy, way)

                cp.start(
                    lambda way=way, step=step: (
                        src, self.zr.at[way, yy], self.zsend + far, self.zrecv + 2 * way + yy, f + step, r
                    ),
                    toward,
                )

        def gathered(self, yy):
            for way, cond in enumerate((z > 0, z < NZ - 1)):

                @pl.when(jnp.logical_and(z == r, cond))
                def _(way=way):
                    self.add(yy, way)

        def cross(self):
            self.gathered(1 - y)
            cp.start(lambda: (self.grad.at[self.rows(1 - y)], self.yr, self.ysend, self.yrecv, yn, r), z == r)

        def dst(self):
            return self.out.at[at(self.row, self.height)]

        def final(self):
            self.gathered(y)

            @pl.when(z == r)
            def _():
                cp.arrived(self.yr, self.yrecv, f, r)
                add_into(self.grad, y * self.pitch + self.row, self.yr, self.height)

            src = self.grad.at[self.rows(y)]
            for i, to in enumerate((xn, cn)):
                cp.start(lambda i=i, to=to: (src, self.dst(), self.osend, self.orecv + i, f, to), z == r)

            @pl.when(z == r)
            def _():
                local(src, self.dst(), self.lid)

        def relay(self):
            got = self.dst()

            @pl.when(z == xn)
            def _():
                cp.arrived(got, self.orecv, f, r)

            cp.start(lambda: (got, got, self.osend, self.orecv + 1, f, cn), z == xn)

        def done(self):
            @pl.when(jnp.logical_or(z == cn, z == dn))
            def _():
                cp.arrived(self.dst(), self.orecv + 1, f, r)

            @pl.when(z == r)
            def _():
                pltpu.make_async_copy(self.grad.at[self.rows(y)], self.dst(), k.locals.at[self.lid]).wait()

        def register(self, *deps):
            chains = [task(*deps)(lambda far=far: self.chain(far)) for far in (1, 0)]
            cross = task(*chains)(self.cross)
            task(task(cross)(self.final))(self.relay)

    class Deal:
        def __init__(self, src, dst):
            self.src, self.dst, self.recvs, self.sends = src, dst, cp.recv(micro), cp.send(micro)
            self.lid = lid(micro)
            self.local = {}
            for m in micros:
                cp.at_end(self.most(), self.sends + m)

        def most(self):
            return self.dst.at[pl.ds(0, (NF - 1) * part)]

        def start(self, m):
            dst = self.dst.at[at(m * slot + f * part, part)]
            for o in others:
                cp.start(lambda o=o: (self.src.at[m, o], dst, self.sends + m, self.recvs + m, o, r))
            self.local[m] = local(self.src.at[m, f], dst, self.lid + m)

        def done(self, m):
            cp.arrived(self.most(), self.recvs + m, f, r)
            self.local[m].wait()

    class Back:
        def __init__(self, src, dst):
            self.src, self.dst, self.recvs, self.sends = src, dst, cp.recv(micro), cp.send(micro)
            self.lid = lid(micro)
            for m in micros:
                cp.at_end(self.most(), self.sends + m)

        def most(self):
            return self.src.at[pl.ds(0, (NF - 1) * part)]

        def start(self, m):
            for o in others:
                cp.start(
                    lambda o=o: (
                        self.src.at[at(m * slot + o * part, part)], self.dst.at[m, f], self.sends + m, self.recvs + m, o, r
                    )
                )
            ends.append(local(self.src.at[at(m * slot + f * part, part)], self.dst.at[m, f], self.lid + m))

        def done(self):
            for m in micros:
                cp.arrived(self.dst.at[m, pl.ds(0, NF - 1)], self.recvs + m, f, r)

    count = iter(range(k.locals.shape[0]))

    def lid(n=1):
        first = next(count)
        for _ in range(n - 1):
            next(count)
        return first

    t2 = 2 * sz.tile
    hq = sz.hq
    third, half = sz.ffp // 3, sh // 2
    smalls, lens, gains = k.smalls, k.lens, k.gains
    aall, hall, call, yall = k.aall, k.hall, k.call, k.yall
    part_, gg, slope, dw, dqkv = k.part, k.gg, k.slope, k.dw, k.dqkv
    gd, gi, go, gq, dg = k.gd, k.gi, k.go, k.gq, k.dg
    xs, cs, hbuf, dhbuf, mx, gt = k.xs, k.cs, k.hbuf, k.dhbuf, k.mx, k.gt
    qkv, pbuf, obuf = k.qkv, k.pbuf, k.obuf
    g_q = [ColumnGather(wq, i * hq, hq) for i in range(3)]
    g_o = [RowGather(wo, i * half, half, sh) for i in range(2)]
    g_i = [ColumnGather(wi, col, w) for col, w in sz.units]
    g_d = [LongRowGather(wd, i * third, third, sz.ffp) for i in range(3)]
    r_d = [LongRowReduce(gd, k.yrd.at[i], k.zrd.at[i], k.rd, i * third, third, sz.ffp) for i in range(3)]
    r_i = [
        ColumnReduce(
            gi.at[:, pl.ds(col, w)], k.yri.at[n, :, :, pl.ds(0, w)], k.zri.at[n, :, :, pl.ds(0, w)], k.ri, col, w
        )
        for n, (col, w) in enumerate(sz.units)
    ]
    r_o = [RowReduce(go, k.yro.at[i], k.zro.at[i], k.ro, i * half, half, sh) for i in range(2)]
    r_q = [ColumnReduce(gq.at[n], k.yrq.at[n], k.zrq.at[n], k.rq, n * hq, hq) for n in range(3)]
    small_in, len_in, gs_in, gr_in = (cp.recv() for _ in range(4))
    small_out, len_out, gs_out, gr_out = (cp.send() for _ in range(4))
    cp.at_end(smalls.at[pl.ds(0, NF - 1)], small_out)
    cp.at_end(lens.at[pl.ds(0, NR - 1)], len_out)
    cp.at_end(k.gsend.at[pl.ds(0, NF - 1)], gs_out)
    cp.at_end(k.greps.at[pl.ds(0, NR - 1)], gr_out)
    deal_x, deal_c = Deal(k.tok, xs), Deal(k.cot, cs)
    back_m, back_t = Back(mx, k.o_mixed), Back(gt, k.o_gtok)
    e_a, e_c, e_h, e_y = Spread(aall), Spread(call), Spread(hall), Spread(yall)
    s_1 = Sum(part_, k.sib0, k.xsend, k.xrecv0)
    s_m = Sum(k.part2, k.sib1, k.xsend2, k.xrecv1)
    s_h = Sum(part_, k.sib0, k.xsend, k.xrecv0)
    s_a = Sum(part_, k.sib0, k.xsend, k.xrecv0)
    blocks = [dn, xn, cn, r]

    lane = lax.broadcasted_iota(jnp.int32, (1, 128), 1)
    front = lax.rem(lane, 64) < 32
    low = lane < 64
    low_b = low.astype(F32).astype(BF16)
    high_b = (1.0 - low.astype(F32)).astype(BF16)
    npair = hq // 128
    scale = 64 ** (-0.5)
    tile_ = sz.tile
    NL = 32

    def live(m, t, n):
        pos = lax.broadcasted_iota(jnp.int32, (n, 1), 0) + t * n
        return pos.astype(F32) < lens[r, m : m + 1, 0:1]

    def normed(v):
        center = v - jnp.mean(v, axis=-1, keepdims=True)
        root = lax.rsqrt(jnp.mean(center * center, axis=-1, keepdims=True) + NORM_EPS)
        return center * root, root

    def norm_back(dy, gain, vhat, root):
        e = dy * gain
        return root * (e - jnp.mean(e, axis=-1, keepdims=True) - vhat * jnp.mean(e * vhat, axis=-1, keepdims=True))

    def swap(v):
        return jnp.where(front, pltpu.roll(v, 96, 1), pltpu.roll(v, 32, 1))

    def both(v):
        return jnp.concatenate([v * low_b, v * high_b], axis=0)

    def joined(v):
        return jnp.where(low, v[:slot], v[slot:])

    def fold(v):
        return jnp.sum(v.reshape(NL // 8, 8, d), axis=0)

    def triple(s, p):
        return [qkv[at(s * slot, slot), i * hq + p * 128 : i * hq + (p + 1) * 128] for i in range(3)]

    mini = k.mini
    mini[...] = jnp.zeros_like(mini)
    mini[0:1, :] = k.g1[...].astype(BF16).astype(F32)
    mini[1:2, :] = k.g2[...].astype(BF16).astype(F32)
    for m in micros:
        mini[2:3, :] += jnp.where(lane == m, k.len[0:1, m : m + 1].astype(F32), 0.0)
    smalls[f] = mini[...]
    qf, of = k.hbuf.at[pl.ds(0, sh)], k.hbuf.at[pl.ds(sh, sh)]
    q_in = [local(k.fq.at[:, at(i * d + r * hq, hq, 128)], qf.at[:, pl.ds(i * hq, hq)], lid()) for i in range(3)]
    o_lid, i_in, d_lid = lid(), [], lid()
    mine = z == r
    df = k.part2.at[pl.ds(0, sz.ffs)]

    @pl.when(mine)
    def _():
        local(k.fo, of, o_lid)

    shifts = []
    for i in range(2):
        first = i * NF * sz.ffs + r * 2 * sz.ffs
        base = lax.div(first, 128) * 128
        shifts.append(first - base)
        i_in.append(local(k.fi.at[:, at(base, sz.fq, 128)], k.dhbuf.at[pl.ds(i * sh, sh), pl.ds(0, sz.fq)], lid()))

    @pl.when(mine)
    def _():
        local(k.fd, df, d_lid)

    @task()
    def met():
        pl.semaphore_wait(barrier, len(friends))
        for o in others:
            cp.start(lambda o=o: (mini, smalls.at[f], small_out, small_in, o, r))

    @task()
    def prepare_q():
        for copy in q_in:
            copy.wait()

        def cast_q(t):
            wq[at(f * sh + t * 32, 32), :] = qf[at(t * 32, 32), pl.ds(0, 3 * hq)].astype(BF16)

        loop(sh // 32, cast_q)

    @task()
    def prepare_o():
        @pl.when(mine)
        def _():
            pltpu.make_async_copy(k.fo, of, k.locals.at[o_lid]).wait()

            def cast_o(t):
                wo[at(y * sh + t * 32, 32), :] = of[at(t * 32, 32), :].astype(BF16)

            loop(sh // 32, cast_o)

    @task()
    def prepare_i():
        for i in range(2):
            i_in[i].wait()
        lane_f = lax.broadcasted_iota(jnp.int32, (1, sz.fq), 1)
        first = lane_f < sz.ffs
        second = jnp.logical_and(lane_f >= sz.ffp, lane_f < sz.ffp + sz.ffs)

        def cast_i(t):
            halves = []
            for i in range(2):
                v = k.dhbuf[at(i * sh + t * 32, 32), pl.ds(0, sz.fq)]
                v = pltpu.roll(v, lax.rem(sz.fq - shifts[i], sz.fq), 1)
                halves.append(jnp.where(first, v, jnp.where(second, pltpu.roll(v, sz.ffp - sz.ffs, 1), 0.0)))
            for n, (col, w) in enumerate(sz.units):
                one, two = [v[:, n * tile_ : (n + 1) * tile_] for v in halves]
                wi[at(f * sh + t * 32, 32), pl.ds(col, w)] = side_by_side(sz, n, one, two).astype(BF16)

        loop(sh // 32, cast_i)

    @task()
    def prepare_d():
        @pl.when(mine)
        def _():
            pltpu.make_async_copy(k.fd, df, k.locals.at[d_lid]).wait()

            def cast_d(t):
                wd[at(y * sz.ffp + t * 16, 16), :] = df[at(t * 16, 16), :].astype(BF16)

            loop(sz.ffs // 16, cast_d)
            left = sz.ffs % 16
            if left:
                v = df[pl.ds(sz.ffs - left, left), :]
                v = jnp.concatenate([v, jnp.zeros((sz.ffp - sz.ffs, d), F32)], axis=0)
                wd[at(y * sz.ffp + sz.ffp - 16, 16), :] = v.astype(BF16)

    for u in g_q:
        u.register(met, prepare_q)
    for u in g_o:
        u.register(met, prepare_o)
    for u in g_i:
        u.register(met, prepare_i)
    for u in g_d:
        u.register(met, prepare_d)
    q_needs, o_needs, i_needs, d_needs = [[n for u in g for n in u.needs] for g in (g_q, g_o, g_i, g_d)]

    @task()
    def zero():
        wd[pl.ds(2 * sz.ffp, sz.fq - 2 * sz.ffp), :] = jnp.zeros((sz.fq - 2 * sz.ffp, d), BF16)
        dg[...] = jnp.zeros_like(dg)

    deals = [task(met)(lambda m=m: deal_x.start(m)) for m in micros]

    @task(met)
    def small():
        cp.arrived(smalls.at[pl.ds(0, NF - 1)], small_in, f, r)
        for j in range(NF):
            gains[0:2, j * sh : (j + 1) * sh] = smalls[j, 0:2, :]
        sub = lax.broadcasted_iota(jnp.int32, (NF, 128), 0)
        row8 = lax.broadcasted_iota(jnp.int32, (8, 128), 0)
        lane8 = lax.broadcasted_iota(jnp.int32, (1, NF), 1)
        len_tab = smalls[:, 2, :]
        table = jnp.zeros((8, 128), F32)
        for m in micros:
            dealt = jnp.where(lane8 == f, k.deal[m : m + 1, :].astype(F32), 0.0)
            dealt = jnp.sum(dealt, axis=1, keepdims=True)
            col = jnp.sum(jnp.where(sub.astype(F32) == dealt, len_tab, 0.0), axis=0, keepdims=True)
            length = jnp.sum(jnp.where(lane == m, col, 0.0), axis=1, keepdims=True)
            table = jnp.where(row8 == m, length, table)
        lens[r] = table
        for to in (xn, dn, cn):
            cp.start(lambda to=to: (lens.at[r], lens.at[r], len_out, len_in, f, to))

    @task(small)
    def lengths():
        cp.arrived(lens.at[pl.ds(0, NR - 1)], len_in, f, r)

    norm1s = []
    for m in micros:

        @task(small, deals[m])
        def step(m=m):
            deal_x.done(m)

            def norm1(t):
                vhat, _ = normed(xs[at(m * slot + t * NL, NL), :].astype(F32))
                aall[at(r * rows + m * slot + t * NL, NL), :] = (vhat * gains[0:1, :]).astype(BF16)

            loop(slot // NL, norm1)
            e_a.start(m)

        norm1s.append(step)
    e_a.register(norm1s)

    def project(b):
        a = aall[block(b), :]
        for i in range(3):
            t = nn(a, wq[:, i * hq : (i + 1) * hq])
            for p in range(npair):
                v = t[:, p * 128 : (p + 1) * 128]
                for m in micros:
                    u = v[m * slot : (m + 1) * slot]
                    if i < 2:
                        u = u * k.cos[...] + swap(u) * k.sin[...]
                    qkv[at(b * rows + m * slot, slot), i * hq + p * 128 : i * hq + (p + 1) * 128] = u.astype(BF16)

    def attend(b):
        def attend_one(m):
            s = b * micro + m
            length = lens[b, pl.ds(m, 1), :]
            for p in range(npair):
                q_, k_, v_ = triple(s, p)
                scores = nt(both(q_), k_) * scale
                scores = jnp.where(lane.astype(F32) < length, scores, -1e30)
                e = jnp.exp(scores - jnp.max(scores, axis=-1, keepdims=True))
                prob = e / jnp.sum(e, axis=-1, keepdims=True)
                pbuf[s, p] = prob
                out = nn(prob.astype(BF16), v_)
                obuf[at(s * slot, slot), p * 128 : (p + 1) * 128] = joined(out).astype(BF16)

        loop(micro, attend_one)

    def branch_one(b):
        def branch_tile(n):
            cols = at(n * 256, 256, 128)
            part_[block(b), cols] = nn(obuf[block(b), :], wo[:, cols])

        loop(d // 256, branch_tile)

    firsts = []
    for w in range(NR):

        @task(*e_a.need[w], *q_needs)
        def projected(w=w):
            project(blocks[w])

        @task(projected, lengths, *o_needs)
        def attended(w=w):
            attend(blocks[w])
            branch_one(blocks[w])
            s_1.ready(w)

        firsts.append(attended)
    crossed = task(firsts[DN], firsts[XN])(s_1.over_x)

    masks = []
    for m in micros:
        dealt = task(met)(lambda m=m: deal_c.start(m))

        @task(dealt, small)
        def step(m=m):
            deal_c.done(m)

            def mask_c(t):
                s = at(m * slot + t * NL, NL)
                masked = jnp.where(live(m, t, NL), cs[s, :].astype(F32), 0.0)
                call[at(r * rows + m * slot + t * NL, NL), :] = masked.astype(BF16)

            loop(slot // NL, mask_c)

        masks.append(step)

    @task(*masks)
    def spread_c():
        for m in micros:
            e_c.start(m)

    e_c.register([spread_c])

    norm2s = []
    for m in micros:

        @task(crossed, *firsts, *norm2s)
        def step(m=m):
            s_1.done(m)

            def norm2(t):
                row = m * slot + t * NL
                s = at(row, NL)
                h = xs[s, :].astype(F32) + jnp.where(live(m, t, NL), s_1.value(row, NL), 0.0)
                hbuf[s, :] = h
                vhat, _ = normed(h)
                hall[at(r * rows + row, NL), :] = (vhat * gains[1:2, :]).astype(BF16)

            loop(slot // NL, norm2)
            e_h.start(m)

        norm2s.append(step)
    freed = task(*norm2s)(s_1.free)
    e_h.register(norm2s)

    feeds = []
    for w in range(NR):

        @task(freed, *e_h.need[w], *i_needs)
        def step(w=w):
            rs = block(blocks[w])

            def feed(n):
                col, w = sz.units[n]
                w1, w2 = apart(sz, n, nn(hall[rs, :], wi[:, pl.ds(col, w)]))
                cdf = 0.5 * (1.0 + lax.erf(w1 * (0.5**0.5)))
                act = w1 * cdf
                pdf = jnp.exp(-0.5 * w1 * w1) * 0.3989422804014327
                cols = pl.ds(n * tile_, tile_)
                gg[rs, cols] = (act * w2).astype(BF16)
                part_[rs, cols] = act
                slope[rs, cols] = w2 * (cdf + w1 * pdf)

            for n in range(sz.ntile):
                once(n, feed)

        feeds.append(step)

    @task(*feeds, *e_c.all)
    def gdown():
        def grad_down(i):
            m, n = lax.div(i, 2), lax.rem(i, 2)
            cols = at(n * (d // 2), d // 2, 128)
            gd[at(m * 256, 256), cols] = tn(gg[:, at(m * 256, 256, 128)], call[:, cols]).astype(BF16)

        loop(sz.fq // 256 * 2, grad_down)
        for u in r_d:
            u.send()

    hids = []
    for w in range(NR):

        @task(feeds[w], zero, *e_c.need[w], *d_needs)
        def step(w=w):
            rs = block(blocks[w])

            def hidden(n):
                cols = pl.ds(n * tile_, tile_)
                dgg = nt(call[rs, :], wd[pl.ds(n * tile_, tile_), :])
                v = side_by_side(sz, n, dgg * slope[rs, cols], dgg * part_[rs, cols])
                dw[rs, pl.ds(*sz.units[n])] = v.astype(BF16)

            for n in range(sz.ntile):
                once(n, hidden)

        hids.append(step)

    gins = []
    for n in range(sz.ntile):
        for which in range(2):

            @task(*hids, *e_h.all)
            def step(n=n, which=which):
                def grad_in(i):
                    j = 2 * i + (y if which else 1 - y)
                    cols = pl.ds(*sz.units[n])
                    gi[at(j * sh, sh), cols] = tn(hall[:, at(j * sh, sh, 128)], dw[:, cols]).astype(BF16)

                loop(NZ, grad_in)
                if not which:
                    for owner in order_z:
                        r_i[n].send(2 * owner + 1 - y)

            gins.append(step)

    dhns = []
    for w in range(NR):

        @task(hids[w])
        def step(w=w):
            b = blocks[w]

            def dhn_tile(n):
                part_[block(b), at(n * 256, 256, 128)] = nt(dw[block(b), :], wi[at(n * 256, 256), :])

            loop(d // 256, dhn_tile)
            s_h.ready(w)

        dhns.append(step)
    crossed = task(dhns[DN], dhns[XN])(s_h.over_x)
    back2s = []
    for m in micros:

        @task(crossed, zero, *dhns, *back2s)
        def step(m=m):
            s_h.done(m)

            def back2(t):
                row = m * slot + t * NL
                s = at(row, NL)
                dy = s_h.value(row, NL)
                vhat, root = normed(hbuf[s, :])
                dg[1] += fold(dy * vhat)
                dh = cs[s, :].astype(F32) + norm_back(dy, gains[1:2, :], vhat, root)
                dhbuf[s, :] = dh
                yall[at(r * rows + row, NL), :] = jnp.where(live(m, t, NL), dh, 0.0).astype(BF16)

            loop(slot // NL, back2)
            e_y.start(m)

        back2s.append(step)
    freed = task(*back2s)(s_h.free)
    e_y.register(back2s)

    mixes = []
    for w in range(NR):

        @task(zero, feeds[w], *d_needs)
        def step(w=w):
            b = blocks[w]

            def mix_tile(n):
                cols = at(n * 256, 256, 128)
                k.part2[block(b), cols] = nn(gg[block(b), :], wd[:, cols])

            loop(d // 256, mix_tile)
            s_m.ready(w)

        mixes.append(step)
    crossed = task(mixes[DN], mixes[XN])(s_m.over_x)
    mixeds = []
    for m in micros:

        @task(crossed, *mixes, *mixeds)
        def step(m=m):
            s_m.done(m)

            def mix(t):
                row = m * slot + t * NL
                s = at(row, NL)
                mx[s, :] = (hbuf[s, :] + jnp.where(live(m, t, NL), s_m.value(row, NL), 0.0)).astype(BF16)

            loop(slot // NL, mix)

        mixeds.append(step)
        task(step)(lambda m=m: back_m.start(m))

    @task(*firsts, *e_y.all)
    def gout():
        def grad_out(i):
            cols = at(i * 256, 256, 128)
            go[:, cols] = tn(obuf[...], yall[:, cols]).astype(BF16)

        loop(d // 256, grad_out)

    abacks = []
    for w in range(NR):

        @task(firsts[w], *e_y.need[w])
        def step(w=w):
            def attend_back(m):
                s = blocks[w] * micro + m
                do_all = nt(yall[at(s * slot, slot), :], wo[...]).astype(BF16)
                for p in range(npair):
                    q_, k_, v_ = triple(s, p)
                    q2, do2 = both(q_), both(do_all[:, p * 128 : (p + 1) * 128])
                    prob = pbuf[s, p]
                    dp = nt(do2, v_)
                    ds = (prob * (dp - jnp.sum(dp * prob, axis=-1, keepdims=True))).astype(BF16)
                    dq = joined(nn(ds, k_)) * scale
                    dk = tn(ds, q2) * scale
                    dv = tn(prob.astype(BF16), do2)
                    cosine, sine = k.cos[...], k.sin[...]
                    dq = dq * cosine - swap(dq) * sine
                    dk = dk * cosine - swap(dk) * sine
                    for i, v in enumerate((dq, dk, dv)):
                        dqkv[at(s * slot, slot), i * hq + p * 128 : i * hq + (p + 1) * 128] = v.astype(BF16)

            loop(micro, attend_back)

        abacks.append(step)

    gqkvs = []
    for which in range(2):

        @task(*abacks, *e_a.all)
        def step(which=which):
            def grad_qkv(i):
                j = 2 * i + (y if which else 1 - y)
                g = tn(aall[:, at(j * sh, sh, 128)], dqkv[...]).astype(BF16)
                for n in range(3):
                    gq[n, at(j * sh, sh), :] = g[:, n * hq : (n + 1) * hq]

            loop(NZ, grad_qkv)
            if not which:
                for n in range(3):
                    for owner in order_z:
                        r_q[n].send(2 * owner + 1 - y)

        gqkvs.append(step)

    das = []
    for w in range(NR):

        @task(abacks[w], freed)
        def step(w=w):
            b = blocks[w]

            def da_tile(n):
                part_[block(b), at(n * 256, 256, 128)] = nt(dqkv[block(b), :], wq[at(n * 256, 256), :])

            loop(d // 256, da_tile)
            s_a.ready(w)

        das.append(step)
    crossed = task(das[DN], das[XN])(s_a.over_x)
    back1s = []
    for m in micros:

        @task(crossed, *das, *back1s)
        def step(m=m):
            s_a.done(m)

            def back1(t):
                row = m * slot + t * NL
                s = at(row, NL)
                dy = s_a.value(row, NL)
                vhat, root = normed(xs[s, :].astype(F32))
                dg[0] += fold(dy * vhat)
                gt[s, :] = (dhbuf[s, :] + norm_back(dy, gains[0:1, :], vhat, root)).astype(BF16)

            loop(slot // NL, back1)
            back_t.start(m)

        back1s.append(step)

    gsend, gslots, greps, gout_ = k.gsend, k.gslots, k.greps, k.gout

    @task(*back1s, *back2s)
    def gain_parts():
        for which in range(2):
            total = jnp.sum(dg[which], axis=0, keepdims=True)
            for j in range(NF):
                gsend[j, which : which + 1, :] = total[:, j * sh : (j + 1) * sh]
        for o in others:
            cp.start(lambda o=o: (gsend.at[o], gslots.at[f], gs_out, gs_in, o, r))
        gslots[f] = gsend[f]

    @task(gain_parts)
    def gain_sums():
        cp.arrived(gslots.at[pl.ds(0, NF - 1)], gs_in, f, r)
        total = gslots[0]
        for j in range(1, NF):
            total = total + gslots[j]
        greps[r] = total
        for to in (xn, dn, cn):
            cp.start(lambda to=to: (greps.at[r], greps.at[r], gr_out, gr_in, f, to))

    glid = lid()

    @task(gain_sums)
    def gain_totals():
        cp.arrived(greps.at[pl.ds(0, NR - 1)], gr_in, f, r)
        gout_[...] = greps[0] + greps[1] + greps[2] + greps[3]
        ends.append(local(gout_, k.o_small, glid))

    for u in r_d:
        u.register(gdown)
    for n, u in enumerate(r_i):
        u.register(*gins[2 * n : 2 * n + 2])
    for u in r_o:
        u.register(gout)
    for u in r_q:
        u.register(*gqkvs)

    @task(*range(len(tasks)))
    def end():
        for u in r_d + r_i + r_o + r_q + [back_m, back_t]:
            u.done()
        s_a.free()
        s_m.free()
        for e in (e_a, e_c, e_h, e_y):
            e.free()
        for ref, send, cond in cp.left:
            cp.gone(ref, send, f, r, cond)
        for copy in ends:
            copy.wait()

    run_tasks(tasks)


def fused(sz, tok, cot, g1, g2, length, deal, cos, sin, fq, fo, fi, fd):
    d, sh, all_, rows = sz.d, sz.shard, sz.all, sz.rows
    t2 = 2 * sz.tile
    third, half = sz.ffp // 3, sh // 2
    hq3 = 3 * sz.hq
    bf = lambda *s: pltpu.VMEM(s, BF16)
    fl = lambda *s: pltpu.VMEM(s, F32)
    ins = dict(tok=tok, cot=cot, g1=g1, g2=g2, len=length, deal=deal, cos=cos, sin=sin, fq=fq, fo=fo, fi=fi, fd=fd)
    outs = dict(
        o_mixed=jax.ShapeDtypeStruct((sz.micro, NF, sz.part, d), BF16),
        o_gtok=jax.ShapeDtypeStruct((sz.micro, NF, sz.part, d), BF16),
        o_small=jax.ShapeDtypeStruct((8, 128), F32),
        rq=jax.ShapeDtypeStruct((NR, sh, hq3), BF16),
        ro=jax.ShapeDtypeStruct((sh, d), BF16),
        ri=jax.ShapeDtypeStruct((NR, sh, sz.iw), BF16),
        rd=jax.ShapeDtypeStruct((sz.ffp, d), BF16),
    )
    scratch = dict(
        wq=bf(d, hq3), wo=bf(2 * sh, d), wi=bf(d, sz.iw), wd=bf(sz.fq, d),
        xs=bf(rows, d), cs=bf(rows, d), mx=bf(rows, d), gt=bf(rows, d),
        aall=bf(all_, d), hall=bf(all_, d), call=bf(all_, d), yall=bf(all_, d),
        smalls=fl(NF, 8, 128), mini=fl(8, 128), lens=fl(NR, 8, 128), gains=fl(8, d),
        qkv=bf(all_, hq3), pbuf=fl(NR * sz.micro, sz.hq // 128, 2 * sz.slot, 128), obuf=bf(all_, sz.hq),
        part=fl(all_, d), part2=fl(all_, d), sib0=fl(2, rows, d), sib1=fl(2, rows, d),
        xsend=bf(rows, d), xsend2=bf(rows, d), xrecv0=bf(rows, d), xrecv1=bf(rows, d),
        hbuf=fl(rows, d), dhbuf=fl(rows, d), dg=fl(2, 8, d),
        gg=bf(all_, sz.fq), slope=fl(all_, sz.fq), dw=bf(all_, sz.iw), dqkv=bf(all_, hq3),
        gd=bf(sz.fq, d), gi=bf(d, sz.iw), go=bf(2 * sh, d), gq=bf(3, d, sz.hq),
        yrd=bf(3, third, d), zrd=bf(3, 2, third, d),
        yri=bf(sz.ntile, NZ, sh, t2), zri=bf(sz.ntile, NZ + 1, sh, t2),
        yro=bf(2, half, d), zro=bf(2, 2, 2, half, d),
        yrq=bf(3, NZ, sh, sz.hq), zrq=bf(3, NZ + 1, sh, sz.hq),
        gsend=fl(NF, 8, 128), gslots=fl(NF, 8, 128), greps=fl(NR, 8, 128), gout=fl(8, 128),
        sends=pltpu.SemaphoreType.DMA((90,)), recvs=pltpu.SemaphoreType.DMA((187,)),
        locals=pltpu.SemaphoreType.DMA((32,)),
    )
    any_ = pl.BlockSpec(memory_space=pl.ANY)
    vmem = pl.BlockSpec(memory_space=pltpu.VMEM)
    names = (*ins, *outs, *scratch)
    return pl.pallas_call(
        functools.partial(kernel, sz, names),
        out_shape=list(outs.values()),
        in_specs=[any_] * 2 + [vmem] * 6 + [any_] * 4,
        out_specs=[any_] * len(outs),
        scratch_shapes=list(scratch.values()),
        compiler_params=pltpu.CompilerParams(collective_id=0, has_side_effects=True, vmem_limit_bytes=64 * MIB),
    )(*ins.values())


def finish_kernel(sz, small, mixed, gtok, rq, ro, ri, rd, out_m, out_t, g1, gq, go, g2, gi, gd):
    hq, ffs, ffp = sz.hq, sz.ffs, sz.ffp
    for i in range(3):
        for q in range(NR):
            gq[:, i * sz.d + q * hq : i * sz.d + (q + 1) * hq] = rq[q, :, i * hq : (i + 1) * hq].astype(F32)
    g1[...], g2[...] = small[0:1, :], small[1:2, :]
    out_m[...], out_t[...] = mixed[...], gtok[...]
    go[...] = ro[...].astype(F32)
    gd[...] = rd[...].astype(F32)
    pieces = [[], []]
    for q in range(NR):
        tiles = [apart(sz, n, ri[q, :, col : col + w].astype(F32)) for n, (col, w) in enumerate(sz.units)]
        for i in range(2):
            v = jnp.concatenate([two[i] for two in tiles], axis=1)
            pieces[i] += [v[:, :ffs], v[:, ffp : ffp + ffs]]
    gi[...] = jnp.concatenate(pieces[0] + pieces[1], axis=1)


def finish(sz, small, mixed, gtok, rq, ro, ri, rd):
    d, sh = sz.d, sz.shard
    grain = 64
    steps, n = sh // grain, sz.ffp // 16
    down = -(-n // steps) * 16
    last = -(-sz.ffp // down) - 1
    row = lambda w: pl.BlockSpec((grain, w), lambda i: (i, 0))
    low = pl.BlockSpec((down, d), lambda i: (jnp.minimum(i, last), 0))
    rows = sz.micro * NF * sz.part // steps
    each = pl.BlockSpec((rows, d), lambda i: (i, 0))
    one = lambda n: pl.BlockSpec((n, sh), lambda i: (0, 0))
    quarters = lambda w: pl.BlockSpec((NR, grain, w), lambda i: (0, i, 0))
    return pl.pallas_call(
        functools.partial(finish_kernel, sz),
        grid=(steps,),
        out_shape=[
            jax.ShapeDtypeStruct((rows * steps, d), BF16),
            jax.ShapeDtypeStruct((rows * steps, d), BF16),
            jax.ShapeDtypeStruct((1, sh), F32),
            jax.ShapeDtypeStruct((sh, 3 * d), F32),
            jax.ShapeDtypeStruct((sh, d), F32),
            jax.ShapeDtypeStruct((1, sh), F32),
            jax.ShapeDtypeStruct((sh, 2 * NF * sz.ffs), F32),
            jax.ShapeDtypeStruct((sz.ffs, d), F32),
        ],
        in_specs=[one(8), each, each, quarters(rq.shape[2]), row(d), quarters(ri.shape[2]), low],
        out_specs=[each, each, one(1), row(3 * d), row(d), one(1), row(2 * NF * sz.ffs), low],
        compiler_params=pltpu.CompilerParams(vmem_limit_bytes=60 * MIB),
    )(small, mixed.reshape(-1, d), gtok.reshape(-1, d), rq, ro, ri, rd)


def routed(tokens, cotangent, deal, lengths, ln1_gain, w_qkv, w_out, ln2_gain, w_in, w_down):
    micro, _, part, d = tokens.shape
    ffs = w_down.shape[0]
    sz = Sizes(micro, part, d, ffs)
    half = d // HEADS // 2
    freq = np.float32(ROPE_BASE) ** (-(np.arange(half, dtype=np.float32) * np.float32(2.0 / (2 * half))))
    angles = np.arange(sz.slot, dtype=np.float32)[:, None] * freq[None, :]
    cos = jnp.asarray(np.tile(np.cos(angles), (1, 4)))
    sin = jnp.asarray(np.tile(np.concatenate([-np.sin(angles), np.sin(angles)], axis=1), (1, 2)))
    mixed, gtok, osmall, rq, ro, ri, rd = fused(
        sz, tokens, cotangent, ln1_gain[None], ln2_gain[None], lengths.reshape(1, micro), deal[:, 0],
        cos, sin, w_qkv, w_out, w_in, w_down,
    )
    mixed, gtok, g_1, g_qkv, g_out, g_2, g_in, g_down = finish(sz, osmall, mixed, gtok, rq, ro, ri, rd)
    return mixed.reshape(tokens.shape), gtok.reshape(tokens.shape), g_1[0], g_qkv, g_out, g_2[0], g_in, g_down


def solution(mesh):
    small = mesh.shape["fsdp"] == NF and mesh.shape["rep"] == NR
    rows = P(None, "rep", "fsdp", None)
    return jax.shard_map(
        routed if small else plain,
        mesh=mesh,
        in_specs=(
            rows, rows, P(None, "rep", None), P(None, "rep", "fsdp"),
            P("fsdp"), P("fsdp", None), P("fsdp", None), P("fsdp"), P("fsdp", None), P("fsdp", None),
        ),
        out_specs=(rows, rows, P("fsdp"), P("fsdp", None), P("fsdp", None), P("fsdp"), P("fsdp", None), P("fsdp", None)),
        check_vma=False,
    )
```
